32 devices in a mesh: section: 2 (over core), dp: 4 (over y, x), tensor: 4 (over z).
Axes of the slice: x: 2, y: 2, z: 4, core: 2. Of those that a mesh axis runs over, the one named last changes fastest.
Arguments:
- codes: bfloat16 [8, 256, 3, 1024], P('dp', 'tensor'), may hold values from -4 to 4
- lengths: int32 [8], P('dp'), may hold values from 33 to 256, as said below
- gains: float32 [2, 2, 1024], P('section'), may hold values from 0.5 to 1.5
- w_qkv: bfloat16 [2, 1024, 3, 1024], P('section', None, None, 'tensor'), may hold values from -0.1875 to 0.1875
- w_out: bfloat16 [2, 1024, 1024], P('section', 'tensor'), may hold values from -0.5 to 0.5
- w_up: bfloat16 [2, 1024, 4096], P('section', None, 'tensor'), may hold values from -0.1875 to 0.1875
- w_down: bfloat16 [2, 4096, 1024], P('section', 'tensor'), may hold values from -0.09375 to 0.09375
- cotangent: bfloat16 [8, 256, 3, 1024], P('dp', 'tensor'), may hold values from -6 to 6
Outputs:
- output: bfloat16 [8, 256, 3, 1024], P('dp', 'tensor', None, 'section')
- code_grad: float32 [8, 256, 3, 1024], P('dp', 'tensor', None, 'section')
- gain_grad: float32 [2, 2, 1024], P('section')
- qkv_grad: float32 [2, 1024, 3, 1024], P('section', None, None, 'tensor')
- out_grad: float32 [2, 1024, 1024], P('section', 'tensor')
- up_grad: float32 [2, 1024, 4096], P('section', None, 'tensor')
- down_grad: float32 [2, 4096, 1024], P('section', 'tensor')
The draws below stay inside these ranges and needn't reach their ends.
Inputs may be any that keep to these rules, and one draw needn't show every extreme that they name: `lengths`: each utterance's valid frames come first; in every draw some utterance has all 256 frames valid.
All inputs are finite; a program needn't handle non-finite values.
Results may differ from the reference program's by a relative error of at most 0.017.
Values may be sent and summed in bfloat16 or wider, within the bound.
No kernel may reach another device: no remote copies, remote signals or barrier semaphores. Data moves between devices by JAX's collectives and lax.ppermute only.
A program may use at most 256 MiB of HBM per device.

```python
import jax
import jax.numpy as jnp
from jax import lax

D = 1024
HEADS = 16
HEAD_DIM = 64
FF = 4096
CODES = 3
UTT_LEN = 256
UTTS = 8


def draw_lengths(key, part):
    key = jax.random.fold_in(key, 7)
    first_key, second_key = jax.random.split(key)
    drawn = jax.random.randint(first_key, (UTTS,), UTT_LEN // 8 + 1, UTT_LEN + 1)
    chosen = jax.random.randint(second_key, (), 0, UTTS)
    return jnp.where(jnp.arange(UTTS) == chosen, UTT_LEN, drawn).astype(jnp.int32)


def steps_of(rng, dims, pieces, low, high):
    def one(position, shards_of):
        draws = jax.random.uniform(jax.random.fold_in(jax.random.fold_in(rng, 6), position), (shards_of,), jnp.float32, low / len(pieces), high / len(pieces))
        return jnp.repeat(jnp.exp(draws), dims[position] // shards_of).reshape((-1,) + (1,) * (len(dims) - position - 1))

    loudness = one(*pieces[0])
    for cut in pieces[1:]:
        loudness = loudness * one(*cut)
    return loudness


def scatter_about(own_key, dims, spread, limit, shards=(), held_as=jnp.bfloat16):
    values = spread * jax.random.normal(own_key, dims, jnp.float32)
    if shards:
        values = values * steps_of(own_key, dims, shards, -0.22, 0.18)
    return jnp.clip(values, -limit, limit).astype(held_as)


def setup_inputs(seed: int = 0) -> dict:
    key_list = jax.random.split(jax.random.key(seed), 9)
    return {
        "codes": scatter_about(key_list[0], (UTTS, UTT_LEN, CODES, D), 0.6, 4.0, ((0, 4), (1, 4))),
        "lengths": draw_lengths(jax.random.fold_in(key_list[8], 71), 0),
        "gains": jnp.clip(1.0 + 0.1 * jax.random.normal(key_list[2], (2, 2, D), jnp.float32), 0.5, 1.5),
        "w_qkv": scatter_about(key_list[3], (2, D, 3, D), D ** -0.5, 0.1875, ((0, 2), (3, 4))),
        "w_out": scatter_about(key_list[4], (2, D, D), (D // 8) ** -0.5, 0.5, ((0, 2), (1, 4))),
        "w_up": scatter_about(key_list[5], (2, D, FF), D ** -0.5, 0.1875, ((0, 2), (2, 4))),
        "w_down": scatter_about(key_list[6], (2, FF, D), FF ** -0.5, 0.09375, ((0, 2), (1, 4))),
        "cotangent": scatter_about(key_list[7], (UTTS, UTT_LEN, CODES, D), 1.0, 6.0, ((0, 4), (1, 4))),
    }


@jax.custom_vjp
def low(v):
    return lax.optimization_barrier(v.astype(jnp.bfloat16)).astype(jnp.float32)

@jax.custom_vjp
def low_back(v):
    return v

def low_keep(v):
    return (low(v), None)

def low_pass(kept, grad):
    return (grad,)

def back_keep(v):
    return (v, None)

def back_low(kept, grad):
    return (low(grad),)
low.defvjp(low_keep, low_pass)
low_back.defvjp(back_keep, back_low)
epsilon = 1e-06
highest = lax.Precision.HIGHEST

def normalized(values, gain_vector):
    factor = lax.rsqrt(lax.optimization_barrier(jnp.mean(values * values, axis=-1, keepdims=True)) + epsilon)
    return values * factor * gain_vector

def attention(shaped, allowed):
    queries = shaped[:, :, 0]
    key_rows = shaped[:, :, 1]
    value_rows = shaped[:, :, 2]
    scores = low_back(jnp.einsum('gqhd,gkhd->ghqk', queries, key_rows, precision=highest) * HEAD_DIM ** (-0.5))
    scores = jnp.where(allowed[:, None], scores, -1e+30)
    weights = low(jax.nn.softmax(scores, axis=-1))
    mixed = jnp.einsum('ghqk,gkhd->gqhd', weights, value_rows, precision=highest)
    return low(low_back(mixed))

def block(start, gain_pair, w_query, w_mix, w_lift, w_drop, span, allowed):
    row_count = start.shape[0]
    first_norm = low(normalized(start, gain_pair[0]))
    packed = low(low_back(jnp.einsum('rd,dce->rce', first_norm, w_query, precision=highest)))
    shaped = packed.reshape(row_count // span, span, 3, HEADS, HEAD_DIM)
    mixed = attention(shaped, allowed).reshape(row_count, D)
    hidden = start + low_back(jnp.dot(mixed, w_mix, precision=highest))
    second_norm = low(normalized(hidden, gain_pair[1]))
    lifted = low_back(jnp.dot(second_norm, w_lift, precision=highest))
    active = low(jax.nn.gelu(lifted, approximate=False))
    return hidden + low_back(jnp.dot(active, w_drop, precision=highest))

def utterance(codes_one, length, gains, w_qkv, w_out, w_up, w_down):
    positions = jnp.arange(UTT_LEN)
    valid = positions < length
    allowed = ((positions[None, :] <= positions[:, None]) & valid[None, :])[None]
    start = lax.optimization_barrier(jnp.sum(codes_one, axis=1))
    top_result = block(start, gains[0], w_qkv[0], w_out[0], w_up[0], w_down[0], UTT_LEN, allowed)
    global_sent = low(low_back(top_result))
    local_input = (global_sent[:, None, :] + codes_one).reshape(UTT_LEN * CODES, D)
    code_positions = jnp.arange(CODES)
    code_allowed = (code_positions[None, :] <= code_positions[:, None])[None]
    final = block(local_input, gains[1], w_qkv[1], w_out[1], w_up[1], w_down[1], CODES, code_allowed)
    return jnp.where(valid[:, None, None], final.reshape(UTT_LEN, CODES, D), 0.0)

def reference(codes, lengths, gains, w_qkv, w_out, w_up, w_down, cotangent):
    floats = tuple((argument.astype(jnp.float32) for argument in (codes, gains, w_qkv, w_out, w_up, w_down)))

    def forward(codes_all, gains_all, qkv_all, out_all, up_all, down_all):

        def single(operands):
            return utterance(operands[0], operands[1], gains_all, qkv_all, out_all, up_all, down_all)
        return lax.map(jax.checkpoint(single), (codes_all, lengths))
    result, pullback = jax.vjp(forward, *floats)
    gradients = pullback(cotangent.astype(jnp.float32))
    return (result.astype(jnp.bfloat16), gradients[0], gradients[1], gradients[2], gradients[3], gradients[4], gradients[5])
```

```python
import jax
import jax.numpy as jnp
from jax import lax
from jax.sharding import PartitionSpec as P

HEAD_DIM = 64
SCALE = HEAD_DIM ** (-0.5)
QUARTERS = 4
epsilon = 1e-06
negative = -1e30
f32 = jnp.float32
low16 = jnp.bfloat16


def swap(value, axis, flip):
    count = lax.axis_size(axis)
    return lax.ppermute(value, axis, [(i, i ^ flip) for i in range(count)])


def dot(a, b):
    return jnp.dot(a, b, preferred_element_type=f32)


def dot_tn(a, b):
    return lax.dot_general(a, b, (((0,), (0,)), ((), ())), preferred_element_type=f32)


def dot_nt(a, b):
    return lax.dot_general(a, b, (((1,), (1,)), ((), ())), preferred_element_type=f32)


def norm_forward(values, gain_vector):
    factor = lax.rsqrt(jnp.mean(values * values, axis=-1, keepdims=True) + epsilon)
    return (values * factor * gain_vector, factor)


def norm_backward(values, factor, gain_vector, upstream):
    weighted = upstream * gain_vector
    inner = jnp.mean(weighted * values, axis=-1, keepdims=True)
    grad_values = factor * weighted - values * (factor * factor * factor) * inner
    return (grad_values, jnp.sum(upstream * values * factor, axis=0))


def gelu_exact(values):
    return jax.nn.gelu(values, approximate=False)


def gelu_grad(values, upstream):
    return jax.vjp(gelu_exact, values)[1](upstream)[0]


def row_gather(rows):
    return jnp.concatenate([rows] + [swap(rows, "tensor", k) for k in (1, 2, 3)], axis=0)


def row_scatter(partial):
    pieces = partial.astype(low16).reshape(4, -1, partial.shape[-1])
    total = pieces[0].astype(f32)
    for k in (1, 2, 3):
        total = total + swap(pieces[k], "tensor", k).astype(f32)
    return total


def pair_sum(partial):
    mine = partial.astype(low16)
    return mine.astype(f32) + swap(mine, "section", 1).astype(f32)


def reorder(values, low, axis):
    axis = axis % values.ndim
    width = values.shape[axis] // QUARTERS
    parts = [
        lax.dynamic_slice_in_dim(values, (low ^ m) * width, width, axis) for m in range(QUARTERS)
    ]
    return jnp.concatenate(parts, axis=axis)


def half_of(values, index, axis):
    width = values.shape[axis] // 2
    return lax.dynamic_slice_in_dim(values, index * width, width, axis)


def attention_units(w_query, w_mix):
    unit_a = jnp.concatenate([w_query[:, 0], w_query[:, 1]], axis=1)
    stacked = jnp.concatenate([w_mix[:, :128], w_mix[:, 128:]], axis=0)
    unit_b = jnp.concatenate([w_query[:, 2], stacked], axis=1)
    return (unit_a, unit_b)


def gather_chunk(unit_a, unit_b):
    own = jnp.stack([unit_a, unit_b])
    far = swap(own, "tensor", 2)
    near = swap(jnp.stack([own, far]), "tensor", 1)
    parts_a = jnp.stack([near[0, 0], far[0], near[1, 0]])
    parts_b = jnp.stack([near[0, 1], far[1], near[1, 1]])
    a1 = swap(parts_a, "dp", 1)
    b2 = swap(parts_b, "dp", 2)
    a23 = swap(jnp.stack([parts_a, a1]), "dp", 2)
    b13 = swap(jnp.stack([parts_b, b2]), "dp", 1)
    table_a = [parts_a, a1, a23[0], a23[1]]
    table_b = [parts_b, b13[0], b2, b13[1]]
    return (table_a, table_b)


def sum_rest(value):
    step = QUARTERS
    while step < lax.axis_size("dp"):
        value = (value.astype(f32) + swap(value, "dp", step).astype(f32)).astype(low16)
        step *= 2
    return value


def add16(a, b):
    return (a.astype(f32) + b.astype(f32)).astype(low16)


def scatter_dp(table_a, table_b):
    a = swap(jnp.stack([table_a[1], table_a[3]]), "dp", 1)
    b = swap(jnp.stack([table_b[2], table_b[3]]), "dp", 2)
    a0, a2 = add16(table_a[0], a[0]), add16(table_a[2], a[1])
    b0, b1 = add16(table_b[0], b[0]), add16(table_b[1], b[1])
    a = swap(a2, "dp", 2)
    b = swap(b1, "dp", 1)
    return sum_rest(jnp.stack([add16(a0, a), add16(b0, b)]))


def scatter_z(units):
    arrived = swap(jnp.stack([units[:, 1], units[:, 3]]), "tensor", 1)
    own = add16(units[:, 0], arrived[0])
    far = add16(units[:, 2], arrived[1])
    return add16(own, swap(far, "tensor", 2))


def gather_dp(piece_a, piece_b):
    a1 = swap(piece_a, "dp", 1)
    b2 = swap(piece_b, "dp", 2)
    a23 = swap(jnp.stack([piece_a, a1]), "dp", 2)
    b13 = swap(jnp.stack([piece_b, b2]), "dp", 1)
    return ([piece_a, a1, a23[0], a23[1]], [piece_b, b13[0], b2, b13[1]])


def global_attention(packed, allowed):
    rows = packed.shape[0]
    shaped = packed.reshape(rows, 3, -1, HEAD_DIM)
    queries, keys, values = shaped[:, 0], shaped[:, 1], shaped[:, 2]
    scores = jnp.einsum("qhd,khd->hqk", queries, keys, preferred_element_type=f32) * SCALE
    scores = jnp.where(allowed[None], scores, negative)
    peak = jnp.max(scores, axis=-1, keepdims=True)
    raised = jnp.exp(scores - peak)
    probs = raised / jnp.sum(raised, axis=-1, keepdims=True)
    mixed = jnp.einsum(
        "hqk,khd->qhd", probs.astype(low16), values, preferred_element_type=f32
    ).astype(low16)
    return (mixed.reshape(rows, -1), probs)


def global_attention_back(packed, probs, grad_mixed):
    rows = packed.shape[0]
    shaped = packed.reshape(rows, 3, -1, HEAD_DIM)
    queries, keys, values = shaped[:, 0], shaped[:, 1], shaped[:, 2]
    grad_mixed = grad_mixed.reshape(rows, -1, HEAD_DIM)
    grad_values = jnp.einsum(
        "hqk,qhd->khd", probs.astype(low16), grad_mixed, preferred_element_type=f32
    )
    grad_probs = jnp.einsum("qhd,khd->hqk", grad_mixed, values, preferred_element_type=f32)
    center = jnp.sum(grad_probs * probs, axis=-1, keepdims=True)
    grad_scores = (probs * (grad_probs - center)).astype(low16)
    grad_queries = jnp.einsum("hqk,khd->qhd", grad_scores, keys, preferred_element_type=f32)
    grad_keys = jnp.einsum("hqk,qhd->khd", grad_scores, queries, preferred_element_type=f32)
    grads = jnp.stack([grad_queries * SCALE, grad_keys * SCALE, grad_values], axis=1)
    return grads.astype(low16).reshape(rows, -1)


def head_table(width):
    lane = jnp.arange(width)[:, None] // HEAD_DIM
    return (lane == jnp.arange(width // HEAD_DIM)[None, :]).astype(f32)


def head_sums(products):
    return lax.dot_general(
        products,
        head_table(products.shape[-1]),
        (((products.ndim - 1,), (0,)), ((), ())),
        precision=lax.Precision.HIGHEST,
        preferred_element_type=f32,
    )


def head_spread(values, width):
    return lax.dot_general(
        values,
        head_table(width).astype(low16),
        (((values.ndim - 1,), (1,)), ((), ())),
        preferred_element_type=f32,
    )


PAIRS = [(i, j) for i in range(3) for j in range(i + 1)]


def local_attention(queries, keys, values):
    width = queries.shape[-1]
    products = jnp.stack([queries[i] * keys[j] for i, j in PAIRS])
    scores = head_sums(products) * SCALE
    probs = {}
    for i in range(3):
        own = jnp.stack([scores[PAIRS.index((i, j))] for j in range(i + 1)])
        raised = jnp.exp(own - jnp.max(own, axis=0, keepdims=True))
        raised = raised / jnp.sum(raised, axis=0, keepdims=True)
        for j in range(i + 1):
            probs[(i, j)] = raised[j]
    stacked = jnp.stack([probs[pair] for pair in PAIRS])
    spread = head_spread(stacked.astype(low16), width)
    mixed = jnp.stack(
        [sum(spread[PAIRS.index((i, j))] * values[j] for j in range(i + 1)) for i in range(3)]
    )
    return (mixed.astype(low16), stacked, spread)


def local_attention_back(queries, keys, values, stacked, spread, grad_mixed):
    width = queries.shape[-1]
    products = jnp.stack([grad_mixed[i] * values[j] for i, j in PAIRS])
    grad_probs = head_sums(products)
    weighted = grad_probs * stacked
    grad_scores = []
    for p, (i, j) in enumerate(PAIRS):
        center = sum(weighted[PAIRS.index((i, t))] for t in range(i + 1))
        grad_scores.append(stacked[p] * (grad_probs[p] - center))
    wide = head_spread(jnp.stack(grad_scores).astype(low16), width)
    grad_queries = jnp.stack(
        [sum(wide[PAIRS.index((i, j))] * keys[j] for j in range(i + 1)) for i in range(3)]
    )
    grad_keys = jnp.stack(
        [sum(wide[PAIRS.index((i, j))] * queries[i] for i in range(j, 3)) for j in range(3)]
    )
    grad_values = jnp.stack(
        [sum(spread[PAIRS.index((i, j))] * grad_mixed[i] for i in range(j, 3)) for j in range(3)]
    )
    return (
        (grad_queries * SCALE).astype(low16),
        (grad_keys * SCALE).astype(low16),
        grad_values.astype(low16),
    )


def on_device(codes, lengths, gains, w_qkv, w_out, w_up, w_down, cotangent):
    sec = lax.axis_index("section")
    low = lax.axis_index("dp") % QUARTERS
    z = lax.axis_index("tensor")
    first = sec == 0
    utts, frames, code_count, width = codes.shape
    block = width // QUARTERS
    rows_local = utts * frames * code_count
    heads_width = w_out.shape[1]
    half_width = heads_width // 2
    hidden_width = w_up.shape[2]
    half_hidden = hidden_width // 2

    def choose(a, b):
        return jnp.where(first, a, b)

    code_rows = reorder(jnp.transpose(codes, (2, 0, 1, 3)), low, 3)
    cot_rows = reorder(jnp.transpose(cotangent, (2, 0, 1, 3)), low, 3)

    other_gains = swap(gains[0], "section", 1)
    gain_g = reorder(choose(gains[0], other_gains), low, 1)
    gain_l = reorder(choose(other_gains, gains[0]), low, 1)

    own_w = (w_qkv[0].reshape(width, 3 * heads_width), w_out[0], w_up[0], w_down[0])
    other_w = tuple(swap(w, "section", 1) for w in own_w)
    full_g = tuple(choose(a, b) for a, b in zip(own_w, other_w))
    full_l = tuple(choose(b, a) for a, b in zip(own_w, other_w))
    qkv_g = reorder(full_g[0], low, 0)
    out_g = reorder(full_g[1], low, 1)
    up_g = reorder(full_g[2], low, 0)
    down_g = reorder(full_g[3], low, 1)

    qkv_l = reorder(half_of(full_l[0].reshape(width, 3, heads_width), sec, 2), low, 0)
    out_l = reorder(half_of(full_l[1], sec, 0), low, 1)
    up_l = reorder(half_of(full_l[2], sec, 1), low, 0)
    down_l = reorder(half_of(full_l[3], sec, 0), low, 1)

    def units_of(m):
        span = slice(m * block, (m + 1) * block)
        attn = attention_units(qkv_l[span], out_l[:, span])
        lift = (up_l[span, : half_hidden // 2], up_l[span, half_hidden // 2 :])
        drop = (down_l[: half_hidden // 2, span], down_l[half_hidden // 2 :, span])
        return (attn, lift, drop)

    own_units = [units_of(m) for m in range(QUARTERS)]
    tables = [gather_chunk(*own_units[0][chunk]) for chunk in range(3)]

    def unit(chunk, part, k, m):
        if k == 0:
            return own_units[m][chunk][part]
        return tables[chunk][part][m][k - 1]

    def assembled(make):
        return jnp.concatenate(
            [jnp.concatenate([make(k, m) for k in range(4)], axis=1) for m in range(QUARTERS)],
            axis=0,
        )

    def assembled_t(make):
        return jnp.concatenate(
            [jnp.concatenate([make(k, m) for m in range(QUARTERS)], axis=1) for k in range(4)],
            axis=0,
        )

    def mix_block(k, m):
        stacked = unit(0, 1, k, m)[:, half_width:]
        return jnp.concatenate([stacked[:half_width], stacked[half_width:]], axis=1)

    local_q = assembled(lambda k, m: unit(0, 0, k, m)[:, :half_width])
    local_k = assembled(lambda k, m: unit(0, 0, k, m)[:, half_width:])
    local_v = assembled(lambda k, m: unit(0, 1, k, m)[:, :half_width])
    local_qkv = jnp.concatenate([local_q, local_k, local_v], axis=1)
    local_out = assembled_t(mix_block)
    local_up = assembled(
        lambda k, m: jnp.concatenate([unit(1, 0, k, m), unit(1, 1, k, m)], axis=1)
    )
    local_down = assembled_t(
        lambda k, m: jnp.concatenate([unit(2, 0, k, m), unit(2, 1, k, m)], axis=0)
    )

    own_codes = lax.dynamic_index_in_dim(code_rows, sec, 1, keepdims=False).astype(f32)
    start_g = jnp.sum(own_codes, axis=0)
    length = lax.dynamic_index_in_dim(lengths, sec, 0, keepdims=False)
    order = jnp.stack([z ^ k for k in range(4)])
    positions = (order[:, None] * frames + jnp.arange(frames)[None, :]).reshape(-1)
    allowed = (positions[None, :] <= positions[:, None]) & (positions < length)[None, :]

    n1, r1 = norm_forward(start_g, gain_g[0])
    first_g = row_gather(n1.astype(low16))
    packed_g = dot(first_g, qkv_g).astype(low16)
    mixed_g, probs_g = global_attention(packed_g, allowed)
    hidden_g = start_g + row_scatter(dot(mixed_g, out_g))
    n2, r2 = norm_forward(hidden_g, gain_g[1])
    second_g = row_gather(n2.astype(low16))
    lifted_g = dot(second_g, up_g)
    active_g = gelu_exact(lifted_g).astype(low16)
    result_g = hidden_g + row_scatter(dot(active_g, down_g))
    sent = result_g.astype(low16)

    other_sent = swap(sent, "section", 1)
    both_sent = jnp.stack([choose(sent, other_sent), choose(other_sent, sent)])
    start_l = (both_sent.astype(f32)[None] + code_rows.astype(f32)).reshape(rows_local, width)
    n1l, r1l = norm_forward(start_l, gain_l[0])
    first_l = n1l.astype(low16)
    packed_l = dot(first_l, local_qkv).astype(low16)
    split = packed_l.reshape(code_count, utts * frames, 3, 4 * half_width).astype(f32)
    q_l, k_l, v_l = split[:, :, 0], split[:, :, 1], split[:, :, 2]
    mixed_l, probs_l, spread_l = local_attention(q_l, k_l, v_l)
    mixed_l = mixed_l.reshape(rows_local, -1)
    hidden_l = start_l + pair_sum(dot(mixed_l, local_out))
    n2l, r2l = norm_forward(hidden_l, gain_l[1])
    second_l = n2l.astype(low16)
    lifted_l = dot(second_l, local_up)
    active_l = gelu_exact(lifted_l).astype(low16)

    own_frames = z * frames + jnp.arange(frames)
    valid = (own_frames[None, :] < lengths[:, None])[None, :, :, None]
    top_l = jnp.where(valid, cot_rows, jnp.zeros_like(cot_rows)).reshape(rows_local, width)
    grad_down_l = dot_tn(active_l, top_l).astype(low16)
    grad_lifted_l = gelu_grad(lifted_l, dot_nt(top_l, local_down)).astype(low16)
    grad_up_l = dot_tn(second_l, grad_lifted_l).astype(low16)
    grad_second_l = pair_sum(dot_nt(grad_lifted_l, local_up))
    through, gain2_l = norm_backward(hidden_l, r2l, gain_l[1], grad_second_l)
    grad_hidden_l = top_l.astype(f32) + through
    mid_l = grad_hidden_l.astype(low16)
    grad_out_l = dot_tn(mixed_l, mid_l).astype(low16)
    grad_mixed_l = dot_nt(mid_l, local_out).astype(low16)
    grad_mixed_l = grad_mixed_l.reshape(code_count, utts * frames, -1).astype(f32)
    grad_q, grad_k, grad_v = local_attention_back(
        q_l, k_l, v_l, probs_l, spread_l, grad_mixed_l
    )
    grad_packed_l = jnp.concatenate([grad_q, grad_k, grad_v], axis=2).reshape(rows_local, -1)
    grad_qkv_l = dot_tn(first_l, grad_packed_l).astype(low16)
    grad_first_l = pair_sum(dot_nt(grad_packed_l, local_qkv))
    through, gain1_l = norm_backward(start_l, r1l, gain_l[0], grad_first_l)
    grad_codes = (grad_hidden_l + through).reshape(code_count, utts, frames, width)

    absolute = lambda value: half_of(reorder(value, low, -1), sec, value.ndim - 1)
    other_half = lambda value: half_of(reorder(value, low, -1), 1 - sec, value.ndim - 1)
    branch_l = dot(active_l, local_down)
    arrived = swap(other_half(branch_l).astype(low16), "section", 1)
    final = absolute(hidden_l) + absolute(branch_l) + arrived.astype(f32)
    final = final.reshape(code_count, utts, frames, width // 2)
    final = jnp.where(valid, final, 0.0).astype(low16)
    output = jnp.transpose(final, (1, 2, 0, 3))

    returned = jnp.sum(
        lax.dynamic_index_in_dim(grad_codes, sec, 1, keepdims=False), axis=0
    ).astype(low16)
    top_g = row_gather(returned)
    grad_down_g = dot_tn(active_g, top_g).astype(low16)
    grad_lifted_g = gelu_grad(lifted_g, dot_nt(top_g, down_g)).astype(low16)
    grad_up_g = dot_tn(second_g, grad_lifted_g).astype(low16)
    grad_second_g = row_scatter(dot_nt(grad_lifted_g, up_g))
    through, gain2_g = norm_backward(hidden_g, r2, gain_g[1], grad_second_g)
    grad_hidden_g = returned.astype(f32) + through
    mid_g = row_gather(grad_hidden_g.astype(low16))
    grad_out_g = dot_tn(mixed_g, mid_g).astype(low16)
    grad_mixed_g = dot_nt(mid_g, out_g).astype(low16)
    grad_packed_g = global_attention_back(packed_g, probs_g, grad_mixed_g)
    grad_qkv_g = dot_tn(first_g, grad_packed_g).astype(low16)
    grad_first_g = row_scatter(dot_nt(grad_packed_g, qkv_g))
    through, gain1_g = norm_backward(start_g, r1, gain_g[0], grad_first_g)
    grad_start = grad_hidden_g + through

    other_start = swap(other_half(grad_start), "section", 1)
    own_start = absolute(grad_start)
    both_start = jnp.stack([choose(own_start, other_start), choose(other_start, own_start)])
    code_grad = absolute(grad_codes) + both_start[None]
    code_grad = jnp.transpose(code_grad, (1, 2, 0, 3))

    own_g = jnp.stack([gain1_g, gain2_g])
    total_g = own_g + swap(own_g, "section", 1)
    gain_total = reorder(choose(total_g, jnp.stack([gain1_l, gain2_l])), low, 1)
    for axis in ("tensor", "dp"):
        step = 1
        while step < lax.axis_size(axis):
            gain_total = gain_total + swap(gain_total, axis, step)
            step *= 2

    def local_unit(chunk, part, k, m):
        span = slice(m * block, (m + 1) * block)
        if chunk == 0:
            at = [
                grad_qkv_l[span, c * 4 * half_width + k * half_width :][:, :half_width]
                for c in range(3)
            ]
            if part == 0:
                return jnp.concatenate([at[0], at[1]], axis=1)
            mix = grad_out_l[k * half_width : (k + 1) * half_width, span]
            stacked = jnp.concatenate([mix[:, :half_width], mix[:, half_width:]], axis=0)
            return jnp.concatenate([at[2], stacked], axis=1)
        offset = k * half_hidden + part * (half_hidden // 2)
        if chunk == 1:
            return grad_up_l[span, offset : offset + half_hidden // 2]
        return grad_down_l[offset : offset + half_hidden // 2, span]

    def global_unit(chunk, part, half, m):
        span = slice(m * block, (m + 1) * block)
        if chunk == 0:
            at = [
                lax.dynamic_slice_in_dim(
                    grad_qkv_g[span], c * heads_width + half * half_width, half_width, 1
                )
                for c in range(3)
            ]
            if part == 0:
                return jnp.concatenate([at[0], at[1]], axis=1)
            mix = lax.dynamic_slice_in_dim(grad_out_g[:, span], half * half_width, half_width, 0)
            stacked = jnp.concatenate([mix[:, :half_width], mix[:, half_width:]], axis=0)
            return jnp.concatenate([at[2], stacked], axis=1)
        offset = half * half_hidden + part * (half_hidden // 2)
        if chunk == 1:
            return lax.dynamic_slice_in_dim(grad_up_g[span], offset, half_hidden // 2, 1)
        return lax.dynamic_slice_in_dim(grad_down_g[:, span], offset, half_hidden // 2, 0)

    finished = []
    for chunk in (2, 1, 0):
        tables_l = [
            [
                jnp.stack([local_unit(chunk, part, k, m) for k in range(4)])
                for m in range(QUARTERS)
            ]
            for part in range(2)
        ]
        piece_l = scatter_z(scatter_dp(*tables_l))
        away = jnp.stack(
            [
                jnp.stack([global_unit(chunk, part, 1 - sec, m) for m in range(QUARTERS)])
                for part in range(2)
            ]
        )
        own = jnp.stack(
            [
                jnp.stack([global_unit(chunk, part, sec, m) for m in range(QUARTERS)])
                for part in range(2)
            ]
        )
        both = add16(own, swap(away, "section", 1))
        piece_g = scatter_dp(
            [both[0, m] for m in range(QUARTERS)], [both[1, m] for m in range(QUARTERS)]
        )
        arrived = swap(choose(piece_l, piece_g), "section", 1)
        kept = choose(piece_g, piece_l)
        halves = jnp.stack([choose(kept, arrived), choose(arrived, kept)])
        finished.append(gather_dp(halves[:, 0], halves[:, 1]))
    tables_down, tables_up, tables_attn = finished

    def absolute_order(table):
        stacked = jnp.stack(table)
        return [
            lax.dynamic_index_in_dim(stacked, low ^ j, 0, keepdims=False)
            for j in range(QUARTERS)
        ]

    up_a, up_b = (absolute_order(table) for table in tables_up)
    up_grad = jnp.concatenate(
        [
            jnp.concatenate([up_a[j][0], up_b[j][0], up_a[j][1], up_b[j][1]], axis=1)
            for j in range(QUARTERS)
        ],
        axis=0,
    ).astype(f32)
    down_a, down_b = (absolute_order(table) for table in tables_down)
    down_grad = jnp.concatenate(
        [
            jnp.concatenate([down_a[j][0], down_b[j][0], down_a[j][1], down_b[j][1]], axis=0)
            for j in range(QUARTERS)
        ],
        axis=1,
    ).astype(f32)
    attn_a, attn_b = (absolute_order(table) for table in tables_attn)

    def part_of(unit_pair, start):
        return jnp.concatenate(
            [unit_pair[h][:, start * half_width : (start + 1) * half_width] for h in range(2)],
            axis=1,
        )

    qkv_grad = jnp.concatenate(
        [
            jnp.stack(
                [part_of(attn_a[j], 0), part_of(attn_a[j], 1), part_of(attn_b[j], 0)], axis=1
            )
            for j in range(QUARTERS)
        ],
        axis=0,
    ).astype(f32)

    def mix_of(stacked):
        stacked = stacked[:, half_width:]
        return jnp.concatenate([stacked[:half_width], stacked[half_width:]], axis=1)

    out_grad = jnp.concatenate(
        [
            jnp.concatenate([mix_of(attn_b[j][h]) for h in range(2)], axis=0)
            for j in range(QUARTERS)
        ],
        axis=1,
    ).astype(f32)
    return (
        output,
        code_grad,
        gain_total[None],
        qkv_grad[None],
        out_grad[None],
        up_grad[None],
        down_grad[None],
    )


def solution(mesh):
    in_specs = (
        P("dp", "tensor", None, None),
        P("dp"),
        P("section", None, None),
        P("section", None, None, "tensor"),
        P("section", "tensor", None),
        P("section", None, "tensor"),
        P("section", "tensor", None),
        P("dp", "tensor", None, None),
    )
    out_specs = (
        P("dp", "tensor", None, "section"),
        P("dp", "tensor", None, "section"),
        P("section", None, None),
        P("section", None, None, "tensor"),
        P("section", "tensor", None),
        P("section", None, "tensor"),
        P("section", "tensor", None),
    )
    return jax.shard_map(
        on_device, mesh=mesh, in_specs=in_specs, out_specs=out_specs, check_vma=False
    )
```

```python
import functools

import jax
import jax.numpy as jnp
from jax import lax
from jax.experimental import pallas as pl
from jax.experimental.pallas import tpu as pltpu
from jax.sharding import PartitionSpec as P

HEAD_DIM = 64
SCALE = HEAD_DIM ** (-0.5)
QUARTERS = 4
UNIT = 256
epsilon = 1e-06
negative = -1e30
f32 = jnp.float32
low16 = jnp.bfloat16

VM = pl.BlockSpec(memory_space=pltpu.VMEM)
SM = pl.BlockSpec(memory_space=pltpu.SMEM)
ANY = pl.BlockSpec(memory_space=pl.ANY)
MIB = 1 << 20

LOW, SEC, SHARD, LENGTHS = 0, 1, 2, 3


def shape(dims, dtype):
    return jax.ShapeDtypeStruct(tuple(dims), dtype)


def call(body, outs, args, specs, scratch=(), limit=24, flops=0, moved=0, out_specs=None):
    return pl.pallas_call(
        body,
        out_shape=tuple(outs),
        in_specs=list(specs),
        out_specs=tuple(out_specs or [VM] * len(outs)),
        scratch_shapes=list(scratch),
        compiler_params=pltpu.CompilerParams(vmem_limit_bytes=limit * MIB),
        cost_estimate=pl.CostEstimate(flops=flops, bytes_accessed=moved, transcendentals=0),
    )(*args)


def swap(value, axis, flip):
    count = lax.axis_size(axis)
    return lax.ppermute(value, axis, [(i, i ^ flip) for i in range(count)])


def dot(a, b):
    return jnp.dot(a, b, preferred_element_type=f32)


def dot_tn(a, b):
    return lax.dot_general(a, b, (((0,), (0,)), ((), ())), preferred_element_type=f32)


def dot_nt(a, b):
    return lax.dot_general(a, b, (((1,), (1,)), ((), ())), preferred_element_type=f32)


def factor_of(values):
    return lax.rsqrt(jnp.mean(values * values, axis=-1, keepdims=True) + epsilon)


def norm_back(values, gain, upstream):
    factor = factor_of(values)
    weighted = upstream * gain
    inner = jnp.mean(weighted * values, axis=-1, keepdims=True)
    through = factor * weighted - values * (factor * factor * factor) * inner
    return through, jnp.sum(upstream * values * factor, axis=0, keepdims=True)


def normal_cdf(values):
    return 0.5 * (1.0 + lax.erf(values * (0.5**0.5)))


def gelu_slope(values, cdf):
    return cdf + values * (jnp.exp(-0.5 * values * values) * 0.3989422804014327)


def block_at(low, m):
    return pl.multiple_of((low ^ m) * UNIT, UNIT)


def span(m):
    return slice(m * UNIT, (m + 1) * UNIT)


class Copies:
    def __init__(self, sems):
        self.sems = sems
        self.made = []

    def start(self, src, dst):
        copy = pltpu.make_async_copy(src, dst, self.sems.at[len(self.made)])
        copy.start()
        self.made.append(copy)
        return copy

    def pick(self, own_first, sec, own, other, dst):
        sem = self.sems.at[len(self.made)]

        @pl.when((sec == 0) == own_first)
        def _():
            pltpu.make_async_copy(own, dst, sem).start()

        @pl.when((sec == 0) != own_first)
        def _():
            pltpu.make_async_copy(other, dst, sem).start()

        copy = pltpu.make_async_copy(own, dst, sem)
        self.made.append(copy)
        return copy

    def wait(self):
        for copy in self.made:
            copy.wait()


def start_kernel(info, codes, own_gain, other_gain, first, start, gain_g, gain_l):
    low, sec = info[LOW], info[SEC]
    for m in range(QUARTERS):
        at = pl.ds(block_at(low, m), UNIT)
        own, other = own_gain[:, at], other_gain[:, at]
        gain_g[:, span(m)] = jnp.where(sec == 0, own, other)
        gain_l[:, span(m)] = jnp.where(sec == 0, other, own)
        total = codes[sec, 0, :, at].astype(f32)
        for c in range(1, codes.shape[1]):
            total = total + codes[sec, c, :, at].astype(f32)
        start[:, span(m)] = total
    values = start[...]
    first[...] = (values * factor_of(values) * gain_g[0:1, :]).astype(low16)


def piece_kernel(quarters, info, own_qkv, other_qkv, own_out, other_out, own_up, other_up,
                 own_down, other_down, pieces, sems):
    low, sec = info[LOW], info[SEC]
    half = own_qkv.shape[2] // 2
    wide = own_up.shape[1] // 2

    def branch(half_index, qkv, out, up, down):
        made = Copies(sems)
        for place, m in enumerate(quarters):
            at = pl.ds(block_at(low, m), UNIT)
            at_right = pl.ds(pl.multiple_of(block_at(low, m) + half, half), half)
            at_left = pl.ds(block_at(low, m), half)
            lanes = slice(half_index * half, (half_index + 1) * half)
            target = pieces.at[place]
            made.start(qkv.at[0, at, lanes], target.at[0, :, 0:half])
            made.start(qkv.at[1, at, lanes], target.at[0, :, half : 2 * half])
            made.start(qkv.at[2, at, lanes], target.at[1, :, 0:half])
            made.start(out.at[lanes, at_left], target.at[1, 0:half, half : 2 * half])
            made.start(out.at[lanes, at_right], target.at[1, half : 2 * half, half : 2 * half])
            for part in range(2):
                begin = half_index * wide + part * UNIT
                hidden = slice(begin, begin + UNIT)
                made.start(up.at[at, hidden], target.at[2 + part])
                made.start(down.at[hidden, at], target.at[4 + part])
        made.wait()

    @pl.when(sec == 0)
    def _():
        branch(0, other_qkv, other_out, other_up, other_down)

    @pl.when(sec != 0)
    def _():
        branch(1, own_qkv, own_out, own_up, own_down)


def fetch_attention(made, low, sec, own_qkv, other_qkv, own_out, other_out, qkv, out):
    for m in range(QUARTERS):
        at = pl.ds(block_at(low, m), UNIT)
        made.pick(True, sec, own_qkv.at[:, at, :], other_qkv.at[:, at, :], qkv.at[:, span(m), :])
    for m in range(QUARTERS):
        at = pl.ds(block_at(low, m), UNIT)
        made.pick(True, sec, own_out.at[:, at], other_out.at[:, at], out.at[:, span(m)])


def global_attention_kernel(info, rows, own_qkv, other_qkv, own_out, other_out,
                            packed, probs, mixed, partial, qkv, out, sems):
    low, sec = info[LOW], info[SEC]
    made = Copies(sems)
    fetch_attention(made, low, sec, own_qkv, other_qkv, own_out, other_out, qkv, out)
    count = rows.shape[0]
    length = info[LENGTHS + sec]
    query_at = lax.broadcasted_iota(jnp.int32, (count, count), 0)
    key_at = lax.broadcasted_iota(jnp.int32, (count, count), 1)
    allowed = (key_at <= query_at) & (key_at < length)
    made.wait()
    values = rows[...]
    for c in range(3):
        packed[c] = dot(values, qkv[c]).astype(low16)
    heads = []
    for h in range(packed.shape[2] // HEAD_DIM):
        lanes = slice(h * HEAD_DIM, (h + 1) * HEAD_DIM)
        scores = dot_nt(packed[0, :, lanes], packed[1, :, lanes]) * SCALE
        scores = jnp.where(allowed, scores, negative)
        raised = jnp.exp(scores - jnp.max(scores, axis=-1, keepdims=True))
        exact = raised / jnp.sum(raised, axis=-1, keepdims=True)
        probs[h] = exact
        heads.append(dot(exact.astype(low16), packed[2, :, lanes]).astype(low16))
    mixed[...] = jnp.concatenate(heads, axis=1)
    partial[...] = dot(mixed[...], out[...]).astype(low16).reshape(partial.shape)


def total_of(arrived):
    total = arrived[0].astype(f32)
    for k in range(1, arrived.shape[0]):
        total = total + arrived[k].astype(f32)
    return total


def middle_kernel(start, arrived, gain, hidden, second):
    values = start[...] + total_of(arrived)
    hidden[...] = values
    second[...] = (values * factor_of(values) * gain[1:2, :]).astype(low16)


def fetch_feed(made, low, sec, own_up, other_up, own_down, other_down, up, down):
    for m in range(QUARTERS):
        at = pl.ds(block_at(low, m), UNIT)
        made.pick(True, sec, own_up.at[at, :], other_up.at[at, :], up.at[span(m), :])
    for m in range(QUARTERS):
        at = pl.ds(block_at(low, m), UNIT)
        made.pick(True, sec, own_down.at[:, at], other_down.at[:, at], down.at[:, span(m)])


def global_feed_kernel(info, rows, own_up, other_up, own_down, other_down,
                       lifted, active, partial, up, down, total, sems):
    made = Copies(sems)
    fetch_feed(made, info[LOW], info[SEC], own_up, other_up, own_down, other_down, up, down)
    made.wait()
    values = rows[...]
    for t in range(up.shape[1] // UNIT):
        tile = dot(values, up[:, span(t)])
        lifted[:, span(t)] = tile
        low_tile = (tile * normal_cdf(tile)).astype(low16)
        active[:, span(t)] = low_tile
        branch = dot(low_tile, down[span(t), :])
        total[...] = branch if t == 0 else total[...] + branch
    partial[...] = total[...].astype(low16).reshape(partial.shape)


def sent_kernel(hidden, arrived, sent):
    sent[...] = (hidden[...] + total_of(arrived)).astype(low16)


def global_feed_back_kernel(info, top, lifted, own_up, other_up, own_down, other_down,
                            grad_lifted, partial, up, down, total, sems):
    made = Copies(sems)
    fetch_feed(made, info[LOW], info[SEC], own_up, other_up, own_down, other_down, up, down)
    made.wait()
    values = top[...]
    for t in range(up.shape[1] // UNIT):
        tile = lifted[:, span(t)]
        grad = dot_nt(values, down[span(t), :]) * gelu_slope(tile, normal_cdf(tile))
        grad = grad.astype(low16)
        grad_lifted[:, span(t)] = grad
        back = dot_nt(grad, up[:, span(t)])
        total[...] = back if t == 0 else total[...] + back
    partial[...] = total[...].astype(low16).reshape(partial.shape)


def middle_back_kernel(arrived, hidden, gain, returned, grad_hidden, mid, gain_grad):
    through, gain_grad[...] = norm_back(hidden[...], gain[1:2, :], total_of(arrived))
    values = returned[...].astype(f32) + through
    grad_hidden[...] = values
    mid[...] = values.astype(low16)


def global_attention_back_kernel(info, mid, packed, probs, own_qkv, other_qkv, own_out, other_out,
                                 grads, partial, qkv, out, sems):
    low, sec = info[LOW], info[SEC]
    made = Copies(sems)
    fetch_attention(made, low, sec, own_qkv, other_qkv, own_out, other_out, qkv, out)
    made.wait()
    grad_mixed = dot_nt(mid[...], out[...]).astype(low16)
    columns = [[], [], []]
    for h in range(packed.shape[2] // HEAD_DIM):
        lanes = slice(h * HEAD_DIM, (h + 1) * HEAD_DIM)
        exact = probs[h]
        grad = grad_mixed[:, lanes]
        columns[2].append(dot_tn(exact.astype(low16), grad).astype(low16))
        grad_probs = dot_nt(grad, packed[2, :, lanes])
        center = jnp.sum(grad_probs * exact, axis=-1, keepdims=True)
        grad_scores = (exact * (grad_probs - center)).astype(low16)
        columns[0].append((dot(grad_scores, packed[1, :, lanes]) * SCALE).astype(low16))
        columns[1].append((dot_tn(grad_scores, packed[0, :, lanes]) * SCALE).astype(low16))
    total = None
    for c in range(3):
        grads[c] = jnp.concatenate(columns[c], axis=1)
        back = dot_nt(grads[c], qkv[c])
        total = back if c == 0 else total + back
    partial[...] = total.astype(low16).reshape(partial.shape)


def start_back_kernel(info, arrived, start, gain, grad_hidden, kept, given, gain_grad, values):
    low, sec = info[LOW], info[SEC]
    through, gain_grad[...] = norm_back(start[...], gain[0:1, :], total_of(arrived))
    values[...] = grad_hidden[...] + through
    for j in range(2):
        kept[:, span(j)] = values[:, pl.ds(block_at(low, 2 * sec + j), UNIT)]
        given[:, span(j)] = values[:, pl.ds(block_at(low, 2 * (1 - sec) + j), UNIT)]


class LocalWeights:
    def __init__(self, refs):
        self.refs = refs

    def unit(self, k, m, u):
        own, rest = self.refs[0], self.refs[1]
        if k == 0:
            return own.at[0, u] if m == 0 else rest.at[m - 1, u]
        base = self.refs[2 + 5 * (k - 1) : 7 + 5 * (k - 1)]
        if m < 3:
            return base[m].at[0, u]
        return base[3].at[0, u] if u < 3 else base[4].at[0, u - 3]


def pair_rows(a, b, size):
    return jnp.concatenate([a * b, a[size:] * b[: 2 * size], a[2 * size :] * b[:size]], axis=0)


def by_pair(stacked, size):
    names = [(0, 0), (1, 1), (2, 2), (1, 0), (2, 1), (2, 0)]
    return {name: stacked[n * size : (n + 1) * size] for n, name in enumerate(names)}


def from_pairs(pairs):
    names = [(0, 0), (1, 1), (2, 2), (1, 0), (2, 1), (2, 0)]
    return jnp.concatenate([pairs[name] for name in names], axis=0)


def head_sums(products, table):
    upper = products.astype(low16)
    lower = (products - upper.astype(f32)).astype(low16)
    return dot(upper, table) + dot(lower, table)


def head_table(width):
    row = lax.broadcasted_iota(jnp.int32, (width, width), 0) // HEAD_DIM
    column = lax.broadcasted_iota(jnp.int32, (width, width), 1) // HEAD_DIM
    return (row == column).astype(f32).astype(low16)


def gather_mix(weights, mix, k, half):
    for m in range(QUARTERS):
        begin = m * UNIT
        mix[k * half : (k + 1) * half, begin : begin + half] = weights[
            k, 1, begin : begin + half, half:
        ]
        mix[k * half : (k + 1) * half, begin + half : begin + UNIT] = weights[
            k, 1, begin + half : begin + UNIT, half:
        ]


def local_attention_kernel(info, codes, sent_own, sent_other, gain, *rest):
    refs, (start, first, query_keys, values_out, probs, mixed, partial, weights, mix, sems) = (
        rest[:17], rest[17:]
    )
    low, sec = info[LOW], info[SEC]
    local = LocalWeights(refs)
    made = Copies(sems)
    groups = []
    for k in range(4):
        groups.append(
            [
                made.start(local.unit(k, m, u), weights.at[k, u, span(m), :])
                for u in range(2)
                for m in range(QUARTERS)
            ]
        )
    utts, code_count, frames, _ = codes.shape
    for u in range(utts):
        sent = jnp.where(sec == u, sent_own[...], sent_other[...]).astype(f32)
        for c in range(code_count):
            row = (u * code_count + c) * frames
            for m in range(QUARTERS):
                code = codes[u, c, :, pl.ds(block_at(low, m), UNIT)].astype(f32)
                start[row : row + frames, span(m)] = sent[:, span(m)] + code
    values = start[...]
    first[...] = (values * factor_of(values) * gain[0:1, :]).astype(low16)
    half = values_out.shape[2]
    table = head_table(half)
    rows = first[...]
    size = frames
    group = code_count * frames
    for k in range(4):
        for copy in groups[k]:
            copy.wait()
        query_keys[k] = dot(rows, weights[k, 0]).astype(low16)
        values_out[k] = dot(rows, weights[k, 1, :, :half]).astype(low16)
        gather_mix(weights, mix, k, half)
        for u in range(utts):
            at = slice(u * group, (u + 1) * group)
            q = query_keys[k, at, :half].astype(f32)
            key = query_keys[k, at, half:].astype(f32)
            val = values_out[k, at, :].astype(f32)
            scores = by_pair(head_sums(pair_rows(q, key, size), table) * SCALE, size)
            exact = {}
            for i in range(3):
                peak = scores[(i, 0)]
                for j in range(1, i + 1):
                    peak = jnp.maximum(peak, scores[(i, j)])
                raised = [jnp.exp(scores[(i, j)] - peak) for j in range(i + 1)]
                whole = raised[0]
                for j in range(1, i + 1):
                    whole = whole + raised[j]
                for j in range(i + 1):
                    exact[(i, j)] = raised[j] / whole
            probs[k, u] = from_pairs(exact)
            for i in range(3):
                total = None
                for j in range(i + 1):
                    weight = exact[(i, j)].astype(low16).astype(f32)
                    term = weight * val[j * size : (j + 1) * size]
                    total = term if total is None else total + term
                begin = u * group + i * size
                mixed[begin : begin + size, k * half : (k + 1) * half] = total.astype(low16)
    partial[...] = dot(mixed[...], mix[...]).astype(low16)


def local_feed_kernel(info, start, own_part, other_part, gain, cotangent, *rest):
    refs = rest[:17]
    (hidden, second, top, active, grad_lifted, grad_second, branch_out,
     up, down, branch, back, sems) = rest[17:]
    low = info[LOW]
    local = LocalWeights(refs)
    tiles = active.shape[0]
    made = Copies(sems)
    for t in range(tiles):
        for m in range(QUARTERS):
            made.start(local.unit(t // 2, m, 2 + t % 2), up.at[t, span(m), :])
        for m in range(QUARTERS):
            made.start(local.unit(t // 2, m, 4 + t % 2), down.at[t, :, span(m)])
    utts, code_count, frames, _ = cotangent.shape
    frame_at = lax.broadcasted_iota(jnp.int32, (frames, 1), 0) + info[SHARD] * frames
    for u in range(utts):
        valid = frame_at < info[LENGTHS + u]
        for c in range(code_count):
            row = (u * code_count + c) * frames
            for m in range(QUARTERS):
                part = cotangent[u, c, :, pl.ds(block_at(low, m), UNIT)].astype(f32)
                top[row : row + frames, span(m)] = jnp.where(valid, part, 0.0).astype(low16)
    values = start[...] + (own_part[...].astype(f32) + other_part[...].astype(f32))
    hidden[...] = values
    second[...] = (values * factor_of(values) * gain[1:2, :]).astype(low16)
    branch[...] = jnp.zeros_like(branch)
    back[...] = jnp.zeros_like(back)

    @pl.loop(0, tiles)
    def _(t):
        for m in range(QUARTERS):
            pltpu.make_async_copy(
                refs[0].at[0, 0], up.at[t, span(m), :], sems.at[8 * t + m]
            ).wait()
        for m in range(QUARTERS):
            pltpu.make_async_copy(
                refs[0].at[0, 0], down.at[t, :, span(m)], sems.at[8 * t + 4 + m]
            ).wait()
        tile = dot(second[...], up[t])
        cdf = normal_cdf(tile)
        low_tile = (tile * cdf).astype(low16)
        active[t] = low_tile
        branch[...] += dot(low_tile, down[t])
        grad = (dot_nt(top[...], down[t]) * gelu_slope(tile, cdf)).astype(low16)
        grad_lifted[t] = grad
        back[...] += dot_nt(grad, up[t])

    branch_out[...] = branch[...].astype(low16)
    grad_second[...] = back[...].astype(low16)


def local_attention_back_kernel(hidden, own_back, other_back, top, gain, query_keys, values_in,
                                probs, *rest):
    refs = rest[:17]
    (grad_hidden, mid, grad_query_keys, grad_values, grad_first, gain_grad,
     weights, mix, total, sems) = rest[17:]
    local = LocalWeights(refs)
    made = Copies(sems)
    groups = []
    for k in range(4):
        groups.append(
            [
                made.start(local.unit(k, m, u), weights.at[k, u, span(m), :])
                for u in range(2)
                for m in range(QUARTERS)
            ]
        )
    upstream = own_back[...].astype(f32) + other_back[...].astype(f32)
    through, gain_grad[...] = norm_back(hidden[...], gain[1:2, :], upstream)
    grads = top[...].astype(f32) + through
    grad_hidden[...] = grads
    mid[...] = grads.astype(low16)
    utts = probs.shape[1]
    half = values_in.shape[2]
    group = query_keys.shape[1] // utts
    size = group // 3
    table = head_table(half)
    for k in range(4):
        for copy in groups[k]:
            copy.wait()
        gather_mix(weights, mix, k, half)
        grad_mixed = dot_nt(mid[...], mix[k * half : (k + 1) * half, :]).astype(low16)
        grad_mixed = grad_mixed.astype(f32)
        for u in range(utts):
            at = slice(u * group, (u + 1) * group)
            q = query_keys[k, at, :half].astype(f32)
            key = query_keys[k, at, half:].astype(f32)
            val = values_in[k, at, :].astype(f32)
            grad = grad_mixed[at]
            exact = by_pair(probs[k, u], size)
            grad_probs = by_pair(head_sums(pair_rows(grad, val, size), table), size)
            scored = {}
            for i in range(3):
                center = grad_probs[(i, 0)] * exact[(i, 0)]
                for j in range(1, i + 1):
                    center = center + grad_probs[(i, j)] * exact[(i, j)]
                for j in range(i + 1):
                    score = exact[(i, j)] * (grad_probs[(i, j)] - center)
                    scored[(i, j)] = score.astype(low16).astype(f32)

            def rows_of(array, n):
                return array[n * size : (n + 1) * size]

            for i in range(3):
                begin = u * group + i * size
                to_query = sum(scored[(i, j)] * rows_of(key, j) for j in range(i + 1))
                to_key = sum(scored[(n, i)] * rows_of(q, n) for n in range(i, 3))
                to_value = sum(
                    exact[(n, i)].astype(low16).astype(f32) * rows_of(grad, n)
                    for n in range(i, 3)
                )
                grad_query_keys[k, begin : begin + size, :half] = (to_query * SCALE).astype(low16)
                grad_query_keys[k, begin : begin + size, half:] = (to_key * SCALE).astype(low16)
                grad_values[k, begin : begin + size, :] = to_value.astype(low16)
        back = dot_nt(grad_query_keys[k], weights[k, 0])
        back = back + dot_nt(grad_values[k], weights[k, 1, :, :half])
        total[...] = back if k == 0 else total[...] + back
    grad_first[...] = total[...].astype(low16)


def local_end_kernel(info, own_back, other_back, start, grad_hidden, gain,
                     returned, code_part, gain_grad, values):
    low, sec = info[LOW], info[SEC]
    upstream = own_back[...].astype(f32) + other_back[...].astype(f32)
    through, gain_grad[...] = norm_back(start[...], gain[0:1, :], upstream)
    values[...] = grad_hidden[...] + through
    utts, code_count, frames, _ = code_part.shape
    total = None
    for c in range(code_count):
        begin = pl.multiple_of((sec * code_count + c) * frames, frames)
        part = values[pl.ds(begin, frames), :]
        total = part if total is None else total + part
    returned[...] = total.astype(low16)
    for u in range(utts):
        for c in range(code_count):
            row = (u * code_count + c) * frames
            for j in range(2):
                at = pl.ds(block_at(low, 2 * sec + j), UNIT)
                code_part[u, c, :, span(j)] = values[row : row + frames, at]


def output_kernel(info, hidden, own_part, other_part, output):
    low, sec = info[LOW], info[SEC]
    utts, code_count, frames, _ = output.shape
    frame_at = lax.broadcasted_iota(jnp.int32, (frames, 1), 0) + info[SHARD] * frames
    for u in range(utts):
        valid = frame_at < info[LENGTHS + u]
        for c in range(code_count):
            row = (u * code_count + c) * frames
            rows = slice(row, row + frames)
            for j in range(2):
                at = pl.ds(block_at(low, 2 * sec + j), UNIT)
                value = hidden[rows, at] + (
                    own_part[rows, at].astype(f32) + other_part[rows, at].astype(f32)
                )
                output[u, c, :, span(j)] = jnp.where(valid, value, 0.0).astype(low16)


SEND_A, KEEP_A, SEND_B, KEEP_B = (1, 3), (0, 2), (2, 3), (0, 1)


def local_up_kernel(second, grad_lifted, send_a, send_b, keep_a, keep_b, turned):
    turned[...] = jnp.transpose(second[...])
    for k in range(4):
        for part, pairs in enumerate(
            (((send_a, SEND_A), (keep_a, KEEP_A)), ((send_b, SEND_B), (keep_b, KEEP_B)))
        ):
            right = grad_lifted[2 * k + part]
            for target, order in pairs:
                for place, m in enumerate(order):
                    target[place, k] = dot(turned[span(m), :], right).astype(low16)


def local_down_kernel(active, top, send_a, send_b, keep_a, keep_b):
    for k in range(4):
        for part, pairs in enumerate(
            (((send_a, SEND_A), (keep_a, KEEP_A)), ((send_b, SEND_B), (keep_b, KEEP_B)))
        ):
            left = jnp.transpose(active[2 * k + part])
            for target, order in pairs:
                for place, m in enumerate(order):
                    target[place, k] = dot(left, top[:, span(m)]).astype(low16)


def local_mix_kernel(first, grad_query_keys, grad_values, mixed, mid,
                     send_a, send_b, keep_a, keep_b, turned):
    turned[...] = jnp.transpose(first[...])
    half = grad_values.shape[2]
    for k in range(4):
        left = jnp.transpose(mixed[:, k * half : (k + 1) * half])
        for target, order in ((send_a, SEND_A), (keep_a, KEEP_A)):
            for place, m in enumerate(order):
                target[place, k] = dot(turned[span(m), :], grad_query_keys[k]).astype(low16)
        for target, order in ((send_b, SEND_B), (keep_b, KEEP_B)):
            for place, m in enumerate(order):
                value = dot(turned[span(m), :], grad_values[k]).astype(low16)
                out = dot(left, mid[:, span(m)]).astype(low16)
                target[place, k, :, :half] = value
                target[place, k, :half, half:] = out[:, :half]
                target[place, k, half:, half:] = out[:, half:]


def global_feed_grad_kernel(info, second, grad_lifted, active, top, away, kept, turned):
    sec = info[SEC]
    turned[...] = jnp.transpose(second[...])
    wide = active.shape[1] // 2
    for target, half in ((away, 1 - sec), (kept, sec)):
        for part in range(2):
            at = pl.ds(pl.multiple_of(half * wide + part * UNIT, UNIT), UNIT)
            right = grad_lifted[:, at]
            left = jnp.transpose(active[:, at])
            for m in range(QUARTERS):
                target[m, part, 0] = dot(turned[span(m), :], right).astype(low16)
                target[m, part, 1] = dot(left, top[:, span(m)]).astype(low16)


def global_mix_grad_kernel(info, first, grads, mixed, mid, away, kept, turned):
    sec = info[SEC]
    turned[...] = jnp.transpose(first[...])
    width = mixed.shape[1] // 2
    for target, half in ((away, 1 - sec), (kept, sec)):
        at = pl.ds(pl.multiple_of(half * width, width), width)
        left = jnp.transpose(mixed[:, at])
        for m in range(QUARTERS):
            for c in range(2):
                target[m, 0, 0, :, c * width : (c + 1) * width] = dot(
                    turned[span(m), :], grads[c, :, at]
                ).astype(low16)
            target[m, 1, 0, :, :width] = dot(turned[span(m), :], grads[2, :, at]).astype(low16)
            out = dot(left, mid[:, span(m)]).astype(low16)
            target[m, 1, 0, :width, width:] = out[:, :width]
            target[m, 1, 0, width:, width:] = out[:, width:]


def add16(a, b):
    return (a.astype(f32) + b.astype(f32)).astype(low16)


def merge_kernel(kept, arrived, send_a, send_b, keep_a, keep_b):
    for part, pairs in enumerate(
        (((send_a, SEND_A), (keep_a, KEEP_A)), ((send_b, SEND_B), (keep_b, KEEP_B)))
    ):
        for target, order in pairs:
            for place, m in enumerate(order):
                target[place] = add16(kept[m, part], arrived[m, part])


def pick_kernel(info, *refs):
    sec = info[SEC]
    *units, given, kept = refs
    half = len(units) // 2
    place = 0
    for mine, theirs in zip(units[:half], units[half:]):
        for n in range(mine.shape[0]):
            local, world = mine[n], theirs[n]
            given[place] = jnp.where(sec == 0, local, world)
            kept[place] = jnp.where(sec == 0, world, local)
            place += 1


def whole_quarters(refs):
    own, x_part, y_part, far_kept, far_arrived = refs
    count = own.shape[0] // 2

    def unit(m, index):
        if m < 3:
            return (own, x_part, y_part)[m][index]
        return far_kept[index] if index < count else far_arrived[index - count]

    return unit, count


def feed_final_kernel(info, own, x_part, y_part, far_kept, far_arrived, up, down):
    low, sec = info[LOW], info[SEC]
    unit, count = whole_quarters((own, x_part, y_part, far_kept, far_arrived))
    wide = up.shape[1] // 2
    for m in range(QUARTERS):
        at = pl.ds(block_at(low, m), UNIT)
        for source, half in ((0, sec), (count, 1 - sec)):
            for part in range(2):
                hidden = pl.ds(pl.multiple_of(half * wide + part * UNIT, UNIT), UNIT)
                up[at, hidden] = unit(m, source + part).astype(f32)
                down[hidden, at] = unit(m, source + 2 + part).astype(f32)


def mix_final_kernel(info, own, x_part, y_part, far_kept, far_arrived, qkv, out):
    low, sec = info[LOW], info[SEC]
    unit, count = whole_quarters((own, x_part, y_part, far_kept, far_arrived))
    width = out.shape[0] // 2
    for m in range(QUARTERS):
        at = pl.ds(block_at(low, m), UNIT)
        at_left = pl.ds(block_at(low, m), width)
        at_right = pl.ds(pl.multiple_of(block_at(low, m) + width, width), width)
        for source, half in ((0, sec), (count, 1 - sec)):
            lanes = pl.ds(pl.multiple_of(half * width, width), width)
            query_keys = unit(m, source).astype(f32)
            qkv[0, at, lanes] = query_keys[:, :width]
            qkv[1, at, lanes] = query_keys[:, width:]
            rest = unit(m, source + 1).astype(f32)
            qkv[2, at, lanes] = rest[:, :width]
            out[lanes, at_left] = rest[:width, width:]
            out[lanes, at_right] = rest[width:, width:]


def sum_rest(value):
    step = QUARTERS
    while step < lax.axis_size("dp"):
        value = add16(value, swap(value, "dp", step))
        step *= 2
    return value


def reduce_dp(send_a, send_b, keep_a, keep_b):
    from_x = swap(send_a, "dp", 1)
    from_y = swap(send_b, "dp", 2)
    own_a, far_a = add16(keep_a[0], from_x[0]), add16(keep_a[1], from_x[1])
    own_b, far_b = add16(keep_b[0], from_y[0]), add16(keep_b[1], from_y[1])
    from_y = swap(far_a, "dp", 2)
    from_x = swap(far_b, "dp", 1)
    return sum_rest(add16(own_a, from_y)), sum_rest(add16(own_b, from_x))


def reduce_tensor(a, b):
    total = jnp.stack([a[0], b[0]]).astype(f32)
    for k in (1, 2, 3):
        total = total + swap(jnp.stack([a[k], b[k]]), "tensor", k).astype(f32)
    return total.astype(low16)


def gather_dp(units):
    count = units.shape[0] // 2
    x_part = swap(units, "dp", 1)
    y_part = swap(units, "dp", 2)
    far_kept = swap(x_part[:count], "dp", 2)
    far_arrived = swap(y_part[count:], "dp", 1)
    return units, x_part, y_part, far_kept, far_arrived


def on_device(codes, lengths, gains, w_qkv, w_out, w_up, w_down, cotangent):
    sec = lax.axis_index("section")
    low = lax.axis_index("dp") % QUARTERS
    z = lax.axis_index("tensor")
    first_core = sec == 0
    utts, frames, code_count, width = codes.shape
    heads_width = w_out.shape[1]
    half = heads_width // 2
    wide = w_up.shape[2]
    rows_g = 4 * frames
    rows_l = utts * code_count * frames
    tiles = 2 * wide // UNIT
    info = jnp.concatenate([jnp.stack([low, sec, z]).astype(jnp.int32), lengths])

    code_rows = jnp.transpose(codes, (0, 2, 1, 3))
    cot_rows = jnp.transpose(cotangent, (0, 2, 1, 3))
    own_w = (jnp.transpose(w_qkv[0], (1, 0, 2)), w_out[0], w_up[0], w_down[0])

    def sem(count):
        return pltpu.SemaphoreType.DMA((count,))

    other_gain = swap(gains[0], "section", 1)
    other_w = tuple(swap(w, "section", 1) for w in own_w)
    both_w = tuple(w for pair in zip(own_w, other_w) for w in pair)
    attention_w, feed_w = both_w[:4], both_w[4:]

    first_rows, start_g, gain_g, gain_l = call(
        start_kernel,
        [
            shape((frames, width), low16),
            shape((frames, width), f32),
            shape((2, width), f32),
            shape((2, width), f32),
        ],
        (info, code_rows, gains[0], other_gain),
        [SM, VM, VM, VM],
        moved=2 * MIB,
    )

    def pieces(quarters):
        return call(
            functools.partial(piece_kernel, quarters),
            [shape((len(quarters), 6, UNIT, UNIT), low16)],
            (info,) + both_w,
            [SM] + [ANY] * 8,
            [sem(9 * len(quarters))],
            out_specs=[ANY],
            moved=2 * len(quarters) * MIB,
        )[0]

    own_piece = pieces((0,))
    rest_pieces = pieces((1, 2, 3))
    by_z = {1: swap(own_piece, "tensor", 1), 2: swap(own_piece, "tensor", 2)}
    by_z[3] = swap(by_z[2], "tensor", 1)
    local_w = [own_piece, rest_pieces]
    for k in (1, 2, 3):
        x_part = swap(by_z[k], "dp", 1)
        y_part = swap(by_z[k], "dp", 2)
        local_w += [
            by_z[k],
            x_part,
            y_part,
            swap(x_part[:, :3], "dp", 2),
            swap(y_part[:, 3:], "dp", 1),
        ]
    local_w = tuple(local_w)

    def gather(rows):
        return lax.all_gather(rows, "tensor", axis=0, tiled=True)

    def scatter(partial):
        return lax.all_to_all(partial, "tensor", 0, 0)

    first_g = gather(first_rows)
    packed_g, probs_g, mixed_g, partial = call(
        global_attention_kernel,
        [
            shape((3, rows_g, heads_width), low16),
            shape((heads_width // HEAD_DIM, rows_g, rows_g), f32),
            shape((rows_g, heads_width), low16),
            shape((4, frames, width), low16),
        ],
        (info, first_g) + attention_w,
        [SM, VM] + [ANY] * 4,
        [
            pltpu.VMEM((3, width, heads_width), low16),
            pltpu.VMEM((heads_width, width), low16),
            sem(8),
        ],
        flops=2 * 10**9,
        moved=8 * MIB,
    )
    hidden_g, second_rows = call(
        middle_kernel,
        [shape((frames, width), f32), shape((frames, width), low16)],
        (start_g, scatter(partial), gain_g),
        [VM] * 3,
        moved=2 * MIB,
    )
    second_g = gather(second_rows)
    lifted_g, active_g, partial = call(
        global_feed_kernel,
        [
            shape((rows_g, wide), f32),
            shape((rows_g, wide), low16),
            shape((4, frames, width), low16),
        ],
        (info, second_g) + feed_w,
        [SM, VM] + [ANY] * 4,
        [
            pltpu.VMEM((width, wide), low16),
            pltpu.VMEM((wide, width), low16),
            pltpu.VMEM((rows_g, width), f32),
            sem(8),
        ],
        flops=2 * 10**9,
        moved=8 * MIB,
    )
    sent = call(
        sent_kernel,
        [shape((frames, width), low16)],
        (hidden_g, scatter(partial)),
        [VM] * 2,
        moved=MIB,
    )[0]

    start_l, first_l, query_keys, values_l, probs_l, mixed_l, partial = call(
        local_attention_kernel,
        [
            shape((rows_l, width), f32),
            shape((rows_l, width), low16),
            shape((4, rows_l, 2 * half), low16),
            shape((4, rows_l, half), low16),
            shape((4, utts, 2 * rows_l // utts, half), f32),
            shape((rows_l, 4 * half), low16),
            shape((rows_l, width), low16),
        ],
        (info, code_rows, sent, swap(sent, "section", 1), gain_l) + local_w,
        [SM] + [VM] * 4 + [ANY] * 17,
        [
            pltpu.VMEM((4, 2, width, UNIT), low16),
            pltpu.VMEM((4 * half, width), low16),
            sem(32),
        ],
        limit=40,
        flops=4 * 10**9,
        moved=20 * MIB,
    )
    hidden_l, second_l, top_l, active_l, grad_lifted_l, back, branch_l = call(
        local_feed_kernel,
        [
            shape((rows_l, width), f32),
            shape((rows_l, width), low16),
            shape((rows_l, width), low16),
            shape((tiles, rows_l, UNIT), low16),
            shape((tiles, rows_l, UNIT), low16),
            shape((rows_l, width), low16),
            shape((rows_l, width), low16),
        ],
        (info, start_l, partial, swap(partial, "section", 1), gain_l, cot_rows) + local_w,
        [SM] + [VM] * 5 + [ANY] * 17,
        [
            pltpu.VMEM((tiles, width, UNIT), low16),
            pltpu.VMEM((tiles, UNIT, width), low16),
            pltpu.VMEM((rows_l, width), f32),
            pltpu.VMEM((rows_l, width), f32),
            sem(8 * tiles),
        ],
        limit=48,
        flops=10 * 10**9,
        moved=24 * MIB,
    )

    send_shape = shape((2, 4, UNIT, UNIT), low16)
    turned_l = pltpu.VMEM((width, rows_l), low16)
    down_units = call(
        local_down_kernel,
        [send_shape] * 4,
        (active_l, top_l),
        [VM] * 2,
        flops=3 * 10**9,
        moved=8 * MIB,
    )
    up_units = call(
        local_up_kernel,
        [send_shape] * 4,
        (second_l, grad_lifted_l),
        [VM] * 2,
        [turned_l],
        flops=3 * 10**9,
        moved=8 * MIB,
    )
    grad_hidden_l, mid_l, grad_query_keys, grad_values, back, gain2_l = call(
        local_attention_back_kernel,
        [
            shape((rows_l, width), f32),
            shape((rows_l, width), low16),
            shape((4, rows_l, 2 * half), low16),
            shape((4, rows_l, half), low16),
            shape((rows_l, width), low16),
            shape((1, width), f32),
        ],
        (hidden_l, back, swap(back, "section", 1), top_l, gain_l, query_keys, values_l, probs_l)
        + local_w,
        [VM] * 8 + [ANY] * 17,
        [
            pltpu.VMEM((4, 2, width, UNIT), low16),
            pltpu.VMEM((4 * half, width), low16),
            pltpu.VMEM((rows_l, width), f32),
            sem(32),
        ],
        limit=40,
        flops=5 * 10**9,
        moved=20 * MIB,
    )
    mix_units = call(
        local_mix_kernel,
        [send_shape] * 4,
        (first_l, grad_query_keys, grad_values, mixed_l, mid_l),
        [VM] * 5,
        [turned_l],
        flops=3 * 10**9,
        moved=8 * MIB,
    )
    returned, code_part, gain1_l = call(
        local_end_kernel,
        [
            shape((frames, width), low16),
            shape((utts, code_count, frames, width // 2), f32),
            shape((1, width), f32),
        ],
        (info, back, swap(back, "section", 1), start_l, grad_hidden_l, gain_l),
        [SM] + [VM] * 5,
        [pltpu.VMEM((rows_l, width), f32)],
        moved=6 * MIB,
    )
    output = call(
        output_kernel,
        [shape((utts, code_count, frames, width // 2), low16)],
        (info, hidden_l, branch_l, swap(branch_l, "section", 1)),
        [SM] + [VM] * 3,
        moved=4 * MIB,
    )[0]

    top_g = gather(returned)
    grad_lifted_g, partial = call(
        global_feed_back_kernel,
        [shape((rows_g, wide), low16), shape((4, frames, width), low16)],
        (info, top_g, lifted_g) + feed_w,
        [SM, VM, VM] + [ANY] * 4,
        [
            pltpu.VMEM((width, wide), low16),
            pltpu.VMEM((wide, width), low16),
            pltpu.VMEM((rows_g, width), f32),
            sem(8),
        ],
        flops=2 * 10**9,
        moved=8 * MIB,
    )
    grad_hidden_g, mid_rows, gain2_g = call(
        middle_back_kernel,
        [shape((frames, width), f32), shape((frames, width), low16), shape((1, width), f32)],
        (scatter(partial), hidden_g, gain_g, returned),
        [VM] * 4,
        moved=2 * MIB,
    )
    away_feed, kept_feed = call(
        global_feed_grad_kernel,
        [shape((QUARTERS, 2, 2, UNIT, UNIT), low16)] * 2,
        (info, second_g, grad_lifted_g, active_g, top_g),
        [SM] + [VM] * 4,
        [pltpu.VMEM((width, rows_g), low16)],
        flops=4 * 10**9,
        moved=8 * MIB,
    )
    mid_g = gather(mid_rows)
    grads_g, partial = call(
        global_attention_back_kernel,
        [shape((3, rows_g, heads_width), low16), shape((4, frames, width), low16)],
        (info, mid_g, packed_g, probs_g) + attention_w,
        [SM, VM, VM, VM] + [ANY] * 4,
        [
            pltpu.VMEM((3, width, heads_width), low16),
            pltpu.VMEM((heads_width, width), low16),
            sem(8),
        ],
        flops=2 * 10**9,
        moved=8 * MIB,
    )
    away_mix, kept_mix = call(
        global_mix_grad_kernel,
        [shape((QUARTERS, 2, 1, UNIT, UNIT), low16)] * 2,
        (info, first_g, grads_g, mixed_g, mid_g),
        [SM] + [VM] * 4,
        [pltpu.VMEM((width, rows_g), low16)],
        flops=2 * 10**9,
        moved=4 * MIB,
    )
    kept_start, given_start, gain1_g = call(
        start_back_kernel,
        [
            shape((frames, width // 2), f32),
            shape((frames, width // 2), f32),
            shape((1, width), f32),
        ],
        (info, scatter(partial), start_g, gain_g, grad_hidden_g),
        [SM] + [VM] * 4,
        [pltpu.VMEM((frames, width), f32)],
        moved=2 * MIB,
    )
    arrived_start = swap(given_start, "section", 1)
    both_start = jnp.stack(
        [
            jnp.where(first_core, kept_start, arrived_start),
            jnp.where(first_core, arrived_start, kept_start),
        ]
    )
    code_grad = jnp.transpose(code_part + both_start[:, None], (0, 2, 1, 3))

    own_gain = jnp.concatenate([gain1_g, gain2_g], axis=0)
    total_gain = own_gain + swap(own_gain, "section", 1)
    local_gain = jnp.concatenate([gain1_l, gain2_l], axis=0)
    gain_total = jnp.where(first_core, total_gain, local_gain)
    gain_total = jnp.concatenate(
        [
            lax.dynamic_slice_in_dim(gain_total, (low ^ m) * UNIT, UNIT, 1)
            for m in range(QUARTERS)
        ],
        axis=1,
    )
    for axis in ("tensor", "dp"):
        step = 1
        while step < lax.axis_size(axis):
            gain_total = gain_total + swap(gain_total, axis, step)
            step *= 2

    local_down = reduce_tensor(*reduce_dp(*down_units))
    local_up = reduce_tensor(*reduce_dp(*up_units))
    local_mix = reduce_tensor(*reduce_dp(*mix_units))

    def global_sum(away, kept, count):
        units = call(
            merge_kernel,
            [shape((2, count, UNIT, UNIT), low16)] * 4,
            (kept, swap(away, "section", 1)),
            [VM] * 2,
            moved=2 * count * MIB,
        )
        return reduce_dp(*units)

    def finish(local_units, global_units, body, outs):
        count = sum(unit.shape[0] for unit in local_units)
        given, kept = call(
            pick_kernel,
            [shape((count, UNIT, UNIT), low16)] * 2,
            (info,) + tuple(local_units) + tuple(global_units),
            [SM] + [VM] * (len(local_units) + len(global_units)),
            moved=2 * MIB,
        )
        arrived = swap(given, "section", 1)
        return call(
            body,
            outs,
            (info,) + gather_dp(jnp.concatenate([kept, arrived])),
            [SM] + [VM] * 5,
            limit=32,
            moved=16 * MIB,
        )

    feed_a, feed_b = global_sum(away_feed, kept_feed, 2)
    mix_a, mix_b = global_sum(away_mix, kept_mix, 1)
    global_up = jnp.stack([feed_a[0], feed_b[0]])
    global_down = jnp.stack([feed_a[1], feed_b[1]])
    up_grad, down_grad = finish(
        (local_up, local_down),
        (global_up, global_down),
        feed_final_kernel,
        [shape((width, wide), f32), shape((wide, width), f32)],
    )
    qkv_grad, out_grad = finish(
        (local_mix,),
        (jnp.concatenate([mix_a, mix_b]),),
        mix_final_kernel,
        [shape((3, width, heads_width), f32), shape((heads_width, width), f32)],
    )
    return (
        jnp.transpose(output, (0, 2, 1, 3)),
        code_grad,
        gain_total[None],
        jnp.transpose(qkv_grad, (1, 0, 2))[None],
        out_grad[None],
        up_grad[None],
        down_grad[None],
    )


def solution(mesh):
    in_specs = (
        P("dp", "tensor", None, None),
        P("dp"),
        P("section", None, None),
        P("section", None, None, "tensor"),
        P("section", "tensor", None),
        P("section", None, "tensor"),
        P("section", "tensor", None),
        P("dp", "tensor", None, None),
    )
    out_specs = (
        P("dp", "tensor", None, "section"),
        P("dp", "tensor", None, "section"),
        P("section", None, None),
        P("section", None, None, "tensor"),
        P("section", "tensor", None),
        P("section", None, "tensor"),
        P("section", "tensor", None),
    )
    return jax.shard_map(
        on_device, mesh=mesh, in_specs=in_specs, out_specs=out_specs, check_vma=False
    )
```

```python
import functools

import jax
import jax.numpy as jnp
from jax import lax
from jax.experimental import pallas as pl
from jax.experimental.pallas import tpu as pltpu
from jax.sharding import PartitionSpec as P

HEAD_DIM = 64
SCALE = HEAD_DIM ** (-0.5)
QUARTERS = 4
UNIT = 256
epsilon = 1e-06
negative = -1e30
f32 = jnp.float32
low16 = jnp.bfloat16

VM = pl.BlockSpec(memory_space=pltpu.VMEM)
SM = pl.BlockSpec(memory_space=pltpu.SMEM)
ANY = pl.BlockSpec(memory_space=pltpu.HBM)
MIB = 1 << 20

LOW, SEC, SHARD, LENGTHS = 0, 1, 2, 3


def shape(dims, dtype):
    return jax.ShapeDtypeStruct(tuple(dims), dtype)


class Order:
    def __init__(self):
        self.token = None

    def after(self, value):
        if self.token is None:
            return value
        return lax.optimization_barrier((value, self.token))[0]

    def call(self, body, outs, args, specs, scratch=(), limit=56, flops=0, moved=0, grid=()):
        args = (self.after(args[0]),) + tuple(args[1:])
        results = pl.pallas_call(
            body,
            out_shape=tuple(outs),
            grid=grid,
            in_specs=list(specs),
            out_specs=tuple(VM for _ in outs),
            scratch_shapes=list(scratch),
            compiler_params=pltpu.CompilerParams(vmem_limit_bytes=limit * MIB),
            cost_estimate=pl.CostEstimate(flops=flops, bytes_accessed=moved, transcendentals=0),
        )(*args)
        self.token = results[-1]
        return results


def swap(value, axis, flip):
    count = lax.axis_size(axis)
    return lax.ppermute(value, axis, [(i, i ^ flip) for i in range(count)])


def swap_one(value, axis, flip, section):
    count = lax.axis_size(axis)
    base = section * count
    pairs = [(base + i, base + (i ^ flip)) for i in range(count)]
    return lax.ppermute(value, ("section", axis), pairs)


def dot(a, b):
    return jnp.dot(a, b, preferred_element_type=f32)


def dot_tn(a, b):
    return lax.dot_general(a, b, (((0,), (0,)), ((), ())), preferred_element_type=f32)


def dot_nt(a, b):
    return lax.dot_general(a, b, (((1,), (1,)), ((), ())), preferred_element_type=f32)


def factor_of(values):
    return lax.rsqrt(jnp.mean(values * values, axis=-1, keepdims=True) + epsilon)


def norm_back(values, gain, upstream):
    factor = factor_of(values)
    weighted = upstream * gain
    inner = jnp.mean(weighted * values, axis=-1, keepdims=True)
    through = factor * weighted - values * (factor * factor * factor) * inner
    return through, jnp.sum(upstream * values * factor, axis=0, keepdims=True)


def normal_cdf(values):
    return 0.5 * (1.0 + lax.erf(values * (0.5**0.5)))


def gelu_slope(values, cdf):
    return cdf + values * (jnp.exp(-0.5 * values * values) * 0.3989422804014327)


def block_at(low, m):
    return pl.multiple_of((low ^ m) * UNIT, UNIT)


def span(m):
    return slice(m * UNIT, (m + 1) * UNIT)


class Copies:
    def __init__(self, sems):
        self.sems = sems
        self.made = []

    def start(self, src, dst):
        copy = pltpu.make_async_copy(src, dst, self.sems.at[len(self.made)])
        copy.start()
        self.made.append(copy)
        return copy

    def pick(self, own_first, sec, own, other, dst):
        sem = self.sems.at[len(self.made)]

        @pl.when((sec == 0) == own_first)
        def _():
            pltpu.make_async_copy(own, dst, sem).start()

        @pl.when((sec == 0) != own_first)
        def _():
            pltpu.make_async_copy(other, dst, sem).start()

        copy = pltpu.make_async_copy(own, dst, sem)
        self.made.append(copy)
        return copy

    def wait(self, begin=0, end=None):
        for copy in self.made[begin:end]:
            copy.wait()


def start_kernel(info, codes, own_gain, other_gain, first, start, gain_g, gain_l):
    low, sec = info[LOW], info[SEC]
    for m in range(QUARTERS):
        at = pl.ds(block_at(low, m), UNIT)
        own, other = own_gain[:, at], other_gain[:, at]
        gain_g[:, span(m)] = jnp.where(sec == 0, own, other)
        gain_l[:, span(m)] = jnp.where(sec == 0, other, own)
        total = codes[sec, 0, :, at].astype(f32)
        for c in range(1, codes.shape[1]):
            total = total + codes[sec, c, :, at].astype(f32)
        start[:, span(m)] = total
    values = start[...]
    first[...] = (values * factor_of(values) * gain_g[0:1, :]).astype(low16)


def from_local(sec, own, other, branch):
    @pl.when(sec == 0)
    def _():
        branch(0, *other)

    @pl.when(sec != 0)
    def _():
        branch(1, *own)


def mix_piece_kernel(info, own_qkv, other_qkv, own_out, other_out, piece, whole, sems):
    low, sec = info[LOW], info[SEC]
    half = own_qkv.shape[2] // 2

    def branch(half_index, qkv, out):
        made = Copies(sems)
        for m in range(QUARTERS):
            at = pl.ds(block_at(low, m), UNIT)
            at_right = pl.ds(pl.multiple_of(block_at(low, m) + half, half), half)
            at_left = pl.ds(block_at(low, m), half)
            lanes = slice(half_index * half, (half_index + 1) * half)
            target = whole.at[m]
            made.start(qkv.at[0, at, lanes], target.at[0, :, 0:half])
            made.start(qkv.at[1, at, lanes], target.at[0, :, half : 2 * half])
            made.start(qkv.at[2, at, lanes], target.at[1, :, 0:half])
            made.start(out.at[lanes, at_left], target.at[1, 0:half, half : 2 * half])
            made.start(out.at[lanes, at_right], target.at[1, half : 2 * half, half : 2 * half])
        made.wait()

    from_local(sec, (own_qkv, own_out), (other_qkv, other_out), branch)
    piece[...] = whole[0]


def feed_piece_kernel(info, own_up, other_up, own_down, other_down, piece, whole, sems):
    low, sec = info[LOW], info[SEC]
    wide = own_up.shape[1] // 2

    def branch(half_index, up, down):
        made = Copies(sems)
        for m in range(QUARTERS):
            at = pl.ds(block_at(low, m), UNIT)
            for part in range(2):
                begin = half_index * wide + part * UNIT
                hidden = slice(begin, begin + UNIT)
                made.start(up.at[at, hidden], whole.at[m, part])
                made.start(down.at[hidden, at], whole.at[m, 2 + part])
        made.wait()

    from_local(sec, (own_up, own_down), (other_up, other_down), branch)
    piece[...] = whole[0]


def fetch_attention(made, low, sec, own_qkv, other_qkv, own_out, other_out, qkv, out):
    for m in range(QUARTERS):
        at = pl.ds(block_at(low, m), UNIT)
        made.pick(True, sec, own_qkv.at[:, at, :], other_qkv.at[:, at, :], qkv.at[:, span(m), :])
    for m in range(QUARTERS):
        at = pl.ds(block_at(low, m), UNIT)
        made.pick(True, sec, own_out.at[:, at], other_out.at[:, at], out.at[:, span(m)])


def global_attention_kernel(info, rows, own_qkv, other_qkv, own_out, other_out,
                            packed, probs, mixed, partial, qkv, out, sems):
    low, sec = info[LOW], info[SEC]
    made = Copies(sems)
    fetch_attention(made, low, sec, own_qkv, other_qkv, own_out, other_out, qkv, out)
    count = rows.shape[0]
    length = info[LENGTHS + sec]
    query_at = lax.broadcasted_iota(jnp.int32, (count, count), 0)
    key_at = lax.broadcasted_iota(jnp.int32, (count, count), 1)
    allowed = (key_at <= query_at) & (key_at < length)
    made.wait(0, QUARTERS)
    values = rows[...]
    for c in range(3):
        packed[c] = dot(values, qkv[c]).astype(low16)
    heads = []
    for h in range(packed.shape[2] // HEAD_DIM):
        lanes = slice(h * HEAD_DIM, (h + 1) * HEAD_DIM)
        scores = dot_nt(packed[0, :, lanes], packed[1, :, lanes]) * SCALE
        scores = jnp.where(allowed, scores, negative)
        raised = jnp.exp(scores - jnp.max(scores, axis=-1, keepdims=True))
        exact = raised / jnp.sum(raised, axis=-1, keepdims=True)
        probs[h] = exact
        heads.append(dot(exact.astype(low16), packed[2, :, lanes]).astype(low16))
    mixed[...] = jnp.concatenate(heads, axis=1)
    made.wait(QUARTERS)
    partial[...] = dot(mixed[...], out[...]).astype(low16).reshape(partial.shape)


def total_of(arrived):
    total = arrived[0].astype(f32)
    for k in range(1, arrived.shape[0]):
        total = total + arrived[k].astype(f32)
    return total


def middle_kernel(start, arrived, gain, hidden, second):
    values = start[...] + total_of(arrived)
    hidden[...] = values
    second[...] = (values * factor_of(values) * gain[1:2, :]).astype(low16)


def fetch_feed(made, low, sec, own_up, other_up, own_down, other_down, up, down):
    for m in range(QUARTERS):
        at = pl.ds(block_at(low, m), UNIT)
        made.pick(True, sec, own_up.at[at, :], other_up.at[at, :], up.at[span(m), :])
    for m in range(QUARTERS):
        at = pl.ds(block_at(low, m), UNIT)
        made.pick(True, sec, own_down.at[:, at], other_down.at[:, at], down.at[:, span(m)])


def global_feed_kernel(info, rows, own_up, other_up, own_down, other_down,
                       lifted, active, partial, up, down, total, sems):
    made = Copies(sems)
    fetch_feed(made, info[LOW], info[SEC], own_up, other_up, own_down, other_down, up, down)
    made.wait(0, QUARTERS)
    values = rows[...]
    for t in range(up.shape[1] // UNIT):
        tile = dot(values, up[:, span(t)])
        lifted[:, span(t)] = tile
        low_tile = (tile * normal_cdf(tile)).astype(low16)
        active[:, span(t)] = low_tile
        if t == 0:
            made.wait(QUARTERS)
        branch = dot(low_tile, down[span(t), :])
        total[...] = branch if t == 0 else total[...] + branch
    partial[...] = total[...].astype(low16).reshape(partial.shape)


def sent_kernel(hidden, arrived, sent):
    sent[...] = (hidden[...] + total_of(arrived)).astype(low16)


def global_feed_back_kernel(info, top, lifted, own_up, other_up, own_down, other_down,
                            grad_lifted, partial, up, down, total, sems):
    made = Copies(sems)
    fetch_feed(made, info[LOW], info[SEC], own_up, other_up, own_down, other_down, up, down)
    made.wait(QUARTERS)
    values = top[...]
    for t in range(up.shape[1] // UNIT):
        tile = lifted[:, span(t)]
        grad = dot_nt(values, down[span(t), :]) * gelu_slope(tile, normal_cdf(tile))
        grad = grad.astype(low16)
        grad_lifted[:, span(t)] = grad
        if t == 0:
            made.wait(0, QUARTERS)
        back = dot_nt(grad, up[:, span(t)])
        total[...] = back if t == 0 else total[...] + back
    partial[...] = total[...].astype(low16).reshape(partial.shape)


def middle_back_kernel(arrived, hidden, gain, returned, grad_hidden, mid, gain_grad):
    through, gain_grad[...] = norm_back(hidden[...], gain[1:2, :], total_of(arrived))
    values = returned[...].astype(f32) + through
    grad_hidden[...] = values
    mid[...] = values.astype(low16)


def global_attention_back_kernel(info, mid, packed, probs, own_qkv, other_qkv, own_out, other_out,
                                 grads, partial, qkv, out, sems):
    low, sec = info[LOW], info[SEC]
    made = Copies(sems)
    fetch_attention(made, low, sec, own_qkv, other_qkv, own_out, other_out, qkv, out)
    made.wait(QUARTERS)
    grad_mixed = dot_nt(mid[...], out[...]).astype(low16)
    columns = [[], [], []]
    for h in range(packed.shape[2] // HEAD_DIM):
        lanes = slice(h * HEAD_DIM, (h + 1) * HEAD_DIM)
        exact = probs[h]
        grad = grad_mixed[:, lanes]
        columns[2].append(dot_tn(exact.astype(low16), grad).astype(low16))
        grad_probs = dot_nt(grad, packed[2, :, lanes])
        center = jnp.sum(grad_probs * exact, axis=-1, keepdims=True)
        grad_scores = (exact * (grad_probs - center)).astype(low16)
        columns[0].append((dot(grad_scores, packed[1, :, lanes]) * SCALE).astype(low16))
        columns[1].append((dot_tn(grad_scores, packed[0, :, lanes]) * SCALE).astype(low16))
    total = None
    made.wait(0, QUARTERS)
    for c in range(3):
        grads[c] = jnp.concatenate(columns[c], axis=1)
        back = dot_nt(grads[c], qkv[c])
        total = back if c == 0 else total + back
    partial[...] = total.astype(low16).reshape(partial.shape)


def start_back_kernel(info, arrived, start, gain, grad_hidden, kept, given, gain_grad, values):
    low, sec = info[LOW], info[SEC]
    through, gain_grad[...] = norm_back(start[...], gain[0:1, :], total_of(arrived))
    values[...] = grad_hidden[...] + through
    for j in range(2):
        kept[:, span(j)] = values[:, pl.ds(block_at(low, 2 * sec + j), UNIT)]
        given[:, span(j)] = values[:, pl.ds(block_at(low, 2 * (1 - sec) + j), UNIT)]


def mix_unit(refs, k, m, u):
    whole, near, x_part, y_part, far = refs[0], refs[1:4], refs[4], refs[5], refs[6:8]
    if k == 0:
        return whole.at[m, u]
    if m == 0:
        return near[k - 1].at[u]
    if m == 3:
        return far[u].at[k - 1]
    return (x_part if m == 1 else y_part).at[k - 1, u]


def feed_unit(refs, k, m, u):
    if k == 0:
        return refs[0].at[m, u]
    base = refs[5 * k - 4 : 5 * k + 1]
    if m < 3:
        return base[m].at[u]
    return base[3].at[u] if u < 2 else base[4].at[u - 2]


MIX_REFS, FEED_REFS = 8, 16


def pair_rows(a, b, size):
    return jnp.concatenate([a * b, a[size:] * b[: 2 * size], a[2 * size :] * b[:size]], axis=0)


def by_pair(stacked, size):
    names = [(0, 0), (1, 1), (2, 2), (1, 0), (2, 1), (2, 0)]
    return {name: stacked[n * size : (n + 1) * size] for n, name in enumerate(names)}


def from_pairs(pairs):
    names = [(0, 0), (1, 1), (2, 2), (1, 0), (2, 1), (2, 0)]
    return jnp.concatenate([pairs[name] for name in names], axis=0)


def head_sums(products, table):
    upper = products.astype(low16)
    lower = (products - upper.astype(f32)).astype(low16)
    return dot(upper, table) + dot(lower, table)


def head_table(width):
    row = lax.broadcasted_iota(jnp.int32, (width, width), 0) // HEAD_DIM
    column = lax.broadcasted_iota(jnp.int32, (width, width), 1) // HEAD_DIM
    return (row == column).astype(f32).astype(low16)


def gather_mix(weights, mix, k, half):
    for m in range(QUARTERS):
        begin = m * UNIT
        mix[k * half : (k + 1) * half, begin : begin + half] = weights[
            k, 1, begin : begin + half, half:
        ]
        mix[k * half : (k + 1) * half, begin + half : begin + UNIT] = weights[
            k, 1, begin + half : begin + UNIT, half:
        ]


def local_attention_kernel(info, codes, sent_own, sent_other, gain, *rest):
    refs, (start, first, query_keys, values_out, probs, mixed, partial, weights, mix, sems) = (
        rest[:MIX_REFS], rest[MIX_REFS:]
    )
    low, sec = info[LOW], info[SEC]
    made = Copies(sems)
    groups = []
    for k in range(4):
        groups.append(
            [
                made.start(mix_unit(refs, k, m, u), weights.at[k, u, span(m), :])
                for u in range(2)
                for m in range(QUARTERS)
            ]
        )
    utts, code_count, frames, _ = codes.shape
    for u in range(utts):
        sent = jnp.where(sec == u, sent_own[...], sent_other[...]).astype(f32)
        for c in range(code_count):
            row = (u * code_count + c) * frames
            for m in range(QUARTERS):
                code = codes[u, c, :, pl.ds(block_at(low, m), UNIT)].astype(f32)
                start[row : row + frames, span(m)] = sent[:, span(m)] + code
    values = start[...]
    first[...] = (values * factor_of(values) * gain[0:1, :]).astype(low16)
    half = values_out.shape[2]
    table = head_table(half)
    rows = first[...]
    size = frames
    group = code_count * frames
    for k in range(4):
        for copy in groups[k]:
            copy.wait()
        query_keys[k] = dot(rows, weights[k, 0]).astype(low16)
        values_out[k] = dot(rows, weights[k, 1, :, :half]).astype(low16)
        gather_mix(weights, mix, k, half)
        for u in range(utts):
            at = slice(u * group, (u + 1) * group)
            q = query_keys[k, at, :half].astype(f32)
            key = query_keys[k, at, half:].astype(f32)
            val = values_out[k, at, :].astype(f32)
            scores = by_pair(head_sums(pair_rows(q, key, size), table) * SCALE, size)
            exact = {}
            for i in range(3):
                peak = scores[(i, 0)]
                for j in range(1, i + 1):
                    peak = jnp.maximum(peak, scores[(i, j)])
                raised = [jnp.exp(scores[(i, j)] - peak) for j in range(i + 1)]
                whole = raised[0]
                for j in range(1, i + 1):
                    whole = whole + raised[j]
                for j in range(i + 1):
                    exact[(i, j)] = raised[j] / whole
            probs[k, u] = from_pairs(exact)
            for i in range(3):
                total = None
                for j in range(i + 1):
                    weight = exact[(i, j)].astype(low16).astype(f32)
                    term = weight * val[j * size : (j + 1) * size]
                    total = term if total is None else total + term
                begin = u * group + i * size
                mixed[begin : begin + size, k * half : (k + 1) * half] = total.astype(low16)
    partial[...] = dot(mixed[...], mix[...]).astype(low16)


def local_feed_kernel(info, start, own_part, other_part, gain, cotangent, *rest):
    refs = rest[:FEED_REFS]
    (hidden, second, top, active, grad_lifted, grad_second,
     up, down, back, sems) = rest[FEED_REFS:]
    low = info[LOW]
    tiles = active.shape[0]
    made = Copies(sems)
    for t in range(tiles):
        for m in range(QUARTERS):
            made.start(feed_unit(refs, t // 2, m, t % 2), up.at[t, span(m), :])
        for m in range(QUARTERS):
            made.start(feed_unit(refs, t // 2, m, 2 + t % 2), down.at[t, :, span(m)])
    utts, code_count, frames, _ = cotangent.shape
    frame_at = lax.broadcasted_iota(jnp.int32, (frames, 1), 0) + info[SHARD] * frames
    for u in range(utts):
        valid = frame_at < info[LENGTHS + u]
        for c in range(code_count):
            row = (u * code_count + c) * frames
            for m in range(QUARTERS):
                part = cotangent[u, c, :, pl.ds(block_at(low, m), UNIT)].astype(f32)
                top[row : row + frames, span(m)] = jnp.where(valid, part, 0.0).astype(low16)
    values = start[...] + (own_part[...].astype(f32) + other_part[...].astype(f32))
    hidden[...] = values
    second[...] = (values * factor_of(values) * gain[1:2, :]).astype(low16)
    back[...] = jnp.zeros_like(back)

    @pl.loop(0, tiles)
    def _(t):
        for m in range(QUARTERS):
            pltpu.make_async_copy(
                refs[0].at[0, 0], up.at[t, span(m), :], sems.at[8 * t + m]
            ).wait()
        for m in range(QUARTERS):
            pltpu.make_async_copy(
                refs[0].at[0, 0], down.at[t, :, span(m)], sems.at[8 * t + 4 + m]
            ).wait()
        tile = dot(second[...], up[t])
        cdf = normal_cdf(tile)
        low_tile = (tile * cdf).astype(low16)
        active[t] = low_tile
        grad = (dot_nt(top[...], down[t]) * gelu_slope(tile, cdf)).astype(low16)
        grad_lifted[t] = grad
        back[...] += dot_nt(grad, up[t])

    grad_second[...] = back[...].astype(low16)


def local_attention_back_kernel(hidden, own_back, other_back, top, gain, query_keys, values_in,
                                probs, *rest):
    refs = rest[:MIX_REFS]
    (grad_hidden, mid, grad_query_keys, grad_values, grad_first, gain_grad,
     weights, mix, total, sems) = rest[MIX_REFS:]
    made = Copies(sems)
    groups = []
    for k in range(4):
        groups.append(
            [
                made.start(mix_unit(refs, k, m, u), weights.at[k, u, span(m), :])
                for u in range(2)
                for m in range(QUARTERS)
            ]
        )
    upstream = own_back[...].astype(f32) + other_back[...].astype(f32)
    through, gain_grad[...] = norm_back(hidden[...], gain[1:2, :], upstream)
    grads = top[...].astype(f32) + through
    grad_hidden[...] = grads
    mid[...] = grads.astype(low16)
    utts = probs.shape[1]
    half = values_in.shape[2]
    group = query_keys.shape[1] // utts
    size = group // 3
    table = head_table(half)
    for k in range(4):
        for copy in groups[k]:
            copy.wait()
        gather_mix(weights, mix, k, half)
        grad_mixed = dot_nt(mid[...], mix[k * half : (k + 1) * half, :]).astype(low16)
        grad_mixed = grad_mixed.astype(f32)
        for u in range(utts):
            at = slice(u * group, (u + 1) * group)
            q = query_keys[k, at, :half].astype(f32)
            key = query_keys[k, at, half:].astype(f32)
            val = values_in[k, at, :].astype(f32)
            grad = grad_mixed[at]
            exact = by_pair(probs[k, u], size)
            grad_probs = by_pair(head_sums(pair_rows(grad, val, size), table), size)
            scored = {}
            for i in range(3):
                center = grad_probs[(i, 0)] * exact[(i, 0)]
                for j in range(1, i + 1):
                    center = center + grad_probs[(i, j)] * exact[(i, j)]
                for j in range(i + 1):
                    score = exact[(i, j)] * (grad_probs[(i, j)] - center)
                    scored[(i, j)] = score.astype(low16).astype(f32)

            def rows_of(array, n):
                return array[n * size : (n + 1) * size]

            for i in range(3):
                begin = u * group + i * size
                to_query = sum(scored[(i, j)] * rows_of(key, j) for j in range(i + 1))
                to_key = sum(scored[(n, i)] * rows_of(q, n) for n in range(i, 3))
                to_value = sum(
                    exact[(n, i)].astype(low16).astype(f32) * rows_of(grad, n)
                    for n in range(i, 3)
                )
                grad_query_keys[k, begin : begin + size, :half] = (to_query * SCALE).astype(low16)
                grad_query_keys[k, begin : begin + size, half:] = (to_key * SCALE).astype(low16)
                grad_values[k, begin : begin + size, :] = to_value.astype(low16)
        back = dot_nt(grad_query_keys[k], weights[k, 0])
        back = back + dot_nt(grad_values[k], weights[k, 1, :, :half])
        total[...] = back if k == 0 else total[...] + back
    grad_first[...] = total[...].astype(low16)


def local_end_kernel(info, own_back, other_back, start, grad_hidden, gain,
                     returned, code_part, gain_grad, values):
    low, sec = info[LOW], info[SEC]
    upstream = own_back[...].astype(f32) + other_back[...].astype(f32)
    through, gain_grad[...] = norm_back(start[...], gain[0:1, :], upstream)
    values[...] = grad_hidden[...] + through
    utts, code_count, frames, _ = code_part.shape
    total = None
    for c in range(code_count):
        begin = pl.multiple_of((sec * code_count + c) * frames, frames)
        part = values[pl.ds(begin, frames), :]
        total = part if total is None else total + part
    returned[...] = total.astype(low16)
    for u in range(utts):
        for c in range(code_count):
            row = (u * code_count + c) * frames
            for j in range(2):
                at = pl.ds(block_at(low, 2 * sec + j), UNIT)
                code_part[u, c, :, span(j)] = values[row : row + frames, at]


def output_kernel(info, hidden, own_part, other_part, output):
    low, sec = info[LOW], info[SEC]
    utts, code_count, frames, _ = output.shape
    frame_at = lax.broadcasted_iota(jnp.int32, (frames, 1), 0) + info[SHARD] * frames
    for u in range(utts):
        valid = frame_at < info[LENGTHS + u]
        for c in range(code_count):
            row = (u * code_count + c) * frames
            rows = slice(row, row + frames)
            for j in range(2):
                at = pl.ds(block_at(low, 2 * sec + j), UNIT)
                value = hidden[rows, at] + (
                    own_part[rows, at].astype(f32) + other_part[rows, at].astype(f32)
                )
                output[u, c, :, span(j)] = jnp.where(valid, value, 0.0).astype(low16)


SEND_A, KEEP_A, SEND_B, KEEP_B = (1, 3), (0, 2), (2, 3), (0, 1)


def local_drop_kernel(active, *rest):
    refs, (branch_out, down, branch, sems) = rest[:FEED_REFS], rest[FEED_REFS:]
    tiles = active.shape[0]
    made = Copies(sems)
    for t in range(tiles):
        for m in range(QUARTERS):
            made.start(feed_unit(refs, t // 2, m, 2 + t % 2), down.at[t, :, span(m)])
    branch[...] = jnp.zeros_like(branch)

    @pl.loop(0, tiles)
    def _(t):
        for m in range(QUARTERS):
            pltpu.make_async_copy(
                refs[0].at[0, 0], down.at[t, :, span(m)], sems.at[QUARTERS * t + m]
            ).wait()
        branch[...] += dot(active[t], down[t])

    branch_out[...] = branch[...].astype(low16)


def local_feed_grad_kernel(second, grad_lifted, active, top,
                           send_a, send_b, keep_a, keep_b, turned):
    turned[...] = jnp.transpose(second[...])
    for k in range(4):
        for part, pairs in enumerate(
            (((send_a, SEND_A), (keep_a, KEEP_A)), ((send_b, SEND_B), (keep_b, KEEP_B)))
        ):
            right = grad_lifted[2 * k + part]
            left = jnp.transpose(active[2 * k + part])
            for target, order in pairs:
                for place, m in enumerate(order):
                    target[place, 2 * k] = dot(turned[span(m), :], right).astype(low16)
                    target[place, 2 * k + 1] = dot(left, top[:, span(m)]).astype(low16)


def local_mix_kernel(first, grad_query_keys, grad_values, mixed, mid,
                     send_a, send_b, keep_a, keep_b, turned):
    turned[...] = jnp.transpose(first[...])
    half = grad_values.shape[2]
    for k in range(4):
        left = jnp.transpose(mixed[:, k * half : (k + 1) * half])
        for target, order in ((send_a, SEND_A), (keep_a, KEEP_A)):
            for place, m in enumerate(order):
                target[place, k] = dot(turned[span(m), :], grad_query_keys[k]).astype(low16)
        for target, order in ((send_b, SEND_B), (keep_b, KEEP_B)):
            for place, m in enumerate(order):
                value = dot(turned[span(m), :], grad_values[k]).astype(low16)
                out = dot(left, mid[:, span(m)]).astype(low16)
                target[place, k, :, :half] = value
                target[place, k, :half, half:] = out[:, :half]
                target[place, k, half:, half:] = out[:, half:]


def global_feed_grad_kernel(info, second, grad_lifted, active, top, away, kept, turned):
    sec = info[SEC]
    turned[...] = jnp.transpose(second[...])
    wide = active.shape[1] // 2
    for target, half in ((away, 1 - sec), (kept, sec)):
        for part in range(2):
            at = pl.ds(pl.multiple_of(half * wide + part * UNIT, UNIT), UNIT)
            right = grad_lifted[:, at]
            left = jnp.transpose(active[:, at])
            for m in range(QUARTERS):
                target[m, part, 0] = dot(turned[span(m), :], right).astype(low16)
                target[m, part, 1] = dot(left, top[:, span(m)]).astype(low16)


def global_mix_grad_kernel(info, first, grads, mixed, mid, away, kept, turned):
    sec = info[SEC]
    turned[...] = jnp.transpose(first[...])
    width = mixed.shape[1] // 2
    for target, half in ((away, 1 - sec), (kept, sec)):
        at = pl.ds(pl.multiple_of(half * width, width), width)
        left = jnp.transpose(mixed[:, at])
        for m in range(QUARTERS):
            for c in range(2):
                target[m, 0, 0, :, c * width : (c + 1) * width] = dot(
                    turned[span(m), :], grads[c, :, at]
                ).astype(low16)
            target[m, 1, 0, :, :width] = dot(turned[span(m), :], grads[2, :, at]).astype(low16)
            out = dot(left, mid[:, span(m)]).astype(low16)
            target[m, 1, 0, :width, width:] = out[:, :width]
            target[m, 1, 0, width:, width:] = out[:, width:]


def add16(a, b):
    return (a.astype(f32) + b.astype(f32)).astype(low16)


def merge_kernel(kept, arrived, send_a, send_b, keep_a, keep_b):
    for part, pairs in enumerate(
        (((send_a, SEND_A), (keep_a, KEEP_A)), ((send_b, SEND_B), (keep_b, KEEP_B)))
    ):
        for target, order in pairs:
            for place, m in enumerate(order):
                target[place] = add16(kept[m, part], arrived[m, part])


def far_kernel(keep_a, from_x, keep_b, from_y, far_a, far_b):
    far_a[...] = add16(keep_a[0], from_x[0])
    far_b[...] = add16(keep_b[0], from_y[0])


def sum_kernel(*refs):
    parts, outs = (refs[:3], refs[3:6]), refs[6:]
    for part, (keep, once, twice) in enumerate(parts):
        total = keep[0].astype(f32) + once[0].astype(f32) + twice[...].astype(f32)
        total = total.astype(low16)
        if len(outs) == 1:
            count = total.shape[0]
            outs[0][part * count : (part + 1) * count] = total
        else:
            count = total.shape[0] // 4
            for k in range(4):
                outs[(k + 1) % 2][k // 2, part * count : (part + 1) * count] = total[
                    k * count : (k + 1) * count
                ]


def far_tensor_kernel(keep, arrived, far):
    far[...] = add16(keep[0], arrived[0])


def total_kernel(keep, once, twice, total):
    for n in range(total.shape[0]):
        value = keep[0, n].astype(f32) + once[0, n].astype(f32) + twice[n].astype(f32)
        total[n] = value.astype(low16)


def half_at(index, count):
    return pl.BlockSpec(
        (1, count, UNIT, UNIT), lambda i: (index, 0, 0, 0), memory_space=pltpu.VMEM
    )


def fetch_quarters(sec, refs, target, sems):
    made = Copies(sems)
    count = target.shape[1]
    for index in range(3):
        made.pick(True, sec, refs[index], refs[5 + index], target.at[index])
    for index in range(2):
        at = pl.ds(index * (count // 2), count // 2)
        made.pick(True, sec, refs[3 + index], refs[8 + index], target.at[3, at])
    return made


def feed_final_kernel(info, *rest):
    refs, (up, down, units, sems) = rest[:10], rest[10:]
    low, sec = info[LOW], info[SEC]
    fetch_quarters(sec, refs, units, sems).wait()
    wide = up.shape[1] // 2
    count = units.shape[1] // 2
    for m in range(QUARTERS):
        at = pl.ds(block_at(low, m), UNIT)
        for source, half in ((0, sec), (count, 1 - sec)):
            for part in range(2):
                hidden = pl.ds(pl.multiple_of(half * wide + part * UNIT, UNIT), UNIT)
                up[at, hidden] = units[m, source + 2 * part].astype(f32)
                down[hidden, at] = units[m, source + 2 * part + 1].astype(f32)


def mix_final_kernel(info, *rest):
    refs, (qkv, out, units, sems) = rest[:10], rest[10:]
    low, sec = info[LOW], info[SEC]
    fetch_quarters(sec, refs, units, sems).wait()
    width = out.shape[0] // 2
    count = units.shape[1] // 2
    for m in range(QUARTERS):
        at = pl.ds(block_at(low, m), UNIT)
        at_left = pl.ds(block_at(low, m), width)
        at_right = pl.ds(pl.multiple_of(block_at(low, m) + width, width), width)
        for source, half in ((0, sec), (count, 1 - sec)):
            lanes = pl.ds(pl.multiple_of(half * width, width), width)
            query_keys = units[m, source].astype(f32)
            qkv[0, at, lanes] = query_keys[:, :width]
            qkv[1, at, lanes] = query_keys[:, width:]
            rest_unit = units[m, source + 1].astype(f32)
            qkv[2, at, lanes] = rest_unit[:, :width]
            out[lanes, at_left] = rest_unit[:width, width:]
            out[lanes, at_right] = rest_unit[width:, width:]


def sum_rest(value):
    step = QUARTERS
    while step < lax.axis_size("dp"):
        value = add16(value, swap(value, "dp", step))
        step *= 2
    return value


class Sum:
    def __init__(self, order, send_a, send_b, keep_a, keep_b, split):
        self.order, self.split = order, split
        self.keep = (keep_a, keep_b)
        self.count = keep_a.shape[1]
        self.once = (swap(send_a, "dp", 1), swap(send_b, "dp", 2))

    def second(self):
        far = half_at(1, self.count)
        far_a, far_b = self.order.call(
            far_kernel,
            [shape((self.count, UNIT, UNIT), low16)] * 2,
            (self.keep[0], self.once[0], self.keep[1], self.once[1]),
            [far] * 4,
            moved=self.count * MIB,
            grid=(1,),
        )
        self.twice = (swap(far_a, "dp", 2), swap(far_b, "dp", 1))

    def third(self):
        if self.split:
            outs = [shape((2, self.count // 2, UNIT, UNIT), low16)] * 2
        else:
            outs = [shape((2 * self.count, UNIT, UNIT), low16)]
        near = half_at(0, self.count)
        totals = self.order.call(
            sum_kernel,
            outs,
            (self.keep[0], self.once[0], self.twice[0], self.keep[1], self.once[1], self.twice[1]),
            [near, near, VM] * 2,
            moved=self.count * MIB,
            grid=(1,),
        )
        totals = [sum_rest(total) for total in totals]
        if not self.split:
            return totals[0]
        self.keep = totals[1]
        self.count = self.keep.shape[1]
        self.once = swap(totals[0], "tensor", 1)

    def fourth(self):
        far = self.order.call(
            far_tensor_kernel,
            [shape((self.count, UNIT, UNIT), low16)],
            (self.keep, self.once),
            [half_at(1, self.count)] * 2,
            moved=self.count * MIB // 2,
            grid=(1,),
        )[0]
        self.twice = swap(far, "tensor", 2)

    def last(self):
        near = half_at(0, self.count)
        return self.order.call(
            total_kernel,
            [shape((self.count, UNIT, UNIT), low16)],
            (self.keep, self.once, self.twice),
            [near, near, VM],
            moved=self.count * MIB // 2,
            grid=(1,),
        )[0]


def gather_dp(kept, section):
    arrived = lax.ppermute(kept, "section", [(1 - section, section)])
    units = jnp.concatenate([kept, arrived])
    count = kept.shape[0]
    x_part = swap_one(units, "dp", 1, section)
    y_part = swap_one(units, "dp", 2, section)
    far_kept = swap_one(x_part[:count], "dp", 2, section)
    far_arrived = swap_one(y_part[count:], "dp", 1, section)
    return units, x_part, y_part, far_kept, far_arrived


def on_device(codes, lengths, gains, w_qkv, w_out, w_up, w_down, cotangent):
    sec = lax.axis_index("section")
    low = lax.axis_index("dp") % QUARTERS
    z = lax.axis_index("tensor")
    first_core = sec == 0
    utts, frames, code_count, width = codes.shape
    heads_width = w_out.shape[1]
    half = heads_width // 2
    wide = w_up.shape[2]
    rows_g = 4 * frames
    rows_l = utts * code_count * frames
    tiles = 2 * wide // UNIT
    info = jnp.concatenate([jnp.stack([low, sec, z]).astype(jnp.int32), lengths])
    order = Order()
    call = order.call

    code_rows = jnp.transpose(codes, (0, 2, 1, 3))
    cot_rows = jnp.transpose(cotangent, (0, 2, 1, 3))
    own_w = (jnp.transpose(w_qkv[0], (1, 0, 2)), w_out[0], w_up[0], w_down[0])

    def sem(count):
        return pltpu.SemaphoreType.DMA((count,))

    def gather(rows):
        gathered = lax.all_gather(rows, "tensor", axis=0, tiled=True)
        order.token = gathered
        return gathered

    def scatter(partial):
        return lax.all_to_all(partial, "tensor", 0, 0)

    other_gain = swap(gains[0], "section", 1)
    own_w, other_gain = lax.optimization_barrier((own_w, other_gain))
    other_w = tuple(swap(w, "section", 1) for w in own_w)
    both_w = tuple(w for pair in zip(own_w, other_w) for w in pair)
    attention_w, feed_w = both_w[:4], both_w[4:]

    first_rows, start_g, gain_g, gain_l = call(
        start_kernel,
        [
            shape((frames, width), low16),
            shape((frames, width), f32),
            shape((2, width), f32),
            shape((2, width), f32),
        ],
        (info, code_rows, gains[0], other_gain),
        [SM, VM, VM, VM],
        moved=2 * MIB,
    )
    first_g = gather(first_rows)

    mix_piece, mix_whole = call(
        mix_piece_kernel,
        [shape((2, UNIT, UNIT), low16), shape((QUARTERS, 2, UNIT, UNIT), low16)],
        (info,) + attention_w,
        [SM] + [ANY] * 4,
        [sem(5 * QUARTERS)],
        moved=2 * MIB,
    )
    mix_z1 = swap(mix_piece, "tensor", 1)
    mix_z2 = swap(mix_piece, "tensor", 2)

    packed_g, probs_g, mixed_g, partial = call(
        global_attention_kernel,
        [
            shape((3, rows_g, heads_width), low16),
            shape((heads_width // HEAD_DIM, rows_g, rows_g), f32),
            shape((rows_g, heads_width), low16),
            shape((4, frames, width), low16),
        ],
        (info, first_g) + attention_w,
        [SM, VM] + [ANY] * 4,
        [
            pltpu.VMEM((3, width, heads_width), low16),
            pltpu.VMEM((heads_width, width), low16),
            sem(8),
        ],
        flops=2 * 10**9,
        moved=8 * MIB,
    )
    arrived = scatter(partial)
    feed_piece, feed_whole = call(
        feed_piece_kernel,
        [shape((4, UNIT, UNIT), low16), shape((QUARTERS, 4, UNIT, UNIT), low16)],
        (info,) + feed_w,
        [SM] + [ANY] * 4,
        [sem(4 * QUARTERS)],
        moved=4 * MIB,
    )
    feed_z1 = swap(feed_piece, "tensor", 1)
    mix_z3 = swap(mix_z2, "tensor", 1)
    mix_far = jnp.stack([mix_z1, mix_z2, mix_z3])
    mix_x = swap(mix_far, "dp", 1)
    mix_y = swap(mix_far, "dp", 2)
    mix_w = (
        mix_whole,
        mix_z1,
        mix_z2,
        mix_z3,
        mix_x,
        mix_y,
        swap(mix_x[:, 0], "dp", 2),
        swap(mix_y[:, 1], "dp", 1),
    )
    hidden_g, second_rows = call(
        middle_kernel,
        [shape((frames, width), f32), shape((frames, width), low16)],
        (start_g, arrived, gain_g),
        [VM] * 3,
        moved=2 * MIB,
    )
    second_g = gather(second_rows)
    feed_z2 = swap(order.after(feed_piece), "tensor", 2)
    feed_z3 = swap(feed_z2, "tensor", 1)
    feed_l = [feed_whole]
    for part in (feed_z1, feed_z2, feed_z3):
        x_part = swap(part, "dp", 1)
        y_part = swap(part, "dp", 2)
        feed_l += [
            part, x_part, y_part, swap(x_part[:2], "dp", 2), swap(y_part[2:], "dp", 1)
        ]
    feed_l = tuple(feed_l)
    lifted_g, active_g, partial = call(
        global_feed_kernel,
        [
            shape((rows_g, wide), f32),
            shape((rows_g, wide), low16),
            shape((4, frames, width), low16),
        ],
        (info, second_g) + feed_w,
        [SM, VM] + [ANY] * 4,
        [
            pltpu.VMEM((width, wide), low16),
            pltpu.VMEM((wide, width), low16),
            pltpu.VMEM((rows_g, width), f32),
            sem(8),
        ],
        flops=2 * 10**9,
        moved=8 * MIB,
    )
    sent = call(
        sent_kernel,
        [shape((frames, width), low16)],
        (hidden_g, scatter(partial)),
        [VM] * 2,
        moved=MIB,
    )[0]

    start_l, first_l, query_keys, values_l, probs_l, mixed_l, partial = call(
        local_attention_kernel,
        [
            shape((rows_l, width), f32),
            shape((rows_l, width), low16),
            shape((4, rows_l, 2 * half), low16),
            shape((4, rows_l, half), low16),
            shape((4, utts, 2 * rows_l // utts, half), f32),
            shape((rows_l, 4 * half), low16),
            shape((rows_l, width), low16),
        ],
        (info, code_rows, sent, swap(sent, "section", 1), gain_l) + mix_w,
        [SM] + [VM] * 4 + [ANY] * MIX_REFS,
        [
            pltpu.VMEM((4, 2, width, UNIT), low16),
            pltpu.VMEM((4 * half, width), low16),
            sem(32),
        ],
        flops=4 * 10**9,
        moved=20 * MIB,
    )
    hidden_l, second_l, top_l, active_l, grad_lifted_l, back = call(
        local_feed_kernel,
        [
            shape((rows_l, width), f32),
            shape((rows_l, width), low16),
            shape((rows_l, width), low16),
            shape((tiles, rows_l, UNIT), low16),
            shape((tiles, rows_l, UNIT), low16),
            shape((rows_l, width), low16),
        ],
        (info, start_l, partial, swap(partial, "section", 1), gain_l, cot_rows) + feed_l,
        [SM] + [VM] * 5 + [ANY] * FEED_REFS,
        [
            pltpu.VMEM((tiles, width, UNIT), low16),
            pltpu.VMEM((tiles, UNIT, width), low16),
            pltpu.VMEM((rows_l, width), f32),
            sem(8 * tiles),
        ],
        flops=10 * 10**9,
        moved=24 * MIB,
    )
    other_back = swap(back, "section", 1)
    turned_l = pltpu.VMEM((width, rows_l), low16)
    local_feed = Sum(
        order,
        *call(
            local_feed_grad_kernel,
            [shape((2, 8, UNIT, UNIT), low16)] * 4,
            (second_l, grad_lifted_l, active_l, top_l),
            [VM] * 4,
            [turned_l],
            flops=6 * 10**9,
            moved=16 * MIB,
        ),
        True,
    )
    grad_hidden_l, mid_l, grad_query_keys, grad_values, back, gain2_l = call(
        local_attention_back_kernel,
        [
            shape((rows_l, width), f32),
            shape((rows_l, width), low16),
            shape((4, rows_l, 2 * half), low16),
            shape((4, rows_l, half), low16),
            shape((rows_l, width), low16),
            shape((1, width), f32),
        ],
        (hidden_l, back, other_back, top_l, gain_l, query_keys, values_l, probs_l) + mix_w,
        [VM] * 8 + [ANY] * MIX_REFS,
        [
            pltpu.VMEM((4, 2, width, UNIT), low16),
            pltpu.VMEM((4 * half, width), low16),
            pltpu.VMEM((rows_l, width), f32),
            sem(32),
        ],
        flops=5 * 10**9,
        moved=20 * MIB,
    )
    other_back = swap(back, "section", 1)
    local_mix = Sum(
        order,
        *call(
            local_mix_kernel,
            [shape((2, 4, UNIT, UNIT), low16)] * 4,
            (first_l, grad_query_keys, grad_values, mixed_l, mid_l),
            [VM] * 5,
            [turned_l],
            flops=3 * 10**9,
            moved=8 * MIB,
        ),
        True,
    )
    returned, code_part, gain1_l = call(
        local_end_kernel,
        [
            shape((frames, width), low16),
            shape((utts, code_count, frames, width // 2), f32),
            shape((1, width), f32),
        ],
        (info, back, other_back, start_l, grad_hidden_l, gain_l),
        [SM] + [VM] * 5,
        [pltpu.VMEM((rows_l, width), f32)],
        moved=6 * MIB,
    )

    top_g = gather(returned)
    grad_lifted_g, partial = call(
        global_feed_back_kernel,
        [shape((rows_g, wide), low16), shape((4, frames, width), low16)],
        (info, top_g, lifted_g) + feed_w,
        [SM, VM, VM] + [ANY] * 4,
        [
            pltpu.VMEM((width, wide), low16),
            pltpu.VMEM((wide, width), low16),
            pltpu.VMEM((rows_g, width), f32),
            sem(8),
        ],
        flops=2 * 10**9,
        moved=8 * MIB,
    )
    arrived = scatter(partial)
    away_feed, kept_feed = call(
        global_feed_grad_kernel,
        [shape((QUARTERS, 2, 2, UNIT, UNIT), low16)] * 2,
        (info, second_g, grad_lifted_g, active_g, top_g),
        [SM] + [VM] * 4,
        [pltpu.VMEM((width, rows_g), low16)],
        flops=4 * 10**9,
        moved=8 * MIB,
    )
    away_feed = swap(away_feed, "section", 1)
    local_feed.second()
    grad_hidden_g, mid_rows, gain2_g = call(
        middle_back_kernel,
        [shape((frames, width), f32), shape((frames, width), low16), shape((1, width), f32)],
        (arrived, hidden_g, gain_g, returned),
        [VM] * 4,
        moved=2 * MIB,
    )
    mid_g = gather(mid_rows)
    grads_g, partial = call(
        global_attention_back_kernel,
        [shape((3, rows_g, heads_width), low16), shape((4, frames, width), low16)],
        (info, mid_g, packed_g, probs_g) + attention_w,
        [SM, VM, VM, VM] + [ANY] * 4,
        [
            pltpu.VMEM((3, width, heads_width), low16),
            pltpu.VMEM((heads_width, width), low16),
            sem(8),
        ],
        flops=2 * 10**9,
        moved=8 * MIB,
    )
    arrived = scatter(partial)
    local_mix.second()

    def merged(away, kept, count):
        units = call(
            merge_kernel,
            [shape((2, count, UNIT, UNIT), low16)] * 4,
            (kept, away),
            [VM] * 2,
            moved=2 * count * MIB,
        )
        return Sum(order, *units, False)

    global_feed = merged(away_feed, kept_feed, 2)
    away_mix, kept_mix = call(
        global_mix_grad_kernel,
        [shape((QUARTERS, 2, 1, UNIT, UNIT), low16)] * 2,
        (info, first_g, grads_g, mixed_g, mid_g),
        [SM] + [VM] * 4,
        [pltpu.VMEM((width, rows_g), low16)],
        flops=2 * 10**9,
        moved=4 * MIB,
    )
    away_mix = swap(away_mix, "section", 1)
    local_feed.third()
    global_mix = merged(away_mix, kept_mix, 1)
    kept_start, given_start, gain1_g = call(
        start_back_kernel,
        [
            shape((frames, width // 2), f32),
            shape((frames, width // 2), f32),
            shape((1, width), f32),
        ],
        (info, arrived, start_g, gain_g, grad_hidden_g),
        [SM] + [VM] * 4,
        [pltpu.VMEM((frames, width), f32)],
        moved=2 * MIB,
    )
    local_mix.third()
    global_feed.second()
    global_mix.second()
    arrived_start = swap(given_start, "section", 1)
    both_start = jnp.stack(
        [
            jnp.where(first_core, kept_start, arrived_start),
            jnp.where(first_core, arrived_start, kept_start),
        ]
    )
    code_grad = jnp.transpose(code_part + both_start[:, None], (0, 2, 1, 3))

    own_gain = jnp.concatenate([gain1_g, gain2_g], axis=0)
    total_gain = own_gain + swap(own_gain, "section", 1)
    local_gain = jnp.concatenate([gain1_l, gain2_l], axis=0)
    gain_total = jnp.where(first_core, total_gain, local_gain)
    gain_total = jnp.concatenate(
        [
            lax.dynamic_slice_in_dim(gain_total, (low ^ m) * UNIT, UNIT, 1)
            for m in range(QUARTERS)
        ],
        axis=1,
    )
    for axis in ("tensor", "dp"):
        step = 1
        while step < lax.axis_size(axis):
            gain_total = gain_total + swap(gain_total, axis, step)
            step *= 2

    branch_l = call(
        local_drop_kernel,
        [shape((rows_l, width), low16)],
        (active_l,) + feed_l,
        [VM] + [ANY] * FEED_REFS,
        [
            pltpu.VMEM((tiles, UNIT, width), low16),
            pltpu.VMEM((rows_l, width), f32),
            sem(QUARTERS * tiles),
        ],
        flops=2 * 10**9,
        moved=8 * MIB,
    )[0]
    global_feed = gather_dp(global_feed.third(), 0)
    global_mix = gather_dp(global_mix.third(), 0)
    local_feed.fourth()
    output = call(
        output_kernel,
        [shape((utts, code_count, frames, width // 2), low16)],
        (info, hidden_l, branch_l, swap(branch_l, "section", 1)),
        [SM] + [VM] * 3,
        moved=4 * MIB,
    )[0]
    local_mix.fourth()
    local_feed = gather_dp(local_feed.last(), 1)
    local_mix = gather_dp(local_mix.last(), 1)
    up_grad, down_grad = call(
        feed_final_kernel,
        [shape((width, wide), f32), shape((wide, width), f32)],
        (info,) + global_feed + local_feed,
        [SM] + [ANY] * 10,
        [pltpu.VMEM((QUARTERS, 8, UNIT, UNIT), low16), sem(5)],
        moved=16 * MIB,
    )
    qkv_grad, out_grad = call(
        mix_final_kernel,
        [shape((3, width, heads_width), f32), shape((heads_width, width), f32)],
        (info,) + global_mix + local_mix,
        [SM] + [ANY] * 10,
        [pltpu.VMEM((QUARTERS, 4, UNIT, UNIT), low16), sem(5)],
        moved=8 * MIB,
    )
    return (
        jnp.transpose(output, (0, 2, 1, 3)),
        code_grad,
        gain_total[None],
        jnp.transpose(qkv_grad, (1, 0, 2))[None],
        out_grad[None],
        up_grad[None],
        down_grad[None],
    )


def solution(mesh):
    in_specs = (
        P("dp", "tensor", None, None),
        P("dp"),
        P("section", None, None),
        P("section", None, None, "tensor"),
        P("section", "tensor", None),
        P("section", None, "tensor"),
        P("section", "tensor", None),
        P("dp", "tensor", None, None),
    )
    out_specs = (
        P("dp", "tensor", None, "section"),
        P("dp", "tensor", None, "section"),
        P("section", None, None),
        P("section", None, None, "tensor"),
        P("section", "tensor", None),
        P("section", None, "tensor"),
        P("section", "tensor", None),
    )
    return jax.shard_map(
        on_device, mesh=mesh, in_specs=in_specs, out_specs=out_specs, check_vma=False
    )
```

```python
import functools

import jax
import jax.numpy as jnp
from jax import lax
from jax.experimental import pallas as pl
from jax.experimental.pallas import tpu as pltpu
from jax.sharding import PartitionSpec as P

HEAD_DIM = 64
SCALE = HEAD_DIM ** (-0.5)
QUARTERS = 4
UNIT = 256
epsilon = 1e-06
negative = -1e30
f32 = jnp.float32
low16 = jnp.bfloat16

VM = pl.BlockSpec(memory_space=pltpu.VMEM)
SM = pl.BlockSpec(memory_space=pltpu.SMEM)
ANY = pl.BlockSpec(memory_space=pltpu.HBM)
MIB = 1 << 20
PACE = 2 * 10**8

LOW, SEC, SHARD, LENGTHS = 0, 1, 2, 3


def shape(dims, dtype):
    return jax.ShapeDtypeStruct(tuple(dims), dtype)


class Order:
    def __init__(self):
        self.tokens = ()

    def after(self, value):
        if not self.tokens:
            return value
        return lax.optimization_barrier((value,) + self.tokens)[0]

    def until(self, *values):
        self.tokens += values

    def call(self, body, outs, args, specs, scratch=(), limit=56, us=2.0, grid=()):
        args = (self.after(args[0]),) + tuple(args[1:])
        results = pl.pallas_call(
            body,
            out_shape=tuple(outs),
            grid=grid,
            in_specs=list(specs),
            out_specs=tuple(VM for _ in outs),
            scratch_shapes=list(scratch),
            compiler_params=pltpu.CompilerParams(vmem_limit_bytes=limit * MIB),
            cost_estimate=pl.CostEstimate(
                flops=int(us * PACE), bytes_accessed=0, transcendentals=0
            ),
        )(*args)
        self.tokens = (results[-1],)
        return results


def swap(value, axis, flip):
    count = lax.axis_size(axis)
    return lax.ppermute(value, axis, [(i, i ^ flip) for i in range(count)])


def dot(a, b):
    return jnp.dot(a, b, preferred_element_type=f32)


def dot_tn(a, b):
    return lax.dot_general(a, b, (((0,), (0,)), ((), ())), preferred_element_type=f32)


def dot_nt(a, b):
    return lax.dot_general(a, b, (((1,), (1,)), ((), ())), preferred_element_type=f32)


def factor_of(values):
    return lax.rsqrt(jnp.mean(values * values, axis=-1, keepdims=True) + epsilon)


def norm_back(values, gain, upstream):
    factor = factor_of(values)
    weighted = upstream * gain
    inner = jnp.mean(weighted * values, axis=-1, keepdims=True)
    through = factor * weighted - values * (factor * factor * factor) * inner
    return through, jnp.sum(upstream * values * factor, axis=0, keepdims=True)


def normal_cdf(values):
    return 0.5 * (1.0 + lax.erf(values * (0.5**0.5)))


def gelu_slope(values, cdf):
    return cdf + values * (jnp.exp(-0.5 * values * values) * 0.3989422804014327)


def block_at(low, m):
    return pl.multiple_of((low ^ m) * UNIT, UNIT)


def span(m):
    return slice(m * UNIT, (m + 1) * UNIT)


class Copies:
    def __init__(self, sems):
        self.sems = sems
        self.made = []

    def start(self, src, dst):
        copy = pltpu.make_async_copy(src, dst, self.sems.at[len(self.made)])
        copy.start()
        self.made.append(copy)
        return copy

    def pick(self, own_first, sec, own, other, dst):
        sem = self.sems.at[len(self.made)]

        @pl.when((sec == 0) == own_first)
        def _():
            pltpu.make_async_copy(own, dst, sem).start()

        @pl.when((sec == 0) != own_first)
        def _():
            pltpu.make_async_copy(other, dst, sem).start()

        copy = pltpu.make_async_copy(own, dst, sem)
        self.made.append(copy)
        return copy

    def wait(self, begin=0, end=None):
        for copy in self.made[begin:end]:
            copy.wait()


def start_kernel(info, codes, own_gain, other_gain, first, start, gain_g, gain_l):
    low, sec = info[LOW], info[SEC]
    for m in range(QUARTERS):
        at = pl.ds(block_at(low, m), UNIT)
        own, other = own_gain[:, at], other_gain[:, at]
        gain_g[:, span(m)] = jnp.where(sec == 0, own, other)
        gain_l[:, span(m)] = jnp.where(sec == 0, other, own)
        total = codes[sec, 0, :, at].astype(f32)
        for c in range(1, codes.shape[1]):
            total = total + codes[sec, c, :, at].astype(f32)
        start[:, span(m)] = total
    values = start[...]
    first[...] = (values * factor_of(values) * gain_g[0:1, :]).astype(low16)


def from_local(sec, own, other, branch):
    @pl.when(sec == 0)
    def _():
        branch(0, *other)

    @pl.when(sec != 0)
    def _():
        branch(1, *own)


def mix_piece_kernel(info, own_qkv, other_qkv, own_out, other_out, piece, whole, sems):
    low, sec = info[LOW], info[SEC]
    half = own_qkv.shape[2] // 2

    def branch(half_index, qkv, out):
        made = Copies(sems)
        for m in range(QUARTERS):
            at = pl.ds(block_at(low, m), UNIT)
            at_right = pl.ds(pl.multiple_of(block_at(low, m) + half, half), half)
            at_left = pl.ds(block_at(low, m), half)
            lanes = slice(half_index * half, (half_index + 1) * half)
            target = whole.at[m]
            made.start(qkv.at[0, at, lanes], target.at[0, :, 0:half])
            made.start(qkv.at[1, at, lanes], target.at[0, :, half : 2 * half])
            made.start(qkv.at[2, at, lanes], target.at[1, :, 0:half])
            made.start(out.at[lanes, at_left], target.at[1, 0:half, half : 2 * half])
            made.start(out.at[lanes, at_right], target.at[1, half : 2 * half, half : 2 * half])
        made.wait()

    from_local(sec, (own_qkv, own_out), (other_qkv, other_out), branch)
    piece[...] = whole[0]


def feed_piece_kernel(info, own_up, other_up, own_down, other_down, piece, whole, sems):
    low, sec = info[LOW], info[SEC]
    wide = own_up.shape[1] // 2

    def branch(half_index, up, down):
        made = Copies(sems)
        for m in range(QUARTERS):
            at = pl.ds(block_at(low, m), UNIT)
            for part in range(2):
                begin = half_index * wide + part * UNIT
                hidden = slice(begin, begin + UNIT)
                made.start(up.at[at, hidden], whole.at[m, part])
                made.start(down.at[hidden, at], whole.at[m, 2 + part])
        made.wait()

    from_local(sec, (own_up, own_down), (other_up, other_down), branch)
    piece[...] = whole[0]


def fetch_attention(made, low, sec, own_qkv, other_qkv, own_out, other_out, qkv, out):
    for m in range(QUARTERS):
        at = pl.ds(block_at(low, m), UNIT)
        made.pick(True, sec, own_qkv.at[:, at, :], other_qkv.at[:, at, :], qkv.at[:, span(m), :])
    for m in range(QUARTERS):
        at = pl.ds(block_at(low, m), UNIT)
        made.pick(True, sec, own_out.at[:, at], other_out.at[:, at], out.at[:, span(m)])


def by_shard(info, blocks):
    count = blocks.shape[0]
    return jnp.concatenate([blocks[info[SHARD] ^ k] for k in range(count)], axis=0)


def other_half(info, width):
    half = width // 2
    return pl.ds(pl.multiple_of((1 - info[SEC]) * half, half), half)


def spread_blocks(info, target, values):
    frames = target.shape[1]
    for k in range(target.shape[0]):
        target[info[SHARD] ^ k] = values[k * frames : (k + 1) * frames].astype(low16)


def row_places(info, count, frames, dimension):
    at = lax.broadcasted_iota(jnp.int32, (count, count), dimension)
    return (lax.div(at, frames) ^ info[SHARD]) * frames + lax.rem(at, frames)


def global_attention_kernel(info, *rest):
    (blocks, own_qkv, other_qkv, own_out, other_out,
     rows, packed, probs, mixed, given, partial, qkv, out, sems) = rest
    low, sec = info[LOW], info[SEC]
    made = Copies(sems)
    fetch_attention(made, low, sec, own_qkv, other_qkv, own_out, other_out, qkv, out)
    count, frames = rows.shape[0], blocks.shape[1]
    length = info[LENGTHS + sec]
    query_at = row_places(info, count, frames, 0)
    key_at = row_places(info, count, frames, 1)
    allowed = (key_at <= query_at) & (key_at < length)
    values = by_shard(info, blocks)
    rows[...] = values
    made.wait(0, QUARTERS)
    for c in range(3):
        packed[c] = dot(values, qkv[c]).astype(low16)
    heads = []
    for h in range(packed.shape[2] // HEAD_DIM):
        lanes = slice(h * HEAD_DIM, (h + 1) * HEAD_DIM)
        scores = dot_nt(packed[0, :, lanes], packed[1, :, lanes]) * SCALE
        scores = jnp.where(allowed, scores, negative)
        raised = jnp.exp(scores - jnp.max(scores, axis=-1, keepdims=True))
        exact = raised / jnp.sum(raised, axis=-1, keepdims=True)
        probs[h] = exact
        heads.append(dot(exact.astype(low16), packed[2, :, lanes]).astype(low16))
    mixed[...] = jnp.concatenate(heads, axis=1)
    given[...] = mixed[:, other_half(info, mixed.shape[1])]
    made.wait(QUARTERS)
    spread_blocks(info, partial, dot(mixed[...], out[...]))


def total_of(arrived):
    total = arrived[0].astype(f32)
    for k in range(1, arrived.shape[0]):
        total = total + arrived[k].astype(f32)
    return total


def middle_kernel(start, arrived, gain, hidden, second):
    values = start[...] + total_of(arrived)
    hidden[...] = values
    second[...] = (values * factor_of(values) * gain[1:2, :]).astype(low16)


def fetch_feed(made, low, sec, own_up, other_up, own_down, other_down, up, down):
    for m in range(QUARTERS):
        at = pl.ds(block_at(low, m), UNIT)
        made.pick(True, sec, own_up.at[at, :], other_up.at[at, :], up.at[span(m), :])
    for m in range(QUARTERS):
        at = pl.ds(block_at(low, m), UNIT)
        made.pick(True, sec, own_down.at[:, at], other_down.at[:, at], down.at[:, span(m)])


def global_feed_kernel(info, *rest):
    (blocks, own_up, other_up, own_down, other_down,
     rows, lifted, active, given, partial, up, down, total, sems) = rest
    made = Copies(sems)
    fetch_feed(made, info[LOW], info[SEC], own_up, other_up, own_down, other_down, up, down)
    values = by_shard(info, blocks)
    rows[...] = values
    made.wait(0, QUARTERS)
    for t in range(up.shape[1] // UNIT):
        tile = dot(values, up[:, span(t)])
        lifted[:, span(t)] = tile
        low_tile = (tile * normal_cdf(tile)).astype(low16)
        active[:, span(t)] = low_tile
        if t == 0:
            made.wait(QUARTERS)
        branch = dot(low_tile, down[span(t), :])
        total[...] = branch if t == 0 else total[...] + branch
    spread_blocks(info, partial, total[...])
    given[...] = active[:, other_half(info, active.shape[1])]


def sent_kernel(hidden, arrived, sent):
    sent[...] = (hidden[...] + total_of(arrived)).astype(low16)


def global_feed_back_kernel(info, *rest):
    (blocks, lifted, own_up, other_up, own_down, other_down,
     rows, grad_lifted, given, partial, up, down, total, sems) = rest
    made = Copies(sems)
    fetch_feed(made, info[LOW], info[SEC], own_up, other_up, own_down, other_down, up, down)
    values = by_shard(info, blocks)
    rows[...] = values
    made.wait(QUARTERS)
    for t in range(up.shape[1] // UNIT):
        tile = lifted[:, span(t)]
        grad = dot_nt(values, down[span(t), :]) * gelu_slope(tile, normal_cdf(tile))
        grad = grad.astype(low16)
        grad_lifted[:, span(t)] = grad
        if t == 0:
            made.wait(0, QUARTERS)
        back = dot_nt(grad, up[:, span(t)])
        total[...] = back if t == 0 else total[...] + back
    spread_blocks(info, partial, total[...])
    given[...] = grad_lifted[:, other_half(info, grad_lifted.shape[1])]


def middle_back_kernel(arrived, hidden, gain, returned, grad_hidden, mid, gain_grad):
    through, gain_grad[...] = norm_back(hidden[...], gain[1:2, :], total_of(arrived))
    values = returned[...].astype(f32) + through
    grad_hidden[...] = values
    mid[...] = values.astype(low16)


def global_attention_back_kernel(info, *rest):
    (blocks, packed, probs, own_qkv, other_qkv, own_out, other_out,
     rows, grads, given, partial, qkv, out, sems) = rest
    low, sec = info[LOW], info[SEC]
    made = Copies(sems)
    fetch_attention(made, low, sec, own_qkv, other_qkv, own_out, other_out, qkv, out)
    values = by_shard(info, blocks)
    rows[...] = values
    made.wait(QUARTERS)
    grad_mixed = dot_nt(values, out[...]).astype(low16)
    columns = [[], [], []]
    for h in range(packed.shape[2] // HEAD_DIM):
        lanes = slice(h * HEAD_DIM, (h + 1) * HEAD_DIM)
        exact = probs[h]
        grad = grad_mixed[:, lanes]
        columns[2].append(dot_tn(exact.astype(low16), grad).astype(low16))
        grad_probs = dot_nt(grad, packed[2, :, lanes])
        center = jnp.sum(grad_probs * exact, axis=-1, keepdims=True)
        grad_scores = (exact * (grad_probs - center)).astype(low16)
        columns[0].append((dot(grad_scores, packed[1, :, lanes]) * SCALE).astype(low16))
        columns[1].append((dot_tn(grad_scores, packed[0, :, lanes]) * SCALE).astype(low16))
    total = None
    made.wait(0, QUARTERS)
    for c in range(3):
        grads[c] = jnp.concatenate(columns[c], axis=1)
        back = dot_nt(grads[c], qkv[c])
        total = back if c == 0 else total + back
    spread_blocks(info, partial, total)
    given[...] = grads[:, :, other_half(info, grads.shape[2])]


def start_back_kernel(info, arrived, start, gain, grad_hidden, kept, given, gain_grad, values):
    low, sec = info[LOW], info[SEC]
    through, gain_grad[...] = norm_back(start[...], gain[0:1, :], total_of(arrived))
    values[...] = grad_hidden[...] + through
    for j in range(2):
        kept[:, span(j)] = values[:, pl.ds(block_at(low, 2 * sec + j), UNIT)]
        given[:, span(j)] = values[:, pl.ds(block_at(low, 2 * (1 - sec) + j), UNIT)]


def mix_unit(refs, k, m, u):
    whole, near = refs[0], refs[1:4]
    both = refs[4:8]
    last = refs[8:12]
    if k == 0:
        return whole.at[m, u]
    if m == 0:
        return near[k - 1].at[u]
    if k == 3:
        return last[m - 1].at[u] if m < 3 else last[2 + u].at[0]
    return both[m - 1].at[k - 1, u] if m < 3 else both[2 + u].at[k - 1]


def feed_unit(refs, k, m, u):
    if k == 0:
        return refs[0].at[m, u]
    if m < 3:
        return refs[1 + m].at[u]
    return refs[4].at[u] if u < 2 else refs[5].at[u - 2]


MIX_REFS, FEED_REFS = 12, 6


def pair_rows(a, b, size):
    return jnp.concatenate([a * b, a[size:] * b[: 2 * size], a[2 * size :] * b[:size]], axis=0)


def by_pair(stacked, size):
    names = [(0, 0), (1, 1), (2, 2), (1, 0), (2, 1), (2, 0)]
    return {name: stacked[n * size : (n + 1) * size] for n, name in enumerate(names)}


def from_pairs(pairs):
    names = [(0, 0), (1, 1), (2, 2), (1, 0), (2, 1), (2, 0)]
    return jnp.concatenate([pairs[name] for name in names], axis=0)


def head_sums(products, table):
    upper = products.astype(low16)
    lower = (products - upper.astype(f32)).astype(low16)
    return dot(upper, table) + dot(lower, table)


def head_table(width):
    row = lax.broadcasted_iota(jnp.int32, (width, width), 0) // HEAD_DIM
    column = lax.broadcasted_iota(jnp.int32, (width, width), 1) // HEAD_DIM
    return (row == column).astype(f32).astype(low16)


def gather_mix(weights, mix, k, half):
    for m in range(QUARTERS):
        begin = m * UNIT
        mix[k * half : (k + 1) * half, begin : begin + half] = weights[
            k, 1, begin : begin + half, half:
        ]
        mix[k * half : (k + 1) * half, begin + half : begin + UNIT] = weights[
            k, 1, begin + half : begin + UNIT, half:
        ]


def local_attention_kernel(info, codes, sent_own, sent_other, gain, *rest):
    refs, (start, first, query_keys, values_out, probs, mixed, partial, weights, mix, sems) = (
        rest[:MIX_REFS], rest[MIX_REFS:]
    )
    low, sec = info[LOW], info[SEC]
    made = Copies(sems)
    groups = []
    for k in range(4):
        groups.append(
            [
                made.start(mix_unit(refs, k, m, u), weights.at[k, u, span(m), :])
                for u in range(2)
                for m in range(QUARTERS)
            ]
        )
    utts, code_count, frames, _ = codes.shape
    for u in range(utts):
        sent = jnp.where(sec == u, sent_own[...], sent_other[...]).astype(f32)
        for c in range(code_count):
            row = (u * code_count + c) * frames
            for m in range(QUARTERS):
                code = codes[u, c, :, pl.ds(block_at(low, m), UNIT)].astype(f32)
                start[row : row + frames, span(m)] = sent[:, span(m)] + code
    values = start[...]
    first[...] = (values * factor_of(values) * gain[0:1, :]).astype(low16)
    half = values_out.shape[2]
    table = head_table(half)
    rows = first[...]
    size = frames
    group = code_count * frames
    for k in range(4):
        for copy in groups[k]:
            copy.wait()
        query_keys[k] = dot(rows, weights[k, 0]).astype(low16)
        values_out[k] = dot(rows, weights[k, 1, :, :half]).astype(low16)
        gather_mix(weights, mix, k, half)
        for u in range(utts):
            at = slice(u * group, (u + 1) * group)
            q = query_keys[k, at, :half].astype(f32)
            key = query_keys[k, at, half:].astype(f32)
            val = values_out[k, at, :].astype(f32)
            scores = by_pair(head_sums(pair_rows(q, key, size), table) * SCALE, size)
            exact = {}
            for i in range(3):
                peak = scores[(i, 0)]
                for j in range(1, i + 1):
                    peak = jnp.maximum(peak, scores[(i, j)])
                raised = [jnp.exp(scores[(i, j)] - peak) for j in range(i + 1)]
                whole = raised[0]
                for j in range(1, i + 1):
                    whole = whole + raised[j]
                for j in range(i + 1):
                    exact[(i, j)] = raised[j] / whole
            probs[k, u] = from_pairs(exact)
            for i in range(3):
                total = None
                for j in range(i + 1):
                    weight = exact[(i, j)].astype(low16).astype(f32)
                    term = weight * val[j * size : (j + 1) * size]
                    total = term if total is None else total + term
                begin = u * group + i * size
                mixed[begin : begin + size, k * half : (k + 1) * half] = total.astype(low16)
    partial[...] = dot(mixed[...], mix[...]).astype(low16)


def local_top_kernel(info, cotangent, top, given):
    low, sec = info[LOW], info[SEC]
    utts, code_count, frames, _ = cotangent.shape
    group = code_count * frames
    frame_at = lax.broadcasted_iota(jnp.int32, (frames, 1), 0) + info[SHARD] * frames
    for u in range(utts):
        valid = frame_at < info[LENGTHS + u]
        for c in range(code_count):
            row = u * group + c * frames
            for m in range(QUARTERS):
                part = cotangent[u, c, :, pl.ds(block_at(low, m), UNIT)].astype(f32)
                top[row : row + frames, span(m)] = jnp.where(valid, part, 0.0).astype(low16)
    given[...] = top[pl.ds(pl.multiple_of(sec * group, group), group), :]


def local_norm_kernel(info, start, own_part, other_part, gain, hidden, second, given):
    values = start[...] + (own_part[...].astype(f32) + other_part[...].astype(f32))
    hidden[...] = values
    second[...] = (values * factor_of(values) * gain[1:2, :]).astype(low16)
    group = given.shape[0]
    given[...] = second[pl.ds(pl.multiple_of(info[SEC] * group, group), group), :]


def feed_tiles(refs, second, top, active, grad_lifted, up, down, back, sems):
    tiles = active.shape[0]
    made = Copies(sems)
    for t in range(tiles):
        for m in range(QUARTERS):
            made.start(feed_unit(refs, t // 2, m, t % 2), up.at[t, span(m), :])
        for m in range(QUARTERS):
            made.start(feed_unit(refs, t // 2, m, 2 + t % 2), down.at[t, :, span(m)])
    back[...] = jnp.zeros_like(back)

    @pl.loop(0, tiles)
    def _(t):
        for m in range(QUARTERS):
            pltpu.make_async_copy(
                refs[0].at[0, 0], up.at[t, span(m), :], sems.at[8 * t + m]
            ).wait()
        for m in range(QUARTERS):
            pltpu.make_async_copy(
                refs[0].at[0, 0], down.at[t, :, span(m)], sems.at[8 * t + 4 + m]
            ).wait()
        tile = dot(second[...], up[t])
        cdf = normal_cdf(tile)
        active[t] = (tile * cdf).astype(low16)
        grad = (dot_nt(top[...], down[t]) * gelu_slope(tile, cdf)).astype(low16)
        grad_lifted[t] = grad
        back[...] += dot_nt(grad, up[t])


def local_feed_kernel(second, top, *rest):
    refs, (active, grad_lifted, grad_second, up, down, back, sems) = (
        rest[:FEED_REFS], rest[FEED_REFS:]
    )
    feed_tiles(refs, second, top, active, grad_lifted, up, down, back, sems)
    grad_second[...] = back[...].astype(low16)


def far_feed_kernel(second_same, second_cross, top_same, top_cross, *rest):
    refs = rest[:FEED_REFS]
    (active, grad_lifted, second, top, same, cross, up, down, back, sems) = rest[FEED_REFS:]
    group = same.shape[0]
    second[:group] = second_same[...]
    second[group:] = second_cross[...]
    top[:group] = top_same[...]
    top[group:] = top_cross[...]
    feed_tiles(refs, second, top, active, grad_lifted, up, down, back, sems)
    same[...] = back[:group].astype(low16)
    cross[...] = back[group:].astype(low16)


def pair_kernel(a, b, total):
    total[...] = add16(a[...], b[...])


def with_far(sec, rows, own, other, far_same, far_cross):
    group = far_same.shape[0]
    parts = []
    for u in range(rows // group):
        at = slice(u * group, (u + 1) * group)
        far = jnp.where(sec == u, far_same[...], far_cross[...]).astype(f32)
        parts.append(own[at, :].astype(f32) + other[at, :].astype(f32) + far)
    return jnp.concatenate(parts, axis=0)


def local_attention_back_kernel(info, hidden, own_back, other_back, far_same, far_cross, top, gain,
                                query_keys, values_in, probs, *rest):
    refs = rest[:MIX_REFS]
    (grad_hidden, mid, grad_query_keys, grad_values, grad_first, gain_grad,
     weights, mix, total, sems) = rest[MIX_REFS:]
    made = Copies(sems)
    groups = []
    for k in range(4):
        groups.append(
            [
                made.start(mix_unit(refs, k, m, u), weights.at[k, u, span(m), :])
                for u in range(2)
                for m in range(QUARTERS)
            ]
        )
    upstream = with_far(info[SEC], hidden.shape[0], own_back, other_back, far_same, far_cross)
    through, gain_grad[...] = norm_back(hidden[...], gain[1:2, :], upstream)
    grads = top[...].astype(f32) + through
    grad_hidden[...] = grads
    mid[...] = grads.astype(low16)
    utts = probs.shape[1]
    half = values_in.shape[2]
    group = query_keys.shape[1] // utts
    size = group // 3
    table = head_table(half)
    for k in range(4):
        for copy in groups[k]:
            copy.wait()
        gather_mix(weights, mix, k, half)
        grad_mixed = dot_nt(mid[...], mix[k * half : (k + 1) * half, :]).astype(low16)
        grad_mixed = grad_mixed.astype(f32)
        for u in range(utts):
            at = slice(u * group, (u + 1) * group)
            q = query_keys[k, at, :half].astype(f32)
            key = query_keys[k, at, half:].astype(f32)
            val = values_in[k, at, :].astype(f32)
            grad = grad_mixed[at]
            exact = by_pair(probs[k, u], size)
            grad_probs = by_pair(head_sums(pair_rows(grad, val, size), table), size)
            scored = {}
            for i in range(3):
                center = grad_probs[(i, 0)] * exact[(i, 0)]
                for j in range(1, i + 1):
                    center = center + grad_probs[(i, j)] * exact[(i, j)]
                for j in range(i + 1):
                    score = exact[(i, j)] * (grad_probs[(i, j)] - center)
                    scored[(i, j)] = score.astype(low16).astype(f32)

            def rows_of(array, n):
                return array[n * size : (n + 1) * size]

            for i in range(3):
                begin = u * group + i * size
                to_query = sum(scored[(i, j)] * rows_of(key, j) for j in range(i + 1))
                to_key = sum(scored[(n, i)] * rows_of(q, n) for n in range(i, 3))
                to_value = sum(
                    exact[(n, i)].astype(low16).astype(f32) * rows_of(grad, n)
                    for n in range(i, 3)
                )
                grad_query_keys[k, begin : begin + size, :half] = (to_query * SCALE).astype(low16)
                grad_query_keys[k, begin : begin + size, half:] = (to_key * SCALE).astype(low16)
                grad_values[k, begin : begin + size, :] = to_value.astype(low16)
        back = dot_nt(grad_query_keys[k], weights[k, 0])
        back = back + dot_nt(grad_values[k], weights[k, 1, :, :half])
        total[...] = back if k == 0 else total[...] + back
    grad_first[...] = total[...].astype(low16)


def local_end_kernel(info, own_back, other_back, start, grad_hidden, gain,
                     returned, code_part, gain_grad, values):
    low, sec = info[LOW], info[SEC]
    upstream = own_back[...].astype(f32) + other_back[...].astype(f32)
    through, gain_grad[...] = norm_back(start[...], gain[0:1, :], upstream)
    values[...] = grad_hidden[...] + through
    utts, code_count, frames, _ = code_part.shape
    total = None
    for c in range(code_count):
        begin = pl.multiple_of((sec * code_count + c) * frames, frames)
        part = values[pl.ds(begin, frames), :]
        total = part if total is None else total + part
    returned[...] = total.astype(low16)
    for u in range(utts):
        for c in range(code_count):
            row = (u * code_count + c) * frames
            for j in range(2):
                at = pl.ds(block_at(low, 2 * sec + j), UNIT)
                code_part[u, c, :, span(j)] = values[row : row + frames, at]


def output_kernel(info, hidden, own_part, other_part, far_same, far_cross, output):
    low, sec = info[LOW], info[SEC]
    utts, code_count, frames, _ = output.shape
    group = code_count * frames
    frame_at = lax.broadcasted_iota(jnp.int32, (frames, 1), 0) + info[SHARD] * frames
    for u in range(utts):
        valid = frame_at < info[LENGTHS + u]
        for c in range(code_count):
            rows = slice(u * group + c * frames, u * group + (c + 1) * frames)
            inner = slice(c * frames, (c + 1) * frames)
            for j in range(2):
                at = pl.ds(block_at(low, 2 * sec + j), UNIT)
                far = jnp.where(sec == u, far_same[inner, at], far_cross[inner, at])
                value = hidden[rows, at] + (
                    own_part[rows, at].astype(f32)
                    + other_part[rows, at].astype(f32)
                    + far.astype(f32)
                )
                output[u, c, :, span(j)] = jnp.where(valid, value, 0.0).astype(low16)


SEND_A, KEEP_A, SEND_B, KEEP_B = (1, 3), (0, 2), (2, 3), (0, 1)


def local_drop_kernel(own_active, far_active, *rest):
    refs, (own_branch, same, cross, down, branch, sems) = rest[:FEED_REFS], rest[FEED_REFS:]
    tiles, count, _ = own_active.shape
    made = Copies(sems)
    for t in range(tiles):
        for m in range(QUARTERS):
            made.start(feed_unit(refs, t // 2, m, 2 + t % 2), down.at[t, :, span(m)])
    branch[...] = jnp.zeros_like(branch)

    @pl.loop(0, tiles)
    def _(t):
        for m in range(QUARTERS):
            pltpu.make_async_copy(
                refs[0].at[0, 0], down.at[t, :, span(m)], sems.at[QUARTERS * t + m]
            ).wait()
        branch[:count] += dot(own_active[t], down[t])
        branch[count:] += dot(far_active[t], down[t])

    own_branch[...] = branch[:count].astype(low16)
    group = same.shape[0]
    same[...] = branch[count : count + group].astype(low16)
    cross[...] = branch[count + group :].astype(low16)


def local_feed_grad_kernel(second, far_second, own_lifted, far_lifted, own_active, far_active,
                           top, far_top, send_a, send_b, keep_a, keep_b, turned, tops):
    count = second.shape[0]
    turned[:, :count] = jnp.transpose(second[...])
    turned[:, count:] = jnp.transpose(far_second[...])
    tops[:count] = top[...]
    tops[count:] = far_top[...]
    for k in range(2):
        for part, pairs in enumerate(
            (((send_a, SEND_A), (keep_a, KEEP_A)), ((send_b, SEND_B), (keep_b, KEEP_B)))
        ):
            t = 2 * k + part
            right = jnp.concatenate([own_lifted[t], far_lifted[t]], axis=0)
            left = jnp.concatenate(
                [jnp.transpose(own_active[t]), jnp.transpose(far_active[t])], axis=1
            )
            for target, order in pairs:
                for place, m in enumerate(order):
                    target[place, 2 * k] = dot(turned[span(m), :], right).astype(low16)
                    target[place, 2 * k + 1] = dot(left, tops[:, span(m)]).astype(low16)


def local_mix_kernel(first, grad_query_keys, grad_values, mixed, mid,
                     send_a, send_b, keep_a, keep_b, turned):
    turned[...] = jnp.transpose(first[...])
    half = grad_values.shape[2]
    for k in range(4):
        left = jnp.transpose(mixed[:, k * half : (k + 1) * half])
        for target, order in ((send_a, SEND_A), (keep_a, KEEP_A)):
            for place, m in enumerate(order):
                target[place, k] = dot(turned[span(m), :], grad_query_keys[k]).astype(low16)
        for target, order in ((send_b, SEND_B), (keep_b, KEEP_B)):
            for place, m in enumerate(order):
                value = dot(turned[span(m), :], grad_values[k]).astype(low16)
                out = dot(left, mid[:, span(m)]).astype(low16)
                target[place, k, :, :half] = value
                target[place, k, :half, half:] = out[:, :half]
                target[place, k, half:, half:] = out[:, half:]


def by_order(send_a, send_b, keep_a, keep_b):
    return (
        (0, ((send_a, SEND_A), (keep_a, KEEP_A))),
        (1, ((send_b, SEND_B), (keep_b, KEEP_B))),
    )


def global_feed_grad_kernel(info, second, far_second, grad_lifted, far_lifted, active, far_active,
                            top, far_top, send_a, send_b, keep_a, keep_b, turned, tops):
    sec, count = info[SEC], second.shape[0]
    turned[:, :count] = jnp.transpose(second[...])
    turned[:, count:] = jnp.transpose(far_second[...])
    tops[:count] = top[...]
    tops[count:] = far_top[...]
    wide = active.shape[1] // 2
    for part, pairs in by_order(send_a, send_b, keep_a, keep_b):
        at = pl.ds(pl.multiple_of(sec * wide + part * UNIT, UNIT), UNIT)
        right = jnp.concatenate([grad_lifted[:, at], far_lifted[:, span(part)]], axis=0)
        left = jnp.concatenate(
            [jnp.transpose(active[:, at]), jnp.transpose(far_active[:, span(part)])], axis=1
        )
        for target, order in pairs:
            for place, m in enumerate(order):
                target[place, 0] = dot(turned[span(m), :], right).astype(low16)
                target[place, 1] = dot(left, tops[:, span(m)]).astype(low16)


def global_mix_grad_kernel(info, first, far_first, grads, far_grads, mixed, far_mixed, mid,
                           far_mid, send_a, send_b, keep_a, keep_b, turned, mids):
    sec, count = info[SEC], first.shape[0]
    turned[:, :count] = jnp.transpose(first[...])
    turned[:, count:] = jnp.transpose(far_first[...])
    mids[:count] = mid[...]
    mids[count:] = far_mid[...]
    width = mixed.shape[1] // 2
    at = pl.ds(pl.multiple_of(sec * width, width), width)
    right = [jnp.concatenate([grads[c, :, at], far_grads[c]], axis=0) for c in range(3)]
    left = jnp.concatenate([jnp.transpose(mixed[:, at]), jnp.transpose(far_mixed[...])], axis=1)
    for part, pairs in by_order(send_a, send_b, keep_a, keep_b):
        for target, order in pairs:
            for place, m in enumerate(order):
                rows = turned[span(m), :]
                if part == 0:
                    for c in range(2):
                        target[place, 0, :, c * width : (c + 1) * width] = dot(
                            rows, right[c]
                        ).astype(low16)
                else:
                    target[place, 0, :, :width] = dot(rows, right[2]).astype(low16)
                    out = dot(left, mids[:, span(m)]).astype(low16)
                    target[place, 0, :width, width:] = out[:, :width]
                    target[place, 0, width:, width:] = out[:, width:]


def add16(a, b):
    return (a.astype(f32) + b.astype(f32)).astype(low16)


def far_kernel(keep_a, from_x, keep_b, from_y, far_a, far_b):
    far_a[...] = add16(keep_a[0], from_x[0])
    far_b[...] = add16(keep_b[0], from_y[0])


def sum_kernel(shards, *refs):
    parts, outs = (refs[:3], refs[3:6]), refs[6:]
    for part, (keep, once, twice) in enumerate(parts):
        total = keep[0].astype(f32) + once[0].astype(f32) + twice[...].astype(f32)
        total = total.astype(low16)
        count = total.shape[0] // shards
        at = slice(part * count, (part + 1) * count)
        if shards == 1:
            outs[0][at] = total
        elif shards == 2:
            outs[1][0, at] = total[:count]
            outs[0][0, at] = total[count:]
        else:
            for k in range(4):
                outs[(k + 1) % 2][k // 2, at] = total[k * count : (k + 1) * count]


def far_tensor_kernel(keep, arrived, far):
    far[...] = add16(keep[0], arrived[0])


def pick_kernel(info, *refs):
    *terms, world, given, kept = refs
    sec = info[SEC]
    local = terms[0][0].astype(f32)
    for term in terms[1:]:
        local = local + (term[0] if len(term.shape) == 4 else term[...]).astype(f32)
    local = local.astype(low16)
    other = world[...]
    given[...] = jnp.where(sec == 0, local, other)
    kept[...] = jnp.where(sec == 0, other, local)


def half_at(index, count):
    return pl.BlockSpec(
        (1, count, UNIT, UNIT), lambda i: (index, 0, 0, 0), memory_space=pltpu.VMEM
    )


def quarter_unit(refs, m, index):
    own, x_part, y_part, far_kept, far_arrived = refs
    count = own.shape[0] // 2
    if m < 3:
        return (own, x_part, y_part)[m][index].astype(f32)
    return (far_kept[index] if index < count else far_arrived[index - count]).astype(f32)


def feed_final_kernel(info, *rest):
    refs, (up, down) = rest[:5], rest[5:]
    low, sec = info[LOW], info[SEC]
    wide = up.shape[1] // 2
    count = refs[0].shape[0] // 2
    for m in range(QUARTERS):
        at = pl.ds(block_at(low, m), UNIT)
        for source, half in ((0, sec), (count, 1 - sec)):
            for part in range(2):
                hidden = pl.ds(pl.multiple_of(half * wide + part * UNIT, UNIT), UNIT)
                up[at, hidden] = quarter_unit(refs, m, source + 2 * part)
                down[hidden, at] = quarter_unit(refs, m, source + 2 * part + 1)


def mix_final_kernel(info, *rest):
    refs, (qkv, out) = rest[:5], rest[5:]
    low, sec = info[LOW], info[SEC]
    width = out.shape[0] // 2
    count = refs[0].shape[0] // 2
    for m in range(QUARTERS):
        at = pl.ds(block_at(low, m), UNIT)
        at_left = pl.ds(block_at(low, m), width)
        at_right = pl.ds(pl.multiple_of(block_at(low, m) + width, width), width)
        for source, half in ((0, sec), (count, 1 - sec)):
            lanes = pl.ds(pl.multiple_of(half * width, width), width)
            query_keys = quarter_unit(refs, m, source)
            qkv[0, at, lanes] = query_keys[:, :width]
            qkv[1, at, lanes] = query_keys[:, width:]
            rest_unit = quarter_unit(refs, m, source + 1)
            qkv[2, at, lanes] = rest_unit[:, :width]
            out[lanes, at_left] = rest_unit[:width, width:]
            out[lanes, at_right] = rest_unit[width:, width:]


def sum_rest(value):
    step = QUARTERS
    while step < lax.axis_size("dp"):
        value = add16(value, swap(value, "dp", step))
        step *= 2
    return value


class Sum:
    def __init__(self, order, shards, send_a, send_b, keep_a, keep_b):
        self.order, self.shards = order, shards
        self.keep = (keep_a, keep_b)
        self.count = keep_a.shape[1]
        self.once = (swap(send_a, "dp", 1), swap(send_b, "dp", 2))

    def second(self):
        far = half_at(1, self.count)
        far_a, far_b = self.order.call(
            far_kernel,
            [shape((self.count, UNIT, UNIT), low16)] * 2,
            (self.keep[0], self.once[0], self.keep[1], self.once[1]),
            [far] * 4,
            grid=(1,),
        )
        self.twice = (swap(far_a, "dp", 2), swap(far_b, "dp", 1))

    def third(self):
        count = 2 * self.count // self.shards
        if self.shards == 1:
            outs = [shape((count, UNIT, UNIT), low16)]
        else:
            outs = [shape((self.shards // 2, count, UNIT, UNIT), low16)] * 2
        near = half_at(0, self.count)
        totals = self.order.call(
            functools.partial(sum_kernel, self.shards),
            outs,
            (self.keep[0], self.once[0], self.twice[0], self.keep[1], self.once[1], self.twice[1]),
            [near, near, VM] * 2,
            grid=(1,),
        )
        totals = [sum_rest(total) for total in totals]
        self.count = count
        if self.shards == 1:
            return totals[0]
        self.keep = totals[1]
        if self.shards == 2:
            self.terms = (self.keep, swap(totals[0], "tensor", 2))
        else:
            self.once = swap(totals[0], "tensor", 1)

    def fourth(self):
        far = self.order.call(
            far_tensor_kernel,
            [shape((self.count, UNIT, UNIT), low16)],
            (self.keep, self.once),
            [half_at(1, self.count)] * 2,
            grid=(1,),
        )[0]
        self.terms = (self.keep, self.once, swap(far, "tensor", 2))

    def gathered(self, info, world):
        near = half_at(0, self.count)
        given, kept = self.order.call(
            pick_kernel,
            [shape((self.count, UNIT, UNIT), low16)] * 2,
            (info,) + self.terms + (world,),
            [SM] + [near if term.ndim == 4 else VM for term in self.terms] + [VM],
            grid=(1,),
        )
        units = jnp.concatenate([kept, swap(given, "section", 1)])
        return Gather(units)


class Gather:
    def __init__(self, units):
        self.units = units
        self.count = units.shape[0] // 2
        self.near = (swap(units, "dp", 1), swap(units, "dp", 2))

    def far(self):
        x_part, y_part = self.near
        self.rest = (
            swap(x_part[: self.count], "dp", 2), swap(y_part[self.count :], "dp", 1)
        )
        return (self.units,) + self.near + self.rest


def on_device(codes, lengths, gains, w_qkv, w_out, w_up, w_down, cotangent):
    sec = lax.axis_index("section")
    low = lax.axis_index("dp") % QUARTERS
    z = lax.axis_index("tensor")
    first_core = sec == 0
    utts, frames, code_count, width = codes.shape
    heads_width = w_out.shape[1]
    half = heads_width // 2
    wide = w_up.shape[2]
    rows_g = 4 * frames
    rows_l = utts * code_count * frames
    tiles = wide // UNIT
    info = jnp.concatenate([jnp.stack([low, sec, z]).astype(jnp.int32), lengths])
    order = Order()
    call = order.call

    code_rows = jnp.transpose(codes, (0, 2, 1, 3))
    cot_rows = jnp.transpose(cotangent, (0, 2, 1, 3))
    own_w = (jnp.transpose(w_qkv[0], (1, 0, 2)), w_out[0], w_up[0], w_down[0])

    def sem(count):
        return pltpu.SemaphoreType.DMA((count,))

    def gather(rows):
        gathered = lax.all_gather(rows, "tensor")
        order.tokens = (gathered,)
        return gathered

    def scatter(partial):
        return lax.all_to_all(partial, "tensor", 0, 0)

    other_gain = swap(gains[0], "section", 1)
    own_w, other_gain = lax.optimization_barrier((own_w, other_gain))

    def with_other(weights):
        return tuple(w for own in weights for w in (own, swap(own, "section", 1)))

    attention_w = with_other(own_w[:2])

    first_rows, start_g, gain_g, gain_l = call(
        start_kernel,
        [
            shape((frames, width), low16),
            shape((frames, width), f32),
            shape((2, width), f32),
            shape((2, width), f32),
        ],
        (info, code_rows, gains[0], other_gain),
        [SM, VM, VM, VM],
        us=2,
    )
    first_blocks = gather(first_rows)

    mix_piece, mix_whole = call(
        mix_piece_kernel,
        [shape((2, UNIT, UNIT), low16), shape((QUARTERS, 2, UNIT, UNIT), low16)],
        (info,) + attention_w,
        [SM] + [ANY] * 4,
        [sem(5 * QUARTERS)],
        us=3.2,
    )
    mix_z1 = swap(mix_piece, "tensor", 1)
    mix_z2 = swap(mix_piece, "tensor", 2)
    feed_w = with_other(order.after(own_w[2:]))

    first_g, packed_g, probs_g, mixed_g, mixed_given, partial = call(
        global_attention_kernel,
        [
            shape((rows_g, width), low16),
            shape((3, rows_g, heads_width), low16),
            shape((heads_width // HEAD_DIM, rows_g, rows_g), f32),
            shape((rows_g, heads_width), low16),
            shape((rows_g, half), low16),
            shape((4, frames, width), low16),
        ],
        (info, first_blocks) + attention_w,
        [SM, VM] + [ANY] * 4,
        [
            pltpu.VMEM((3, width, heads_width), low16),
            pltpu.VMEM((heads_width, width), low16),
            sem(8),
        ],
        us=5.7,
    )
    partial, mix_z1, mix_z2 = lax.optimization_barrier((partial, mix_z1, mix_z2))
    arrived = scatter(partial)
    mix_z3 = swap(order.after(mix_z2), "tensor", 1)
    top_l, top_given = call(
        local_top_kernel,
        [shape((rows_l, width), low16), shape((rows_l // utts, width), low16)],
        (info, cot_rows),
        [SM, VM],
        us=2.3,
    )
    mix_near = jnp.stack(order.after([mix_z1, mix_z2]))
    mix_x = swap(mix_near, "dp", 1)
    mix_y = swap(mix_near, "dp", 2)
    feed_piece, feed_whole = call(
        feed_piece_kernel,
        [shape((4, UNIT, UNIT), low16), shape((QUARTERS, 4, UNIT, UNIT), low16)],
        (info,) + feed_w,
        [SM] + [ANY] * 4,
        [sem(4 * QUARTERS)],
        us=4,
    )
    feed_z2 = swap(feed_piece, "tensor", 2)
    hidden_g, second_rows = call(
        middle_kernel,
        [shape((frames, width), f32), shape((frames, width), low16)],
        (start_g, arrived, gain_g),
        [VM] * 3,
        us=2,
    )
    mix_z3 = order.after(mix_z3)
    mix_x3 = swap(mix_z3, "dp", 1)
    mix_y3 = swap(mix_z3, "dp", 2)
    second_blocks = gather(second_rows)
    order.until(feed_z2, mix_x, mix_y, mix_x3, mix_y3)
    feed_z2, mix_x, mix_y, mix_x3, mix_y3 = order.after((feed_z2, mix_x, mix_y, mix_x3, mix_y3))
    mix_w = (
        mix_whole,
        mix_z1,
        mix_z2,
        mix_z3,
        mix_x,
        mix_y,
        swap(mix_x[:, 0], "dp", 2),
        swap(mix_y[:, 1], "dp", 1),
        mix_x3,
        mix_y3,
        swap(mix_x3[:1], "dp", 2),
        swap(mix_y3[1:], "dp", 1),
    )
    feed_x = swap(feed_z2, "dp", 1)
    feed_y = swap(feed_z2, "dp", 2)
    second_g, lifted_g, active_g, active_given, partial = call(
        global_feed_kernel,
        [
            shape((rows_g, width), low16),
            shape((rows_g, wide), f32),
            shape((rows_g, wide), low16),
            shape((rows_g, wide // 2), low16),
            shape((4, frames, width), low16),
        ],
        (info, second_blocks) + feed_w,
        [SM, VM] + [ANY] * 4,
        [
            pltpu.VMEM((width, wide), low16),
            pltpu.VMEM((wide, width), low16),
            pltpu.VMEM((rows_g, width), f32),
            sem(8),
        ],
        us=5.6,
    )
    arrived = scatter(partial)
    order.until(feed_x, feed_y)
    sent = call(
        sent_kernel,
        [shape((frames, width), low16)],
        (hidden_g, arrived),
        [VM] * 2,
        us=1.9,
    )[0]
    other_sent = swap(sent, "section", 1)
    feed_x, feed_y = order.after((feed_x, feed_y))
    feed_l = (
        feed_whole,
        feed_z2,
        feed_x,
        feed_y,
        swap(feed_x[:2], "dp", 2),
        swap(feed_y[2:], "dp", 1),
    )
    top_same = swap(order.after(top_given), "tensor", 1)

    start_l, first_l, query_keys, values_l, probs_l, mixed_l, partial = call(
        local_attention_kernel,
        [
            shape((rows_l, width), f32),
            shape((rows_l, width), low16),
            shape((4, rows_l, 2 * half), low16),
            shape((4, rows_l, half), low16),
            shape((4, utts, 2 * rows_l // utts, half), f32),
            shape((rows_l, 4 * half), low16),
            shape((rows_l, width), low16),
        ],
        (info, code_rows, sent, other_sent, gain_l) + mix_w,
        [SM] + [VM] * 4 + [ANY] * MIX_REFS,
        [
            pltpu.VMEM((4, 2, width, UNIT), low16),
            pltpu.VMEM((4 * half, width), low16),
            sem(32),
        ],
        us=9,
    )
    order.until(*feed_l, top_same)
    hidden_l, second_l, second_given = call(
        local_norm_kernel,
        [
            shape((rows_l, width), f32),
            shape((rows_l, width), low16),
            shape((rows_l // utts, width), low16),
        ],
        (info, start_l, partial, swap(partial, "section", 1), gain_l),
        [SM] + [VM] * 4,
        us=3.7,
    )
    second_same = swap(second_given, "tensor", 1)
    top_cross = swap(order.after(top_same), "section", 1)
    feed_scratch = [
        pltpu.VMEM((tiles, width, UNIT), low16),
        pltpu.VMEM((tiles, UNIT, width), low16),
        pltpu.VMEM((rows_l, width), f32),
        sem(8 * tiles),
    ]
    wide_rows = shape((rows_l, width), low16)
    half_rows = shape((rows_l // utts, width), low16)
    tiled_rows = shape((tiles, rows_l, UNIT), low16)
    active_l, grad_lifted_l, back = call(
        local_feed_kernel,
        [tiled_rows, tiled_rows, wide_rows],
        (second_l, top_l) + feed_l,
        [VM] * 2 + [ANY] * FEED_REFS,
        feed_scratch,
        us=7.9,
    )
    other_back = swap(back, "section", 1)
    second_same = order.after(second_same)
    second_cross = swap(second_same, "section", 1)
    far_active, far_lifted, far_second, far_top, same, cross = call(
        far_feed_kernel,
        [tiled_rows, tiled_rows, wide_rows, wide_rows, half_rows, half_rows],
        (second_same, second_cross, top_same, top_cross) + feed_l,
        [VM] * 4 + [ANY] * FEED_REFS,
        feed_scratch,
        us=8.2,
    )

    def from_neighbour(same, cross):
        total = call(
            pair_kernel, [half_rows], (same, swap(cross, "section", 1)), [VM] * 2
        )[0]
        return swap(total, "tensor", 1)

    far_same = from_neighbour(same, cross)
    turned_l = pltpu.VMEM((width, rows_l), low16)
    local_feed = Sum(
        order,
        2,
        *call(
            local_feed_grad_kernel,
            [shape((2, 4, UNIT, UNIT), low16)] * 4,
            (
                second_l, far_second, grad_lifted_l, far_lifted, active_l, far_active, top_l,
                far_top,
            ),
            [VM] * 8,
            [pltpu.VMEM((width, 2 * rows_l), low16), pltpu.VMEM((2 * rows_l, width), low16)],
            us=7.6,
        ),
    )
    far_same = order.after(far_same)
    far_back = (far_same, swap(far_same, "section", 1))
    far_first, far_mixed, far_second_g, far_active_g = (
        swap(order.after(value), "section", 1)
        for value in (first_g, mixed_given, second_g, active_given)
    )
    grad_hidden_l, mid_l, grad_query_keys, grad_values, back, gain2_l = call(
        local_attention_back_kernel,
        [
            shape((rows_l, width), f32),
            shape((rows_l, width), low16),
            shape((4, rows_l, 2 * half), low16),
            shape((4, rows_l, half), low16),
            shape((rows_l, width), low16),
            shape((1, width), f32),
        ],
        (info, hidden_l, back, other_back)
        + far_back
        + (top_l, gain_l, query_keys, values_l, probs_l)
        + mix_w,
        [SM] + [VM] * 10 + [ANY] * MIX_REFS,
        [
            pltpu.VMEM((4, 2, width, UNIT), low16),
            pltpu.VMEM((4 * half, width), low16),
            pltpu.VMEM((rows_l, width), f32),
            sem(32),
        ],
        us=11.4,
    )
    other_back = swap(back, "section", 1)
    local_mix = Sum(
        order,
        4,
        *call(
            local_mix_kernel,
            [shape((2, 4, UNIT, UNIT), low16)] * 4,
            (first_l, grad_query_keys, grad_values, mixed_l, mid_l),
            [VM] * 5,
            [turned_l],
            us=6,
        ),
    )
    returned, code_part, gain1_l = call(
        local_end_kernel,
        [
            shape((frames, width), low16),
            shape((utts, code_count, frames, width // 2), f32),
            shape((1, width), f32),
        ],
        (info, back, other_back, start_l, grad_hidden_l, gain_l),
        [SM] + [VM] * 5,
        [pltpu.VMEM((rows_l, width), f32)],
        us=4.4,
    )

    top_blocks = gather(returned)
    local_feed.second()
    order.until(*local_mix.once, far_first, far_mixed, far_second_g, far_active_g)
    top_g, grad_lifted_g, lifted_given, partial = call(
        global_feed_back_kernel,
        [
            shape((rows_g, width), low16),
            shape((rows_g, wide), low16),
            shape((rows_g, wide // 2), low16),
            shape((4, frames, width), low16),
        ],
        (info, top_blocks, lifted_g) + feed_w,
        [SM] + [VM] * 2 + [ANY] * 4,
        [
            pltpu.VMEM((width, wide), low16),
            pltpu.VMEM((wide, width), low16),
            pltpu.VMEM((rows_g, width), f32),
            sem(8),
        ],
        us=6.3,
    )
    arrived = scatter(partial)
    far_top_g, far_lifted_g = swap(top_g, "section", 1), swap(lifted_given, "section", 1)
    local_feed.third()
    local_mix.second()
    global_feed = Sum(
        order,
        1,
        *call(
            global_feed_grad_kernel,
            [shape((2, 2, UNIT, UNIT), low16)] * 4,
            (
                info, second_g, far_second_g, grad_lifted_g, far_lifted_g, active_g, far_active_g,
                top_g, far_top_g,
            ),
            [SM] + [VM] * 8,
            [pltpu.VMEM((width, 2 * rows_g), low16), pltpu.VMEM((2 * rows_g, width), low16)],
            us=3.5,
        ),
    )
    grad_hidden_g, mid_rows, gain2_g = call(
        middle_back_kernel,
        [shape((frames, width), f32), shape((frames, width), low16), shape((1, width), f32)],
        (arrived, hidden_g, gain_g, returned),
        [VM] * 4,
        us=2.1,
    )
    mid_blocks = gather(mid_rows)
    order.until(*local_mix.twice)
    mid_g, grads_g, grads_given, partial = call(
        global_attention_back_kernel,
        [
            shape((rows_g, width), low16),
            shape((3, rows_g, heads_width), low16),
            shape((3, rows_g, half), low16),
            shape((4, frames, width), low16),
        ],
        (info, mid_blocks, packed_g, probs_g) + attention_w,
        [SM] + [VM] * 3 + [ANY] * 4,
        [
            pltpu.VMEM((3, width, heads_width), low16),
            pltpu.VMEM((heads_width, width), low16),
            sem(8),
        ],
        us=6.8,
    )
    arrived = scatter(partial)
    far_mid_g, far_grads_g = swap(mid_g, "section", 1), swap(grads_given, "section", 1)
    global_feed.second()
    local_mix.third()
    global_mix = Sum(
        order,
        1,
        *call(
            global_mix_grad_kernel,
            [shape((2, 1, UNIT, UNIT), low16)] * 4,
            (
                info, first_g, far_first, grads_g, far_grads_g, mixed_g, far_mixed, mid_g,
                far_mid_g,
            ),
            [SM] + [VM] * 8,
            [pltpu.VMEM((width, 2 * rows_g), low16), pltpu.VMEM((2 * rows_g, width), low16)],
            us=3,
        ),
    )
    kept_start, given_start, gain1_g = call(
        start_back_kernel,
        [
            shape((frames, width // 2), f32),
            shape((frames, width // 2), f32),
            shape((1, width), f32),
        ],
        (info, arrived, start_g, gain_g, grad_hidden_g),
        [SM] + [VM] * 4,
        [pltpu.VMEM((frames, width), f32)],
        us=2.1,
    )
    local_mix.fourth()
    feed_sum = local_feed.gathered(info, global_feed.third())
    global_mix.second()
    own_branch, same, cross = call(
        local_drop_kernel,
        [wide_rows, half_rows, half_rows],
        (active_l, far_active) + feed_l,
        [VM] * 2 + [ANY] * FEED_REFS,
        [
            pltpu.VMEM((tiles, UNIT, width), low16),
            pltpu.VMEM((2 * rows_l, width), f32),
            sem(QUARTERS * tiles),
        ],
        us=6.1,
    )
    other_branch = swap(own_branch, "section", 1)
    arrived_start = swap(given_start, "section", 1)
    both_start = jnp.stack(
        [
            jnp.where(first_core, kept_start, arrived_start),
            jnp.where(first_core, arrived_start, kept_start),
        ]
    )
    code_grad = jnp.transpose(code_part + both_start[:, None], (0, 2, 1, 3))
    far_branch = from_neighbour(same, cross)
    far_branch = (far_branch, swap(far_branch, "section", 1))

    own_gain = jnp.concatenate([gain1_g, gain2_g], axis=0)
    total_gain = own_gain + swap(own_gain, "section", 1)
    local_gain = jnp.concatenate([gain1_l, gain2_l], axis=0)
    gain_total = jnp.where(first_core, total_gain, local_gain)
    gain_total = jnp.concatenate(
        [
            lax.dynamic_slice_in_dim(gain_total, (low ^ m) * UNIT, UNIT, 1)
            for m in range(QUARTERS)
        ],
        axis=1,
    )
    def over(value, axis):
        copies = jnp.broadcast_to(value, (lax.axis_size(axis),) + value.shape)
        return jnp.sum(lax.all_to_all(order.after(copies), axis, 0, 0), axis=0)

    gain_total = over(gain_total, "tensor")
    order.until(gain_total)

    mix_sum = local_mix.gathered(info, global_mix.third())
    output = call(
        output_kernel,
        [shape((utts, code_count, frames, width // 2), low16)],
        (info, hidden_l, own_branch, other_branch) + far_branch,
        [SM] + [VM] * 5,
        us=3.1,
    )[0]
    feed_parts = feed_sum.far()
    gain_total = over(gain_total, "dp")
    order.until(gain_total)
    mix_parts = mix_sum.far()
    up_grad, down_grad = call(
        feed_final_kernel,
        [shape((width, wide), f32), shape((wide, width), f32)],
        (info,) + feed_parts,
        [SM] + [VM] * 5,
        us=6.8,
    )
    qkv_grad, out_grad = call(
        mix_final_kernel,
        [shape((3, width, heads_width), f32), shape((heads_width, width), f32)],
        (info,) + mix_parts,
        [SM] + [VM] * 5,
        us=4.5,
    )
    return (
        jnp.transpose(output, (0, 2, 1, 3)),
        code_grad,
        gain_total[None],
        jnp.transpose(qkv_grad, (1, 0, 2))[None],
        out_grad[None],
        up_grad[None],
        down_grad[None],
    )


def solution(mesh):
    in_specs = (
        P("dp", "tensor", None, None),
        P("dp"),
        P("section", None, None),
        P("section", None, None, "tensor"),
        P("section", "tensor", None),
        P("section", None, "tensor"),
        P("section", "tensor", None),
        P("dp", "tensor", None, None),
    )
    out_specs = (
        P("dp", "tensor", None, "section"),
        P("dp", "tensor", None, "section"),
        P("section", None, None),
        P("section", None, None, "tensor"),
        P("section", "tensor", None),
        P("section", None, "tensor"),
        P("section", "tensor", None),
    )
    return jax.shard_map(
        on_device, mesh=mesh, in_specs=in_specs, out_specs=out_specs, check_vma=False
    )
```

```python
import functools

import jax
import jax.numpy as jnp
from jax import lax
from jax.experimental import pallas as pl
from jax.experimental.pallas import tpu as pltpu
from jax.sharding import PartitionSpec as P

HEAD_DIM = 64
SCALE = HEAD_DIM ** (-0.5)
QUARTERS = 4
UNIT = 256
epsilon = 1e-06
negative = -1e30
f32 = jnp.float32
low16 = jnp.bfloat16

VM = pl.BlockSpec(memory_space=pltpu.VMEM)
SM = pl.BlockSpec(memory_space=pltpu.SMEM)
ANY = pl.BlockSpec(memory_space=pltpu.HBM)
MIB = 1 << 20
PACE = 2 * 10**8

LOW, SEC, SHARD, LENGTHS = 0, 1, 2, 3


def shape(dims, dtype):
    return jax.ShapeDtypeStruct(tuple(dims), dtype)


class Order:
    def __init__(self):
        self.tokens = ()

    def after(self, value):
        if not self.tokens:
            return value
        return lax.optimization_barrier((value,) + self.tokens)[0]

    def until(self, *values):
        self.tokens += values

    def call(self, body, outs, args, specs, scratch=(), limit=56, us=2.0, grid=()):
        args = (self.after(args[0]),) + tuple(args[1:])
        results = pl.pallas_call(
            body,
            out_shape=tuple(outs),
            grid=grid,
            in_specs=list(specs),
            out_specs=tuple(VM for _ in outs),
            scratch_shapes=list(scratch),
            compiler_params=pltpu.CompilerParams(vmem_limit_bytes=limit * MIB),
            cost_estimate=pl.CostEstimate(
                flops=int(us * PACE), bytes_accessed=0, transcendentals=0
            ),
        )(*args)
        self.tokens = (results[-1],)
        return results


def swap(value, axis, flip):
    count = lax.axis_size(axis)
    return lax.ppermute(value, axis, [(i, i ^ flip) for i in range(count)])


def dot(a, b):
    return jnp.dot(a, b, preferred_element_type=f32)


def dot_tn(a, b):
    return lax.dot_general(a, b, (((0,), (0,)), ((), ())), preferred_element_type=f32)


def dot_nt(a, b):
    return lax.dot_general(a, b, (((1,), (1,)), ((), ())), preferred_element_type=f32)


def factor_of(values):
    return lax.rsqrt(jnp.mean(values * values, axis=-1, keepdims=True) + epsilon)


def norm_back(values, gain, upstream):
    factor = factor_of(values)
    weighted = upstream * gain
    inner = jnp.mean(weighted * values, axis=-1, keepdims=True)
    through = factor * weighted - values * (factor * factor * factor) * inner
    return through, jnp.sum(upstream * values * factor, axis=0, keepdims=True)


def normal_cdf(values):
    return 0.5 * (1.0 + lax.erf(values * (0.5**0.5)))


def gelu_slope(values, cdf):
    return cdf + values * (jnp.exp(-0.5 * values * values) * 0.3989422804014327)


def block_at(low, m):
    return pl.multiple_of((low ^ m) * UNIT, UNIT)


def span(m):
    return slice(m * UNIT, (m + 1) * UNIT)


class Copies:
    def __init__(self, sems):
        self.sems = sems
        self.made = []

    def start(self, src, dst):
        copy = pltpu.make_async_copy(src, dst, self.sems.at[len(self.made)])
        copy.start()
        self.made.append(copy)
        return copy

    def pick(self, own_first, sec, own, other, dst):
        sem = self.sems.at[len(self.made)]

        @pl.when((sec == 0) == own_first)
        def _():
            pltpu.make_async_copy(own, dst, sem).start()

        @pl.when((sec == 0) != own_first)
        def _():
            pltpu.make_async_copy(other, dst, sem).start()

        copy = pltpu.make_async_copy(own, dst, sem)
        self.made.append(copy)
        return copy

    def wait(self, begin=0, end=None):
        for copy in self.made[begin:end]:
            copy.wait()


def start_kernel(info, codes, own_gain, other_gain, first, start, gain_g, gain_l):
    low, sec = info[LOW], info[SEC]
    for m in range(QUARTERS):
        at = pl.ds(block_at(low, m), UNIT)
        own, other = own_gain[:, at], other_gain[:, at]
        gain_g[:, span(m)] = jnp.where(sec == 0, own, other)
        gain_l[:, span(m)] = jnp.where(sec == 0, other, own)
        total = codes[sec, 0, :, at].astype(f32)
        for c in range(1, codes.shape[1]):
            total = total + codes[sec, c, :, at].astype(f32)
        start[:, span(m)] = total
    values = start[...]
    first[...] = (values * factor_of(values) * gain_g[0:1, :]).astype(low16)


def from_local(sec, own, other, branch):
    @pl.when(sec == 0)
    def _():
        branch(0, *other)

    @pl.when(sec != 0)
    def _():
        branch(1, *own)


def mix_piece_kernel(info, own_qkv, other_qkv, own_out, other_out, piece, whole, sems):
    low, sec = info[LOW], info[SEC]
    half = own_qkv.shape[2] // 2

    def branch(half_index, qkv, out):
        made = Copies(sems)
        for m in range(QUARTERS):
            at = pl.ds(block_at(low, m), UNIT)
            at_right = pl.ds(pl.multiple_of(block_at(low, m) + half, half), half)
            at_left = pl.ds(block_at(low, m), half)
            lanes = slice(half_index * half, (half_index + 1) * half)
            target = whole.at[m]
            made.start(qkv.at[0, at, lanes], target.at[0, :, 0:half])
            made.start(qkv.at[1, at, lanes], target.at[0, :, half : 2 * half])
            made.start(qkv.at[2, at, lanes], target.at[1, :, 0:half])
            made.start(out.at[lanes, at_left], target.at[1, 0:half, half : 2 * half])
            made.start(out.at[lanes, at_right], target.at[1, half : 2 * half, half : 2 * half])
        made.wait()

    from_local(sec, (own_qkv, own_out), (other_qkv, other_out), branch)
    piece[...] = whole[0]


def feed_piece_kernel(info, own_up, other_up, own_down, other_down, piece, whole, sems):
    low, sec = info[LOW], info[SEC]
    wide = own_up.shape[1] // 2

    def branch(half_index, up, down):
        made = Copies(sems)
        for m in range(QUARTERS):
            at = pl.ds(block_at(low, m), UNIT)
            for part in range(2):
                begin = half_index * wide + part * UNIT
                hidden = slice(begin, begin + UNIT)
                made.start(up.at[at, hidden], whole.at[m, part])
                made.start(down.at[hidden, at], whole.at[m, 2 + part])
        made.wait()

    from_local(sec, (own_up, own_down), (other_up, other_down), branch)
    piece[...] = whole[0]


def fetch_attention(made, low, sec, own_qkv, other_qkv, own_out, other_out, qkv, out):
    for m in range(QUARTERS):
        at = pl.ds(block_at(low, m), UNIT)
        made.pick(True, sec, own_qkv.at[:, at, :], other_qkv.at[:, at, :], qkv.at[:, span(m), :])
    for m in range(QUARTERS):
        at = pl.ds(block_at(low, m), UNIT)
        made.pick(True, sec, own_out.at[:, at], other_out.at[:, at], out.at[:, span(m)])


def by_shard(info, blocks):
    count = blocks.shape[0]
    return jnp.concatenate([blocks[info[SHARD] ^ k] for k in range(count)], axis=0)


def other_half(info, width):
    half = width // 2
    return pl.ds(pl.multiple_of((1 - info[SEC]) * half, half), half)


def spread_blocks(info, target, values):
    frames = target.shape[1]
    for k in range(target.shape[0]):
        target[info[SHARD] ^ k] = values[k * frames : (k + 1) * frames].astype(low16)


def row_places(info, count, frames, dimension):
    at = lax.broadcasted_iota(jnp.int32, (count, count), dimension)
    return (lax.div(at, frames) ^ info[SHARD]) * frames + lax.rem(at, frames)


def global_attention_kernel(info, *rest):
    (blocks, own_qkv, other_qkv, own_out, other_out,
     rows, packed, probs, mixed, given, partial, qkv, out, sems) = rest
    low, sec = info[LOW], info[SEC]
    made = Copies(sems)
    fetch_attention(made, low, sec, own_qkv, other_qkv, own_out, other_out, qkv, out)
    count, frames = rows.shape[0], blocks.shape[1]
    length = info[LENGTHS + sec]
    query_at = row_places(info, count, frames, 0)
    key_at = row_places(info, count, frames, 1)
    allowed = (key_at <= query_at) & (key_at < length)
    values = by_shard(info, blocks)
    rows[...] = values
    made.wait(0, QUARTERS)
    for c in range(3):
        packed[c] = dot(values, qkv[c]).astype(low16)
    heads = []
    for h in range(packed.shape[2] // HEAD_DIM):
        lanes = slice(h * HEAD_DIM, (h + 1) * HEAD_DIM)
        scores = dot_nt(packed[0, :, lanes], packed[1, :, lanes]) * SCALE
        scores = jnp.where(allowed, scores, negative)
        raised = jnp.exp(scores - jnp.max(scores, axis=-1, keepdims=True))
        exact = raised / jnp.sum(raised, axis=-1, keepdims=True)
        probs[h] = exact
        heads.append(dot(exact.astype(low16), packed[2, :, lanes]).astype(low16))
    mixed[...] = jnp.concatenate(heads, axis=1)
    given[...] = mixed[:, other_half(info, mixed.shape[1])]
    made.wait(QUARTERS)
    spread_blocks(info, partial, dot(mixed[...], out[...]))


def total_of(arrived):
    total = arrived[0].astype(f32)
    for k in range(1, arrived.shape[0]):
        total = total + arrived[k].astype(f32)
    return total


def middle_kernel(start, arrived, gain, hidden, second):
    values = start[...] + total_of(arrived)
    hidden[...] = values
    second[...] = (values * factor_of(values) * gain[1:2, :]).astype(low16)


def fetch_feed(made, low, sec, own_up, other_up, own_down, other_down, up, down):
    for m in range(QUARTERS):
        at = pl.ds(block_at(low, m), UNIT)
        made.pick(True, sec, own_up.at[at, :], other_up.at[at, :], up.at[span(m), :])
    for m in range(QUARTERS):
        at = pl.ds(block_at(low, m), UNIT)
        made.pick(True, sec, own_down.at[:, at], other_down.at[:, at], down.at[:, span(m)])


def global_feed_kernel(info, *rest):
    (blocks, own_up, other_up, own_down, other_down,
     rows, lifted, active, given, partial, up, down, total, sems) = rest
    made = Copies(sems)
    fetch_feed(made, info[LOW], info[SEC], own_up, other_up, own_down, other_down, up, down)
    values = by_shard(info, blocks)
    rows[...] = values
    made.wait(0, QUARTERS)
    for t in range(up.shape[1] // UNIT):
        tile = dot(values, up[:, span(t)])
        lifted[:, span(t)] = tile
        low_tile = (tile * normal_cdf(tile)).astype(low16)
        active[:, span(t)] = low_tile
        if t == 0:
            made.wait(QUARTERS)
        branch = dot(low_tile, down[span(t), :])
        total[...] = branch if t == 0 else total[...] + branch
    spread_blocks(info, partial, total[...])
    given[...] = active[:, other_half(info, active.shape[1])]


def sent_kernel(hidden, arrived, sent):
    sent[...] = (hidden[...] + total_of(arrived)).astype(low16)


def global_feed_back_kernel(info, *rest):
    (blocks, lifted, own_up, other_up, own_down, other_down,
     rows, grad_lifted, given, partial, up, down, total, sems) = rest
    made = Copies(sems)
    fetch_feed(made, info[LOW], info[SEC], own_up, other_up, own_down, other_down, up, down)
    values = by_shard(info, blocks)
    rows[...] = values
    made.wait(QUARTERS)
    for t in range(up.shape[1] // UNIT):
        tile = lifted[:, span(t)]
        grad = dot_nt(values, down[span(t), :]) * gelu_slope(tile, normal_cdf(tile))
        grad = grad.astype(low16)
        grad_lifted[:, span(t)] = grad
        if t == 0:
            made.wait(0, QUARTERS)
        back = dot_nt(grad, up[:, span(t)])
        total[...] = back if t == 0 else total[...] + back
    spread_blocks(info, partial, total[...])
    given[...] = grad_lifted[:, other_half(info, grad_lifted.shape[1])]


def middle_back_kernel(arrived, hidden, gain, returned, grad_hidden, mid, gain_grad):
    through, gain_grad[...] = norm_back(hidden[...], gain[1:2, :], total_of(arrived))
    values = returned[...].astype(f32) + through
    grad_hidden[...] = values
    mid[...] = values.astype(low16)


def global_attention_back_kernel(info, *rest):
    (blocks, packed, probs, own_qkv, other_qkv, own_out, other_out,
     rows, grads, given, partial, qkv, out, sems) = rest
    low, sec = info[LOW], info[SEC]
    made = Copies(sems)
    fetch_attention(made, low, sec, own_qkv, other_qkv, own_out, other_out, qkv, out)
    values = by_shard(info, blocks)
    rows[...] = values
    made.wait(QUARTERS)
    grad_mixed = dot_nt(values, out[...]).astype(low16)
    columns = [[], [], []]
    for h in range(packed.shape[2] // HEAD_DIM):
        lanes = slice(h * HEAD_DIM, (h + 1) * HEAD_DIM)
        exact = probs[h]
        grad = grad_mixed[:, lanes]
        columns[2].append(dot_tn(exact.astype(low16), grad).astype(low16))
        grad_probs = dot_nt(grad, packed[2, :, lanes])
        center = jnp.sum(grad_probs * exact, axis=-1, keepdims=True)
        grad_scores = (exact * (grad_probs - center)).astype(low16)
        columns[0].append((dot(grad_scores, packed[1, :, lanes]) * SCALE).astype(low16))
        columns[1].append((dot_tn(grad_scores, packed[0, :, lanes]) * SCALE).astype(low16))
    total = None
    made.wait(0, QUARTERS)
    for c in range(3):
        grads[c] = jnp.concatenate(columns[c], axis=1)
        back = dot_nt(grads[c], qkv[c])
        total = back if c == 0 else total + back
    spread_blocks(info, partial, total)
    given[...] = grads[:, :, other_half(info, grads.shape[2])]


def start_back_kernel(info, arrived, start, gain, grad_hidden, kept, given, gain_grad, values):
    low, sec = info[LOW], info[SEC]
    through, gain_grad[...] = norm_back(start[...], gain[0:1, :], total_of(arrived))
    values[...] = grad_hidden[...] + through
    for j in range(2):
        kept[:, span(j)] = values[:, pl.ds(block_at(low, 2 * sec + j), UNIT)]
        given[:, span(j)] = values[:, pl.ds(block_at(low, 2 * (1 - sec) + j), UNIT)]


def mix_unit(refs, k, m, u):
    whole, near = refs[0], refs[1:4]
    both = refs[4:8]
    last = refs[8:12]
    if k == 0:
        return whole.at[m, u]
    if m == 0:
        return near[k - 1].at[u]
    if k == 3:
        return last[m - 1].at[u] if m < 3 else last[2 + u].at[0]
    return both[m - 1].at[k - 1, u] if m < 3 else both[2 + u].at[k - 1]


def feed_unit(refs, k, m, u):
    if k == 0:
        return refs[0].at[m, u]
    if m < 3:
        return refs[1 + m].at[u]
    return refs[4].at[u] if u < 2 else refs[5].at[u - 2]


MIX_REFS, FEED_REFS = 12, 6


def pair_rows(a, b, size):
    return jnp.concatenate([a * b, a[size:] * b[: 2 * size], a[2 * size :] * b[:size]], axis=0)


def by_pair(stacked, size):
    names = [(0, 0), (1, 1), (2, 2), (1, 0), (2, 1), (2, 0)]
    return {name: stacked[n * size : (n + 1) * size] for n, name in enumerate(names)}


def from_pairs(pairs):
    names = [(0, 0), (1, 1), (2, 2), (1, 0), (2, 1), (2, 0)]
    return jnp.concatenate([pairs[name] for name in names], axis=0)


def head_sums(products, table):
    upper = products.astype(low16)
    lower = (products - upper.astype(f32)).astype(low16)
    return dot(upper, table) + dot(lower, table)


def head_table(width):
    row = lax.broadcasted_iota(jnp.int32, (width, width), 0) // HEAD_DIM
    column = lax.broadcasted_iota(jnp.int32, (width, width), 1) // HEAD_DIM
    return (row == column).astype(f32).astype(low16)


def gather_mix(weights, mix, k, half):
    for m in range(QUARTERS):
        begin = m * UNIT
        mix[k * half : (k + 1) * half, begin : begin + half] = weights[
            k, 1, begin : begin + half, half:
        ]
        mix[k * half : (k + 1) * half, begin + half : begin + UNIT] = weights[
            k, 1, begin + half : begin + UNIT, half:
        ]


def local_attention_kernel(info, codes, sent_own, sent_other, gain, *rest):
    refs, (start, first, query_keys, values_out, probs, mixed, partial, weights, mix, sems) = (
        rest[:MIX_REFS], rest[MIX_REFS:]
    )
    low, sec = info[LOW], info[SEC]
    made = Copies(sems)
    groups = []
    for k in range(4):
        groups.append(
            [
                made.start(mix_unit(refs, k, m, u), weights.at[k, u, span(m), :])
                for u in range(2)
                for m in range(QUARTERS)
            ]
        )
    utts, code_count, frames, _ = codes.shape
    for u in range(utts):
        sent = jnp.where(sec == u, sent_own[...], sent_other[...]).astype(f32)
        for c in range(code_count):
            row = (u * code_count + c) * frames
            for m in range(QUARTERS):
                code = codes[u, c, :, pl.ds(block_at(low, m), UNIT)].astype(f32)
                start[row : row + frames, span(m)] = sent[:, span(m)] + code
    values = start[...]
    first[...] = (values * factor_of(values) * gain[0:1, :]).astype(low16)
    half = values_out.shape[2]
    table = head_table(half)
    rows = first[...]
    size = frames
    group = code_count * frames
    for k in range(4):
        for copy in groups[k]:
            copy.wait()
        query_keys[k] = dot(rows, weights[k, 0]).astype(low16)
        values_out[k] = dot(rows, weights[k, 1, :, :half]).astype(low16)
        gather_mix(weights, mix, k, half)
        for u in range(utts):
            at = slice(u * group, (u + 1) * group)
            q = query_keys[k, at, :half].astype(f32)
            key = query_keys[k, at, half:].astype(f32)
            val = values_out[k, at, :].astype(f32)
            scores = by_pair(head_sums(pair_rows(q, key, size), table) * SCALE, size)
            exact = {}
            for i in range(3):
                peak = scores[(i, 0)]
                for j in range(1, i + 1):
                    peak = jnp.maximum(peak, scores[(i, j)])
                raised = [jnp.exp(scores[(i, j)] - peak) for j in range(i + 1)]
                whole = raised[0]
                for j in range(1, i + 1):
                    whole = whole + raised[j]
                for j in range(i + 1):
                    exact[(i, j)] = raised[j] / whole
            probs[k, u] = from_pairs(exact)
            for i in range(3):
                total = None
                for j in range(i + 1):
                    weight = exact[(i, j)].astype(low16).astype(f32)
                    term = weight * val[j * size : (j + 1) * size]
                    total = term if total is None else total + term
                begin = u * group + i * size
                mixed[begin : begin + size, k * half : (k + 1) * half] = total.astype(low16)
    partial[...] = dot(mixed[...], mix[...]).astype(low16)


def local_top_kernel(info, cotangent, top, given):
    low, sec = info[LOW], info[SEC]
    utts, code_count, frames, _ = cotangent.shape
    group = code_count * frames
    frame_at = lax.broadcasted_iota(jnp.int32, (frames, 1), 0) + info[SHARD] * frames
    for u in range(utts):
        valid = frame_at < info[LENGTHS + u]
        for c in range(code_count):
            row = u * group + c * frames
            for m in range(QUARTERS):
                part = cotangent[u, c, :, pl.ds(block_at(low, m), UNIT)].astype(f32)
                top[row : row + frames, span(m)] = jnp.where(valid, part, 0.0).astype(low16)
    given[...] = top[pl.ds(pl.multiple_of(sec * group, group), group), :]


def local_norm_kernel(info, start, own_part, other_part, gain, hidden, second, given):
    values = start[...] + (own_part[...].astype(f32) + other_part[...].astype(f32))
    hidden[...] = values
    second[...] = (values * factor_of(values) * gain[1:2, :]).astype(low16)
    group = given.shape[0]
    given[...] = second[pl.ds(pl.multiple_of(info[SEC] * group, group), group), :]


def feed_tiles(refs, second, top, active, grad_lifted, up, down, back, sems):
    tiles = active.shape[0]
    made = Copies(sems)
    for t in range(tiles):
        for m in range(QUARTERS):
            made.start(feed_unit(refs, t // 2, m, t % 2), up.at[t, span(m), :])
        for m in range(QUARTERS):
            made.start(feed_unit(refs, t // 2, m, 2 + t % 2), down.at[t, :, span(m)])
    back[...] = jnp.zeros_like(back)

    @pl.loop(0, tiles)
    def _(t):
        for m in range(QUARTERS):
            pltpu.make_async_copy(
                refs[0].at[0, 0], up.at[t, span(m), :], sems.at[8 * t + m]
            ).wait()
        for m in range(QUARTERS):
            pltpu.make_async_copy(
                refs[0].at[0, 0], down.at[t, :, span(m)], sems.at[8 * t + 4 + m]
            ).wait()
        tile = dot(second[...], up[t])
        cdf = normal_cdf(tile)
        active[t] = (tile * cdf).astype(low16)
        grad = (dot_nt(top[...], down[t]) * gelu_slope(tile, cdf)).astype(low16)
        grad_lifted[t] = grad
        back[...] += dot_nt(grad, up[t])


def local_feed_kernel(second, top, *rest):
    refs, (active, grad_lifted, grad_second, up, down, back, sems) = (
        rest[:FEED_REFS], rest[FEED_REFS:]
    )
    feed_tiles(refs, second, top, active, grad_lifted, up, down, back, sems)
    grad_second[...] = back[...].astype(low16)


def far_feed_kernel(second_same, second_cross, top_same, top_cross, *rest):
    refs = rest[:FEED_REFS]
    (active, grad_lifted, second, top, same, cross, up, down, back, sems) = rest[FEED_REFS:]
    group = same.shape[0]
    second[:group] = second_same[...]
    second[group:] = second_cross[...]
    top[:group] = top_same[...]
    top[group:] = top_cross[...]
    feed_tiles(refs, second, top, active, grad_lifted, up, down, back, sems)
    same[...] = back[:group].astype(low16)
    cross[...] = back[group:].astype(low16)


def pair_kernel(a, b, total):
    total[...] = add16(a[...], b[...])


def with_far(sec, rows, own, other, far_same, far_cross):
    group = far_same.shape[0]
    parts = []
    for u in range(rows // group):
        at = slice(u * group, (u + 1) * group)
        far = jnp.where(sec == u, far_same[...], far_cross[...]).astype(f32)
        parts.append(own[at, :].astype(f32) + other[at, :].astype(f32) + far)
    return jnp.concatenate(parts, axis=0)


def local_attention_back_kernel(info, hidden, own_back, other_back, far_same, far_cross, top, gain,
                                query_keys, values_in, probs, *rest):
    refs = rest[:MIX_REFS]
    (grad_hidden, mid, grad_query_keys, grad_values, grad_first, gain_grad,
     weights, mix, total, sems) = rest[MIX_REFS:]
    made = Copies(sems)
    groups = []
    for k in range(4):
        groups.append(
            [
                made.start(mix_unit(refs, k, m, u), weights.at[k, u, span(m), :])
                for u in range(2)
                for m in range(QUARTERS)
            ]
        )
    upstream = with_far(info[SEC], hidden.shape[0], own_back, other_back, far_same, far_cross)
    through, gain_grad[...] = norm_back(hidden[...], gain[1:2, :], upstream)
    grads = top[...].astype(f32) + through
    grad_hidden[...] = grads
    mid[...] = grads.astype(low16)
    utts = probs.shape[1]
    half = values_in.shape[2]
    group = query_keys.shape[1] // utts
    size = group // 3
    table = head_table(half)
    for k in range(4):
        for copy in groups[k]:
            copy.wait()
        gather_mix(weights, mix, k, half)
        grad_mixed = dot_nt(mid[...], mix[k * half : (k + 1) * half, :]).astype(low16)
        grad_mixed = grad_mixed.astype(f32)
        for u in range(utts):
            at = slice(u * group, (u + 1) * group)
            q = query_keys[k, at, :half].astype(f32)
            key = query_keys[k, at, half:].astype(f32)
            val = values_in[k, at, :].astype(f32)
            grad = grad_mixed[at]
            exact = by_pair(probs[k, u], size)
            grad_probs = by_pair(head_sums(pair_rows(grad, val, size), table), size)
            scored = {}
            for i in range(3):
                center = grad_probs[(i, 0)] * exact[(i, 0)]
                for j in range(1, i + 1):
                    center = center + grad_probs[(i, j)] * exact[(i, j)]
                for j in range(i + 1):
                    score = exact[(i, j)] * (grad_probs[(i, j)] - center)
                    scored[(i, j)] = score.astype(low16).astype(f32)

            def rows_of(array, n):
                return array[n * size : (n + 1) * size]

            for i in range(3):
                begin = u * group + i * size
                to_query = sum(scored[(i, j)] * rows_of(key, j) for j in range(i + 1))
                to_key = sum(scored[(n, i)] * rows_of(q, n) for n in range(i, 3))
                to_value = sum(
                    exact[(n, i)].astype(low16).astype(f32) * rows_of(grad, n)
                    for n in range(i, 3)
                )
                grad_query_keys[k, begin : begin + size, :half] = (to_query * SCALE).astype(low16)
                grad_query_keys[k, begin : begin + size, half:] = (to_key * SCALE).astype(low16)
                grad_values[k, begin : begin + size, :] = to_value.astype(low16)
        back = dot_nt(grad_query_keys[k], weights[k, 0])
        back = back + dot_nt(grad_values[k], weights[k, 1, :, :half])
        total[...] = back if k == 0 else total[...] + back
    grad_first[...] = total[...].astype(low16)


def local_end_kernel(info, own_back, other_back, start, grad_hidden, gain,
                     returned, code_part, gain_grad, values):
    low, sec = info[LOW], info[SEC]
    upstream = own_back[...].astype(f32) + other_back[...].astype(f32)
    through, gain_grad[...] = norm_back(start[...], gain[0:1, :], upstream)
    values[...] = grad_hidden[...] + through
    utts, code_count, frames, _ = code_part.shape
    total = None
    for c in range(code_count):
        begin = pl.multiple_of((sec * code_count + c) * frames, frames)
        part = values[pl.ds(begin, frames), :]
        total = part if total is None else total + part
    returned[...] = total.astype(low16)
    for u in range(utts):
        for c in range(code_count):
            row = (u * code_count + c) * frames
            for j in range(2):
                at = pl.ds(block_at(low, 2 * sec + j), UNIT)
                code_part[u, c, :, span(j)] = values[row : row + frames, at]


def output_kernel(info, hidden, own_part, other_part, far_same, far_cross, output):
    low, sec = info[LOW], info[SEC]
    utts, code_count, frames, _ = output.shape
    group = code_count * frames
    frame_at = lax.broadcasted_iota(jnp.int32, (frames, 1), 0) + info[SHARD] * frames
    for u in range(utts):
        valid = frame_at < info[LENGTHS + u]
        for c in range(code_count):
            rows = slice(u * group + c * frames, u * group + (c + 1) * frames)
            inner = slice(c * frames, (c + 1) * frames)
            for j in range(2):
                at = pl.ds(block_at(low, 2 * sec + j), UNIT)
                far = jnp.where(sec == u, far_same[inner, at], far_cross[inner, at])
                value = hidden[rows, at] + (
                    own_part[rows, at].astype(f32)
                    + other_part[rows, at].astype(f32)
                    + far.astype(f32)
                )
                output[u, c, :, span(j)] = jnp.where(valid, value, 0.0).astype(low16)


SEND_A, KEEP_A, SEND_B, KEEP_B = (1, 3), (0, 2), (2, 3), (0, 1)


def local_drop_kernel(own_active, far_active, *rest):
    refs, (own_branch, same, cross, down, branch, sems) = rest[:FEED_REFS], rest[FEED_REFS:]
    tiles, count, _ = own_active.shape
    made = Copies(sems)
    for t in range(tiles):
        for m in range(QUARTERS):
            made.start(feed_unit(refs, t // 2, m, 2 + t % 2), down.at[t, :, span(m)])
    branch[...] = jnp.zeros_like(branch)

    @pl.loop(0, tiles)
    def _(t):
        for m in range(QUARTERS):
            pltpu.make_async_copy(
                refs[0].at[0, 0], down.at[t, :, span(m)], sems.at[QUARTERS * t + m]
            ).wait()
        branch[:count] += dot(own_active[t], down[t])
        branch[count:] += dot(far_active[t], down[t])

    own_branch[...] = branch[:count].astype(low16)
    group = same.shape[0]
    same[...] = branch[count : count + group].astype(low16)
    cross[...] = branch[count + group :].astype(low16)


def local_feed_grad_kernel(second, far_second, own_lifted, far_lifted, own_active, far_active,
                           top, far_top, send_a, send_b, keep_a, keep_b, turned, tops):
    count = second.shape[0]
    turned[:, :count] = jnp.transpose(second[...])
    turned[:, count:] = jnp.transpose(far_second[...])
    tops[:count] = top[...]
    tops[count:] = far_top[...]
    for k in range(2):
        for part, pairs in enumerate(
            (((send_a, SEND_A), (keep_a, KEEP_A)), ((send_b, SEND_B), (keep_b, KEEP_B)))
        ):
            t = 2 * k + part
            right = jnp.concatenate([own_lifted[t], far_lifted[t]], axis=0)
            left = jnp.concatenate(
                [jnp.transpose(own_active[t]), jnp.transpose(far_active[t])], axis=1
            )
            for target, order in pairs:
                for place, m in enumerate(order):
                    target[place, 2 * k] = dot(turned[span(m), :], right).astype(low16)
                    target[place, 2 * k + 1] = dot(left, tops[:, span(m)]).astype(low16)


def local_mix_kernel(first, grad_query_keys, grad_values, mixed, mid,
                     send_a, send_b, keep_a, keep_b, turned):
    turned[...] = jnp.transpose(first[...])
    half = grad_values.shape[2]
    for k in range(4):
        left = jnp.transpose(mixed[:, k * half : (k + 1) * half])
        for target, order in ((send_a, SEND_A), (keep_a, KEEP_A)):
            for place, m in enumerate(order):
                target[place, k] = dot(turned[span(m), :], grad_query_keys[k]).astype(low16)
        for target, order in ((send_b, SEND_B), (keep_b, KEEP_B)):
            for place, m in enumerate(order):
                value = dot(turned[span(m), :], grad_values[k]).astype(low16)
                out = dot(left, mid[:, span(m)]).astype(low16)
                target[place, k, :, :half] = value
                target[place, k, :half, half:] = out[:, :half]
                target[place, k, half:, half:] = out[:, half:]


def by_order(send_a, send_b, keep_a, keep_b):
    return (
        (0, ((send_a, SEND_A), (keep_a, KEEP_A))),
        (1, ((send_b, SEND_B), (keep_b, KEEP_B))),
    )


def global_feed_grad_kernel(info, second, far_second, grad_lifted, far_lifted, active, far_active,
                            top, far_top, send_a, send_b, keep_a, keep_b, turned, tops):
    sec, count = info[SEC], second.shape[0]
    turned[:, :count] = jnp.transpose(second[...])
    turned[:, count:] = jnp.transpose(far_second[...])
    tops[:count] = top[...]
    tops[count:] = far_top[...]
    wide = active.shape[1] // 2
    for part, pairs in by_order(send_a, send_b, keep_a, keep_b):
        at = pl.ds(pl.multiple_of(sec * wide + part * UNIT, UNIT), UNIT)
        right = jnp.concatenate([grad_lifted[:, at], far_lifted[:, span(part)]], axis=0)
        left = jnp.concatenate(
            [jnp.transpose(active[:, at]), jnp.transpose(far_active[:, span(part)])], axis=1
        )
        for target, order in pairs:
            for place, m in enumerate(order):
                target[place, 0] = dot(turned[span(m), :], right).astype(low16)
                target[place, 1] = dot(left, tops[:, span(m)]).astype(low16)


def global_mix_grad_kernel(info, first, far_first, grads, far_grads, mixed, far_mixed, mid,
                           far_mid, send_a, send_b, keep_a, keep_b, turned, mids):
    sec, count = info[SEC], first.shape[0]
    turned[:, :count] = jnp.transpose(first[...])
    turned[:, count:] = jnp.transpose(far_first[...])
    mids[:count] = mid[...]
    mids[count:] = far_mid[...]
    width = mixed.shape[1] // 2
    at = pl.ds(pl.multiple_of(sec * width, width), width)
    right = [jnp.concatenate([grads[c, :, at], far_grads[c]], axis=0) for c in range(3)]
    left = jnp.concatenate([jnp.transpose(mixed[:, at]), jnp.transpose(far_mixed[...])], axis=1)
    for part, pairs in by_order(send_a, send_b, keep_a, keep_b):
        for target, order in pairs:
            for place, m in enumerate(order):
                rows = turned[span(m), :]
                if part == 0:
                    for c in range(2):
                        target[place, 0, :, c * width : (c + 1) * width] = dot(
                            rows, right[c]
                        ).astype(low16)
                else:
                    target[place, 0, :, :width] = dot(rows, right[2]).astype(low16)
                    out = dot(left, mids[:, span(m)]).astype(low16)
                    target[place, 0, :width, width:] = out[:, :width]
                    target[place, 0, width:, width:] = out[:, width:]


def add16(a, b):
    return (a.astype(f32) + b.astype(f32)).astype(low16)


def far_kernel(keep_a, from_x, keep_b, from_y, far_a, far_b):
    far_a[...] = add16(keep_a[0], from_x[0])
    far_b[...] = add16(keep_b[0], from_y[0])


def sum_kernel(shards, *refs):
    parts, outs = (refs[:3], refs[3:6]), refs[6:]
    for part, (keep, once, twice) in enumerate(parts):
        total = keep[0].astype(f32) + once[0].astype(f32) + twice[...].astype(f32)
        total = total.astype(low16)
        count = total.shape[0] // shards
        at = slice(part * count, (part + 1) * count)
        if shards == 1:
            outs[0][at] = total
        elif shards == 2:
            outs[1][0, at] = total[:count]
            outs[0][0, at] = total[count:]
        else:
            for k in range(4):
                outs[(k + 1) % 2][k // 2, at] = total[k * count : (k + 1) * count]


def far_tensor_kernel(keep, arrived, far):
    far[...] = add16(keep[0], arrived[0])


def pick_kernel(info, *refs):
    *terms, world, given, kept = refs
    sec = info[SEC]
    local = terms[0][0].astype(f32)
    for term in terms[1:]:
        local = local + (term[0] if len(term.shape) == 4 else term[...]).astype(f32)
    local = local.astype(low16)
    other = world[...]
    given[...] = jnp.where(sec == 0, local, other)
    kept[...] = jnp.where(sec == 0, other, local)


def half_at(index, count):
    return pl.BlockSpec(
        (1, count, UNIT, UNIT), lambda i: (index, 0, 0, 0), memory_space=pltpu.VMEM
    )


def quarter_unit(refs, m, index):
    own, x_part, y_part, far_kept, far_arrived = refs
    count = own.shape[0] // 2
    if m < 3:
        return (own, x_part, y_part)[m][index].astype(f32)
    return (far_kept[index] if index < count else far_arrived[index - count]).astype(f32)


def feed_final_kernel(info, *rest):
    refs, (up, down) = rest[:5], rest[5:]
    low, sec = info[LOW], info[SEC]
    wide = up.shape[1] // 2
    count = refs[0].shape[0] // 2
    for m in range(QUARTERS):
        at = pl.ds(block_at(low, m), UNIT)
        for source, half in ((0, sec), (count, 1 - sec)):
            for part in range(2):
                hidden = pl.ds(pl.multiple_of(half * wide + part * UNIT, UNIT), UNIT)
                up[at, hidden] = quarter_unit(refs, m, source + 2 * part)
                down[hidden, at] = quarter_unit(refs, m, source + 2 * part + 1)


def mix_final_kernel(info, *rest):
    refs, (qkv, out) = rest[:5], rest[5:]
    low, sec = info[LOW], info[SEC]
    width = out.shape[0] // 2
    count = refs[0].shape[0] // 2
    for m in range(QUARTERS):
        at = pl.ds(block_at(low, m), UNIT)
        at_left = pl.ds(block_at(low, m), width)
        at_right = pl.ds(pl.multiple_of(block_at(low, m) + width, width), width)
        for source, half in ((0, sec), (count, 1 - sec)):
            lanes = pl.ds(pl.multiple_of(half * width, width), width)
            query_keys = quarter_unit(refs, m, source)
            qkv[0, at, lanes] = query_keys[:, :width]
            qkv[1, at, lanes] = query_keys[:, width:]
            rest_unit = quarter_unit(refs, m, source + 1)
            qkv[2, at, lanes] = rest_unit[:, :width]
            out[lanes, at_left] = rest_unit[:width, width:]
            out[lanes, at_right] = rest_unit[width:, width:]


def sum_rest(value):
    step = QUARTERS
    while step < lax.axis_size("dp"):
        value = add16(value, swap(value, "dp", step))
        step *= 2
    return value


class Sum:
    def __init__(self, order, shards, send_a, send_b, keep_a, keep_b):
        self.order, self.shards = order, shards
        self.keep = (keep_a, keep_b)
        self.count = keep_a.shape[1]
        self.once = (swap(send_a, "dp", 1), swap(send_b, "dp", 2))

    def second(self):
        far = half_at(1, self.count)
        far_a, far_b = self.order.call(
            far_kernel,
            [shape((self.count, UNIT, UNIT), low16)] * 2,
            (self.keep[0], self.once[0], self.keep[1], self.once[1]),
            [far] * 4,
            grid=(1,),
        )
        self.twice = (swap(far_a, "dp", 2), swap(far_b, "dp", 1))

    def third(self):
        count = 2 * self.count // self.shards
        if self.shards == 1:
            outs = [shape((count, UNIT, UNIT), low16)]
        else:
            outs = [shape((self.shards // 2, count, UNIT, UNIT), low16)] * 2
        near = half_at(0, self.count)
        totals = self.order.call(
            functools.partial(sum_kernel, self.shards),
            outs,
            (self.keep[0], self.once[0], self.twice[0], self.keep[1], self.once[1], self.twice[1]),
            [near, near, VM] * 2,
            grid=(1,),
        )
        totals = [sum_rest(total) for total in totals]
        self.count = count
        if self.shards == 1:
            return totals[0]
        self.keep = totals[1]
        if self.shards == 2:
            self.terms = (self.keep, swap(totals[0], "tensor", 2))
        else:
            self.once = swap(totals[0], "tensor", 1)

    def fourth(self):
        far = self.order.call(
            far_tensor_kernel,
            [shape((self.count, UNIT, UNIT), low16)],
            (self.keep, self.once),
            [half_at(1, self.count)] * 2,
            grid=(1,),
        )[0]
        self.terms = (self.keep, self.once, swap(far, "tensor", 2))

    def gathered(self, info, world):
        near = half_at(0, self.count)
        given, kept = self.order.call(
            pick_kernel,
            [shape((self.count, UNIT, UNIT), low16)] * 2,
            (info,) + self.terms + (world,),
            [SM] + [near if term.ndim == 4 else VM for term in self.terms] + [VM],
            grid=(1,),
        )
        units = jnp.concatenate([kept, swap(given, "section", 1)])
        return Gather(units)


class Gather:
    def __init__(self, units):
        self.units = units
        self.count = units.shape[0] // 2
        self.near = (swap(units, "dp", 1), swap(units, "dp", 2))

    def far(self):
        x_part, y_part = self.near
        self.rest = (
            swap(x_part[: self.count], "dp", 2), swap(y_part[self.count :], "dp", 1)
        )
        return (self.units,) + self.near + self.rest


def on_device(codes, lengths, gains, w_qkv, w_out, w_up, w_down, cotangent):
    sec = lax.axis_index("section")
    low = lax.axis_index("dp") % QUARTERS
    z = lax.axis_index("tensor")
    first_core = sec == 0
    utts, frames, code_count, width = codes.shape
    heads_width = w_out.shape[1]
    half = heads_width // 2
    wide = w_up.shape[2]
    rows_g = 4 * frames
    rows_l = utts * code_count * frames
    tiles = wide // UNIT
    info = jnp.concatenate([jnp.stack([low, sec, z]).astype(jnp.int32), lengths])
    order = Order()
    call = order.call

    code_rows = jnp.transpose(codes, (0, 2, 1, 3))
    cot_rows = jnp.transpose(cotangent, (0, 2, 1, 3))
    own_w = (jnp.transpose(w_qkv[0], (1, 0, 2)), w_out[0], w_up[0], w_down[0])

    def sem(count):
        return pltpu.SemaphoreType.DMA((count,))

    def gather(rows):
        gathered = lax.all_gather(rows, "tensor")
        order.tokens = (gathered,)
        return gathered

    def scatter(partial):
        return lax.all_to_all(partial, "tensor", 0, 0)

    other_gain = swap(gains[0], "section", 1)
    own_w, other_gain = lax.optimization_barrier((own_w, other_gain))

    def with_other(weights):
        return tuple(w for own in weights for w in (own, swap(own, "section", 1)))

    attention_w = with_other(own_w[:2])

    first_rows, start_g, gain_g, gain_l = call(
        start_kernel,
        [
            shape((frames, width), low16),
            shape((frames, width), f32),
            shape((2, width), f32),
            shape((2, width), f32),
        ],
        (info, code_rows, gains[0], other_gain),
        [SM, VM, VM, VM],
        us=2,
    )
    first_blocks = gather(first_rows)

    mix_piece, mix_whole = call(
        mix_piece_kernel,
        [shape((2, UNIT, UNIT), low16), shape((QUARTERS, 2, UNIT, UNIT), low16)],
        (info,) + attention_w,
        [SM] + [ANY] * 4,
        [sem(5 * QUARTERS)],
        us=3.2,
    )
    mix_z1 = swap(mix_piece, "tensor", 1)
    mix_z2 = swap(mix_piece, "tensor", 2)
    feed_w = with_other(order.after(own_w[2:]))

    first_g, packed_g, probs_g, mixed_g, mixed_given, partial = call(
        global_attention_kernel,
        [
            shape((rows_g, width), low16),
            shape((3, rows_g, heads_width), low16),
            shape((heads_width // HEAD_DIM, rows_g, rows_g), f32),
            shape((rows_g, heads_width), low16),
            shape((rows_g, half), low16),
            shape((4, frames, width), low16),
        ],
        (info, first_blocks) + attention_w,
        [SM, VM] + [ANY] * 4,
        [
            pltpu.VMEM((3, width, heads_width), low16),
            pltpu.VMEM((heads_width, width), low16),
            sem(8),
        ],
        us=5.7,
    )
    partial, mix_z1, mix_z2 = lax.optimization_barrier((partial, mix_z1, mix_z2))
    arrived = scatter(partial)
    mix_z3 = swap(order.after(mix_z2), "tensor", 1)
    top_l, top_given = call(
        local_top_kernel,
        [shape((rows_l, width), low16), shape((rows_l // utts, width), low16)],
        (info, cot_rows),
        [SM, VM],
        us=2.3,
    )
    mix_near = jnp.stack(order.after([mix_z1, mix_z2]))
    mix_x = swap(mix_near, "dp", 1)
    mix_y = swap(mix_near, "dp", 2)
    feed_piece, feed_whole = call(
        feed_piece_kernel,
        [shape((4, UNIT, UNIT), low16), shape((QUARTERS, 4, UNIT, UNIT), low16)],
        (info,) + feed_w,
        [SM] + [ANY] * 4,
        [sem(4 * QUARTERS)],
        us=4,
    )
    feed_z2 = swap(feed_piece, "tensor", 2)
    top_same = swap(order.after(top_given), "tensor", 1)
    hidden_g, second_rows = call(
        middle_kernel,
        [shape((frames, width), f32), shape((frames, width), low16)],
        (start_g, arrived, gain_g),
        [VM] * 3,
        us=2,
    )
    mix_z3 = order.after(mix_z3)
    mix_x3 = swap(mix_z3, "dp", 1)
    mix_y3 = swap(mix_z3, "dp", 2)
    second_blocks = gather(second_rows)
    order.until(feed_z2, mix_x, mix_y, mix_x3, mix_y3, top_same)
    feed_z2, mix_x, mix_y, mix_x3, mix_y3 = order.after((feed_z2, mix_x, mix_y, mix_x3, mix_y3))
    mix_w = (
        mix_whole,
        mix_z1,
        mix_z2,
        mix_z3,
        mix_x,
        mix_y,
        swap(mix_x[:, 0], "dp", 2),
        swap(mix_y[:, 1], "dp", 1),
        mix_x3,
        mix_y3,
        swap(mix_x3[:1], "dp", 2),
        swap(mix_y3[1:], "dp", 1),
    )
    feed_x = swap(feed_z2, "dp", 1)
    feed_y = swap(feed_z2, "dp", 2)
    second_g, lifted_g, active_g, active_given, partial = call(
        global_feed_kernel,
        [
            shape((rows_g, width), low16),
            shape((rows_g, wide), f32),
            shape((rows_g, wide), low16),
            shape((rows_g, wide // 2), low16),
            shape((4, frames, width), low16),
        ],
        (info, second_blocks) + feed_w,
        [SM, VM] + [ANY] * 4,
        [
            pltpu.VMEM((width, wide), low16),
            pltpu.VMEM((wide, width), low16),
            pltpu.VMEM((rows_g, width), f32),
            sem(8),
        ],
        us=5.6,
    )
    arrived = scatter(partial)
    order.until(feed_x, feed_y, mix_w[6], mix_w[7], mix_w[10], mix_w[11])
    sent = call(
        sent_kernel,
        [shape((frames, width), low16)],
        (hidden_g, arrived),
        [VM] * 2,
        us=1.9,
    )[0]
    other_sent = swap(sent, "section", 1)
    feed_l = (
        feed_whole,
        feed_z2,
        feed_x,
        feed_y,
        swap(feed_x[:2], "dp", 2),
        swap(feed_y[2:], "dp", 1),
    )

    order.until(*feed_l)

    start_l, first_l, query_keys, values_l, probs_l, mixed_l, partial = call(
        local_attention_kernel,
        [
            shape((rows_l, width), f32),
            shape((rows_l, width), low16),
            shape((4, rows_l, 2 * half), low16),
            shape((4, rows_l, half), low16),
            shape((4, utts, 2 * rows_l // utts, half), f32),
            shape((rows_l, 4 * half), low16),
            shape((rows_l, width), low16),
        ],
        (info, code_rows, sent, other_sent, gain_l) + mix_w,
        [SM] + [VM] * 4 + [ANY] * MIX_REFS,
        [
            pltpu.VMEM((4, 2, width, UNIT), low16),
            pltpu.VMEM((4 * half, width), low16),
            sem(32),
        ],
        us=9,
    )
    hidden_l, second_l, second_given = call(
        local_norm_kernel,
        [
            shape((rows_l, width), f32),
            shape((rows_l, width), low16),
            shape((rows_l // utts, width), low16),
        ],
        (info, start_l, partial, swap(partial, "section", 1), gain_l),
        [SM] + [VM] * 4,
        us=3.7,
    )
    second_same = swap(second_given, "tensor", 1)
    top_cross = swap(order.after(top_same), "section", 1)
    feed_scratch = [
        pltpu.VMEM((tiles, width, UNIT), low16),
        pltpu.VMEM((tiles, UNIT, width), low16),
        pltpu.VMEM((rows_l, width), f32),
        sem(8 * tiles),
    ]
    wide_rows = shape((rows_l, width), low16)
    half_rows = shape((rows_l // utts, width), low16)
    tiled_rows = shape((tiles, rows_l, UNIT), low16)
    active_l, grad_lifted_l, back = call(
        local_feed_kernel,
        [tiled_rows, tiled_rows, wide_rows],
        (second_l, top_l) + feed_l,
        [VM] * 2 + [ANY] * FEED_REFS,
        feed_scratch,
        us=7.9,
    )
    other_back = swap(back, "section", 1)
    second_same = order.after(second_same)
    second_cross = swap(second_same, "section", 1)
    far_active, far_lifted, far_second, far_top, same, cross = call(
        far_feed_kernel,
        [tiled_rows, tiled_rows, wide_rows, wide_rows, half_rows, half_rows],
        (second_same, second_cross, top_same, top_cross) + feed_l,
        [VM] * 4 + [ANY] * FEED_REFS,
        feed_scratch,
        us=8.2,
    )

    def from_neighbour(same, cross):
        total = call(
            pair_kernel, [half_rows], (same, cross), [VM] * 2
        )[0]
        return swap(total, "tensor", 1)

    far_same = from_neighbour(same, swap(cross, "section", 1))
    turned_l = pltpu.VMEM((width, rows_l), low16)
    local_feed = Sum(
        order,
        2,
        *call(
            local_feed_grad_kernel,
            [shape((2, 4, UNIT, UNIT), low16)] * 4,
            (
                second_l, far_second, grad_lifted_l, far_lifted, active_l, far_active, top_l,
                far_top,
            ),
            [VM] * 8,
            [pltpu.VMEM((width, 2 * rows_l), low16), pltpu.VMEM((2 * rows_l, width), low16)],
            us=7.6,
        ),
    )
    far_same = order.after(far_same)
    far_back = (far_same, swap(far_same, "section", 1))
    far_first, far_mixed, far_second_g, far_active_g = (
        swap(order.after(value), "section", 1)
        for value in (first_g, mixed_given, second_g, active_given)
    )
    grad_hidden_l, mid_l, grad_query_keys, grad_values, back, gain2_l = call(
        local_attention_back_kernel,
        [
            shape((rows_l, width), f32),
            shape((rows_l, width), low16),
            shape((4, rows_l, 2 * half), low16),
            shape((4, rows_l, half), low16),
            shape((rows_l, width), low16),
            shape((1, width), f32),
        ],
        (info, hidden_l, back, other_back)
        + far_back
        + (top_l, gain_l, query_keys, values_l, probs_l)
        + mix_w,
        [SM] + [VM] * 10 + [ANY] * MIX_REFS,
        [
            pltpu.VMEM((4, 2, width, UNIT), low16),
            pltpu.VMEM((4 * half, width), low16),
            pltpu.VMEM((rows_l, width), f32),
            sem(32),
        ],
        us=11.4,
    )
    other_back = swap(back, "section", 1)
    local_mix = Sum(
        order,
        4,
        *call(
            local_mix_kernel,
            [shape((2, 4, UNIT, UNIT), low16)] * 4,
            (first_l, grad_query_keys, grad_values, mixed_l, mid_l),
            [VM] * 5,
            [turned_l],
            us=6,
        ),
    )
    returned, code_part, gain1_l = call(
        local_end_kernel,
        [
            shape((frames, width), low16),
            shape((utts, code_count, frames, width // 2), f32),
            shape((1, width), f32),
        ],
        (info, back, other_back, start_l, grad_hidden_l, gain_l),
        [SM] + [VM] * 5,
        [pltpu.VMEM((rows_l, width), f32)],
        us=4.4,
    )

    top_blocks = gather(returned)
    local_feed.second()
    order.until(*local_mix.once, far_first, far_mixed, far_second_g, far_active_g)
    top_g, grad_lifted_g, lifted_given, partial = call(
        global_feed_back_kernel,
        [
            shape((rows_g, width), low16),
            shape((rows_g, wide), low16),
            shape((rows_g, wide // 2), low16),
            shape((4, frames, width), low16),
        ],
        (info, top_blocks, lifted_g) + feed_w,
        [SM] + [VM] * 2 + [ANY] * 4,
        [
            pltpu.VMEM((width, wide), low16),
            pltpu.VMEM((wide, width), low16),
            pltpu.VMEM((rows_g, width), f32),
            sem(8),
        ],
        us=6.3,
    )
    arrived = scatter(partial)
    far_top_g, far_lifted_g = swap(top_g, "section", 1), swap(lifted_given, "section", 1)
    local_feed.third()
    local_mix.second()
    global_feed = Sum(
        order,
        1,
        *call(
            global_feed_grad_kernel,
            [shape((2, 2, UNIT, UNIT), low16)] * 4,
            (
                info, second_g, far_second_g, grad_lifted_g, far_lifted_g, active_g, far_active_g,
                top_g, far_top_g,
            ),
            [SM] + [VM] * 8,
            [pltpu.VMEM((width, 2 * rows_g), low16), pltpu.VMEM((2 * rows_g, width), low16)],
            us=3.5,
        ),
    )
    grad_hidden_g, mid_rows, gain2_g = call(
        middle_back_kernel,
        [shape((frames, width), f32), shape((frames, width), low16), shape((1, width), f32)],
        (arrived, hidden_g, gain_g, returned),
        [VM] * 4,
        us=2.1,
    )
    mid_blocks = gather(mid_rows)
    order.until(*local_mix.twice)
    mid_g, grads_g, grads_given, partial = call(
        global_attention_back_kernel,
        [
            shape((rows_g, width), low16),
            shape((3, rows_g, heads_width), low16),
            shape((3, rows_g, half), low16),
            shape((4, frames, width), low16),
        ],
        (info, mid_blocks, packed_g, probs_g) + attention_w,
        [SM] + [VM] * 3 + [ANY] * 4,
        [
            pltpu.VMEM((3, width, heads_width), low16),
            pltpu.VMEM((heads_width, width), low16),
            sem(8),
        ],
        us=6.8,
    )
    arrived = scatter(partial)
    far_mid_g, far_grads_g = swap(mid_g, "section", 1), swap(grads_given, "section", 1)
    global_feed.second()
    local_mix.third()
    global_mix = Sum(
        order,
        1,
        *call(
            global_mix_grad_kernel,
            [shape((2, 1, UNIT, UNIT), low16)] * 4,
            (
                info, first_g, far_first, grads_g, far_grads_g, mixed_g, far_mixed, mid_g,
                far_mid_g,
            ),
            [SM] + [VM] * 8,
            [pltpu.VMEM((width, 2 * rows_g), low16), pltpu.VMEM((2 * rows_g, width), low16)],
            us=3,
        ),
    )
    kept_start, given_start, gain1_g = call(
        start_back_kernel,
        [
            shape((frames, width // 2), f32),
            shape((frames, width // 2), f32),
            shape((1, width), f32),
        ],
        (info, arrived, start_g, gain_g, grad_hidden_g),
        [SM] + [VM] * 4,
        [pltpu.VMEM((frames, width), f32)],
        us=2.1,
    )
    world_feed = global_feed.third()
    global_mix.second()
    local_mix.fourth()
    world_mix = global_mix.third()
    feed_sum = local_feed.gathered(info, world_feed)
    own_branch, same, cross = call(
        local_drop_kernel,
        [wide_rows, half_rows, half_rows],
        (active_l, far_active) + feed_l,
        [VM] * 2 + [ANY] * FEED_REFS,
        [
            pltpu.VMEM((tiles, UNIT, width), low16),
            pltpu.VMEM((2 * rows_l, width), f32),
            sem(QUARTERS * tiles),
        ],
        us=6.1,
    )
    other_branch = swap(own_branch, "section", 1)
    branch_cross = swap(cross, "section", 1)
    arrived_start = swap(given_start, "section", 1)
    both_start = jnp.stack(
        [
            jnp.where(first_core, kept_start, arrived_start),
            jnp.where(first_core, arrived_start, kept_start),
        ]
    )
    code_grad = jnp.transpose(code_part + both_start[:, None], (0, 2, 1, 3))

    own_gain = jnp.concatenate([gain1_g, gain2_g], axis=0)
    total_gain = own_gain + swap(own_gain, "section", 1)
    local_gain = jnp.concatenate([gain1_l, gain2_l], axis=0)
    gain_total = jnp.where(first_core, total_gain, local_gain)
    gain_total = jnp.concatenate(
        [
            lax.dynamic_slice_in_dim(gain_total, (low ^ m) * UNIT, UNIT, 1)
            for m in range(QUARTERS)
        ],
        axis=1,
    )
    def over(value, axis):
        copies = jnp.broadcast_to(value, (lax.axis_size(axis),) + value.shape)
        return jnp.sum(lax.all_to_all(order.after(copies), axis, 0, 0), axis=0)

    mix_sum = local_mix.gathered(info, world_mix)
    far_branch = from_neighbour(same, branch_cross)
    gain_total = over(gain_total, "tensor")
    order.until(gain_total, *feed_sum.near)
    feed_parts = feed_sum.far()
    far_branch = (far_branch, swap(far_branch, "section", 1))
    output = call(
        output_kernel,
        [shape((utts, code_count, frames, width // 2), low16)],
        (info, hidden_l, own_branch, other_branch) + far_branch,
        [SM] + [VM] * 5,
        us=3.1,
    )[0]
    mix_parts = mix_sum.far()
    gain_total = over(gain_total, "dp")
    order.until(gain_total)
    up_grad, down_grad = call(
        feed_final_kernel,
        [shape((width, wide), f32), shape((wide, width), f32)],
        (info,) + feed_parts,
        [SM] + [VM] * 5,
        us=6.8,
    )
    qkv_grad, out_grad = call(
        mix_final_kernel,
        [shape((3, width, heads_width), f32), shape((heads_width, width), f32)],
        (info,) + mix_parts,
        [SM] + [VM] * 5,
        us=4.5,
    )
    return (
        jnp.transpose(output, (0, 2, 1, 3)),
        code_grad,
        gain_total[None],
        jnp.transpose(qkv_grad, (1, 0, 2))[None],
        out_grad[None],
        up_grad[None],
        down_grad[None],
    )


def solution(mesh):
    in_specs = (
        P("dp", "tensor", None, None),
        P("dp"),
        P("section", None, None),
        P("section", None, None, "tensor"),
        P("section", "tensor", None),
        P("section", None, "tensor"),
        P("section", "tensor", None),
        P("dp", "tensor", None, None),
    )
    out_specs = (
        P("dp", "tensor", None, "section"),
        P("dp", "tensor", None, "section"),
        P("section", None, None),
        P("section", None, None, "tensor"),
        P("section", "tensor", None),
        P("section", None, "tensor"),
        P("section", "tensor", None),
    )
    return jax.shard_map(
        on_device, mesh=mesh, in_specs=in_specs, out_specs=out_specs, check_vma=False
    )
```

```python
import functools

import jax
import jax.numpy as jnp
from jax import lax
from jax.experimental import pallas as pl
from jax.experimental.pallas import tpu as pltpu
from jax.sharding import PartitionSpec as P

HEAD_DIM = 64
SCALE = HEAD_DIM ** (-0.5)
QUARTERS = 4
UNIT = 256
epsilon = 1e-06
negative = -1e30
f32 = jnp.float32
low16 = jnp.bfloat16

VM = pl.BlockSpec(memory_space=pltpu.VMEM)
SM = pl.BlockSpec(memory_space=pltpu.SMEM)
ANY = pl.BlockSpec(memory_space=pltpu.HBM)
MIB = 1 << 20
PACE = 2 * 10**8

LOW, SEC, SHARD, LENGTHS = 0, 1, 2, 3


def shape(dims, dtype):
    return jax.ShapeDtypeStruct(tuple(dims), dtype)


class Order:
    def __init__(self):
        self.tokens = ()

    def after(self, value):
        if not self.tokens:
            return value
        return lax.optimization_barrier((value,) + self.tokens)[0]

    def until(self, *values):
        self.tokens += values

    def call(self, body, outs, args, specs, scratch=(), limit=28, us=2.0, grid=()):
        args = (self.after(args[0]),) + tuple(args[1:])
        results = pl.pallas_call(
            body,
            out_shape=tuple(outs),
            grid=grid,
            in_specs=list(specs),
            out_specs=tuple(VM for _ in outs),
            scratch_shapes=list(scratch),
            compiler_params=pltpu.CompilerParams(vmem_limit_bytes=limit * MIB),
            cost_estimate=pl.CostEstimate(
                flops=int(us * PACE), bytes_accessed=0, transcendentals=0
            ),
        )(*args)
        self.tokens = (results[-1],)
        return results


def swap(value, axis, flip):
    count = lax.axis_size(axis)
    return lax.ppermute(value, axis, [(i, i ^ flip) for i in range(count)])


def dot(a, b):
    return jnp.dot(a, b, preferred_element_type=f32)


def dot_tn(a, b):
    return lax.dot_general(a, b, (((0,), (0,)), ((), ())), preferred_element_type=f32)


def dot_nt(a, b):
    return lax.dot_general(a, b, (((1,), (1,)), ((), ())), preferred_element_type=f32)


def factor_of(values):
    return lax.rsqrt(jnp.mean(values * values, axis=-1, keepdims=True) + epsilon)


def norm_back(values, gain, upstream):
    factor = factor_of(values)
    weighted = upstream * gain
    inner = jnp.mean(weighted * values, axis=-1, keepdims=True)
    through = factor * weighted - values * (factor * factor * factor) * inner
    return through, jnp.sum(upstream * values * factor, axis=0, keepdims=True)


def normal_cdf(values):
    return 0.5 * (1.0 + lax.erf(values * (0.5**0.5)))


def gelu_slope(values, cdf):
    return cdf + values * (jnp.exp(-0.5 * values * values) * 0.3989422804014327)


def block_at(low, m):
    return pl.multiple_of((low ^ m) * UNIT, UNIT)


def span(m):
    return slice(m * UNIT, (m + 1) * UNIT)


class Copies:
    def __init__(self, sems):
        self.sems = sems
        self.made = []

    def start(self, src, dst):
        copy = pltpu.make_async_copy(src, dst, self.sems.at[len(self.made)])
        copy.start()
        self.made.append(copy)
        return copy

    def pick(self, own_first, sec, own, other, dst):
        sem = self.sems.at[len(self.made)]

        @pl.when((sec == 0) == own_first)
        def _():
            pltpu.make_async_copy(own, dst, sem).start()

        @pl.when((sec == 0) != own_first)
        def _():
            pltpu.make_async_copy(other, dst, sem).start()

        copy = pltpu.make_async_copy(own, dst, sem)
        self.made.append(copy)
        return copy

    def wait(self, begin=0, end=None):
        for copy in self.made[begin:end]:
            copy.wait()


def start_kernel(info, codes, own_gain, other_gain, first, start, gain_g, gain_l):
    low, sec = info[LOW], info[SEC]
    for m in range(QUARTERS):
        at = pl.ds(block_at(low, m), UNIT)
        own, other = own_gain[:, at], other_gain[:, at]
        gain_g[:, span(m)] = jnp.where(sec == 0, own, other)
        gain_l[:, span(m)] = jnp.where(sec == 0, other, own)
        total = codes[sec, 0, :, at].astype(f32)
        for c in range(1, codes.shape[1]):
            total = total + codes[sec, c, :, at].astype(f32)
        start[:, span(m)] = total
    values = start[...]
    first[...] = (values * factor_of(values) * gain_g[0:1, :]).astype(low16)


def from_local(sec, own, other, branch):
    @pl.when(sec == 0)
    def _():
        branch(0, *other)

    @pl.when(sec != 0)
    def _():
        branch(1, *own)


def mix_piece_kernel(info, own_qkv, other_qkv, own_out, other_out, piece, whole, sems):
    low, sec = info[LOW], info[SEC]
    half = own_qkv.shape[2] // 2

    def branch(half_index, qkv, out):
        made = Copies(sems)
        for m in range(QUARTERS):
            at = pl.ds(block_at(low, m), UNIT)
            at_right = pl.ds(pl.multiple_of(block_at(low, m) + half, half), half)
            at_left = pl.ds(block_at(low, m), half)
            lanes = slice(half_index * half, (half_index + 1) * half)
            target = whole.at[m]
            made.start(qkv.at[0, at, lanes], target.at[0, :, 0:half])
            made.start(qkv.at[1, at, lanes], target.at[0, :, half : 2 * half])
            made.start(qkv.at[2, at, lanes], target.at[1, :, 0:half])
            made.start(out.at[lanes, at_left], target.at[1, 0:half, half : 2 * half])
            made.start(out.at[lanes, at_right], target.at[1, half : 2 * half, half : 2 * half])
        made.wait()

    from_local(sec, (own_qkv, own_out), (other_qkv, other_out), branch)
    piece[...] = whole[0]


def feed_piece_kernel(info, own_up, other_up, own_down, other_down, piece, whole, sems):
    low, sec = info[LOW], info[SEC]
    wide = own_up.shape[1] // 2

    def branch(half_index, up, down):
        made = Copies(sems)
        for m in range(QUARTERS):
            at = pl.ds(block_at(low, m), UNIT)
            for part in range(2):
                begin = half_index * wide + part * UNIT
                hidden = slice(begin, begin + UNIT)
                made.start(up.at[at, hidden], whole.at[m, part])
                made.start(down.at[hidden, at], whole.at[m, 2 + part])
        made.wait()

    from_local(sec, (own_up, own_down), (other_up, other_down), branch)
    piece[...] = whole[0]


def fetch_attention(made, low, sec, own_qkv, other_qkv, own_out, other_out, qkv, out):
    for m in range(QUARTERS):
        at = pl.ds(block_at(low, m), UNIT)
        made.pick(True, sec, own_qkv.at[:, at, :], other_qkv.at[:, at, :], qkv.at[:, span(m), :])
    for m in range(QUARTERS):
        at = pl.ds(block_at(low, m), UNIT)
        made.pick(True, sec, own_out.at[:, at], other_out.at[:, at], out.at[:, span(m)])


def by_shard(info, blocks):
    count = blocks.shape[0]
    return jnp.concatenate([blocks[info[SHARD] ^ k] for k in range(count)], axis=0)


def other_half(info, width):
    half = width // 2
    return pl.ds(pl.multiple_of((1 - info[SEC]) * half, half), half)


def spread_blocks(info, target, values):
    frames = target.shape[1]
    for k in range(target.shape[0]):
        target[info[SHARD] ^ k] = values[k * frames : (k + 1) * frames].astype(low16)


def row_places(info, count, frames, dimension):
    at = lax.broadcasted_iota(jnp.int32, (count, count), dimension)
    return (lax.div(at, frames) ^ info[SHARD]) * frames + lax.rem(at, frames)


def global_attention_kernel(info, *rest):
    (blocks, own_qkv, other_qkv, own_out, other_out,
     rows, packed, probs, mixed, given, partial, qkv, out, sems) = rest
    low, sec = info[LOW], info[SEC]
    made = Copies(sems)
    fetch_attention(made, low, sec, own_qkv, other_qkv, own_out, other_out, qkv, out)
    count, frames = rows.shape[0], blocks.shape[1]
    length = info[LENGTHS + sec]
    query_at = row_places(info, count, frames, 0)
    key_at = row_places(info, count, frames, 1)
    allowed = (key_at <= query_at) & (key_at < length)
    values = by_shard(info, blocks)
    rows[...] = values
    made.wait(0, QUARTERS)
    for c in range(3):
        packed[c] = dot(values, qkv[c]).astype(low16)
    heads = []
    for h in range(packed.shape[2] // HEAD_DIM):
        lanes = slice(h * HEAD_DIM, (h + 1) * HEAD_DIM)
        scores = dot_nt(packed[0, :, lanes], packed[1, :, lanes]) * SCALE
        scores = jnp.where(allowed, scores, negative)
        raised = jnp.exp(scores - jnp.max(scores, axis=-1, keepdims=True))
        exact = raised / jnp.sum(raised, axis=-1, keepdims=True)
        probs[h] = exact.astype(low16)
        heads.append(dot(exact.astype(low16), packed[2, :, lanes]).astype(low16))
    mixed[...] = jnp.concatenate(heads, axis=1)
    given[...] = mixed[:, other_half(info, mixed.shape[1])]
    made.wait(QUARTERS)
    spread_blocks(info, partial, dot(mixed[...], out[...]))


def total_of(arrived):
    total = arrived[0].astype(f32)
    for k in range(1, arrived.shape[0]):
        total = total + arrived[k].astype(f32)
    return total


def middle_kernel(start, arrived, gain, hidden, second):
    values = start[...] + total_of(arrived)
    hidden[...] = values
    second[...] = (values * factor_of(values) * gain[1:2, :]).astype(low16)


def fetch_feed(made, low, sec, own_up, other_up, own_down, other_down, up, down):
    for m in range(QUARTERS):
        at = pl.ds(block_at(low, m), UNIT)
        made.pick(True, sec, own_up.at[at, :], other_up.at[at, :], up.at[span(m), :])
    for m in range(QUARTERS):
        at = pl.ds(block_at(low, m), UNIT)
        made.pick(True, sec, own_down.at[:, at], other_down.at[:, at], down.at[:, span(m)])


def global_feed_kernel(info, *rest):
    (blocks, own_up, other_up, own_down, other_down,
     rows, lifted, active, given, partial, up, down, total, sems) = rest
    made = Copies(sems)
    fetch_feed(made, info[LOW], info[SEC], own_up, other_up, own_down, other_down, up, down)
    values = by_shard(info, blocks)
    rows[...] = values
    made.wait(0, QUARTERS)
    for t in range(up.shape[1] // UNIT):
        tile = dot(values, up[:, span(t)])
        lifted[:, span(t)] = tile
        low_tile = (tile * normal_cdf(tile)).astype(low16)
        active[:, span(t)] = low_tile
        if t == 0:
            made.wait(QUARTERS)
        branch = dot(low_tile, down[span(t), :])
        total[...] = branch if t == 0 else total[...] + branch
    spread_blocks(info, partial, total[...])
    given[...] = active[:, other_half(info, active.shape[1])]


def sent_kernel(hidden, arrived, sent):
    sent[...] = (hidden[...] + total_of(arrived)).astype(low16)


def global_feed_back_kernel(info, *rest):
    (blocks, lifted, own_up, other_up, own_down, other_down,
     rows, grad_lifted, given, partial, up, down, total, sems) = rest
    made = Copies(sems)
    fetch_feed(made, info[LOW], info[SEC], own_up, other_up, own_down, other_down, up, down)
    values = by_shard(info, blocks)
    rows[...] = values
    made.wait(QUARTERS)
    for t in range(up.shape[1] // UNIT):
        tile = lifted[:, span(t)]
        grad = dot_nt(values, down[span(t), :]) * gelu_slope(tile, normal_cdf(tile))
        grad = grad.astype(low16)
        grad_lifted[:, span(t)] = grad
        if t == 0:
            made.wait(0, QUARTERS)
        back = dot_nt(grad, up[:, span(t)])
        total[...] = back if t == 0 else total[...] + back
    spread_blocks(info, partial, total[...])
    given[...] = grad_lifted[:, other_half(info, grad_lifted.shape[1])]


def middle_back_kernel(arrived, hidden, gain, returned, grad_hidden, mid, gain_grad):
    through, gain_grad[...] = norm_back(hidden[...], gain[1:2, :], total_of(arrived))
    values = returned[...].astype(f32) + through
    grad_hidden[...] = values
    mid[...] = values.astype(low16)


def global_attention_back_kernel(info, *rest):
    (blocks, packed, probs, own_qkv, other_qkv, own_out, other_out,
     rows, grads, given, partial, qkv, out, sems) = rest
    low, sec = info[LOW], info[SEC]
    made = Copies(sems)
    fetch_attention(made, low, sec, own_qkv, other_qkv, own_out, other_out, qkv, out)
    values = by_shard(info, blocks)
    rows[...] = values
    made.wait(QUARTERS)
    grad_mixed = dot_nt(values, out[...]).astype(low16)
    columns = [[], [], []]
    for h in range(packed.shape[2] // HEAD_DIM):
        lanes = slice(h * HEAD_DIM, (h + 1) * HEAD_DIM)
        exact = probs[h].astype(f32)
        grad = grad_mixed[:, lanes]
        columns[2].append(dot_tn(exact.astype(low16), grad).astype(low16))
        grad_probs = dot_nt(grad, packed[2, :, lanes])
        center = jnp.sum(grad_probs * exact, axis=-1, keepdims=True)
        grad_scores = (exact * (grad_probs - center)).astype(low16)
        columns[0].append((dot(grad_scores, packed[1, :, lanes]) * SCALE).astype(low16))
        columns[1].append((dot_tn(grad_scores, packed[0, :, lanes]) * SCALE).astype(low16))
    total = None
    made.wait(0, QUARTERS)
    for c in range(3):
        grads[c] = jnp.concatenate(columns[c], axis=1)
        back = dot_nt(grads[c], qkv[c])
        total = back if c == 0 else total + back
    spread_blocks(info, partial, total)
    given[...] = grads[:, :, other_half(info, grads.shape[2])]


def start_back_kernel(info, arrived, start, gain, grad_hidden, kept, given, gain_grad, values):
    low, sec = info[LOW], info[SEC]
    through, gain_grad[...] = norm_back(start[...], gain[0:1, :], total_of(arrived))
    values[...] = grad_hidden[...] + through
    for j in range(2):
        kept[:, span(j)] = values[:, pl.ds(block_at(low, 2 * sec + j), UNIT)]
        given[:, span(j)] = values[:, pl.ds(block_at(low, 2 * (1 - sec) + j), UNIT)]


def mix_unit(refs, k, m, u):
    whole, near = refs[0], refs[1:4]
    both = refs[4:8]
    last = refs[8:12]
    if k == 0:
        return whole.at[m, u]
    if m == 0:
        return near[k - 1].at[u]
    if k == 3:
        return last[m - 1].at[u] if m < 3 else last[2 + u].at[0]
    return both[m - 1].at[k - 1, u] if m < 3 else both[2 + u].at[k - 1]


def feed_unit(refs, k, m, u):
    if k == 0:
        return refs[0].at[m, u]
    if m < 3:
        return refs[1 + m].at[u]
    return refs[4].at[u] if u < 2 else refs[5].at[u - 2]


MIX_REFS, FEED_REFS = 12, 6


def pair_rows(a, b, size):
    return jnp.concatenate([a * b, a[size:] * b[: 2 * size], a[2 * size :] * b[:size]], axis=0)


def by_pair(stacked, size):
    names = [(0, 0), (1, 1), (2, 2), (1, 0), (2, 1), (2, 0)]
    return {name: stacked[n * size : (n + 1) * size] for n, name in enumerate(names)}


def from_pairs(pairs):
    names = [(0, 0), (1, 1), (2, 2), (1, 0), (2, 1), (2, 0)]
    return jnp.concatenate([pairs[name] for name in names], axis=0)


def head_sums(products, table):
    upper = products.astype(low16)
    lower = (products - upper.astype(f32)).astype(low16)
    return dot(upper, table) + dot(lower, table)


def head_table(width):
    row = lax.broadcasted_iota(jnp.int32, (width, width), 0) // HEAD_DIM
    column = lax.broadcasted_iota(jnp.int32, (width, width), 1) // HEAD_DIM
    return (row == column).astype(f32).astype(low16)


def gather_mix(weights, mix, k, half):
    for m in range(QUARTERS):
        begin = m * UNIT
        mix[k * half : (k + 1) * half, begin : begin + half] = weights[
            k, 1, begin : begin + half, half:
        ]
        mix[k * half : (k + 1) * half, begin + half : begin + UNIT] = weights[
            k, 1, begin + half : begin + UNIT, half:
        ]


def local_attention_kernel(info, codes, sent_own, sent_other, gain, *rest):
    refs, (start, first, query_keys, values_out, probs, mixed, partial, weights, mix, sems) = (
        rest[:MIX_REFS], rest[MIX_REFS:]
    )
    low, sec = info[LOW], info[SEC]
    made = Copies(sems)
    groups = []
    for k in range(4):
        groups.append(
            [
                made.start(mix_unit(refs, k, m, u), weights.at[k, u, span(m), :])
                for u in range(2)
                for m in range(QUARTERS)
            ]
        )
    utts, code_count, frames, _ = codes.shape
    for u in range(utts):
        sent = jnp.where(sec == u, sent_own[...], sent_other[...]).astype(f32)
        for c in range(code_count):
            row = (u * code_count + c) * frames
            for m in range(QUARTERS):
                code = codes[u, c, :, pl.ds(block_at(low, m), UNIT)].astype(f32)
                start[row : row + frames, span(m)] = sent[:, span(m)] + code
    values = start[...]
    first[...] = (values * factor_of(values) * gain[0:1, :]).astype(low16)
    half = values_out.shape[2]
    table = head_table(half)
    rows = first[...]
    size = frames
    group = code_count * frames
    for k in range(4):
        for copy in groups[k]:
            copy.wait()
        query_keys[k] = dot(rows, weights[k, 0]).astype(low16)
        values_out[k] = dot(rows, weights[k, 1, :, :half]).astype(low16)
        gather_mix(weights, mix, k, half)
        for u in range(utts):
            at = slice(u * group, (u + 1) * group)
            q = query_keys[k, at, :half].astype(f32)
            key = query_keys[k, at, half:].astype(f32)
            val = values_out[k, at, :].astype(f32)
            scores = by_pair(head_sums(pair_rows(q, key, size), table) * SCALE, size)
            exact = {}
            for i in range(3):
                peak = scores[(i, 0)]
                for j in range(1, i + 1):
                    peak = jnp.maximum(peak, scores[(i, j)])
                raised = [jnp.exp(scores[(i, j)] - peak) for j in range(i + 1)]
                whole = raised[0]
                for j in range(1, i + 1):
                    whole = whole + raised[j]
                for j in range(i + 1):
                    exact[(i, j)] = raised[j] / whole
            probs[k, u] = from_pairs(exact).astype(low16)
            for i in range(3):
                total = None
                for j in range(i + 1):
                    weight = exact[(i, j)].astype(low16).astype(f32)
                    term = weight * val[j * size : (j + 1) * size]
                    total = term if total is None else total + term
                begin = u * group + i * size
                mixed[begin : begin + size, k * half : (k + 1) * half] = total.astype(low16)
    partial[...] = dot(mixed[...], mix[...]).astype(low16)


def local_top_kernel(info, cotangent, top, given):
    low, sec = info[LOW], info[SEC]
    utts, code_count, frames, _ = cotangent.shape
    group = code_count * frames
    frame_at = lax.broadcasted_iota(jnp.int32, (frames, 1), 0) + info[SHARD] * frames
    for u in range(utts):
        valid = frame_at < info[LENGTHS + u]
        for c in range(code_count):
            row = u * group + c * frames
            for m in range(QUARTERS):
                part = cotangent[u, c, :, pl.ds(block_at(low, m), UNIT)].astype(f32)
                top[row : row + frames, span(m)] = jnp.where(valid, part, 0.0).astype(low16)
    given[...] = top[pl.ds(pl.multiple_of(sec * group, group), group), :]


def local_norm_kernel(info, start, own_part, other_part, gain, hidden, second, given):
    values = start[...] + (own_part[...].astype(f32) + other_part[...].astype(f32))
    hidden[...] = values
    second[...] = (values * factor_of(values) * gain[1:2, :]).astype(low16)
    group = given.shape[0]
    given[...] = second[pl.ds(pl.multiple_of(info[SEC] * group, group), group), :]


def feed_tiles(refs, second, top, active, grad_lifted, up, down, back, sems):
    tiles = active.shape[0]
    made = Copies(sems)
    for t in range(tiles):
        for m in range(QUARTERS):
            made.start(feed_unit(refs, t // 2, m, t % 2), up.at[t, span(m), :])
        for m in range(QUARTERS):
            made.start(feed_unit(refs, t // 2, m, 2 + t % 2), down.at[t, :, span(m)])
    back[...] = jnp.zeros_like(back)

    @pl.loop(0, tiles)
    def _(t):
        for m in range(QUARTERS):
            pltpu.make_async_copy(
                refs[0].at[0, 0], up.at[t, span(m), :], sems.at[8 * t + m]
            ).wait()
        for m in range(QUARTERS):
            pltpu.make_async_copy(
                refs[0].at[0, 0], down.at[t, :, span(m)], sems.at[8 * t + 4 + m]
            ).wait()
        tile = dot(second[...], up[t])
        cdf = normal_cdf(tile)
        active[t] = (tile * cdf).astype(low16)
        grad = (dot_nt(top[...], down[t]) * gelu_slope(tile, cdf)).astype(low16)
        grad_lifted[t] = grad
        back[...] += dot_nt(grad, up[t])


def local_feed_kernel(second, top, *rest):
    refs, (active, grad_lifted, grad_second, up, down, back, sems) = (
        rest[:FEED_REFS], rest[FEED_REFS:]
    )
    feed_tiles(refs, second, top, active, grad_lifted, up, down, back, sems)
    grad_second[...] = back[...].astype(low16)


def far_feed_kernel(second_same, second_cross, top_same, top_cross, *rest):
    refs = rest[:FEED_REFS]
    (active, grad_lifted, second, top, same, cross, up, down, back, sems) = rest[FEED_REFS:]
    group = same.shape[0]
    second[:group] = second_same[...]
    second[group:] = second_cross[...]
    top[:group] = top_same[...]
    top[group:] = top_cross[...]
    feed_tiles(refs, second, top, active, grad_lifted, up, down, back, sems)
    same[...] = back[:group].astype(low16)
    cross[...] = back[group:].astype(low16)


def pair_kernel(a, b, total):
    total[...] = add16(a[...], b[...])


def with_far(sec, rows, own, other, far_same, far_cross):
    group = far_same.shape[0]
    parts = []
    for u in range(rows // group):
        at = slice(u * group, (u + 1) * group)
        far = jnp.where(sec == u, far_same[...], far_cross[...]).astype(f32)
        parts.append(own[at, :].astype(f32) + other[at, :].astype(f32) + far)
    return jnp.concatenate(parts, axis=0)


def local_attention_back_kernel(info, hidden, own_back, other_back, far_same, far_cross, top, gain,
                                query_keys, values_in, probs, *rest):
    refs = rest[:MIX_REFS]
    (grad_hidden, mid, grad_query_keys, grad_values, grad_first, gain_grad,
     weights, mix, total, sems) = rest[MIX_REFS:]
    made = Copies(sems)
    groups = []
    for k in range(4):
        groups.append(
            [
                made.start(mix_unit(refs, k, m, u), weights.at[k, u, span(m), :])
                for u in range(2)
                for m in range(QUARTERS)
            ]
        )
    upstream = with_far(info[SEC], hidden.shape[0], own_back, other_back, far_same, far_cross)
    through, gain_grad[...] = norm_back(hidden[...], gain[1:2, :], upstream)
    grads = top[...].astype(f32) + through
    grad_hidden[...] = grads
    mid[...] = grads.astype(low16)
    utts = probs.shape[1]
    half = values_in.shape[2]
    group = query_keys.shape[1] // utts
    size = group // 3
    table = head_table(half)
    for k in range(4):
        for copy in groups[k]:
            copy.wait()
        gather_mix(weights, mix, k, half)
        grad_mixed = dot_nt(mid[...], mix[k * half : (k + 1) * half, :]).astype(low16)
        grad_mixed = grad_mixed.astype(f32)
        for u in range(utts):
            at = slice(u * group, (u + 1) * group)
            q = query_keys[k, at, :half].astype(f32)
            key = query_keys[k, at, half:].astype(f32)
            val = values_in[k, at, :].astype(f32)
            grad = grad_mixed[at]
            exact = by_pair(probs[k, u].astype(f32), size)
            grad_probs = by_pair(head_sums(pair_rows(grad, val, size), table), size)
            scored = {}
            for i in range(3):
                center = grad_probs[(i, 0)] * exact[(i, 0)]
                for j in range(1, i + 1):
                    center = center + grad_probs[(i, j)] * exact[(i, j)]
                for j in range(i + 1):
                    score = exact[(i, j)] * (grad_probs[(i, j)] - center)
                    scored[(i, j)] = score.astype(low16).astype(f32)

            def rows_of(array, n):
                return array[n * size : (n + 1) * size]

            for i in range(3):
                begin = u * group + i * size
                to_query = sum(scored[(i, j)] * rows_of(key, j) for j in range(i + 1))
                to_key = sum(scored[(n, i)] * rows_of(q, n) for n in range(i, 3))
                to_value = sum(
                    exact[(n, i)].astype(low16).astype(f32) * rows_of(grad, n)
                    for n in range(i, 3)
                )
                grad_query_keys[k, begin : begin + size, :half] = (to_query * SCALE).astype(low16)
                grad_query_keys[k, begin : begin + size, half:] = (to_key * SCALE).astype(low16)
                grad_values[k, begin : begin + size, :] = to_value.astype(low16)
        back = dot_nt(grad_query_keys[k], weights[k, 0])
        back = back + dot_nt(grad_values[k], weights[k, 1, :, :half])
        total[...] = back if k == 0 else total[...] + back
    grad_first[...] = total[...].astype(low16)


def local_end_kernel(info, own_back, other_back, start, grad_hidden, gain,
                     returned, code_part, gain_grad, values):
    low, sec = info[LOW], info[SEC]
    upstream = own_back[...].astype(f32) + other_back[...].astype(f32)
    through, gain_grad[...] = norm_back(start[...], gain[0:1, :], upstream)
    values[...] = grad_hidden[...] + through
    utts, code_count, frames, _ = code_part.shape
    total = None
    for c in range(code_count):
        begin = pl.multiple_of((sec * code_count + c) * frames, frames)
        part = values[pl.ds(begin, frames), :]
        total = part if total is None else total + part
    returned[...] = total.astype(low16)
    for u in range(utts):
        for c in range(code_count):
            row = (u * code_count + c) * frames
            for j in range(2):
                at = pl.ds(block_at(low, 2 * sec + j), UNIT)
                code_part[u, c, :, span(j)] = values[row : row + frames, at]


def output_kernel(info, hidden, own_part, other_part, far_same, far_cross, output):
    low, sec = info[LOW], info[SEC]
    utts, code_count, frames, _ = output.shape
    group = code_count * frames
    frame_at = lax.broadcasted_iota(jnp.int32, (frames, 1), 0) + info[SHARD] * frames
    for u in range(utts):
        valid = frame_at < info[LENGTHS + u]
        for c in range(code_count):
            rows = slice(u * group + c * frames, u * group + (c + 1) * frames)
            inner = slice(c * frames, (c + 1) * frames)
            for j in range(2):
                at = pl.ds(block_at(low, 2 * sec + j), UNIT)
                far = jnp.where(sec == u, far_same[inner, at], far_cross[inner, at])
                value = hidden[rows, at] + (
                    own_part[rows, at].astype(f32)
                    + other_part[rows, at].astype(f32)
                    + far.astype(f32)
                )
                output[u, c, :, span(j)] = jnp.where(valid, value, 0.0).astype(low16)


SEND_A, KEEP_A, SEND_B, KEEP_B = (1, 3), (0, 2), (2, 3), (0, 1)


def local_drop_kernel(own_active, far_active, *rest):
    refs, (own_branch, same, cross, down, branch, sems) = rest[:FEED_REFS], rest[FEED_REFS:]
    tiles, count, _ = own_active.shape
    made = Copies(sems)
    for t in range(tiles):
        for m in range(QUARTERS):
            made.start(feed_unit(refs, t // 2, m, 2 + t % 2), down.at[t, :, span(m)])
    branch[...] = jnp.zeros_like(branch)

    @pl.loop(0, tiles)
    def _(t):
        for m in range(QUARTERS):
            pltpu.make_async_copy(
                refs[0].at[0, 0], down.at[t, :, span(m)], sems.at[QUARTERS * t + m]
            ).wait()
        branch[:count] += dot(own_active[t], down[t])
        branch[count:] += dot(far_active[t], down[t])

    own_branch[...] = branch[:count].astype(low16)
    group = same.shape[0]
    same[...] = branch[count : count + group].astype(low16)
    cross[...] = branch[count + group :].astype(low16)


def local_feed_grad_kernel(second, far_second, own_lifted, far_lifted, own_active, far_active,
                           top, far_top, send_a, send_b, keep_a, keep_b, turned, tops):
    count = second.shape[0]
    turned[:, :count] = jnp.transpose(second[...])
    turned[:, count:] = jnp.transpose(far_second[...])
    tops[:count] = top[...]
    tops[count:] = far_top[...]
    for k in range(2):
        for part, pairs in enumerate(
            (((send_a, SEND_A), (keep_a, KEEP_A)), ((send_b, SEND_B), (keep_b, KEEP_B)))
        ):
            t = 2 * k + part
            right = jnp.concatenate([own_lifted[t], far_lifted[t]], axis=0)
            left = jnp.concatenate(
                [jnp.transpose(own_active[t]), jnp.transpose(far_active[t])], axis=1
            )
            for target, order in pairs:
                for place, m in enumerate(order):
                    target[place, 2 * k] = dot(turned[span(m), :], right).astype(low16)
                    target[place, 2 * k + 1] = dot(left, tops[:, span(m)]).astype(low16)


def local_mix_kernel(first, grad_query_keys, grad_values, mixed, mid,
                     send_a, send_b, keep_a, keep_b, turned):
    turned[...] = jnp.transpose(first[...])
    half = grad_values.shape[2]
    for k in range(4):
        left = jnp.transpose(mixed[:, k * half : (k + 1) * half])
        for target, order in ((send_a, SEND_A), (keep_a, KEEP_A)):
            for place, m in enumerate(order):
                target[place, k] = dot(turned[span(m), :], grad_query_keys[k]).astype(low16)
        for target, order in ((send_b, SEND_B), (keep_b, KEEP_B)):
            for place, m in enumerate(order):
                value = dot(turned[span(m), :], grad_values[k]).astype(low16)
                out = dot(left, mid[:, span(m)]).astype(low16)
                target[place, k, :, :half] = value
                target[place, k, :half, half:] = out[:, :half]
                target[place, k, half:, half:] = out[:, half:]


def by_order(send_a, send_b, keep_a, keep_b):
    return (
        (0, ((send_a, SEND_A), (keep_a, KEEP_A))),
        (1, ((send_b, SEND_B), (keep_b, KEEP_B))),
    )


def global_feed_grad_kernel(info, second, far_second, grad_lifted, far_lifted, active, far_active,
                            top, far_top, send_a, send_b, keep_a, keep_b, turned, tops):
    sec, count = info[SEC], second.shape[0]
    turned[:, :count] = jnp.transpose(second[...])
    turned[:, count:] = jnp.transpose(far_second[...])
    tops[:count] = top[...]
    tops[count:] = far_top[...]
    wide = active.shape[1] // 2
    for part, pairs in by_order(send_a, send_b, keep_a, keep_b):
        at = pl.ds(pl.multiple_of(sec * wide + part * UNIT, UNIT), UNIT)
        right = jnp.concatenate([grad_lifted[:, at], far_lifted[:, span(part)]], axis=0)
        left = jnp.concatenate(
            [jnp.transpose(active[:, at]), jnp.transpose(far_active[:, span(part)])], axis=1
        )
        for target, order in pairs:
            for place, m in enumerate(order):
                target[place, 0] = dot(turned[span(m), :], right).astype(low16)
                target[place, 1] = dot(left, tops[:, span(m)]).astype(low16)


def global_mix_grad_kernel(info, first, far_first, grads, far_grads, mixed, far_mixed, mid,
                           far_mid, send_a, send_b, keep_a, keep_b, turned, mids):
    sec, count = info[SEC], first.shape[0]
    turned[:, :count] = jnp.transpose(first[...])
    turned[:, count:] = jnp.transpose(far_first[...])
    mids[:count] = mid[...]
    mids[count:] = far_mid[...]
    width = mixed.shape[1] // 2
    at = pl.ds(pl.multiple_of(sec * width, width), width)
    right = [jnp.concatenate([grads[c, :, at], far_grads[c]], axis=0) for c in range(3)]
    left = jnp.concatenate([jnp.transpose(mixed[:, at]), jnp.transpose(far_mixed[...])], axis=1)
    for part, pairs in by_order(send_a, send_b, keep_a, keep_b):
        for target, order in pairs:
            for place, m in enumerate(order):
                rows = turned[span(m), :]
                if part == 0:
                    for c in range(2):
                        target[place, 0, :, c * width : (c + 1) * width] = dot(
                            rows, right[c]
                        ).astype(low16)
                else:
                    target[place, 0, :, :width] = dot(rows, right[2]).astype(low16)
                    out = dot(left, mids[:, span(m)]).astype(low16)
                    target[place, 0, :width, width:] = out[:, :width]
                    target[place, 0, width:, width:] = out[:, width:]


def add16(a, b):
    return (a.astype(f32) + b.astype(f32)).astype(low16)


def far_kernel(keep_a, from_x, keep_b, from_y, far_a, far_b):
    far_a[...] = add16(keep_a[0], from_x[0])
    far_b[...] = add16(keep_b[0], from_y[0])


def sum_kernel(shards, *refs):
    parts, outs = (refs[:3], refs[3:6]), refs[6:]
    for part, (keep, once, twice) in enumerate(parts):
        total = keep[0].astype(f32) + once[0].astype(f32) + twice[...].astype(f32)
        total = total.astype(low16)
        count = total.shape[0] // shards
        at = slice(part * count, (part + 1) * count)
        if shards == 1:
            outs[0][at] = total
        elif shards == 2:
            outs[1][0, at] = total[:count]
            outs[0][0, at] = total[count:]
        else:
            for k in range(4):
                outs[(k + 1) % 2][k // 2, at] = total[k * count : (k + 1) * count]


def far_tensor_kernel(keep, arrived, far):
    far[...] = add16(keep[0], arrived[0])


def pick_kernel(info, *refs):
    *terms, world, given, kept = refs
    sec = info[SEC]
    local = terms[0][0].astype(f32)
    for term in terms[1:]:
        local = local + (term[0] if len(term.shape) == 4 else term[...]).astype(f32)
    local = local.astype(low16)
    other = world[...]
    given[...] = jnp.where(sec == 0, local, other)
    kept[...] = jnp.where(sec == 0, other, local)


def half_at(index, count):
    return pl.BlockSpec(
        (1, count, UNIT, UNIT), lambda i: (index, 0, 0, 0), memory_space=pltpu.VMEM
    )


def quarter_unit(refs, m, index):
    own, x_part, y_part, far_kept, far_arrived = refs
    count = own.shape[0] // 2
    if m < 3:
        return (own, x_part, y_part)[m][index].astype(f32)
    return (far_kept[index] if index < count else far_arrived[index - count]).astype(f32)


def feed_final_kernel(info, *rest):
    refs, (up, down) = rest[:5], rest[5:]
    low, sec = info[LOW], info[SEC]
    wide = up.shape[1] // 2
    count = refs[0].shape[0] // 2
    for m in range(QUARTERS):
        at = pl.ds(block_at(low, m), UNIT)
        for source, half in ((0, sec), (count, 1 - sec)):
            for part in range(2):
                hidden = pl.ds(pl.multiple_of(half * wide + part * UNIT, UNIT), UNIT)
                up[at, hidden] = quarter_unit(refs, m, source + 2 * part)
                down[hidden, at] = quarter_unit(refs, m, source + 2 * part + 1)


def mix_final_kernel(info, *rest):
    refs, (qkv, out) = rest[:5], rest[5:]
    low, sec = info[LOW], info[SEC]
    width = out.shape[0] // 2
    count = refs[0].shape[0] // 2
    for m in range(QUARTERS):
        at = pl.ds(block_at(low, m), UNIT)
        at_left = pl.ds(block_at(low, m), width)
        at_right = pl.ds(pl.multiple_of(block_at(low, m) + width, width), width)
        for source, half in ((0, sec), (count, 1 - sec)):
            lanes = pl.ds(pl.multiple_of(half * width, width), width)
            query_keys = quarter_unit(refs, m, source)
            qkv[0, at, lanes] = query_keys[:, :width]
            qkv[1, at, lanes] = query_keys[:, width:]
            rest_unit = quarter_unit(refs, m, source + 1)
            qkv[2, at, lanes] = rest_unit[:, :width]
            out[lanes, at_left] = rest_unit[:width, width:]
            out[lanes, at_right] = rest_unit[width:, width:]


def sum_rest(value):
    step = QUARTERS
    while step < lax.axis_size("dp"):
        value = add16(value, swap(value, "dp", step))
        step *= 2
    return value


class Sum:
    def __init__(self, order, shards, send_a, send_b, keep_a, keep_b):
        self.order, self.shards = order, shards
        self.keep = (keep_a, keep_b)
        self.count = keep_a.shape[1]
        self.once = (swap(send_a, "dp", 1), swap(send_b, "dp", 2))

    def second(self):
        far = half_at(1, self.count)
        far_a, far_b = self.order.call(
            far_kernel,
            [shape((self.count, UNIT, UNIT), low16)] * 2,
            (self.keep[0], self.once[0], self.keep[1], self.once[1]),
            [far] * 4,
            grid=(1,),
        )
        self.twice = (swap(far_a, "dp", 2), swap(far_b, "dp", 1))

    def third(self):
        count = 2 * self.count // self.shards
        if self.shards == 1:
            outs = [shape((count, UNIT, UNIT), low16)]
        else:
            outs = [shape((self.shards // 2, count, UNIT, UNIT), low16)] * 2
        near = half_at(0, self.count)
        totals = self.order.call(
            functools.partial(sum_kernel, self.shards),
            outs,
            (self.keep[0], self.once[0], self.twice[0], self.keep[1], self.once[1], self.twice[1]),
            [near, near, VM] * 2,
            grid=(1,),
        )
        totals = [sum_rest(total) for total in totals]
        self.count = count
        if self.shards == 1:
            return totals[0]
        self.keep = totals[1]
        if self.shards == 2:
            self.terms = (self.keep, swap(totals[0], "tensor", 2))
        else:
            self.once = swap(totals[0], "tensor", 1)

    def fourth(self):
        far = self.order.call(
            far_tensor_kernel,
            [shape((self.count, UNIT, UNIT), low16)],
            (self.keep, self.once),
            [half_at(1, self.count)] * 2,
            grid=(1,),
        )[0]
        self.terms = (self.keep, self.once, swap(far, "tensor", 2))

    def gathered(self, info, world):
        near = half_at(0, self.count)
        given, kept = self.order.call(
            pick_kernel,
            [shape((self.count, UNIT, UNIT), low16)] * 2,
            (info,) + self.terms + (world,),
            [SM] + [near if term.ndim == 4 else VM for term in self.terms] + [VM],
            grid=(1,),
        )
        units = jnp.concatenate([kept, swap(given, "section", 1)])
        return Gather(units)


class Gather:
    def __init__(self, units):
        self.units = units
        self.count = units.shape[0] // 2
        self.near = (swap(units, "dp", 1), swap(units, "dp", 2))

    def far(self):
        x_part, y_part = self.near
        self.rest = (
            swap(x_part[: self.count], "dp", 2), swap(y_part[self.count :], "dp", 1)
        )
        return (self.units,) + self.near + self.rest


def on_device(codes, lengths, gains, w_qkv, w_out, w_up, w_down, cotangent):
    sec = lax.axis_index("section")
    low = lax.axis_index("dp") % QUARTERS
    z = lax.axis_index("tensor")
    first_core = sec == 0
    utts, frames, code_count, width = codes.shape
    heads_width = w_out.shape[1]
    half = heads_width // 2
    wide = w_up.shape[2]
    rows_g = 4 * frames
    rows_l = utts * code_count * frames
    tiles = wide // UNIT
    info = jnp.concatenate([jnp.stack([low, sec, z]).astype(jnp.int32), lengths])
    order = Order()
    call = order.call

    code_rows = jnp.transpose(codes, (0, 2, 1, 3))
    cot_rows = jnp.transpose(cotangent, (0, 2, 1, 3))
    own_w = (jnp.transpose(w_qkv[0], (1, 0, 2)), w_out[0], w_up[0], w_down[0])

    def sem(count):
        return pltpu.SemaphoreType.DMA((count,))

    def gather(rows):
        gathered = lax.all_gather(rows, "tensor")
        order.tokens = (gathered,)
        return gathered

    def scatter(partial):
        return lax.all_to_all(partial, "tensor", 0, 0)

    other_gain = swap(gains[0], "section", 1)
    own_w, other_gain = lax.optimization_barrier((own_w, other_gain))

    def with_other(weights):
        return tuple(w for own in weights for w in (own, swap(own, "section", 1)))

    attention_w = with_other(own_w[:2])

    first_rows, start_g, gain_g, gain_l = call(
        start_kernel,
        [
            shape((frames, width), low16),
            shape((frames, width), f32),
            shape((2, width), f32),
            shape((2, width), f32),
        ],
        (info, code_rows, gains[0], other_gain),
        [SM, VM, VM, VM],
        us=2,
    )
    first_blocks = gather(first_rows)

    mix_piece, mix_whole = call(
        mix_piece_kernel,
        [shape((2, UNIT, UNIT), low16), shape((QUARTERS, 2, UNIT, UNIT), low16)],
        (info,) + attention_w,
        [SM] + [ANY] * 4,
        [sem(5 * QUARTERS)],
        us=3.2,
    )
    mix_z1 = swap(mix_piece, "tensor", 1)
    mix_z2 = swap(mix_piece, "tensor", 2)
    feed_w = with_other(order.after(own_w[2:]))

    first_g, packed_g, probs_g, mixed_g, mixed_given, partial = call(
        global_attention_kernel,
        [
            shape((rows_g, width), low16),
            shape((3, rows_g, heads_width), low16),
            shape((heads_width // HEAD_DIM, rows_g, rows_g), low16),
            shape((rows_g, heads_width), low16),
            shape((rows_g, half), low16),
            shape((4, frames, width), low16),
        ],
        (info, first_blocks) + attention_w,
        [SM, VM] + [ANY] * 4,
        [
            pltpu.VMEM((3, width, heads_width), low16),
            pltpu.VMEM((heads_width, width), low16),
            sem(8),
        ],
        us=5.7,
        limit=60,
    )
    partial, mix_z1, mix_z2 = lax.optimization_barrier((partial, mix_z1, mix_z2))
    arrived = scatter(partial)
    mix_z3 = swap(order.after(mix_z2), "tensor", 1)
    top_l, top_given = call(
        local_top_kernel,
        [shape((rows_l, width), low16), shape((rows_l // utts, width), low16)],
        (info, cot_rows),
        [SM, VM],
        us=2.3,
    )
    mix_near = jnp.stack(order.after([mix_z1, mix_z2]))
    mix_x = swap(mix_near, "dp", 1)
    mix_y = swap(mix_near, "dp", 2)
    feed_piece, feed_whole = call(
        feed_piece_kernel,
        [shape((4, UNIT, UNIT), low16), shape((QUARTERS, 4, UNIT, UNIT), low16)],
        (info,) + feed_w,
        [SM] + [ANY] * 4,
        [sem(4 * QUARTERS)],
        us=4,
    )
    feed_z2 = swap(feed_piece, "tensor", 2)
    top_same = swap(order.after(top_given), "tensor", 1)
    hidden_g, second_rows = call(
        middle_kernel,
        [shape((frames, width), f32), shape((frames, width), low16)],
        (start_g, arrived, gain_g),
        [VM] * 3,
        us=2,
    )
    mix_z3 = order.after(mix_z3)
    mix_x3 = swap(mix_z3, "dp", 1)
    mix_y3 = swap(mix_z3, "dp", 2)
    second_blocks = gather(second_rows)
    order.until(feed_z2, mix_x, mix_y, mix_x3, mix_y3, top_same)
    feed_z2, mix_x, mix_y, mix_x3, mix_y3 = order.after((feed_z2, mix_x, mix_y, mix_x3, mix_y3))
    mix_w = (
        mix_whole,
        mix_z1,
        mix_z2,
        mix_z3,
        mix_x,
        mix_y,
        swap(mix_x[:, 0], "dp", 2),
        swap(mix_y[:, 1], "dp", 1),
        mix_x3,
        mix_y3,
        swap(mix_x3[:1], "dp", 2),
        swap(mix_y3[1:], "dp", 1),
    )
    feed_x = swap(feed_z2, "dp", 1)
    feed_y = swap(feed_z2, "dp", 2)
    second_g, lifted_g, active_g, active_given, partial = call(
        global_feed_kernel,
        [
            shape((rows_g, width), low16),
            shape((rows_g, wide), f32),
            shape((rows_g, wide), low16),
            shape((rows_g, wide // 2), low16),
            shape((4, frames, width), low16),
        ],
        (info, second_blocks) + feed_w,
        [SM, VM] + [ANY] * 4,
        [
            pltpu.VMEM((width, wide), low16),
            pltpu.VMEM((wide, width), low16),
            pltpu.VMEM((rows_g, width), f32),
            sem(8),
        ],
        us=5.6,
        limit=60,
    )
    arrived = scatter(partial)
    order.until(feed_x, feed_y, mix_w[6], mix_w[7], mix_w[10], mix_w[11])
    sent = call(
        sent_kernel,
        [shape((frames, width), low16)],
        (hidden_g, arrived),
        [VM] * 2,
        us=1.9,
    )[0]
    other_sent = swap(sent, "section", 1)
    feed_l = (
        feed_whole,
        feed_z2,
        feed_x,
        feed_y,
        swap(feed_x[:2], "dp", 2),
        swap(feed_y[2:], "dp", 1),
    )

    order.until(*feed_l)

    start_l, first_l, query_keys, values_l, probs_l, mixed_l, partial = call(
        local_attention_kernel,
        [
            shape((rows_l, width), f32),
            shape((rows_l, width), low16),
            shape((4, rows_l, 2 * half), low16),
            shape((4, rows_l, half), low16),
            shape((4, utts, 2 * rows_l // utts, half), low16),
            shape((rows_l, 4 * half), low16),
            shape((rows_l, width), low16),
        ],
        (info, code_rows, sent, other_sent, gain_l) + mix_w,
        [SM] + [VM] * 4 + [ANY] * MIX_REFS,
        [
            pltpu.VMEM((4, 2, width, UNIT), low16),
            pltpu.VMEM((4 * half, width), low16),
            sem(32),
        ],
        us=9,
        limit=60,
    )
    hidden_l, second_l, second_given = call(
        local_norm_kernel,
        [
            shape((rows_l, width), f32),
            shape((rows_l, width), low16),
            shape((rows_l // utts, width), low16),
        ],
        (info, start_l, partial, swap(partial, "section", 1), gain_l),
        [SM] + [VM] * 4,
        us=3.7,
    )
    second_same = swap(second_given, "tensor", 1)
    top_cross = swap(order.after(top_same), "section", 1)
    feed_scratch = [
        pltpu.VMEM((tiles, width, UNIT), low16),
        pltpu.VMEM((tiles, UNIT, width), low16),
        pltpu.VMEM((rows_l, width), f32),
        sem(8 * tiles),
    ]
    wide_rows = shape((rows_l, width), low16)
    half_rows = shape((rows_l // utts, width), low16)
    tiled_rows = shape((tiles, rows_l, UNIT), low16)
    active_l, grad_lifted_l, back = call(
        local_feed_kernel,
        [tiled_rows, tiled_rows, wide_rows],
        (second_l, top_l) + feed_l,
        [VM] * 2 + [ANY] * FEED_REFS,
        feed_scratch,
        us=7.9,
    )
    other_back = swap(back, "section", 1)
    second_same = order.after(second_same)
    second_cross = swap(second_same, "section", 1)
    far_active, far_lifted, far_second, far_top, same, cross = call(
        far_feed_kernel,
        [tiled_rows, tiled_rows, wide_rows, wide_rows, half_rows, half_rows],
        (second_same, second_cross, top_same, top_cross) + feed_l,
        [VM] * 4 + [ANY] * FEED_REFS,
        feed_scratch,
        us=8.2,
    )

    def from_neighbour(same, cross):
        total = call(
            pair_kernel, [half_rows], (same, cross), [VM] * 2
        )[0]
        return swap(total, "tensor", 1)

    far_same = from_neighbour(same, swap(cross, "section", 1))
    turned_l = pltpu.VMEM((width, rows_l), low16)
    local_feed = Sum(
        order,
        2,
        *call(
            local_feed_grad_kernel,
            [shape((2, 4, UNIT, UNIT), low16)] * 4,
            (
                second_l, far_second, grad_lifted_l, far_lifted, active_l, far_active, top_l,
                far_top,
            ),
            [VM] * 8,
            [pltpu.VMEM((width, 2 * rows_l), low16), pltpu.VMEM((2 * rows_l, width), low16)],
            us=7.6,
        ),
    )
    own_branch, branch_same, branch_cross = call(
        local_drop_kernel,
        [wide_rows, half_rows, half_rows],
        (active_l, far_active) + feed_l,
        [VM] * 2 + [ANY] * FEED_REFS,
        [
            pltpu.VMEM((tiles, UNIT, width), low16),
            pltpu.VMEM((2 * rows_l, width), f32),
            sem(QUARTERS * tiles),
        ],
        us=6.1,
    )
    branch_cross = swap(branch_cross, "section", 1)
    other_branch = swap(own_branch, "section", 1)
    far_same = order.after(far_same)
    far_back = (far_same, swap(far_same, "section", 1))
    far_branch = from_neighbour(branch_same, branch_cross)
    far_first, far_mixed, far_second_g, far_active_g = (
        swap(order.after(value), "section", 1)
        for value in (first_g, mixed_given, second_g, active_given)
    )
    grad_hidden_l, mid_l, grad_query_keys, grad_values, back, gain2_l = call(
        local_attention_back_kernel,
        [
            shape((rows_l, width), f32),
            shape((rows_l, width), low16),
            shape((4, rows_l, 2 * half), low16),
            shape((4, rows_l, half), low16),
            shape((rows_l, width), low16),
            shape((1, width), f32),
        ],
        (info, hidden_l, back, other_back)
        + far_back
        + (top_l, gain_l, query_keys, values_l, probs_l)
        + mix_w,
        [SM] + [VM] * 10 + [ANY] * MIX_REFS,
        [
            pltpu.VMEM((4, 2, width, UNIT), low16),
            pltpu.VMEM((4 * half, width), low16),
            pltpu.VMEM((rows_l, width), f32),
            sem(32),
        ],
        us=11.4,
    )
    other_back = swap(back, "section", 1)
    local_mix = Sum(
        order,
        4,
        *call(
            local_mix_kernel,
            [shape((2, 4, UNIT, UNIT), low16)] * 4,
            (first_l, grad_query_keys, grad_values, mixed_l, mid_l),
            [VM] * 5,
            [turned_l],
            us=6,
        ),
    )
    returned, code_part, gain1_l = call(
        local_end_kernel,
        [
            shape((frames, width), low16),
            shape((utts, code_count, frames, width // 2), f32),
            shape((1, width), f32),
        ],
        (info, back, other_back, start_l, grad_hidden_l, gain_l),
        [SM] + [VM] * 5,
        [pltpu.VMEM((rows_l, width), f32)],
        us=4.4,
    )

    top_blocks = gather(returned)
    local_feed.second()
    order.until(*local_mix.once, far_first, far_mixed, far_second_g, far_active_g)
    top_g, grad_lifted_g, lifted_given, partial = call(
        global_feed_back_kernel,
        [
            shape((rows_g, width), low16),
            shape((rows_g, wide), low16),
            shape((rows_g, wide // 2), low16),
            shape((4, frames, width), low16),
        ],
        (info, top_blocks, lifted_g) + feed_w,
        [SM] + [VM] * 2 + [ANY] * 4,
        [
            pltpu.VMEM((width, wide), low16),
            pltpu.VMEM((wide, width), low16),
            pltpu.VMEM((rows_g, width), f32),
            sem(8),
        ],
        us=6.3,
        limit=60,
    )
    arrived = scatter(partial)
    far_top_g, far_lifted_g = swap(top_g, "section", 1), swap(lifted_given, "section", 1)
    local_feed.third()
    local_mix.second()
    far_branch = order.after(far_branch)
    far_branch = (far_branch, swap(far_branch, "section", 1))
    global_feed = Sum(
        order,
        1,
        *call(
            global_feed_grad_kernel,
            [shape((2, 2, UNIT, UNIT), low16)] * 4,
            (
                info, second_g, far_second_g, grad_lifted_g, far_lifted_g, active_g, far_active_g,
                top_g, far_top_g,
            ),
            [SM] + [VM] * 8,
            [pltpu.VMEM((width, 2 * rows_g), low16), pltpu.VMEM((2 * rows_g, width), low16)],
            us=3.5,
        ),
    )
    grad_hidden_g, mid_rows, gain2_g = call(
        middle_back_kernel,
        [shape((frames, width), f32), shape((frames, width), low16), shape((1, width), f32)],
        (arrived, hidden_g, gain_g, returned),
        [VM] * 4,
        us=2.1,
    )
    mid_blocks = gather(mid_rows)
    order.until(*local_mix.twice)
    mid_g, grads_g, grads_given, partial = call(
        global_attention_back_kernel,
        [
            shape((rows_g, width), low16),
            shape((3, rows_g, heads_width), low16),
            shape((3, rows_g, half), low16),
            shape((4, frames, width), low16),
        ],
        (info, mid_blocks, packed_g, probs_g) + attention_w,
        [SM] + [VM] * 3 + [ANY] * 4,
        [
            pltpu.VMEM((3, width, heads_width), low16),
            pltpu.VMEM((heads_width, width), low16),
            sem(8),
        ],
        us=6.8,
        limit=60,
    )
    arrived = scatter(partial)
    far_mid_g, far_grads_g = swap(mid_g, "section", 1), swap(grads_given, "section", 1)
    global_feed.second()
    local_mix.third()
    global_mix = Sum(
        order,
        1,
        *call(
            global_mix_grad_kernel,
            [shape((2, 1, UNIT, UNIT), low16)] * 4,
            (
                info, first_g, far_first, grads_g, far_grads_g, mixed_g, far_mixed, mid_g,
                far_mid_g,
            ),
            [SM] + [VM] * 8,
            [pltpu.VMEM((width, 2 * rows_g), low16), pltpu.VMEM((2 * rows_g, width), low16)],
            us=3,
        ),
    )
    output = call(
        output_kernel,
        [shape((utts, code_count, frames, width // 2), low16)],
        (info, hidden_l, own_branch, other_branch) + far_branch,
        [SM] + [VM] * 5,
        us=3.1,
    )[0]
    kept_start, given_start, gain1_g = call(
        start_back_kernel,
        [
            shape((frames, width // 2), f32),
            shape((frames, width // 2), f32),
            shape((1, width), f32),
        ],
        (info, arrived, start_g, gain_g, grad_hidden_g),
        [SM] + [VM] * 4,
        [pltpu.VMEM((frames, width), f32)],
        us=2.1,
    )
    world_feed = global_feed.third()
    global_mix.second()
    local_mix.fourth()
    world_mix = global_mix.third()
    feed_sum = local_feed.gathered(info, world_feed)
    arrived_start = swap(given_start, "section", 1)
    both_start = jnp.stack(
        [
            jnp.where(first_core, kept_start, arrived_start),
            jnp.where(first_core, arrived_start, kept_start),
        ]
    )
    code_grad = jnp.transpose(code_part + both_start[:, None], (0, 2, 1, 3))

    own_gain = jnp.concatenate([gain1_g, gain2_g], axis=0)
    total_gain = own_gain + swap(own_gain, "section", 1)
    local_gain = jnp.concatenate([gain1_l, gain2_l], axis=0)
    gain_total = jnp.where(first_core, total_gain, local_gain)
    gain_total = jnp.concatenate(
        [
            lax.dynamic_slice_in_dim(gain_total, (low ^ m) * UNIT, UNIT, 1)
            for m in range(QUARTERS)
        ],
        axis=1,
    )
    def over(value, axis):
        copies = jnp.broadcast_to(value, (lax.axis_size(axis),) + value.shape)
        return jnp.sum(lax.all_to_all(order.after(copies), axis, 0, 0), axis=0)

    gain_total = over(gain_total, "tensor")
    order.until(gain_total)
    mix_sum = local_mix.gathered(info, world_mix)
    gain_total = over(gain_total, "dp")
    order.until(gain_total, *feed_sum.near)
    feed_parts = feed_sum.far()
    mix_parts = mix_sum.far()
    up_grad, down_grad = call(
        feed_final_kernel,
        [shape((width, wide), f32), shape((wide, width), f32)],
        (info,) + feed_parts,
        [SM] + [VM] * 5,
        us=6.8,
    )
    qkv_grad, out_grad = call(
        mix_final_kernel,
        [shape((3, width, heads_width), f32), shape((heads_width, width), f32)],
        (info,) + mix_parts,
        [SM] + [VM] * 5,
        us=4.5,
    )
    return (
        jnp.transpose(output, (0, 2, 1, 3)),
        code_grad,
        gain_total[None],
        jnp.transpose(qkv_grad, (1, 0, 2))[None],
        out_grad[None],
        up_grad[None],
        down_grad[None],
    )


def solution(mesh):
    in_specs = (
        P("dp", "tensor", None, None),
        P("dp"),
        P("section", None, None),
        P("section", None, None, "tensor"),
        P("section", "tensor", None),
        P("section", None, "tensor"),
        P("section", "tensor", None),
        P("dp", "tensor", None, None),
    )
    out_specs = (
        P("dp", "tensor", None, "section"),
        P("dp", "tensor", None, "section"),
        P("section", None, None),
        P("section", None, None, "tensor"),
        P("section", "tensor", None),
        P("section", None, "tensor"),
        P("section", "tensor", None),
    )
    return jax.shard_map(
        on_device, mesh=mesh, in_specs=in_specs, out_specs=out_specs, check_vma=False
    )
```

```python
import functools

import jax
import jax.numpy as jnp
from jax import lax
from jax.experimental import pallas as pl
from jax.experimental.pallas import tpu as pltpu
from jax.sharding import PartitionSpec as P

HEAD_DIM = 64
SCALE = HEAD_DIM ** (-0.5)
QUARTERS = 4
UNIT = 256
epsilon = 1e-06
negative = -1e30
f32 = jnp.float32
low16 = jnp.bfloat16

VM = pl.BlockSpec(memory_space=pltpu.VMEM)
SM = pl.BlockSpec(memory_space=pltpu.SMEM)
ANY = pl.BlockSpec(memory_space=pltpu.HBM)
MIB = 1 << 20
PACE = 2 * 10**8

LOW, SEC, SHARD, LENGTHS = 0, 1, 2, 3


def shape(dims, dtype):
    return jax.ShapeDtypeStruct(tuple(dims), dtype)


class Order:
    def __init__(self):
        self.tokens = ()

    def after(self, value):
        if not self.tokens:
            return value
        return lax.optimization_barrier((value,) + self.tokens)[0]

    def until(self, *values):
        self.tokens += values

    def call(self, body, outs, args, specs, scratch=(), limit=28, us=2.0, grid=(), place=VM, aliases=()):
        args = (self.after(args[0]),) + tuple(args[1:])
        results = pl.pallas_call(
            body,
            out_shape=tuple(outs),
            grid=grid,
            in_specs=list(specs),
            out_specs=place if isinstance(place, tuple) else (place,) * len(outs),
            input_output_aliases=dict(aliases),
            scratch_shapes=list(scratch),
            compiler_params=pltpu.CompilerParams(vmem_limit_bytes=limit * MIB),
            cost_estimate=pl.CostEstimate(
                flops=int(us * PACE), bytes_accessed=0, transcendentals=0
            ),
        )(*args)
        self.tokens = (results[-1],)
        return results


def swap(value, axis, flip):
    count = lax.axis_size(axis)
    return lax.ppermute(value, axis, [(i, i ^ flip) for i in range(count)])


def dot(a, b):
    return jnp.dot(a, b, preferred_element_type=f32)


def dot_tn(a, b):
    return lax.dot_general(a, b, (((0,), (0,)), ((), ())), preferred_element_type=f32)


def dot_nt(a, b):
    return lax.dot_general(a, b, (((1,), (1,)), ((), ())), preferred_element_type=f32)


def factor_of(values):
    return lax.rsqrt(jnp.mean(values * values, axis=-1, keepdims=True) + epsilon)


def norm_back(values, gain, upstream):
    factor = factor_of(values)
    weighted = upstream * gain
    inner = jnp.mean(weighted * values, axis=-1, keepdims=True)
    through = factor * weighted - values * (factor * factor * factor) * inner
    return through, jnp.sum(upstream * values * factor, axis=0, keepdims=True)


def normal_cdf(values):
    return 0.5 * (1.0 + lax.erf(values * (0.5**0.5)))


def gelu_slope(values, cdf):
    return cdf + values * (jnp.exp(-0.5 * values * values) * 0.3989422804014327)


def block_at(low, m):
    return pl.multiple_of((low ^ m) * UNIT, UNIT)


def span(m):
    return slice(m * UNIT, (m + 1) * UNIT)


class Copies:
    def __init__(self, sems):
        self.sems = sems
        self.made = []

    def start(self, src, dst):
        copy = pltpu.make_async_copy(src, dst, self.sems.at[len(self.made)])
        copy.start()
        self.made.append(copy)
        return copy

    def pick(self, own_first, sec, own, other, dst):
        sem = self.sems.at[len(self.made)]

        @pl.when((sec == 0) == own_first)
        def _():
            pltpu.make_async_copy(own, dst, sem).start()

        @pl.when((sec == 0) != own_first)
        def _():
            pltpu.make_async_copy(other, dst, sem).start()

        copy = pltpu.make_async_copy(own, dst, sem)
        self.made.append(copy)
        return copy

    def wait(self, begin=0, end=None):
        for copy in self.made[begin:end]:
            copy.wait()


def start_kernel(info, codes, own_gain, other_gain, first, start, gain_g, gain_l):
    low, sec = info[LOW], info[SEC]
    for m in range(QUARTERS):
        at = pl.ds(block_at(low, m), UNIT)
        own, other = own_gain[:, at], other_gain[:, at]
        gain_g[:, span(m)] = jnp.where(sec == 0, own, other)
        gain_l[:, span(m)] = jnp.where(sec == 0, other, own)
        total = codes[sec, 0, :, at].astype(f32)
        for c in range(1, codes.shape[1]):
            total = total + codes[sec, c, :, at].astype(f32)
        start[:, span(m)] = total
    values = start[...]
    first[...] = (values * factor_of(values) * gain_g[0:1, :]).astype(low16)


def from_local(sec, own, other, branch):
    @pl.when(sec == 0)
    def _():
        branch(0, *other)

    @pl.when(sec != 0)
    def _():
        branch(1, *own)


def mix_piece_kernel(info, own_qkv, other_qkv, own_out, other_out, piece, whole, sems):
    low, sec = info[LOW], info[SEC]
    half = own_qkv.shape[2] // 2

    def branch(half_index, qkv, out):
        made = Copies(sems)
        for m in range(QUARTERS):
            at = pl.ds(block_at(low, m), UNIT)
            at_right = pl.ds(pl.multiple_of(block_at(low, m) + half, half), half)
            at_left = pl.ds(block_at(low, m), half)
            lanes = slice(half_index * half, (half_index + 1) * half)
            target = whole.at[m]
            made.start(qkv.at[0, at, lanes], target.at[0, :, 0:half])
            made.start(qkv.at[1, at, lanes], target.at[0, :, half : 2 * half])
            made.start(qkv.at[2, at, lanes], target.at[1, :, 0:half])
            made.start(out.at[lanes, at_left], target.at[1, 0:half, half : 2 * half])
            made.start(out.at[lanes, at_right], target.at[1, half : 2 * half, half : 2 * half])
        made.wait()

    from_local(sec, (own_qkv, own_out), (other_qkv, other_out), branch)
    piece[...] = whole[0]


def feed_piece_kernel(info, own_up, other_up, own_down, other_down, piece, whole, sems):
    low, sec = info[LOW], info[SEC]
    wide = own_up.shape[1] // 2

    def branch(half_index, up, down):
        made = Copies(sems)
        for m in range(QUARTERS):
            at = pl.ds(block_at(low, m), UNIT)
            for part in range(2):
                begin = half_index * wide + part * UNIT
                hidden = slice(begin, begin + UNIT)
                made.start(up.at[at, hidden], whole.at[m, part])
                made.start(down.at[hidden, at], whole.at[m, 2 + part])
        made.wait()

    from_local(sec, (own_up, own_down), (other_up, other_down), branch)
    piece[...] = whole[0]


def fetch_attention(made, low, sec, own_qkv, other_qkv, own_out, other_out, qkv, out):
    for m in range(QUARTERS):
        at = pl.ds(block_at(low, m), UNIT)
        made.pick(True, sec, own_qkv.at[:, at, :], other_qkv.at[:, at, :], qkv.at[:, span(m), :])
    for m in range(QUARTERS):
        at = pl.ds(block_at(low, m), UNIT)
        made.pick(True, sec, own_out.at[:, at], other_out.at[:, at], out.at[:, span(m)])


def by_shard(info, blocks):
    count = blocks.shape[0]
    return jnp.concatenate([blocks[info[SHARD] ^ k] for k in range(count)], axis=0)


def other_half(info, width):
    half = width // 2
    return pl.ds(pl.multiple_of((1 - info[SEC]) * half, half), half)


def spread_blocks(info, target, values):
    frames = target.shape[1]
    for k in range(target.shape[0]):
        target[info[SHARD] ^ k] = values[k * frames : (k + 1) * frames].astype(low16)


def row_places(info, count, frames, dimension):
    at = lax.broadcasted_iota(jnp.int32, (count, count), dimension)
    return (lax.div(at, frames) ^ info[SHARD]) * frames + lax.rem(at, frames)


def global_attention_kernel(info, *rest):
    (blocks, own_qkv, other_qkv, own_out, other_out,
     rows, packed, probs, mixed, given, partial, qkv, out, sems) = rest
    low, sec = info[LOW], info[SEC]
    made = Copies(sems)
    fetch_attention(made, low, sec, own_qkv, other_qkv, own_out, other_out, qkv, out)
    count, frames = rows.shape[0], blocks.shape[1]
    length = info[LENGTHS + sec]
    query_at = row_places(info, count, frames, 0)
    key_at = row_places(info, count, frames, 1)
    allowed = (key_at <= query_at) & (key_at < length)
    values = by_shard(info, blocks)
    rows[...] = values
    made.wait(0, QUARTERS)
    for c in range(3):
        packed[c] = dot(values, qkv[c]).astype(low16)
    heads = []
    for h in range(packed.shape[2] // HEAD_DIM):
        lanes = slice(h * HEAD_DIM, (h + 1) * HEAD_DIM)
        scores = dot_nt(packed[0, :, lanes], packed[1, :, lanes]) * SCALE
        scores = jnp.where(allowed, scores, negative)
        raised = jnp.exp(scores - jnp.max(scores, axis=-1, keepdims=True))
        exact = raised / jnp.sum(raised, axis=-1, keepdims=True)
        probs[h] = exact.astype(low16)
        heads.append(dot(exact.astype(low16), packed[2, :, lanes]).astype(low16))
    mixed[...] = jnp.concatenate(heads, axis=1)
    given[...] = mixed[:, other_half(info, mixed.shape[1])]
    made.wait(QUARTERS)
    spread_blocks(info, partial, dot(mixed[...], out[...]))


def total_of(arrived):
    total = arrived[0].astype(f32)
    for k in range(1, arrived.shape[0]):
        total = total + arrived[k].astype(f32)
    return total


def middle_kernel(start, arrived, gain, hidden, second):
    values = start[...] + total_of(arrived)
    hidden[...] = values
    second[...] = (values * factor_of(values) * gain[1:2, :]).astype(low16)


def fetch_feed(made, low, sec, own_up, other_up, own_down, other_down, up, down):
    for m in range(QUARTERS):
        at = pl.ds(block_at(low, m), UNIT)
        made.pick(True, sec, own_up.at[at, :], other_up.at[at, :], up.at[span(m), :])
    for m in range(QUARTERS):
        at = pl.ds(block_at(low, m), UNIT)
        made.pick(True, sec, own_down.at[:, at], other_down.at[:, at], down.at[:, span(m)])


def global_feed_kernel(info, *rest):
    (blocks, own_up, other_up, own_down, other_down,
     rows, lifted, active, given, partial, up, down, total, sems) = rest
    made = Copies(sems)
    fetch_feed(made, info[LOW], info[SEC], own_up, other_up, own_down, other_down, up, down)
    values = by_shard(info, blocks)
    rows[...] = values
    made.wait(0, QUARTERS)
    for t in range(up.shape[1] // UNIT):
        tile = dot(values, up[:, span(t)])
        lifted[:, span(t)] = tile
        low_tile = (tile * normal_cdf(tile)).astype(low16)
        active[:, span(t)] = low_tile
        if t == 0:
            made.wait(QUARTERS)
        branch = dot(low_tile, down[span(t), :])
        total[...] = branch if t == 0 else total[...] + branch
    spread_blocks(info, partial, total[...])
    given[...] = active[:, other_half(info, active.shape[1])]


def sent_kernel(hidden, arrived, sent):
    sent[...] = (hidden[...] + total_of(arrived)).astype(low16)


def global_feed_back_kernel(info, *rest):
    (blocks, lifted, own_up, other_up, own_down, other_down,
     rows, grad_lifted, given, partial, up, down, total, sems) = rest
    made = Copies(sems)
    fetch_feed(made, info[LOW], info[SEC], own_up, other_up, own_down, other_down, up, down)
    values = by_shard(info, blocks)
    rows[...] = values
    made.wait(QUARTERS)
    for t in range(up.shape[1] // UNIT):
        tile = lifted[:, span(t)]
        grad = dot_nt(values, down[span(t), :]) * gelu_slope(tile, normal_cdf(tile))
        grad = grad.astype(low16)
        grad_lifted[:, span(t)] = grad
        if t == 0:
            made.wait(0, QUARTERS)
        back = dot_nt(grad, up[:, span(t)])
        total[...] = back if t == 0 else total[...] + back
    spread_blocks(info, partial, total[...])
    given[...] = grad_lifted[:, other_half(info, grad_lifted.shape[1])]


def middle_back_kernel(arrived, hidden, gain, returned, grad_hidden, mid, gain_grad):
    through, gain_grad[...] = norm_back(hidden[...], gain[1:2, :], total_of(arrived))
    values = returned[...].astype(f32) + through
    grad_hidden[...] = values
    mid[...] = values.astype(low16)


def global_attention_back_kernel(info, *rest):
    (blocks, packed, probs, own_qkv, other_qkv, own_out, other_out,
     rows, grads, given, partial, qkv, out, sems) = rest
    low, sec = info[LOW], info[SEC]
    made = Copies(sems)
    fetch_attention(made, low, sec, own_qkv, other_qkv, own_out, other_out, qkv, out)
    values = by_shard(info, blocks)
    rows[...] = values
    made.wait(QUARTERS)
    grad_mixed = dot_nt(values, out[...]).astype(low16)
    columns = [[], [], []]
    for h in range(packed.shape[2] // HEAD_DIM):
        lanes = slice(h * HEAD_DIM, (h + 1) * HEAD_DIM)
        exact = probs[h].astype(f32)
        grad = grad_mixed[:, lanes]
        columns[2].append(dot_tn(exact.astype(low16), grad).astype(low16))
        grad_probs = dot_nt(grad, packed[2, :, lanes])
        center = jnp.sum(grad_probs * exact, axis=-1, keepdims=True)
        grad_scores = (exact * (grad_probs - center)).astype(low16)
        columns[0].append((dot(grad_scores, packed[1, :, lanes]) * SCALE).astype(low16))
        columns[1].append((dot_tn(grad_scores, packed[0, :, lanes]) * SCALE).astype(low16))
    total = None
    made.wait(0, QUARTERS)
    for c in range(3):
        grads[c] = jnp.concatenate(columns[c], axis=1)
        back = dot_nt(grads[c], qkv[c])
        total = back if c == 0 else total + back
    spread_blocks(info, partial, total)
    given[...] = grads[:, :, other_half(info, grads.shape[2])]


def start_back_kernel(info, arrived, start, gain, grad_hidden, kept, given, gain_grad, values):
    low, sec = info[LOW], info[SEC]
    through, gain_grad[...] = norm_back(start[...], gain[0:1, :], total_of(arrived))
    values[...] = grad_hidden[...] + through
    for j in range(2):
        kept[:, span(j)] = values[:, pl.ds(block_at(low, 2 * sec + j), UNIT)]
        given[:, span(j)] = values[:, pl.ds(block_at(low, 2 * (1 - sec) + j), UNIT)]


def mix_unit(refs, k, m, u):
    whole, near, x_part, y_part, far = refs[0], refs[1:4], refs[4], refs[5], refs[6:8]
    if k == 0:
        return whole.at[m, u]
    if m == 0:
        return near[k - 1].at[u]
    if m == 3:
        return far[u].at[k - 1]
    return (x_part if m == 1 else y_part).at[u, k - 1]


def feed_unit(refs, k, m, u):
    if k == 0:
        return refs[0].at[m, u]
    if m < 3:
        return refs[1 + m].at[u]
    return refs[4].at[u] if u < 2 else refs[5].at[u - 2]


MIX_REFS, FEED_REFS = 8, 6


def pair_rows(a, b, size):
    return jnp.concatenate([a * b, a[size:] * b[: 2 * size], a[2 * size :] * b[:size]], axis=0)


def by_pair(stacked, size):
    names = [(0, 0), (1, 1), (2, 2), (1, 0), (2, 1), (2, 0)]
    return {name: stacked[n * size : (n + 1) * size] for n, name in enumerate(names)}


def from_pairs(pairs):
    names = [(0, 0), (1, 1), (2, 2), (1, 0), (2, 1), (2, 0)]
    return jnp.concatenate([pairs[name] for name in names], axis=0)


def head_sums(products, table):
    upper = products.astype(low16)
    lower = (products - upper.astype(f32)).astype(low16)
    return dot(upper, table) + dot(lower, table)


def head_table(width):
    row = lax.broadcasted_iota(jnp.int32, (width, width), 0) // HEAD_DIM
    column = lax.broadcasted_iota(jnp.int32, (width, width), 1) // HEAD_DIM
    return (row == column).astype(f32).astype(low16)


def gather_mix(weights, mix, k, half):
    for m in range(QUARTERS):
        begin = m * UNIT
        mix[k * half : (k + 1) * half, begin : begin + half] = weights[
            k, 1, begin : begin + half, half:
        ]
        mix[k * half : (k + 1) * half, begin + half : begin + UNIT] = weights[
            k, 1, begin + half : begin + UNIT, half:
        ]


def local_attention_kernel(info, codes, sent_own, sent_other, gain, *rest):
    refs, (start, first, query_keys, values_out, probs, mixed, partial, weights, mix, sems) = (
        rest[:MIX_REFS], rest[MIX_REFS:]
    )
    low, sec = info[LOW], info[SEC]
    made = Copies(sems)
    groups = []
    for k in range(4):
        groups.append(
            [
                made.start(mix_unit(refs, k, m, u), weights.at[k, u, span(m), :])
                for u in range(2)
                for m in range(QUARTERS)
            ]
        )
    utts, code_count, frames, _ = codes.shape
    for u in range(utts):
        sent = jnp.where(sec == u, sent_own[...], sent_other[...]).astype(f32)
        for c in range(code_count):
            row = (u * code_count + c) * frames
            for m in range(QUARTERS):
                code = codes[u, c, :, pl.ds(block_at(low, m), UNIT)].astype(f32)
                start[row : row + frames, span(m)] = sent[:, span(m)] + code
    values = start[...]
    first[...] = (values * factor_of(values) * gain[0:1, :]).astype(low16)
    half = values_out.shape[2]
    table = head_table(half)
    rows = first[...]
    size = frames
    group = code_count * frames
    for k in range(4):
        for copy in groups[k]:
            copy.wait()
        query_keys[k] = dot(rows, weights[k, 0]).astype(low16)
        values_out[k] = dot(rows, weights[k, 1, :, :half]).astype(low16)
        gather_mix(weights, mix, k, half)
        for u in range(utts):
            at = slice(u * group, (u + 1) * group)
            q = query_keys[k, at, :half].astype(f32)
            key = query_keys[k, at, half:].astype(f32)
            val = values_out[k, at, :].astype(f32)
            scores = by_pair(head_sums(pair_rows(q, key, size), table) * SCALE, size)
            exact = {}
            for i in range(3):
                peak = scores[(i, 0)]
                for j in range(1, i + 1):
                    peak = jnp.maximum(peak, scores[(i, j)])
                raised = [jnp.exp(scores[(i, j)] - peak) for j in range(i + 1)]
                whole = raised[0]
                for j in range(1, i + 1):
                    whole = whole + raised[j]
                for j in range(i + 1):
                    exact[(i, j)] = raised[j] / whole
            probs[k, u] = from_pairs(exact).astype(low16)
            for i in range(3):
                total = None
                for j in range(i + 1):
                    weight = exact[(i, j)].astype(low16).astype(f32)
                    term = weight * val[j * size : (j + 1) * size]
                    total = term if total is None else total + term
                begin = u * group + i * size
                mixed[begin : begin + size, k * half : (k + 1) * half] = total.astype(low16)
    partial[...] = dot(mixed[...], mix[...]).astype(low16)


def local_top_kernel(info, cotangent, top, given):
    low, sec = info[LOW], info[SEC]
    utts, code_count, frames, _ = cotangent.shape
    group = code_count * frames
    frame_at = lax.broadcasted_iota(jnp.int32, (frames, 1), 0) + info[SHARD] * frames
    for u in range(utts):
        valid = frame_at < info[LENGTHS + u]
        for c in range(code_count):
            row = u * group + c * frames
            for m in range(QUARTERS):
                part = cotangent[u, c, :, pl.ds(block_at(low, m), UNIT)].astype(f32)
                top[row : row + frames, span(m)] = jnp.where(valid, part, 0.0).astype(low16)
    given[...] = top[pl.ds(pl.multiple_of(sec * group, group), group), :]


def local_norm_kernel(info, start, own_part, other_part, gain, hidden, second, given):
    values = start[...] + (own_part[...].astype(f32) + other_part[...].astype(f32))
    hidden[...] = values
    second[...] = (values * factor_of(values) * gain[1:2, :]).astype(low16)
    group = given.shape[0]
    given[...] = second[pl.ds(pl.multiple_of(info[SEC] * group, group), group), :]


def feed_tiles(refs, second, top, active, grad_lifted, up, down, back, sems):
    tiles = active.shape[0]
    made = Copies(sems)
    for t in range(tiles):
        for m in range(QUARTERS):
            made.start(feed_unit(refs, t // 2, m, t % 2), up.at[t, span(m), :])
        for m in range(QUARTERS):
            made.start(feed_unit(refs, t // 2, m, 2 + t % 2), down.at[t, :, span(m)])
    back[...] = jnp.zeros_like(back)

    @pl.loop(0, tiles)
    def _(t):
        for m in range(QUARTERS):
            pltpu.make_async_copy(
                refs[0].at[0, 0], up.at[t, span(m), :], sems.at[8 * t + m]
            ).wait()
        for m in range(QUARTERS):
            pltpu.make_async_copy(
                refs[0].at[0, 0], down.at[t, :, span(m)], sems.at[8 * t + 4 + m]
            ).wait()
        tile = dot(second[...], up[t])
        cdf = normal_cdf(tile)
        active[t] = (tile * cdf).astype(low16)
        grad = (dot_nt(top[...], down[t]) * gelu_slope(tile, cdf)).astype(low16)
        grad_lifted[t] = grad
        back[...] += dot_nt(grad, up[t])


def local_feed_kernel(second, top, *rest):
    refs, (active, grad_lifted, grad_second, up, down, back, sems) = (
        rest[:FEED_REFS], rest[FEED_REFS:]
    )
    feed_tiles(refs, second, top, active, grad_lifted, up, down, back, sems)
    grad_second[...] = back[...].astype(low16)


def far_feed_kernel(second_same, second_cross, top_same, top_cross, *rest):
    refs = rest[:FEED_REFS]
    (active, grad_lifted, second, top, same, cross, up, down, back, sems) = rest[FEED_REFS:]
    group = same.shape[0]
    second[:group] = second_same[...]
    second[group:] = second_cross[...]
    top[:group] = top_same[...]
    top[group:] = top_cross[...]
    feed_tiles(refs, second, top, active, grad_lifted, up, down, back, sems)
    same[...] = back[:group].astype(low16)
    cross[...] = back[group:].astype(low16)


def pair_kernel(a, b, total):
    total[...] = add16(a[...], b[...])


def with_far(sec, rows, own, other, far_same, far_cross):
    group = far_same.shape[0]
    parts = []
    for u in range(rows // group):
        at = slice(u * group, (u + 1) * group)
        far = jnp.where(sec == u, far_same[...], far_cross[...]).astype(f32)
        parts.append(own[at, :].astype(f32) + other[at, :].astype(f32) + far)
    return jnp.concatenate(parts, axis=0)


def local_attention_back_kernel(info, hidden, own_back, other_back, far_same, far_cross, top, gain,
                                query_keys, values_in, probs, *rest):
    refs = rest[:MIX_REFS]
    (grad_hidden, mid, grad_query_keys, grad_values, grad_first, gain_grad,
     weights, mix, total, sems) = rest[MIX_REFS:]
    made = Copies(sems)
    groups = []
    for k in range(4):
        groups.append(
            [
                made.start(mix_unit(refs, k, m, u), weights.at[k, u, span(m), :])
                for u in range(2)
                for m in range(QUARTERS)
            ]
        )
    upstream = with_far(info[SEC], hidden.shape[0], own_back, other_back, far_same, far_cross)
    through, gain_grad[...] = norm_back(hidden[...], gain[1:2, :], upstream)
    grads = top[...].astype(f32) + through
    grad_hidden[...] = grads
    mid[...] = grads.astype(low16)
    utts = probs.shape[1]
    half = values_in.shape[2]
    group = query_keys.shape[1] // utts
    size = group // 3
    table = head_table(half)
    for k in range(4):
        for copy in groups[k]:
            copy.wait()
        gather_mix(weights, mix, k, half)
        grad_mixed = dot_nt(mid[...], mix[k * half : (k + 1) * half, :]).astype(low16)
        grad_mixed = grad_mixed.astype(f32)
        for u in range(utts):
            at = slice(u * group, (u + 1) * group)
            q = query_keys[k, at, :half].astype(f32)
            key = query_keys[k, at, half:].astype(f32)
            val = values_in[k, at, :].astype(f32)
            grad = grad_mixed[at]
            exact = by_pair(probs[k, u].astype(f32), size)
            grad_probs = by_pair(head_sums(pair_rows(grad, val, size), table), size)
            scored = {}
            for i in range(3):
                center = grad_probs[(i, 0)] * exact[(i, 0)]
                for j in range(1, i + 1):
                    center = center + grad_probs[(i, j)] * exact[(i, j)]
                for j in range(i + 1):
                    score = exact[(i, j)] * (grad_probs[(i, j)] - center)
                    scored[(i, j)] = score.astype(low16).astype(f32)

            def rows_of(array, n):
                return array[n * size : (n + 1) * size]

            for i in range(3):
                begin = u * group + i * size
                to_query = sum(scored[(i, j)] * rows_of(key, j) for j in range(i + 1))
                to_key = sum(scored[(n, i)] * rows_of(q, n) for n in range(i, 3))
                to_value = sum(
                    exact[(n, i)].astype(low16).astype(f32) * rows_of(grad, n)
                    for n in range(i, 3)
                )
                grad_query_keys[k, begin : begin + size, :half] = (to_query * SCALE).astype(low16)
                grad_query_keys[k, begin : begin + size, half:] = (to_key * SCALE).astype(low16)
                grad_values[k, begin : begin + size, :] = to_value.astype(low16)
        back = dot_nt(grad_query_keys[k], weights[k, 0])
        back = back + dot_nt(grad_values[k], weights[k, 1, :, :half])
        total[...] = back if k == 0 else total[...] + back
    grad_first[...] = total[...].astype(low16)


def local_end_kernel(info, own_back, other_back, start, grad_hidden, gain,
                     returned, code_part, gain_grad, values):
    low, sec = info[LOW], info[SEC]
    upstream = own_back[...].astype(f32) + other_back[...].astype(f32)
    through, gain_grad[...] = norm_back(start[...], gain[0:1, :], upstream)
    values[...] = grad_hidden[...] + through
    utts, code_count, frames, _ = code_part.shape
    total = None
    for c in range(code_count):
        begin = pl.multiple_of((sec * code_count + c) * frames, frames)
        part = values[pl.ds(begin, frames), :]
        total = part if total is None else total + part
    returned[...] = total.astype(low16)
    for u in range(utts):
        for c in range(code_count):
            row = (u * code_count + c) * frames
            for j in range(2):
                at = pl.ds(block_at(low, 2 * sec + j), UNIT)
                code_part[u, c, :, span(j)] = values[row : row + frames, at]


def output_kernel(info, hidden, own_part, other_part, far_same, far_cross, output):
    low, sec = info[LOW], info[SEC]
    utts, code_count, frames, _ = output.shape
    group = code_count * frames
    frame_at = lax.broadcasted_iota(jnp.int32, (frames, 1), 0) + info[SHARD] * frames
    for u in range(utts):
        valid = frame_at < info[LENGTHS + u]
        for c in range(code_count):
            rows = slice(u * group + c * frames, u * group + (c + 1) * frames)
            inner = slice(c * frames, (c + 1) * frames)
            for j in range(2):
                at = pl.ds(block_at(low, 2 * sec + j), UNIT)
                far = jnp.where(sec == u, far_same[inner, at], far_cross[inner, at])
                value = hidden[rows, at] + (
                    own_part[rows, at].astype(f32)
                    + other_part[rows, at].astype(f32)
                    + far.astype(f32)
                )
                output[u, c, :, span(j)] = jnp.where(valid, value, 0.0).astype(low16)


SEND_A, KEEP_A, SEND_B, KEEP_B = (1, 3), (0, 2), (2, 3), (0, 1)


def local_drop_kernel(own_active, far_active, *rest):
    refs, (own_branch, same, cross, down, branch, sems) = rest[:FEED_REFS], rest[FEED_REFS:]
    tiles, count, _ = own_active.shape
    made = Copies(sems)
    for t in range(tiles):
        for m in range(QUARTERS):
            made.start(feed_unit(refs, t // 2, m, 2 + t % 2), down.at[t, :, span(m)])
    branch[...] = jnp.zeros_like(branch)

    @pl.loop(0, tiles)
    def _(t):
        for m in range(QUARTERS):
            pltpu.make_async_copy(
                refs[0].at[0, 0], down.at[t, :, span(m)], sems.at[QUARTERS * t + m]
            ).wait()
        branch[:count] += dot(own_active[t], down[t])
        branch[count:] += dot(far_active[t], down[t])

    own_branch[...] = branch[:count].astype(low16)
    group = same.shape[0]
    same[...] = branch[count : count + group].astype(low16)
    cross[...] = branch[count + group :].astype(low16)


def local_feed_grad_kernel(second, far_second, own_lifted, far_lifted, own_active, far_active,
                           top, far_top, send_a, send_b, keep_a, keep_b, turned, tops):
    count = second.shape[0]
    turned[:, :count] = jnp.transpose(second[...])
    turned[:, count:] = jnp.transpose(far_second[...])
    tops[:count] = top[...]
    tops[count:] = far_top[...]
    for k in range(2):
        for part, pairs in enumerate(
            (((send_a, SEND_A), (keep_a, KEEP_A)), ((send_b, SEND_B), (keep_b, KEEP_B)))
        ):
            t = 2 * k + part
            right = jnp.concatenate([own_lifted[t], far_lifted[t]], axis=0)
            left = jnp.concatenate(
                [jnp.transpose(own_active[t]), jnp.transpose(far_active[t])], axis=1
            )
            for target, order in pairs:
                for place, m in enumerate(order):
                    target[place, 2 * k] = dot(turned[span(m), :], right).astype(low16)
                    target[place, 2 * k + 1] = dot(left, tops[:, span(m)]).astype(low16)


def local_mix_kernel(first, grad_query_keys, grad_values, mixed, mid,
                     send_a, send_b, keep_a, keep_b, turned):
    turned[...] = jnp.transpose(first[...])
    half = grad_values.shape[2]
    for k in range(4):
        left = jnp.transpose(mixed[:, k * half : (k + 1) * half])
        for target, order in ((send_a, SEND_A), (keep_a, KEEP_A)):
            for place, m in enumerate(order):
                target[place, k] = dot(turned[span(m), :], grad_query_keys[k]).astype(low16)
        for target, order in ((send_b, SEND_B), (keep_b, KEEP_B)):
            for place, m in enumerate(order):
                value = dot(turned[span(m), :], grad_values[k]).astype(low16)
                out = dot(left, mid[:, span(m)]).astype(low16)
                target[place, k, :, :half] = value
                target[place, k, :half, half:] = out[:, :half]
                target[place, k, half:, half:] = out[:, half:]


def by_order(send_a, send_b, keep_a, keep_b):
    return (
        (0, ((send_a, SEND_A), (keep_a, KEEP_A))),
        (1, ((send_b, SEND_B), (keep_b, KEEP_B))),
    )


def global_feed_grad_kernel(info, second, far_second, grad_lifted, far_lifted, active, far_active,
                            top, far_top, send_a, send_b, keep_a, keep_b, turned, tops):
    sec, count = info[SEC], second.shape[0]
    turned[:, :count] = jnp.transpose(second[...])
    turned[:, count:] = jnp.transpose(far_second[...])
    tops[:count] = top[...]
    tops[count:] = far_top[...]
    wide = active.shape[1] // 2
    for part, pairs in by_order(send_a, send_b, keep_a, keep_b):
        at = pl.ds(pl.multiple_of(sec * wide + part * UNIT, UNIT), UNIT)
        right = jnp.concatenate([grad_lifted[:, at], far_lifted[:, span(part)]], axis=0)
        left = jnp.concatenate(
            [jnp.transpose(active[:, at]), jnp.transpose(far_active[:, span(part)])], axis=1
        )
        for target, order in pairs:
            for place, m in enumerate(order):
                target[place, 0] = dot(turned[span(m), :], right).astype(low16)
                target[place, 1] = dot(left, tops[:, span(m)]).astype(low16)


def global_mix_grad_kernel(info, first, far_first, grads, far_grads, mixed, far_mixed, mid,
                           far_mid, send_a, send_b, keep_a, keep_b, turned, mids):
    sec, count = info[SEC], first.shape[0]
    turned[:, :count] = jnp.transpose(first[...])
    turned[:, count:] = jnp.transpose(far_first[...])
    mids[:count] = mid[...]
    mids[count:] = far_mid[...]
    width = mixed.shape[1] // 2
    at = pl.ds(pl.multiple_of(sec * width, width), width)
    right = [jnp.concatenate([grads[c, :, at], far_grads[c]], axis=0) for c in range(3)]
    left = jnp.concatenate([jnp.transpose(mixed[:, at]), jnp.transpose(far_mixed[...])], axis=1)
    for part, pairs in by_order(send_a, send_b, keep_a, keep_b):
        for target, order in pairs:
            for place, m in enumerate(order):
                rows = turned[span(m), :]
                if part == 0:
                    for c in range(2):
                        target[place, 0, :, c * width : (c + 1) * width] = dot(
                            rows, right[c]
                        ).astype(low16)
                else:
                    target[place, 0, :, :width] = dot(rows, right[2]).astype(low16)
                    out = dot(left, mids[:, span(m)]).astype(low16)
                    target[place, 0, :width, width:] = out[:, :width]
                    target[place, 0, width:, width:] = out[:, width:]


def add16(a, b):
    return (a.astype(f32) + b.astype(f32)).astype(low16)


def far_kernel(keep_a, from_x, keep_b, from_y, far_a, far_b):
    far_a[...] = add16(keep_a[0], from_x[0])
    far_b[...] = add16(keep_b[0], from_y[0])


def sum_kernel(shards, *refs):
    parts, outs = (refs[:3], refs[3:6]), refs[6:]
    for part, (keep, once, twice) in enumerate(parts):
        total = keep[0].astype(f32) + once[0].astype(f32) + twice[...].astype(f32)
        total = total.astype(low16)
        count = total.shape[0] // shards
        at = slice(part * count, (part + 1) * count)
        if shards == 1:
            outs[0][at] = total
        elif shards == 2:
            outs[1][0, at] = total[:count]
            outs[0][0, at] = total[count:]
        else:
            for k in range(4):
                outs[(k + 1) % 2][k // 2, at] = total[k * count : (k + 1) * count]


def far_tensor_kernel(keep, arrived, far):
    far[...] = add16(keep[0], arrived[0])


def pick_kernel(info, *refs):
    *terms, world, given, kept = refs
    sec = info[SEC]
    local = terms[0][0].astype(f32)
    for term in terms[1:]:
        local = local + (term[0] if len(term.shape) == 4 else term[...]).astype(f32)
    local = local.astype(low16)
    other = world[...]
    given[...] = jnp.where(sec == 0, local, other)
    kept[...] = jnp.where(sec == 0, other, local)


def half_at(index, count):
    return pl.BlockSpec(
        (1, count, UNIT, UNIT), lambda i: (index, 0, 0, 0), memory_space=pltpu.VMEM
    )


def quarter_unit(refs, m, index):
    own, x_part, y_part, far_kept, far_arrived = refs
    count = own.shape[0] // 2
    if m < 3:
        return (own, x_part, y_part)[m][index].astype(f32)
    return (far_kept[index] if index < count else far_arrived[index - count]).astype(f32)


def write_feed(info, quarters, unit, count, up, down, rows, columns, sems):
    low, sec = info[LOW], info[SEC]
    wide = up.shape[1] // 2
    made = Copies(sems)
    for place, m in enumerate(quarters):
        at = pl.ds(block_at(low, m), UNIT)
        for source, half in ((0, sec), (count, 1 - sec)):
            for part in range(2):
                hidden = pl.ds(pl.multiple_of(half * wide + part * UNIT, UNIT), UNIT)
                rows[place, :, hidden] = unit(m, source + 2 * part)
                columns[place, hidden, :] = unit(m, source + 2 * part + 1)
        made.start(rows.at[place], up.at[at, :])
        made.start(columns.at[place], down.at[:, at])
    made.wait()


def feed_near_kernel(info, own, x_part, y_part, up, down, rows, columns, sems):
    parts = (own, x_part, y_part)
    write_feed(
        info, (0, 1, 2), lambda m, n: parts[m][n].astype(f32), own.shape[0] // 2,
        up, down, rows, columns, sems,
    )


def feed_far_kernel(info, far_kept, far_arrived, up_before, down_before,
                    up, down, rows, columns, sems):
    count = far_kept.shape[0]

    def unit(m, n):
        return (far_kept[n] if n < count else far_arrived[n - count]).astype(f32)

    write_feed(info, (3,), unit, count, up, down, rows, columns, sems)


def write_mix(info, quarters, unit, count, qkv, out, rows, columns, sems):
    low, sec = info[LOW], info[SEC]
    width = out.shape[0] // 2
    made = Copies(sems)
    for place, m in enumerate(quarters):
        at = pl.ds(block_at(low, m), UNIT)
        for source, half in ((0, sec), (count, 1 - sec)):
            lanes = pl.ds(pl.multiple_of(half * width, width), width)
            query_keys = unit(m, source)
            rows[place, 0, :, lanes] = query_keys[:, :width]
            rows[place, 1, :, lanes] = query_keys[:, width:]
            rest_unit = unit(m, source + 1)
            rows[place, 2, :, lanes] = rest_unit[:, :width]
            columns[place, lanes, :width] = rest_unit[:width, width:]
            columns[place, lanes, width:] = rest_unit[width:, width:]
        made.start(rows.at[place], qkv.at[:, at, :])
        made.start(columns.at[place], out.at[:, at])
    made.wait()


GAIN_ROWS = 32


def gain_pack_kernel(gain, packed):
    rows = []
    for g in range(gain.shape[0]):
        rest = gain[g : g + 1, :]
        for _ in range(3):
            part = rest.astype(low16).astype(f32)
            rest = rest - part
            rows += [part[:, span(m)] for m in range(QUARTERS)]
    rows.append(jnp.zeros((GAIN_ROWS - len(rows), UNIT), f32))
    packed[...] = jnp.concatenate(rows, axis=0).astype(low16)


def unit_rows(ref, n):
    return ref[n * UNIT : (n + 1) * UNIT, :].astype(f32)


def mix_near_kernel(info, own, x_part, y_part, qkv, out, rows, columns, sems):
    parts = (own, x_part, y_part)
    count = (own.shape[0] - GAIN_ROWS) // (2 * UNIT)
    write_mix(
        info, (0, 1, 2), lambda m, n: unit_rows(parts[m], n), count, qkv, out, rows, columns, sems
    )


def mix_far_kernel(info, own, x_part, y_part, far_kept, far_arrived, qkv_before, out_before,
                   qkv, out, gain, rows, columns, sems):
    count = far_kept.shape[0] // UNIT

    def unit(m, n):
        return unit_rows(far_kept, n) if n < count else unit_rows(far_arrived, n - count)

    total = None
    for ref in (own, x_part, y_part, far_arrived):
        part = ref[ref.shape[0] - GAIN_ROWS :, :].astype(f32)
        total = part if total is None else total + part
    for g in range(gain.shape[0]):
        for m in range(QUARTERS):
            at = [3 * QUARTERS * g + QUARTERS * t + m for t in range(3)]
            gain[g : g + 1, span(m)] = (
                total[at[0] : at[0] + 1] + total[at[1] : at[1] + 1] + total[at[2] : at[2] + 1]
            )
    write_mix(info, (3,), unit, count, qkv, out, rows, columns, sems)


def sum_rest(value):
    step = QUARTERS
    while step < lax.axis_size("dp"):
        value = add16(value, swap(value, "dp", step))
        step *= 2
    return value


class Sum:
    def __init__(self, order, shards, send_a, send_b, keep_a, keep_b):
        self.order, self.shards = order, shards
        self.keep = (keep_a, keep_b)
        self.count = keep_a.shape[1]
        self.once = (swap(send_a, "dp", 1), swap(send_b, "dp", 2))

    def second(self):
        far = half_at(1, self.count)
        far_a, far_b = self.order.call(
            far_kernel,
            [shape((self.count, UNIT, UNIT), low16)] * 2,
            (self.keep[0], self.once[0], self.keep[1], self.once[1]),
            [far] * 4,
            grid=(1,),
        )
        self.twice = (swap(far_a, "dp", 2), swap(far_b, "dp", 1))

    def third(self):
        count = 2 * self.count // self.shards
        if self.shards == 1:
            outs = [shape((count, UNIT, UNIT), low16)]
        else:
            outs = [shape((self.shards // 2, count, UNIT, UNIT), low16)] * 2
        near = half_at(0, self.count)
        totals = self.order.call(
            functools.partial(sum_kernel, self.shards),
            outs,
            (self.keep[0], self.once[0], self.twice[0], self.keep[1], self.once[1], self.twice[1]),
            [near, near, VM] * 2,
            grid=(1,),
        )
        totals = [sum_rest(total) for total in totals]
        self.count = count
        if self.shards == 1:
            return totals[0]
        self.keep = totals[1]
        if self.shards == 2:
            self.terms = (self.keep, swap(totals[0], "tensor", 2))
        else:
            self.once = swap(totals[0], "tensor", 1)

    def fourth(self):
        far = self.order.call(
            far_tensor_kernel,
            [shape((self.count, UNIT, UNIT), low16)],
            (self.keep, self.once),
            [half_at(1, self.count)] * 2,
            grid=(1,),
        )[0]
        self.terms = (self.keep, self.once, swap(far, "tensor", 2))

    def gathered(self, info, world, extra=None):
        near = half_at(0, self.count)
        given, kept = self.order.call(
            pick_kernel,
            [shape((self.count, UNIT, UNIT), low16)] * 2,
            (info,) + self.terms + (world,),
            [SM] + [near if term.ndim == 4 else VM for term in self.terms] + [VM],
            grid=(1,),
        )
        arrived = swap(given, "section", 1)
        if extra is None:
            return Gather(jnp.concatenate([kept, arrived]), self.count)
        rows = [kept.reshape(-1, UNIT), arrived.reshape(-1, UNIT), extra]
        return Gather(jnp.concatenate(rows), self.count * UNIT)


class Gather:
    def __init__(self, units, count):
        self.units, self.count = units, count
        self.near = (swap(units, "dp", 1), swap(units, "dp", 2))

    def far(self):
        x_part, y_part = self.near
        rest = (swap(x_part[: self.count], "dp", 2), swap(y_part[self.count :], "dp", 1))
        return (self.units,) + self.near + rest


def on_device(codes, lengths, gains, w_qkv, w_out, w_up, w_down, cotangent):
    sec = lax.axis_index("section")
    low = lax.axis_index("dp") % QUARTERS
    z = lax.axis_index("tensor")
    first_core = sec == 0
    utts, frames, code_count, width = codes.shape
    heads_width = w_out.shape[1]
    half = heads_width // 2
    wide = w_up.shape[2]
    rows_g = 4 * frames
    rows_l = utts * code_count * frames
    tiles = wide // UNIT
    info = jnp.concatenate([jnp.stack([low, sec, z]).astype(jnp.int32), lengths])
    order = Order()
    call = order.call

    code_rows = jnp.transpose(codes, (0, 2, 1, 3))
    cot_rows = jnp.transpose(cotangent, (0, 2, 1, 3))
    own_w = (jnp.transpose(w_qkv[0], (1, 0, 2)), w_out[0], w_up[0], w_down[0])

    def sem(count):
        return pltpu.SemaphoreType.DMA((count,))

    def gather(rows):
        gathered = lax.all_gather(rows, "tensor")
        order.tokens = (gathered,)
        return gathered

    def scatter(partial):
        return lax.all_to_all(partial, "tensor", 0, 0)

    other_gain = swap(gains[0], "section", 1)
    own_w, other_gain = lax.optimization_barrier((own_w, other_gain))

    def with_other(weights):
        return tuple(w for own in weights for w in (own, swap(own, "section", 1)))

    attention_w = with_other(own_w[:2])

    first_rows, start_g, gain_g, gain_l = call(
        start_kernel,
        [
            shape((frames, width), low16),
            shape((frames, width), f32),
            shape((2, width), f32),
            shape((2, width), f32),
        ],
        (info, code_rows, gains[0], other_gain),
        [SM, VM, VM, VM],
        us=2,
    )
    first_rows, *attention_w = lax.optimization_barrier((first_rows,) + attention_w)
    attention_w = tuple(attention_w)
    first_blocks = gather(first_rows)
    feed_w = with_other(order.after(own_w[2:]))

    first_g, packed_g, probs_g, mixed_g, mixed_given, partial = call(
        global_attention_kernel,
        [
            shape((rows_g, width), low16),
            shape((3, rows_g, heads_width), low16),
            shape((heads_width // HEAD_DIM, rows_g, rows_g), low16),
            shape((rows_g, heads_width), low16),
            shape((rows_g, half), low16),
            shape((4, frames, width), low16),
        ],
        (info, first_blocks) + attention_w,
        [SM, VM] + [ANY] * 4,
        [
            pltpu.VMEM((3, width, heads_width), low16),
            pltpu.VMEM((heads_width, width), low16),
            sem(8),
        ],
        us=5.7,
        limit=60,
    )
    arrived = scatter(partial)
    mix_piece, mix_whole = call(
        mix_piece_kernel,
        [shape((2, UNIT, UNIT), low16), shape((QUARTERS, 2, UNIT, UNIT), low16)],
        (info,) + attention_w,
        [SM] + [ANY] * 4,
        [sem(5 * QUARTERS)],
        us=3.2,
    )
    mix_z1 = swap(mix_piece, "tensor", 1)
    mix_z2 = swap(mix_piece, "tensor", 2)
    feed_piece, feed_whole = call(
        feed_piece_kernel,
        [shape((4, UNIT, UNIT), low16), shape((QUARTERS, 4, UNIT, UNIT), low16)],
        (info,) + feed_w,
        [SM] + [ANY] * 4,
        [sem(4 * QUARTERS)],
        us=4,
    )
    top_l, top_given = call(
        local_top_kernel,
        [shape((rows_l, width), low16), shape((rows_l // utts, width), low16)],
        (info, cot_rows),
        [SM, VM],
        us=2.3,
    )
    hidden_g, second_rows = call(
        middle_kernel,
        [shape((frames, width), f32), shape((frames, width), low16)],
        (start_g, arrived, gain_g),
        [VM] * 3,
        us=2,
    )
    second_rows, mix_z1, mix_z2, feed_piece = lax.optimization_barrier(
        (second_rows, mix_z1, mix_z2, feed_piece)
    )
    mix_z3 = swap(mix_z2, "tensor", 1)
    second_blocks = gather(second_rows)
    feed_z2 = swap(order.after(feed_piece), "tensor", 2)
    order.until(mix_z3)
    second_g, lifted_g, active_g, active_given, partial = call(
        global_feed_kernel,
        [
            shape((rows_g, width), low16),
            shape((rows_g, wide), f32),
            shape((rows_g, wide), low16),
            shape((rows_g, wide // 2), low16),
            shape((4, frames, width), low16),
        ],
        (info, second_blocks) + feed_w,
        [SM, VM] + [ANY] * 4,
        [
            pltpu.VMEM((width, wide), low16),
            pltpu.VMEM((wide, width), low16),
            pltpu.VMEM((rows_g, width), f32),
            sem(8),
        ],
        us=5.6,
        limit=60,
    )
    arrived = scatter(partial)
    mix_near = jnp.stack(order.after([mix_z1, mix_z2, mix_z3]), axis=1)
    mix_x = swap(mix_near, "dp", 1)
    mix_y = swap(mix_near, "dp", 2)
    mix_far = (swap(mix_x[0], "dp", 2), swap(mix_y[1], "dp", 1))
    order.until(*mix_far, feed_z2)
    sent = call(
        sent_kernel,
        [shape((frames, width), low16)],
        (hidden_g, arrived),
        [VM] * 2,
        us=1.9,
    )[0]
    other_sent = swap(sent, "section", 1)
    mix_w = (mix_whole, mix_z1, mix_z2, mix_z3, mix_x, mix_y) + mix_far
    feed_z2 = order.after(feed_z2)
    feed_x = swap(feed_z2, "dp", 1)
    feed_y = swap(feed_z2, "dp", 2)
    top_same = swap(order.after(top_given), "tensor", 1)

    start_l, first_l, query_keys, values_l, probs_l, mixed_l, partial = call(
        local_attention_kernel,
        [
            shape((rows_l, width), f32),
            shape((rows_l, width), low16),
            shape((4, rows_l, 2 * half), low16),
            shape((4, rows_l, half), low16),
            shape((4, utts, 2 * rows_l // utts, half), low16),
            shape((rows_l, 4 * half), low16),
            shape((rows_l, width), low16),
        ],
        (info, code_rows, sent, other_sent, gain_l) + mix_w,
        [SM] + [VM] * 4 + [ANY] * MIX_REFS,
        [
            pltpu.VMEM((4, 2, width, UNIT), low16),
            pltpu.VMEM((4 * half, width), low16),
            sem(32),
        ],
        us=9,
        limit=60,
    )
    partial, feed_x, feed_y, top_same = lax.optimization_barrier(
        (partial, feed_x, feed_y, top_same)
    )
    feed_l = (
        feed_whole,
        feed_z2,
        feed_x,
        feed_y,
        swap(feed_x[:2], "dp", 2),
        swap(feed_y[2:], "dp", 1),
    )
    hidden_l, second_l, second_given = call(
        local_norm_kernel,
        [
            shape((rows_l, width), f32),
            shape((rows_l, width), low16),
            shape((rows_l // utts, width), low16),
        ],
        (info, start_l, partial, swap(partial, "section", 1), gain_l),
        [SM] + [VM] * 4,
        us=3.7,
    )
    second_same = swap(second_given, "tensor", 1)
    top_cross = swap(top_same, "section", 1)
    feed_scratch = [
        pltpu.VMEM((tiles, width, UNIT), low16),
        pltpu.VMEM((tiles, UNIT, width), low16),
        pltpu.VMEM((rows_l, width), f32),
        sem(8 * tiles),
    ]
    wide_rows = shape((rows_l, width), low16)
    half_rows = shape((rows_l // utts, width), low16)
    tiled_rows = shape((tiles, rows_l, UNIT), low16)
    active_l, grad_lifted_l, back = call(
        local_feed_kernel,
        [tiled_rows, tiled_rows, wide_rows],
        (second_l, top_l) + feed_l,
        [VM] * 2 + [ANY] * FEED_REFS,
        feed_scratch,
        us=7.9,
    )
    other_back = swap(back, "section", 1)
    second_same = order.after(second_same)
    second_cross = swap(second_same, "section", 1)
    far_active, far_lifted, far_second, far_top, same, cross = call(
        far_feed_kernel,
        [tiled_rows, tiled_rows, wide_rows, wide_rows, half_rows, half_rows],
        (second_same, second_cross, top_same, top_cross) + feed_l,
        [VM] * 4 + [ANY] * FEED_REFS,
        feed_scratch,
        us=8.2,
    )

    def from_neighbour(same, cross):
        total = call(
            pair_kernel, [half_rows], (same, cross), [VM] * 2
        )[0]
        return swap(total, "tensor", 1)

    far_same = from_neighbour(same, swap(cross, "section", 1))
    turned_l = pltpu.VMEM((width, rows_l), low16)
    local_feed = Sum(
        order,
        2,
        *call(
            local_feed_grad_kernel,
            [shape((2, 4, UNIT, UNIT), low16)] * 4,
            (
                second_l, far_second, grad_lifted_l, far_lifted, active_l, far_active, top_l,
                far_top,
            ),
            [VM] * 8,
            [pltpu.VMEM((width, 2 * rows_l), low16), pltpu.VMEM((2 * rows_l, width), low16)],
            us=7.6,
        ),
    )
    own_branch, branch_same, branch_cross = call(
        local_drop_kernel,
        [wide_rows, half_rows, half_rows],
        (active_l, far_active) + feed_l,
        [VM] * 2 + [ANY] * FEED_REFS,
        [
            pltpu.VMEM((tiles, UNIT, width), low16),
            pltpu.VMEM((2 * rows_l, width), f32),
            sem(QUARTERS * tiles),
        ],
        us=6.1,
    )
    branch_cross = swap(branch_cross, "section", 1)
    other_branch = swap(own_branch, "section", 1)
    far_same = order.after(far_same)
    far_back = (far_same, swap(far_same, "section", 1))
    far_branch = from_neighbour(branch_same, branch_cross)
    far_first, far_mixed, far_second_g, far_active_g = (
        swap(order.after(value), "section", 1)
        for value in (first_g, mixed_given, second_g, active_given)
    )
    grad_hidden_l, mid_l, grad_query_keys, grad_values, back, gain2_l = call(
        local_attention_back_kernel,
        [
            shape((rows_l, width), f32),
            shape((rows_l, width), low16),
            shape((4, rows_l, 2 * half), low16),
            shape((4, rows_l, half), low16),
            shape((rows_l, width), low16),
            shape((1, width), f32),
        ],
        (info, hidden_l, back, other_back)
        + far_back
        + (top_l, gain_l, query_keys, values_l, probs_l)
        + mix_w,
        [SM] + [VM] * 10 + [ANY] * MIX_REFS,
        [
            pltpu.VMEM((4, 2, width, UNIT), low16),
            pltpu.VMEM((4 * half, width), low16),
            pltpu.VMEM((rows_l, width), f32),
            sem(32),
        ],
        us=11.4,
    )
    other_back = swap(back, "section", 1)
    local_mix = Sum(
        order,
        4,
        *call(
            local_mix_kernel,
            [shape((2, 4, UNIT, UNIT), low16)] * 4,
            (first_l, grad_query_keys, grad_values, mixed_l, mid_l),
            [VM] * 5,
            [turned_l],
            us=6,
        ),
    )
    local_feed.second()
    returned, code_part, gain1_l = call(
        local_end_kernel,
        [
            shape((frames, width), low16),
            shape((utts, code_count, frames, width // 2), f32),
            shape((1, width), f32),
        ],
        (info, back, other_back, start_l, grad_hidden_l, gain_l),
        [SM] + [VM] * 5,
        [pltpu.VMEM((rows_l, width), f32)],
        us=4.4,
    )

    top_blocks = gather(returned)
    order.until(*local_mix.once, far_first, far_mixed, far_second_g, far_active_g)
    top_g, grad_lifted_g, lifted_given, partial = call(
        global_feed_back_kernel,
        [
            shape((rows_g, width), low16),
            shape((rows_g, wide), low16),
            shape((rows_g, wide // 2), low16),
            shape((4, frames, width), low16),
        ],
        (info, top_blocks, lifted_g) + feed_w,
        [SM] + [VM] * 2 + [ANY] * 4,
        [
            pltpu.VMEM((width, wide), low16),
            pltpu.VMEM((wide, width), low16),
            pltpu.VMEM((rows_g, width), f32),
            sem(8),
        ],
        us=6.3,
        limit=60,
    )
    arrived = scatter(partial)
    far_top_g, far_lifted_g = swap(top_g, "section", 1), swap(lifted_given, "section", 1)
    local_feed.third()
    local_mix.second()
    far_branch = order.after(far_branch)
    far_branch = (far_branch, swap(far_branch, "section", 1))
    global_feed = Sum(
        order,
        1,
        *call(
            global_feed_grad_kernel,
            [shape((2, 2, UNIT, UNIT), low16)] * 4,
            (
                info, second_g, far_second_g, grad_lifted_g, far_lifted_g, active_g, far_active_g,
                top_g, far_top_g,
            ),
            [SM] + [VM] * 8,
            [pltpu.VMEM((width, 2 * rows_g), low16), pltpu.VMEM((2 * rows_g, width), low16)],
            us=3.5,
        ),
    )
    grad_hidden_g, mid_rows, gain2_g = call(
        middle_back_kernel,
        [shape((frames, width), f32), shape((frames, width), low16), shape((1, width), f32)],
        (arrived, hidden_g, gain_g, returned),
        [VM] * 4,
        us=2.1,
    )
    mid_blocks = gather(mid_rows)
    order.until(*local_mix.twice)
    mid_g, grads_g, grads_given, partial = call(
        global_attention_back_kernel,
        [
            shape((rows_g, width), low16),
            shape((3, rows_g, heads_width), low16),
            shape((3, rows_g, half), low16),
            shape((4, frames, width), low16),
        ],
        (info, mid_blocks, packed_g, probs_g) + attention_w,
        [SM] + [VM] * 3 + [ANY] * 4,
        [
            pltpu.VMEM((3, width, heads_width), low16),
            pltpu.VMEM((heads_width, width), low16),
            sem(8),
        ],
        us=6.8,
        limit=60,
    )
    arrived = scatter(partial)
    far_mid_g, far_grads_g = swap(mid_g, "section", 1), swap(grads_given, "section", 1)
    global_feed.second()
    local_mix.third()
    global_mix = Sum(
        order,
        1,
        *call(
            global_mix_grad_kernel,
            [shape((2, 1, UNIT, UNIT), low16)] * 4,
            (
                info, first_g, far_first, grads_g, far_grads_g, mixed_g, far_mixed, mid_g,
                far_mid_g,
            ),
            [SM] + [VM] * 8,
            [pltpu.VMEM((width, 2 * rows_g), low16), pltpu.VMEM((2 * rows_g, width), low16)],
            us=3,
        ),
    )
    output = call(
        output_kernel,
        [shape((utts, code_count, frames, width // 2), low16)],
        (info, hidden_l, own_branch, other_branch) + far_branch,
        [SM] + [VM] * 5,
        us=3.1,
    )[0]
    kept_start, given_start, gain1_g = call(
        start_back_kernel,
        [
            shape((frames, width // 2), f32),
            shape((frames, width // 2), f32),
            shape((1, width), f32),
        ],
        (info, arrived, start_g, gain_g, grad_hidden_g),
        [SM] + [VM] * 4,
        [pltpu.VMEM((frames, width), f32)],
        us=2.1,
    )
    world_feed = global_feed.third()
    global_mix.second()
    local_mix.fourth()
    world_mix = global_mix.third()
    feed_sum = local_feed.gathered(info, world_feed)
    arrived_start = swap(given_start, "section", 1)
    both_start = jnp.stack(
        [
            jnp.where(first_core, kept_start, arrived_start),
            jnp.where(first_core, arrived_start, kept_start),
        ]
    )
    code_grad = jnp.transpose(code_part + both_start[:, None], (0, 2, 1, 3))

    own_gain = jnp.concatenate([gain1_g, gain2_g], axis=0)
    total_gain = own_gain + swap(own_gain, "section", 1)
    local_gain = jnp.concatenate([gain1_l, gain2_l], axis=0)
    gain_total = jnp.where(first_core, total_gain, local_gain)
    gain_total = jnp.concatenate(
        [
            lax.dynamic_slice_in_dim(gain_total, (low ^ m) * UNIT, UNIT, 1)
            for m in range(QUARTERS)
        ],
        axis=1,
    )
    def over(value, axis):
        copies = jnp.broadcast_to(value, (lax.axis_size(axis),) + value.shape)
        return jnp.sum(lax.all_to_all(order.after(copies), axis, 0, 0), axis=0)

    gain_total = over(gain_total, "tensor")
    order.until(gain_total)
    packed_gain = call(
        gain_pack_kernel, [shape((GAIN_ROWS, UNIT), low16)], (gain_total,), [VM], us=0.7
    )[0]
    mix_sum = local_mix.gathered(info, world_mix, packed_gain)
    order.until(*feed_sum.near)
    feed_parts = feed_sum.far()
    def finals(count, rows, columns):
        return [
            pltpu.VMEM((count,) + rows, f32), pltpu.VMEM((count,) + columns, f32), sem(2 * count)
        ]

    feed_shapes = [shape((width, wide), f32), shape((wide, width), f32)]
    mix_shapes = [shape((3, width, heads_width), f32), shape((heads_width, width), f32)]
    feed_part = ((UNIT, wide), (wide, UNIT))
    mix_part = ((3, UNIT, heads_width), (heads_width, UNIT))
    feed_grads = call(
        feed_near_kernel,
        feed_shapes,
        (info,) + feed_parts[:3],
        [SM] + [VM] * 3,
        finals(3, *feed_part),
        us=5,
        place=ANY,
    )
    mix_sum.near = order.after(mix_sum.near)
    mix_parts = mix_sum.far()
    mix_grads = call(
        mix_near_kernel,
        mix_shapes,
        (info,) + mix_parts[:3],
        [SM] + [VM] * 3,
        finals(3, *mix_part),
        us=3,
        place=ANY,
    )
    up_grad, down_grad = call(
        feed_far_kernel,
        feed_shapes,
        (info,) + feed_parts[3:] + tuple(feed_grads),
        [SM] + [VM] * 2 + [ANY] * 2,
        finals(1, *feed_part),
        us=2,
        place=ANY,
        aliases=((3, 0), (4, 1)),
    )
    qkv_grad, out_grad, gain_total = call(
        mix_far_kernel,
        mix_shapes + [shape((2, width), f32)],
        (info,) + mix_parts + tuple(mix_grads),
        [SM] + [VM] * 5 + [ANY] * 2,
        finals(1, *mix_part),
        us=1.5,
        place=(ANY, ANY, VM),
        aliases=((6, 0), (7, 1)),
    )
    step = QUARTERS
    while step < lax.axis_size("dp"):
        gain_total = gain_total + swap(gain_total, "dp", step)
        step *= 2
    return (
        jnp.transpose(output, (0, 2, 1, 3)),
        code_grad,
        gain_total[None],
        jnp.transpose(qkv_grad, (1, 0, 2))[None],
        out_grad[None],
        up_grad[None],
        down_grad[None],
    )


def solution(mesh):
    in_specs = (
        P("dp", "tensor", None, None),
        P("dp"),
        P("section", None, None),
        P("section", None, None, "tensor"),
        P("section", "tensor", None),
        P("section", None, "tensor"),
        P("section", "tensor", None),
        P("dp", "tensor", None, None),
    )
    out_specs = (
        P("dp", "tensor", None, "section"),
        P("dp", "tensor", None, "section"),
        P("section", None, None),
        P("section", None, None, "tensor"),
        P("section", "tensor", None),
        P("section", None, "tensor"),
        P("section", "tensor", None),
    )
    return jax.shard_map(
        on_device, mesh=mesh, in_specs=in_specs, out_specs=out_specs, check_vma=False
    )
```

```python
import functools

import jax
import jax.numpy as jnp
from jax import lax
from jax.experimental import pallas as pl
from jax.experimental.pallas import tpu as pltpu
from jax.sharding import PartitionSpec as P

HEAD_DIM = 64
SCALE = HEAD_DIM ** (-0.5)
QUARTERS = 4
UNIT = 256
epsilon = 1e-06
negative = -1e30
f32 = jnp.float32
low16 = jnp.bfloat16

VM = pl.BlockSpec(memory_space=pltpu.VMEM)
SM = pl.BlockSpec(memory_space=pltpu.SMEM)
ANY = pl.BlockSpec(memory_space=pltpu.HBM)
MIB = 1 << 20
PACE = 0

LOW, SEC, SHARD, LENGTHS = 0, 1, 2, 3


def shape(dims, dtype):
    return jax.ShapeDtypeStruct(tuple(dims), dtype)


class Order:
    def __init__(self):
        self.tokens = ()

    def after(self, value):
        if not self.tokens:
            return value
        return lax.optimization_barrier((value,) + self.tokens)[0]

    def until(self, *values):
        self.tokens += values

    def call(self, body, outs, args, specs, scratch=(), limit=28, us=2.0, grid=(), place=VM, aliases=()):
        args = (self.after(args[0]),) + tuple(args[1:])
        results = pl.pallas_call(
            body,
            out_shape=tuple(outs),
            grid=grid,
            in_specs=list(specs),
            out_specs=place if isinstance(place, tuple) else (place,) * len(outs),
            input_output_aliases=dict(aliases),
            scratch_shapes=list(scratch),
            compiler_params=pltpu.CompilerParams(vmem_limit_bytes=limit * MIB),
            cost_estimate=pl.CostEstimate(
                flops=int(us * PACE), bytes_accessed=0, transcendentals=0
            ),
        )(*args)
        self.tokens = (results[-1],)
        return results


def swap(value, axis, flip):
    count = lax.axis_size(axis)
    return lax.ppermute(value, axis, [(i, i ^ flip) for i in range(count)])


def dot(a, b):
    return jnp.dot(a, b, preferred_element_type=f32)


def dot_tn(a, b):
    return lax.dot_general(a, b, (((0,), (0,)), ((), ())), preferred_element_type=f32)


def dot_nt(a, b):
    return lax.dot_general(a, b, (((1,), (1,)), ((), ())), preferred_element_type=f32)


def factor_of(values):
    return lax.rsqrt(jnp.mean(values * values, axis=-1, keepdims=True) + epsilon)


def norm_back(values, gain, upstream):
    factor = factor_of(values)
    weighted = upstream * gain
    inner = jnp.mean(weighted * values, axis=-1, keepdims=True)
    through = factor * weighted - values * (factor * factor * factor) * inner
    return through, jnp.sum(upstream * values * factor, axis=0, keepdims=True)


def normal_cdf(values):
    return 0.5 * (1.0 + lax.erf(values * (0.5**0.5)))


def gelu_slope(values, cdf):
    return cdf + values * (jnp.exp(-0.5 * values * values) * 0.3989422804014327)


def block_at(low, m):
    return pl.multiple_of((low ^ m) * UNIT, UNIT)


def span(m):
    return slice(m * UNIT, (m + 1) * UNIT)


class Copies:
    def __init__(self, sems):
        self.sems = sems
        self.made = []

    def start(self, src, dst):
        copy = pltpu.make_async_copy(src, dst, self.sems.at[len(self.made)])
        copy.start()
        self.made.append(copy)
        return copy

    def pick(self, own_first, sec, own, other, dst):
        sem = self.sems.at[len(self.made)]

        @pl.when((sec == 0) == own_first)
        def _():
            pltpu.make_async_copy(own, dst, sem).start()

        @pl.when((sec == 0) != own_first)
        def _():
            pltpu.make_async_copy(other, dst, sem).start()

        copy = pltpu.make_async_copy(own, dst, sem)
        self.made.append(copy)
        return copy

    def wait(self, begin=0, end=None):
        for copy in self.made[begin:end]:
            copy.wait()


def start_kernel(info, codes, own_gain, other_gain, first, start, gain_g, gain_l):
    low, sec = info[LOW], info[SEC]
    for m in range(QUARTERS):
        at = pl.ds(block_at(low, m), UNIT)
        own, other = own_gain[:, at], other_gain[:, at]
        gain_g[:, span(m)] = jnp.where(sec == 0, own, other)
        gain_l[:, span(m)] = jnp.where(sec == 0, other, own)
        total = codes[sec, 0, :, at].astype(f32)
        for c in range(1, codes.shape[1]):
            total = total + codes[sec, c, :, at].astype(f32)
        start[:, span(m)] = total
    values = start[...]
    first[...] = (values * factor_of(values) * gain_g[0:1, :]).astype(low16)


def from_local(sec, own, other, branch):
    @pl.when(sec == 0)
    def _():
        branch(0, *other)

    @pl.when(sec != 0)
    def _():
        branch(1, *own)


def mix_piece_kernel(info, own_qkv, other_qkv, own_out, other_out, piece, whole, sems):
    low, sec = info[LOW], info[SEC]
    half = own_qkv.shape[2] // 2

    def branch(half_index, qkv, out):
        made = Copies(sems)
        for m in range(QUARTERS):
            at = pl.ds(block_at(low, m), UNIT)
            at_right = pl.ds(pl.multiple_of(block_at(low, m) + half, half), half)
            at_left = pl.ds(block_at(low, m), half)
            lanes = slice(half_index * half, (half_index + 1) * half)
            target = whole.at[m]
            made.start(qkv.at[0, at, lanes], target.at[0, :, 0:half])
            made.start(qkv.at[1, at, lanes], target.at[0, :, half : 2 * half])
            made.start(qkv.at[2, at, lanes], target.at[1, :, 0:half])
            made.start(out.at[lanes, at_left], target.at[1, 0:half, half : 2 * half])
            made.start(out.at[lanes, at_right], target.at[1, half : 2 * half, half : 2 * half])
        made.wait()

    from_local(sec, (own_qkv, own_out), (other_qkv, other_out), branch)
    piece[...] = whole[0]


def feed_piece_kernel(info, own_up, other_up, own_down, other_down, piece, whole, sems):
    low, sec = info[LOW], info[SEC]
    wide = own_up.shape[1] // 2

    def branch(half_index, up, down):
        made = Copies(sems)
        for m in range(QUARTERS):
            at = pl.ds(block_at(low, m), UNIT)
            for part in range(2):
                begin = half_index * wide + part * UNIT
                hidden = slice(begin, begin + UNIT)
                made.start(up.at[at, hidden], whole.at[m, part])
                made.start(down.at[hidden, at], whole.at[m, 2 + part])
        made.wait()

    from_local(sec, (own_up, own_down), (other_up, other_down), branch)
    piece[...] = whole[0]


def fetch_attention(made, low, sec, own_qkv, other_qkv, own_out, other_out, qkv, out):
    for m in range(QUARTERS):
        at = pl.ds(block_at(low, m), UNIT)
        made.pick(True, sec, own_qkv.at[:, at, :], other_qkv.at[:, at, :], qkv.at[:, span(m), :])
    for m in range(QUARTERS):
        at = pl.ds(block_at(low, m), UNIT)
        made.pick(True, sec, own_out.at[:, at], other_out.at[:, at], out.at[:, span(m)])


def by_shard(info, blocks):
    count = blocks.shape[0]
    return jnp.concatenate([blocks[info[SHARD] ^ k] for k in range(count)], axis=0)


def other_half(info, width):
    half = width // 2
    return pl.ds(pl.multiple_of((1 - info[SEC]) * half, half), half)


def spread_blocks(info, target, values):
    frames = target.shape[1]
    for k in range(target.shape[0]):
        target[info[SHARD] ^ k] = values[k * frames : (k + 1) * frames].astype(low16)


def row_places(info, count, frames, dimension):
    at = lax.broadcasted_iota(jnp.int32, (count, count), dimension)
    return (lax.div(at, frames) ^ info[SHARD]) * frames + lax.rem(at, frames)


def global_attention_kernel(info, *rest):
    (blocks, own_qkv, other_qkv, own_out, other_out,
     rows, packed, probs, mixed, given, partial, qkv, out, sems) = rest
    low, sec = info[LOW], info[SEC]
    made = Copies(sems)
    fetch_attention(made, low, sec, own_qkv, other_qkv, own_out, other_out, qkv, out)
    count, frames = rows.shape[0], blocks.shape[1]
    length = info[LENGTHS + sec]
    query_at = row_places(info, count, frames, 0)
    key_at = row_places(info, count, frames, 1)
    allowed = (key_at <= query_at) & (key_at < length)
    values = by_shard(info, blocks)
    rows[...] = values
    made.wait(0, QUARTERS)
    for c in range(3):
        packed[c] = dot(values, qkv[c]).astype(low16)
    heads = []
    for h in range(packed.shape[2] // HEAD_DIM):
        lanes = slice(h * HEAD_DIM, (h + 1) * HEAD_DIM)
        scores = dot_nt(packed[0, :, lanes], packed[1, :, lanes]) * SCALE
        scores = jnp.where(allowed, scores, negative)
        raised = jnp.exp(scores - jnp.max(scores, axis=-1, keepdims=True))
        exact = raised / jnp.sum(raised, axis=-1, keepdims=True)
        probs[h] = exact.astype(low16)
        heads.append(dot(exact.astype(low16), packed[2, :, lanes]).astype(low16))
    mixed[...] = jnp.concatenate(heads, axis=1)
    given[...] = mixed[:, other_half(info, mixed.shape[1])]
    made.wait(QUARTERS)
    spread_blocks(info, partial, dot(mixed[...], out[...]))


def total_of(arrived):
    total = arrived[0].astype(f32)
    for k in range(1, arrived.shape[0]):
        total = total + arrived[k].astype(f32)
    return total


def middle_kernel(start, arrived, gain, hidden, second):
    values = start[...] + total_of(arrived)
    hidden[...] = values
    second[...] = (values * factor_of(values) * gain[1:2, :]).astype(low16)


def fetch_feed(made, low, sec, own_up, other_up, own_down, other_down, up, down):
    for m in range(QUARTERS):
        at = pl.ds(block_at(low, m), UNIT)
        made.pick(True, sec, own_up.at[at, :], other_up.at[at, :], up.at[span(m), :])
    for m in range(QUARTERS):
        at = pl.ds(block_at(low, m), UNIT)
        made.pick(True, sec, own_down.at[:, at], other_down.at[:, at], down.at[:, span(m)])


def global_feed_kernel(info, *rest):
    (blocks, own_up, other_up, own_down, other_down,
     rows, lifted, active, given, partial, up, down, total, sems) = rest
    made = Copies(sems)
    fetch_feed(made, info[LOW], info[SEC], own_up, other_up, own_down, other_down, up, down)
    values = by_shard(info, blocks)
    rows[...] = values
    made.wait(0, QUARTERS)
    for t in range(up.shape[1] // UNIT):
        tile = dot(values, up[:, span(t)])
        lifted[:, span(t)] = tile
        low_tile = (tile * normal_cdf(tile)).astype(low16)
        active[:, span(t)] = low_tile
        if t == 0:
            made.wait(QUARTERS)
        branch = dot(low_tile, down[span(t), :])
        total[...] = branch if t == 0 else total[...] + branch
    spread_blocks(info, partial, total[...])
    given[...] = active[:, other_half(info, active.shape[1])]


def sent_kernel(hidden, arrived, sent):
    sent[...] = (hidden[...] + total_of(arrived)).astype(low16)


def global_feed_back_kernel(info, *rest):
    (blocks, lifted, own_up, other_up, own_down, other_down,
     rows, grad_lifted, given, partial, up, down, total, sems) = rest
    made = Copies(sems)
    fetch_feed(made, info[LOW], info[SEC], own_up, other_up, own_down, other_down, up, down)
    values = by_shard(info, blocks)
    rows[...] = values
    made.wait(QUARTERS)
    for t in range(up.shape[1] // UNIT):
        tile = lifted[:, span(t)]
        grad = dot_nt(values, down[span(t), :]) * gelu_slope(tile, normal_cdf(tile))
        grad = grad.astype(low16)
        grad_lifted[:, span(t)] = grad
        if t == 0:
            made.wait(0, QUARTERS)
        back = dot_nt(grad, up[:, span(t)])
        total[...] = back if t == 0 else total[...] + back
    spread_blocks(info, partial, total[...])
    given[...] = grad_lifted[:, other_half(info, grad_lifted.shape[1])]


def middle_back_kernel(arrived, hidden, gain, returned, grad_hidden, mid, gain_grad):
    through, gain_grad[...] = norm_back(hidden[...], gain[1:2, :], total_of(arrived))
    values = returned[...].astype(f32) + through
    grad_hidden[...] = values
    mid[...] = values.astype(low16)


def global_attention_back_kernel(info, *rest):
    (blocks, packed, probs, own_qkv, other_qkv, own_out, other_out,
     rows, grads, given, partial, qkv, out, sems) = rest
    low, sec = info[LOW], info[SEC]
    made = Copies(sems)
    fetch_attention(made, low, sec, own_qkv, other_qkv, own_out, other_out, qkv, out)
    values = by_shard(info, blocks)
    rows[...] = values
    made.wait(QUARTERS)
    grad_mixed = dot_nt(values, out[...]).astype(low16)
    columns = [[], [], []]
    for h in range(packed.shape[2] // HEAD_DIM):
        lanes = slice(h * HEAD_DIM, (h + 1) * HEAD_DIM)
        exact = probs[h].astype(f32)
        grad = grad_mixed[:, lanes]
        columns[2].append(dot_tn(exact.astype(low16), grad).astype(low16))
        grad_probs = dot_nt(grad, packed[2, :, lanes])
        center = jnp.sum(grad_probs * exact, axis=-1, keepdims=True)
        grad_scores = (exact * (grad_probs - center)).astype(low16)
        columns[0].append((dot(grad_scores, packed[1, :, lanes]) * SCALE).astype(low16))
        columns[1].append((dot_tn(grad_scores, packed[0, :, lanes]) * SCALE).astype(low16))
    total = None
    made.wait(0, QUARTERS)
    for c in range(3):
        grads[c] = jnp.concatenate(columns[c], axis=1)
        back = dot_nt(grads[c], qkv[c])
        total = back if c == 0 else total + back
    spread_blocks(info, partial, total)
    given[...] = grads[:, :, other_half(info, grads.shape[2])]


def start_back_kernel(info, arrived, start, gain, grad_hidden, kept, given, gain_grad, values):
    low, sec = info[LOW], info[SEC]
    through, gain_grad[...] = norm_back(start[...], gain[0:1, :], total_of(arrived))
    values[...] = grad_hidden[...] + through
    for j in range(2):
        kept[:, span(j)] = values[:, pl.ds(block_at(low, 2 * sec + j), UNIT)]
        given[:, span(j)] = values[:, pl.ds(block_at(low, 2 * (1 - sec) + j), UNIT)]


def mix_unit(refs, k, m, u):
    whole, near, x_part, y_part, far = refs[0], refs[1:4], refs[4], refs[5], refs[6:8]
    if k == 0:
        return whole.at[m, u]
    if m == 0:
        return near[k - 1].at[u]
    if m == 3:
        return far[u].at[k - 1]
    return (x_part if m == 1 else y_part).at[u, k - 1]


def feed_unit(refs, k, m, u):
    if k == 0:
        return refs[0].at[m, u]
    if m < 3:
        return refs[1 + m].at[u]
    return refs[4].at[u] if u < 2 else refs[5].at[u - 2]


MIX_REFS, FEED_REFS = 8, 6


def pair_rows(a, b, size):
    return jnp.concatenate([a * b, a[size:] * b[: 2 * size], a[2 * size :] * b[:size]], axis=0)


def by_pair(stacked, size):
    names = [(0, 0), (1, 1), (2, 2), (1, 0), (2, 1), (2, 0)]
    return {name: stacked[n * size : (n + 1) * size] for n, name in enumerate(names)}


def from_pairs(pairs):
    names = [(0, 0), (1, 1), (2, 2), (1, 0), (2, 1), (2, 0)]
    return jnp.concatenate([pairs[name] for name in names], axis=0)


def head_sums(products, table):
    upper = products.astype(low16)
    lower = (products - upper.astype(f32)).astype(low16)
    return dot(upper, table) + dot(lower, table)


def head_table(width):
    row = lax.broadcasted_iota(jnp.int32, (width, width), 0) // HEAD_DIM
    column = lax.broadcasted_iota(jnp.int32, (width, width), 1) // HEAD_DIM
    return (row == column).astype(f32).astype(low16)


def gather_mix(weights, mix, k, half):
    for m in range(QUARTERS):
        begin = m * UNIT
        mix[k * half : (k + 1) * half, begin : begin + half] = weights[
            k, 1, begin : begin + half, half:
        ]
        mix[k * half : (k + 1) * half, begin + half : begin + UNIT] = weights[
            k, 1, begin + half : begin + UNIT, half:
        ]


def local_attention_kernel(info, codes, sent_own, sent_other, gain, *rest):
    refs, (start, first, query_keys, values_out, probs, mixed, partial, weights, mix, sems) = (
        rest[:MIX_REFS], rest[MIX_REFS:]
    )
    low, sec = info[LOW], info[SEC]
    made = Copies(sems)
    groups = []
    for k in range(4):
        groups.append(
            [
                made.start(mix_unit(refs, k, m, u), weights.at[k, u, span(m), :])
                for u in range(2)
                for m in range(QUARTERS)
            ]
        )
    utts, code_count, frames, _ = codes.shape
    for u in range(utts):
        sent = jnp.where(sec == u, sent_own[...], sent_other[...]).astype(f32)
        for c in range(code_count):
            row = (u * code_count + c) * frames
            for m in range(QUARTERS):
                code = codes[u, c, :, pl.ds(block_at(low, m), UNIT)].astype(f32)
                start[row : row + frames, span(m)] = sent[:, span(m)] + code
    values = start[...]
    first[...] = (values * factor_of(values) * gain[0:1, :]).astype(low16)
    half = values_out.shape[2]
    table = head_table(half)
    rows = first[...]
    size = frames
    group = code_count * frames
    for k in range(4):
        for copy in groups[k]:
            copy.wait()
        query_keys[k] = dot(rows, weights[k, 0]).astype(low16)
        values_out[k] = dot(rows, weights[k, 1, :, :half]).astype(low16)
        gather_mix(weights, mix, k, half)
        for u in range(utts):
            at = slice(u * group, (u + 1) * group)
            q = query_keys[k, at, :half].astype(f32)
            key = query_keys[k, at, half:].astype(f32)
            val = values_out[k, at, :].astype(f32)
            scores = by_pair(head_sums(pair_rows(q, key, size), table) * SCALE, size)
            exact = {}
            for i in range(3):
                peak = scores[(i, 0)]
                for j in range(1, i + 1):
                    peak = jnp.maximum(peak, scores[(i, j)])
                raised = [jnp.exp(scores[(i, j)] - peak) for j in range(i + 1)]
                whole = raised[0]
                for j in range(1, i + 1):
                    whole = whole + raised[j]
                for j in range(i + 1):
                    exact[(i, j)] = raised[j] / whole
            probs[k, u] = from_pairs(exact).astype(low16)
            for i in range(3):
                total = None
                for j in range(i + 1):
                    weight = exact[(i, j)].astype(low16).astype(f32)
                    term = weight * val[j * size : (j + 1) * size]
                    total = term if total is None else total + term
                begin = u * group + i * size
                mixed[begin : begin + size, k * half : (k + 1) * half] = total.astype(low16)
    partial[...] = dot(mixed[...], mix[...]).astype(low16)


def local_top_kernel(info, cotangent, top, given):
    low, sec = info[LOW], info[SEC]
    utts, code_count, frames, _ = cotangent.shape
    group = code_count * frames
    frame_at = lax.broadcasted_iota(jnp.int32, (frames, 1), 0) + info[SHARD] * frames
    for u in range(utts):
        valid = frame_at < info[LENGTHS + u]
        for c in range(code_count):
            row = u * group + c * frames
            for m in range(QUARTERS):
                part = cotangent[u, c, :, pl.ds(block_at(low, m), UNIT)].astype(f32)
                top[row : row + frames, span(m)] = jnp.where(valid, part, 0.0).astype(low16)
    given[...] = top[pl.ds(pl.multiple_of(sec * group, group), group), :]


def local_norm_kernel(info, start, own_part, other_part, gain, hidden, second, given):
    values = start[...] + (own_part[...].astype(f32) + other_part[...].astype(f32))
    hidden[...] = values
    second[...] = (values * factor_of(values) * gain[1:2, :]).astype(low16)
    group = given.shape[0]
    given[...] = second[pl.ds(pl.multiple_of(info[SEC] * group, group), group), :]


def feed_tiles(refs, second, top, active, grad_lifted, up, down, back, sems):
    tiles = active.shape[0]
    made = Copies(sems)
    for t in range(tiles):
        for m in range(QUARTERS):
            made.start(feed_unit(refs, t // 2, m, t % 2), up.at[t, span(m), :])
        for m in range(QUARTERS):
            made.start(feed_unit(refs, t // 2, m, 2 + t % 2), down.at[t, :, span(m)])
    back[...] = jnp.zeros_like(back)

    @pl.loop(0, tiles)
    def _(t):
        for m in range(QUARTERS):
            pltpu.make_async_copy(
                refs[0].at[0, 0], up.at[t, span(m), :], sems.at[8 * t + m]
            ).wait()
        for m in range(QUARTERS):
            pltpu.make_async_copy(
                refs[0].at[0, 0], down.at[t, :, span(m)], sems.at[8 * t + 4 + m]
            ).wait()
        tile = dot(second[...], up[t])
        cdf = normal_cdf(tile)
        active[t] = (tile * cdf).astype(low16)
        grad = (dot_nt(top[...], down[t]) * gelu_slope(tile, cdf)).astype(low16)
        grad_lifted[t] = grad
        back[...] += dot_nt(grad, up[t])


def local_feed_kernel(second, top, *rest):
    refs, (active, grad_lifted, grad_second, up, down, back, sems) = (
        rest[:FEED_REFS], rest[FEED_REFS:]
    )
    feed_tiles(refs, second, top, active, grad_lifted, up, down, back, sems)
    grad_second[...] = back[...].astype(low16)


def far_feed_kernel(second_same, second_cross, top_same, top_cross, *rest):
    refs = rest[:FEED_REFS]
    (active, grad_lifted, second, top, same, cross, up, down, back, sems) = rest[FEED_REFS:]
    group = same.shape[0]
    second[:group] = second_same[...]
    second[group:] = second_cross[...]
    top[:group] = top_same[...]
    top[group:] = top_cross[...]
    feed_tiles(refs, second, top, active, grad_lifted, up, down, back, sems)
    same[...] = back[:group].astype(low16)
    cross[...] = back[group:].astype(low16)


def pair_kernel(a, b, total):
    total[...] = add16(a[...], b[...])


def with_far(sec, rows, own, other, far_same, far_cross):
    group = far_same.shape[0]
    parts = []
    for u in range(rows // group):
        at = slice(u * group, (u + 1) * group)
        far = jnp.where(sec == u, far_same[...], far_cross[...]).astype(f32)
        parts.append(own[at, :].astype(f32) + other[at, :].astype(f32) + far)
    return jnp.concatenate(parts, axis=0)


def local_attention_back_kernel(info, hidden, own_back, other_back, far_same, far_cross, top, gain,
                                query_keys, values_in, probs, *rest):
    refs = rest[:MIX_REFS]
    (grad_hidden, mid, grad_query_keys, grad_values, grad_first, gain_grad,
     weights, mix, total, sems) = rest[MIX_REFS:]
    made = Copies(sems)
    groups = []
    for k in range(4):
        groups.append(
            [
                made.start(mix_unit(refs, k, m, u), weights.at[k, u, span(m), :])
                for u in range(2)
                for m in range(QUARTERS)
            ]
        )
    upstream = with_far(info[SEC], hidden.shape[0], own_back, other_back, far_same, far_cross)
    through, gain_grad[...] = norm_back(hidden[...], gain[1:2, :], upstream)
    grads = top[...].astype(f32) + through
    grad_hidden[...] = grads
    mid[...] = grads.astype(low16)
    utts = probs.shape[1]
    half = values_in.shape[2]
    group = query_keys.shape[1] // utts
    size = group // 3
    table = head_table(half)
    for k in range(4):
        for copy in groups[k]:
            copy.wait()
        gather_mix(weights, mix, k, half)
        grad_mixed = dot_nt(mid[...], mix[k * half : (k + 1) * half, :]).astype(low16)
        grad_mixed = grad_mixed.astype(f32)
        for u in range(utts):
            at = slice(u * group, (u + 1) * group)
            q = query_keys[k, at, :half].astype(f32)
            key = query_keys[k, at, half:].astype(f32)
            val = values_in[k, at, :].astype(f32)
            grad = grad_mixed[at]
            exact = by_pair(probs[k, u].astype(f32), size)
            grad_probs = by_pair(head_sums(pair_rows(grad, val, size), table), size)
            scored = {}
            for i in range(3):
                center = grad_probs[(i, 0)] * exact[(i, 0)]
                for j in range(1, i + 1):
                    center = center + grad_probs[(i, j)] * exact[(i, j)]
                for j in range(i + 1):
                    score = exact[(i, j)] * (grad_probs[(i, j)] - center)
                    scored[(i, j)] = score.astype(low16).astype(f32)

            def rows_of(array, n):
                return array[n * size : (n + 1) * size]

            for i in range(3):
                begin = u * group + i * size
                to_query = sum(scored[(i, j)] * rows_of(key, j) for j in range(i + 1))
                to_key = sum(scored[(n, i)] * rows_of(q, n) for n in range(i, 3))
                to_value = sum(
                    exact[(n, i)].astype(low16).astype(f32) * rows_of(grad, n)
                    for n in range(i, 3)
                )
                grad_query_keys[k, begin : begin + size, :half] = (to_query * SCALE).astype(low16)
                grad_query_keys[k, begin : begin + size, half:] = (to_key * SCALE).astype(low16)
                grad_values[k, begin : begin + size, :] = to_value.astype(low16)
        back = dot_nt(grad_query_keys[k], weights[k, 0])
        back = back + dot_nt(grad_values[k], weights[k, 1, :, :half])
        total[...] = back if k == 0 else total[...] + back
    grad_first[...] = total[...].astype(low16)


def local_end_kernel(info, own_back, other_back, start, grad_hidden, gain,
                     returned, code_part, gain_grad, values):
    low, sec = info[LOW], info[SEC]
    upstream = own_back[...].astype(f32) + other_back[...].astype(f32)
    through, gain_grad[...] = norm_back(start[...], gain[0:1, :], upstream)
    values[...] = grad_hidden[...] + through
    utts, code_count, frames, _ = code_part.shape
    total = None
    for c in range(code_count):
        begin = pl.multiple_of((sec * code_count + c) * frames, frames)
        part = values[pl.ds(begin, frames), :]
        total = part if total is None else total + part
    returned[...] = total.astype(low16)
    for u in range(utts):
        for c in range(code_count):
            row = (u * code_count + c) * frames
            for j in range(2):
                at = pl.ds(block_at(low, 2 * sec + j), UNIT)
                code_part[u, c, :, span(j)] = values[row : row + frames, at]


def output_kernel(info, hidden, own_part, other_part, far_same, far_cross, output):
    low, sec = info[LOW], info[SEC]
    utts, code_count, frames, _ = output.shape
    group = code_count * frames
    frame_at = lax.broadcasted_iota(jnp.int32, (frames, 1), 0) + info[SHARD] * frames
    for u in range(utts):
        valid = frame_at < info[LENGTHS + u]
        for c in range(code_count):
            rows = slice(u * group + c * frames, u * group + (c + 1) * frames)
            inner = slice(c * frames, (c + 1) * frames)
            for j in range(2):
                at = pl.ds(block_at(low, 2 * sec + j), UNIT)
                far = jnp.where(sec == u, far_same[inner, at], far_cross[inner, at])
                value = hidden[rows, at] + (
                    own_part[rows, at].astype(f32)
                    + other_part[rows, at].astype(f32)
                    + far.astype(f32)
                )
                output[u, c, :, span(j)] = jnp.where(valid, value, 0.0).astype(low16)


SEND_A, KEEP_A, SEND_B, KEEP_B = (1, 3), (0, 2), (2, 3), (0, 1)


def local_drop_kernel(own_active, far_active, *rest):
    refs, (own_branch, same, cross, down, branch, sems) = rest[:FEED_REFS], rest[FEED_REFS:]
    tiles, count, _ = own_active.shape
    made = Copies(sems)
    for t in range(tiles):
        for m in range(QUARTERS):
            made.start(feed_unit(refs, t // 2, m, 2 + t % 2), down.at[t, :, span(m)])
    branch[...] = jnp.zeros_like(branch)

    @pl.loop(0, tiles)
    def _(t):
        for m in range(QUARTERS):
            pltpu.make_async_copy(
                refs[0].at[0, 0], down.at[t, :, span(m)], sems.at[QUARTERS * t + m]
            ).wait()
        branch[:count] += dot(own_active[t], down[t])
        branch[count:] += dot(far_active[t], down[t])

    own_branch[...] = branch[:count].astype(low16)
    group = same.shape[0]
    same[...] = branch[count : count + group].astype(low16)
    cross[...] = branch[count + group :].astype(low16)


def local_feed_grad_kernel(second, far_second, own_lifted, far_lifted, own_active, far_active,
                           top, far_top, send_a, send_b, keep_a, keep_b, turned, tops):
    count = second.shape[0]
    turned[:, :count] = jnp.transpose(second[...])
    turned[:, count:] = jnp.transpose(far_second[...])
    tops[:count] = top[...]
    tops[count:] = far_top[...]
    for k in range(2):
        for part, pairs in enumerate(
            (((send_a, SEND_A), (keep_a, KEEP_A)), ((send_b, SEND_B), (keep_b, KEEP_B)))
        ):
            t = 2 * k + part
            right = jnp.concatenate([own_lifted[t], far_lifted[t]], axis=0)
            left = jnp.concatenate(
                [jnp.transpose(own_active[t]), jnp.transpose(far_active[t])], axis=1
            )
            for target, order in pairs:
                for place, m in enumerate(order):
                    target[place, 2 * k] = dot(turned[span(m), :], right).astype(low16)
                    target[place, 2 * k + 1] = dot(left, tops[:, span(m)]).astype(low16)


def local_mix_kernel(first, grad_query_keys, grad_values, mixed, mid,
                     send_a, send_b, keep_a, keep_b, turned):
    turned[...] = jnp.transpose(first[...])
    half = grad_values.shape[2]
    for k in range(4):
        left = jnp.transpose(mixed[:, k * half : (k + 1) * half])
        for target, order in ((send_a, SEND_A), (keep_a, KEEP_A)):
            for place, m in enumerate(order):
                target[place, k] = dot(turned[span(m), :], grad_query_keys[k]).astype(low16)
        for target, order in ((send_b, SEND_B), (keep_b, KEEP_B)):
            for place, m in enumerate(order):
                value = dot(turned[span(m), :], grad_values[k]).astype(low16)
                out = dot(left, mid[:, span(m)]).astype(low16)
                target[place, k, :, :half] = value
                target[place, k, :half, half:] = out[:, :half]
                target[place, k, half:, half:] = out[:, half:]


def by_order(send_a, send_b, keep_a, keep_b):
    return (
        (0, ((send_a, SEND_A), (keep_a, KEEP_A))),
        (1, ((send_b, SEND_B), (keep_b, KEEP_B))),
    )


def global_feed_grad_kernel(info, second, far_second, grad_lifted, far_lifted, active, far_active,
                            top, far_top, send_a, send_b, keep_a, keep_b, turned, tops):
    sec, count = info[SEC], second.shape[0]
    turned[:, :count] = jnp.transpose(second[...])
    turned[:, count:] = jnp.transpose(far_second[...])
    tops[:count] = top[...]
    tops[count:] = far_top[...]
    wide = active.shape[1] // 2
    for part, pairs in by_order(send_a, send_b, keep_a, keep_b):
        at = pl.ds(pl.multiple_of(sec * wide + part * UNIT, UNIT), UNIT)
        right = jnp.concatenate([grad_lifted[:, at], far_lifted[:, span(part)]], axis=0)
        left = jnp.concatenate(
            [jnp.transpose(active[:, at]), jnp.transpose(far_active[:, span(part)])], axis=1
        )
        for target, order in pairs:
            for place, m in enumerate(order):
                target[place, 0] = dot(turned[span(m), :], right).astype(low16)
                target[place, 1] = dot(left, tops[:, span(m)]).astype(low16)


def global_mix_grad_kernel(info, first, far_first, grads, far_grads, mixed, far_mixed, mid,
                           far_mid, send_a, send_b, keep_a, keep_b, turned, mids):
    sec, count = info[SEC], first.shape[0]
    turned[:, :count] = jnp.transpose(first[...])
    turned[:, count:] = jnp.transpose(far_first[...])
    mids[:count] = mid[...]
    mids[count:] = far_mid[...]
    width = mixed.shape[1] // 2
    at = pl.ds(pl.multiple_of(sec * width, width), width)
    right = [jnp.concatenate([grads[c, :, at], far_grads[c]], axis=0) for c in range(3)]
    left = jnp.concatenate([jnp.transpose(mixed[:, at]), jnp.transpose(far_mixed[...])], axis=1)
    for part, pairs in by_order(send_a, send_b, keep_a, keep_b):
        for target, order in pairs:
            for place, m in enumerate(order):
                rows = turned[span(m), :]
                if part == 0:
                    for c in range(2):
                        target[place, 0, :, c * width : (c + 1) * width] = dot(
                            rows, right[c]
                        ).astype(low16)
                else:
                    target[place, 0, :, :width] = dot(rows, right[2]).astype(low16)
                    out = dot(left, mids[:, span(m)]).astype(low16)
                    target[place, 0, :width, width:] = out[:, :width]
                    target[place, 0, width:, width:] = out[:, width:]


def add16(a, b):
    return (a.astype(f32) + b.astype(f32)).astype(low16)


def far_kernel(keep_a, from_x, keep_b, from_y, far_a, far_b):
    far_a[...] = add16(keep_a[0], from_x[0])
    far_b[...] = add16(keep_b[0], from_y[0])


def sum_kernel(shards, *refs):
    parts, outs = (refs[:3], refs[3:6]), refs[6:]
    for part, (keep, once, twice) in enumerate(parts):
        total = keep[0].astype(f32) + once[0].astype(f32) + twice[...].astype(f32)
        total = total.astype(low16)
        count = total.shape[0] // shards
        at = slice(part * count, (part + 1) * count)
        if shards == 1:
            outs[0][at] = total
        elif shards == 2:
            outs[1][0, at] = total[:count]
            outs[0][0, at] = total[count:]
        else:
            for k in range(4):
                outs[(k + 1) % 2][k // 2, at] = total[k * count : (k + 1) * count]


def far_tensor_kernel(keep, arrived, far):
    far[...] = add16(keep[0], arrived[0])


def pick_kernel(info, *refs):
    *terms, world, given, kept = refs
    sec = info[SEC]
    local = terms[0][0].astype(f32)
    for term in terms[1:]:
        local = local + (term[0] if len(term.shape) == 4 else term[...]).astype(f32)
    local = local.astype(low16)
    other = world[...]
    given[...] = jnp.where(sec == 0, local, other)
    kept[...] = jnp.where(sec == 0, other, local)


def half_at(index, count):
    return pl.BlockSpec(
        (1, count, UNIT, UNIT), lambda i: (index, 0, 0, 0), memory_space=pltpu.VMEM
    )


def quarter_unit(refs, m, index):
    own, x_part, y_part, far_kept, far_arrived = refs
    count = own.shape[0] // 2
    if m < 3:
        return (own, x_part, y_part)[m][index].astype(f32)
    return (far_kept[index] if index < count else far_arrived[index - count]).astype(f32)


def write_feed(info, quarters, unit, count, up, down, rows, columns, sems):
    low, sec = info[LOW], info[SEC]
    wide = up.shape[1] // 2
    made = Copies(sems)
    for place, m in enumerate(quarters):
        at = pl.ds(block_at(low, m), UNIT)
        for source, half in ((0, sec), (count, 1 - sec)):
            for part in range(2):
                hidden = pl.ds(pl.multiple_of(half * wide + part * UNIT, UNIT), UNIT)
                rows[place, :, hidden] = unit(m, source + 2 * part)
                columns[place, hidden, :] = unit(m, source + 2 * part + 1)
        made.start(rows.at[place], up.at[at, :])
        made.start(columns.at[place], down.at[:, at])
    made.wait()


def feed_near_kernel(info, own, x_part, y_part, up, down, rows, columns, sems):
    parts = (own, x_part, y_part)
    write_feed(
        info, (0, 1, 2), lambda m, n: parts[m][n].astype(f32), own.shape[0] // 2,
        up, down, rows, columns, sems,
    )


def feed_far_kernel(info, far_kept, far_arrived, up_before, down_before,
                    up, down, rows, columns, sems):
    count = far_kept.shape[0]

    def unit(m, n):
        return (far_kept[n] if n < count else far_arrived[n - count]).astype(f32)

    write_feed(info, (3,), unit, count, up, down, rows, columns, sems)


def write_mix(info, quarters, unit, count, qkv, out, rows, columns, sems):
    low, sec = info[LOW], info[SEC]
    width = out.shape[0] // 2
    made = Copies(sems)
    for place, m in enumerate(quarters):
        at = pl.ds(block_at(low, m), UNIT)
        for source, half in ((0, sec), (count, 1 - sec)):
            lanes = pl.ds(pl.multiple_of(half * width, width), width)
            query_keys = unit(m, source)
            rows[place, 0, :, lanes] = query_keys[:, :width]
            rows[place, 1, :, lanes] = query_keys[:, width:]
            rest_unit = unit(m, source + 1)
            rows[place, 2, :, lanes] = rest_unit[:, :width]
            columns[place, lanes, :width] = rest_unit[:width, width:]
            columns[place, lanes, width:] = rest_unit[width:, width:]
        made.start(rows.at[place], qkv.at[:, at, :])
        made.start(columns.at[place], out.at[:, at])
    made.wait()


GAIN_ROWS = 32


def gain_pack_kernel(gain, packed):
    rows = []
    for g in range(gain.shape[0]):
        rest = gain[g : g + 1, :]
        for _ in range(3):
            part = rest.astype(low16).astype(f32)
            rest = rest - part
            rows += [part[:, span(m)] for m in range(QUARTERS)]
    rows.append(jnp.zeros((GAIN_ROWS - len(rows), UNIT), f32))
    packed[...] = jnp.concatenate(rows, axis=0).astype(low16)


def unit_rows(ref, n):
    return ref[n * UNIT : (n + 1) * UNIT, :].astype(f32)


def mix_near_kernel(info, own, x_part, y_part, qkv, out, rows, columns, sems):
    parts = (own, x_part, y_part)
    count = (own.shape[0] - GAIN_ROWS) // (2 * UNIT)
    write_mix(
        info, (0, 1, 2), lambda m, n: unit_rows(parts[m], n), count, qkv, out, rows, columns, sems
    )


def mix_far_kernel(info, own, x_part, y_part, far_kept, far_arrived, qkv_before, out_before,
                   qkv, out, gain, rows, columns, sems):
    count = far_kept.shape[0] // UNIT

    def unit(m, n):
        return unit_rows(far_kept, n) if n < count else unit_rows(far_arrived, n - count)

    total = None
    for ref in (own, x_part, y_part, far_arrived):
        part = ref[ref.shape[0] - GAIN_ROWS :, :].astype(f32)
        total = part if total is None else total + part
    for g in range(gain.shape[0]):
        for m in range(QUARTERS):
            at = [3 * QUARTERS * g + QUARTERS * t + m for t in range(3)]
            gain[g : g + 1, span(m)] = (
                total[at[0] : at[0] + 1] + total[at[1] : at[1] + 1] + total[at[2] : at[2] + 1]
            )
    write_mix(info, (3,), unit, count, qkv, out, rows, columns, sems)


def sum_rest(value):
    step = QUARTERS
    while step < lax.axis_size("dp"):
        value = add16(value, swap(value, "dp", step))
        step *= 2
    return value


class Sum:
    def __init__(self, order, shards, send_a, send_b, keep_a, keep_b):
        self.order, self.shards = order, shards
        self.keep = (keep_a, keep_b)
        self.count = keep_a.shape[1]
        self.once = (swap(send_a, "dp", 1), swap(send_b, "dp", 2))

    def second(self):
        far = half_at(1, self.count)
        far_a, far_b = self.order.call(
            far_kernel,
            [shape((self.count, UNIT, UNIT), low16)] * 2,
            (self.keep[0], self.once[0], self.keep[1], self.once[1]),
            [far] * 4,
            grid=(1,),
        )
        self.twice = (swap(far_a, "dp", 2), swap(far_b, "dp", 1))

    def third(self):
        count = 2 * self.count // self.shards
        if self.shards == 1:
            outs = [shape((count, UNIT, UNIT), low16)]
        else:
            outs = [shape((self.shards // 2, count, UNIT, UNIT), low16)] * 2
        near = half_at(0, self.count)
        totals = self.order.call(
            functools.partial(sum_kernel, self.shards),
            outs,
            (self.keep[0], self.once[0], self.twice[0], self.keep[1], self.once[1], self.twice[1]),
            [near, near, VM] * 2,
            grid=(1,),
        )
        totals = [sum_rest(total) for total in totals]
        self.count = count
        if self.shards == 1:
            return totals[0]
        self.keep = totals[1]
        if self.shards == 2:
            self.terms = (self.keep, swap(totals[0], "tensor", 2))
        else:
            self.once = swap(totals[0], "tensor", 1)

    def fourth(self):
        far = self.order.call(
            far_tensor_kernel,
            [shape((self.count, UNIT, UNIT), low16)],
            (self.keep, self.once),
            [half_at(1, self.count)] * 2,
            grid=(1,),
        )[0]
        self.terms = (self.keep, self.once, swap(far, "tensor", 2))

    def gathered(self, info, world, extra=None):
        near = half_at(0, self.count)
        given, kept = self.order.call(
            pick_kernel,
            [shape((self.count, UNIT, UNIT), low16)] * 2,
            (info,) + self.terms + (world,),
            [SM] + [near if term.ndim == 4 else VM for term in self.terms] + [VM],
            grid=(1,),
        )
        arrived = swap(given, "section", 1)
        if extra is None:
            return Gather(jnp.concatenate([kept, arrived]), self.count)
        rows = [kept.reshape(-1, UNIT), arrived.reshape(-1, UNIT), extra]
        return Gather(jnp.concatenate(rows), self.count * UNIT)


class Gather:
    def __init__(self, units, count):
        self.units, self.count = units, count
        self.near = (swap(units, "dp", 1), swap(units, "dp", 2))

    def far(self):
        x_part, y_part = self.near
        rest = (swap(x_part[: self.count], "dp", 2), swap(y_part[self.count :], "dp", 1))
        return (self.units,) + self.near + rest


def on_device(codes, lengths, gains, w_qkv, w_out, w_up, w_down, cotangent):
    sec = lax.axis_index("section")
    low = lax.axis_index("dp") % QUARTERS
    z = lax.axis_index("tensor")
    first_core = sec == 0
    utts, frames, code_count, width = codes.shape
    heads_width = w_out.shape[1]
    half = heads_width // 2
    wide = w_up.shape[2]
    rows_g = 4 * frames
    rows_l = utts * code_count * frames
    tiles = wide // UNIT
    info = jnp.concatenate([jnp.stack([low, sec, z]).astype(jnp.int32), lengths])
    order = Order()
    call = order.call

    code_rows = jnp.transpose(codes, (0, 2, 1, 3))
    cot_rows = jnp.transpose(cotangent, (0, 2, 1, 3))
    own_w = (jnp.transpose(w_qkv[0], (1, 0, 2)), w_out[0], w_up[0], w_down[0])

    def sem(count):
        return pltpu.SemaphoreType.DMA((count,))

    def gather(rows):
        gathered = lax.all_gather(rows, "tensor")
        order.tokens = (gathered,)
        return gathered

    def scatter(partial):
        return lax.all_to_all(partial, "tensor", 0, 0)

    other_gain = swap(gains[0], "section", 1)
    own_w, other_gain = lax.optimization_barrier((own_w, other_gain))

    def with_other(weights):
        return tuple(w for own in weights for w in (own, swap(own, "section", 1)))

    attention_w = with_other(own_w[:2])

    first_rows, start_g, gain_g, gain_l = call(
        start_kernel,
        [
            shape((frames, width), low16),
            shape((frames, width), f32),
            shape((2, width), f32),
            shape((2, width), f32),
        ],
        (info, code_rows, gains[0], other_gain),
        [SM, VM, VM, VM],
        us=2,
    )
    first_rows, *attention_w = lax.optimization_barrier((first_rows,) + attention_w)
    attention_w = tuple(attention_w)
    first_blocks = gather(first_rows)
    feed_w = with_other(order.after(own_w[2:]))

    first_g, packed_g, probs_g, mixed_g, mixed_given, partial = call(
        global_attention_kernel,
        [
            shape((rows_g, width), low16),
            shape((3, rows_g, heads_width), low16),
            shape((heads_width // HEAD_DIM, rows_g, rows_g), low16),
            shape((rows_g, heads_width), low16),
            shape((rows_g, half), low16),
            shape((4, frames, width), low16),
        ],
        (info, first_blocks) + attention_w,
        [SM, VM] + [ANY] * 4,
        [
            pltpu.VMEM((3, width, heads_width), low16),
            pltpu.VMEM((heads_width, width), low16),
            sem(8),
        ],
        us=5.7,
        limit=60,
    )
    arrived = scatter(partial)
    mix_piece, mix_whole = call(
        mix_piece_kernel,
        [shape((2, UNIT, UNIT), low16), shape((QUARTERS, 2, UNIT, UNIT), low16)],
        (info,) + attention_w,
        [SM] + [ANY] * 4,
        [sem(5 * QUARTERS)],
        us=3.2,
    )
    mix_z1 = swap(mix_piece, "tensor", 1)
    mix_z2 = swap(mix_piece, "tensor", 2)
    feed_piece, feed_whole = call(
        feed_piece_kernel,
        [shape((4, UNIT, UNIT), low16), shape((QUARTERS, 4, UNIT, UNIT), low16)],
        (info,) + feed_w,
        [SM] + [ANY] * 4,
        [sem(4 * QUARTERS)],
        us=4,
    )
    top_l, top_given = call(
        local_top_kernel,
        [shape((rows_l, width), low16), shape((rows_l // utts, width), low16)],
        (info, cot_rows),
        [SM, VM],
        us=2.3,
    )
    hidden_g, second_rows = call(
        middle_kernel,
        [shape((frames, width), f32), shape((frames, width), low16)],
        (start_g, arrived, gain_g),
        [VM] * 3,
        us=2,
    )
    second_rows, mix_z1, mix_z2, feed_piece = lax.optimization_barrier(
        (second_rows, mix_z1, mix_z2, feed_piece)
    )
    mix_z3 = swap(mix_z2, "tensor", 1)
    second_blocks = gather(second_rows)
    feed_z2 = swap(order.after(feed_piece), "tensor", 2)
    order.until(mix_z3)
    second_g, lifted_g, active_g, active_given, partial = call(
        global_feed_kernel,
        [
            shape((rows_g, width), low16),
            shape((rows_g, wide), f32),
            shape((rows_g, wide), low16),
            shape((rows_g, wide // 2), low16),
            shape((4, frames, width), low16),
        ],
        (info, second_blocks) + feed_w,
        [SM, VM] + [ANY] * 4,
        [
            pltpu.VMEM((width, wide), low16),
            pltpu.VMEM((wide, width), low16),
            pltpu.VMEM((rows_g, width), f32),
            sem(8),
        ],
        us=5.6,
        limit=60,
    )
    arrived = scatter(partial)
    mix_near = jnp.stack(order.after([mix_z1, mix_z2, mix_z3]), axis=1)
    mix_x = swap(mix_near, "dp", 1)
    mix_y = swap(mix_near, "dp", 2)
    mix_far = (swap(mix_x[0], "dp", 2), swap(mix_y[1], "dp", 1))
    order.until(*mix_far, feed_z2)
    sent = call(
        sent_kernel,
        [shape((frames, width), low16)],
        (hidden_g, arrived),
        [VM] * 2,
        us=1.9,
    )[0]
    other_sent = swap(sent, "section", 1)
    mix_w = (mix_whole, mix_z1, mix_z2, mix_z3, mix_x, mix_y) + mix_far
    feed_z2 = order.after(feed_z2)
    feed_x = swap(feed_z2, "dp", 1)
    feed_y = swap(feed_z2, "dp", 2)
    top_same = swap(order.after(top_given), "tensor", 1)

    start_l, first_l, query_keys, values_l, probs_l, mixed_l, partial = call(
        local_attention_kernel,
        [
            shape((rows_l, width), f32),
            shape((rows_l, width), low16),
            shape((4, rows_l, 2 * half), low16),
            shape((4, rows_l, half), low16),
            shape((4, utts, 2 * rows_l // utts, half), low16),
            shape((rows_l, 4 * half), low16),
            shape((rows_l, width), low16),
        ],
        (info, code_rows, sent, other_sent, gain_l) + mix_w,
        [SM] + [VM] * 4 + [ANY] * MIX_REFS,
        [
            pltpu.VMEM((4, 2, width, UNIT), low16),
            pltpu.VMEM((4 * half, width), low16),
            sem(32),
        ],
        us=9,
        limit=60,
    )
    partial, feed_x, feed_y, top_same = lax.optimization_barrier(
        (partial, feed_x, feed_y, top_same)
    )
    feed_l = (
        feed_whole,
        feed_z2,
        feed_x,
        feed_y,
        swap(feed_x[:2], "dp", 2),
        swap(feed_y[2:], "dp", 1),
    )
    hidden_l, second_l, second_given = call(
        local_norm_kernel,
        [
            shape((rows_l, width), f32),
            shape((rows_l, width), low16),
            shape((rows_l // utts, width), low16),
        ],
        (info, start_l, partial, swap(partial, "section", 1), gain_l),
        [SM] + [VM] * 4,
        us=3.7,
    )
    second_same = swap(second_given, "tensor", 1)
    top_cross = swap(top_same, "section", 1)
    feed_scratch = [
        pltpu.VMEM((tiles, width, UNIT), low16),
        pltpu.VMEM((tiles, UNIT, width), low16),
        pltpu.VMEM((rows_l, width), f32),
        sem(8 * tiles),
    ]
    wide_rows = shape((rows_l, width), low16)
    half_rows = shape((rows_l // utts, width), low16)
    tiled_rows = shape((tiles, rows_l, UNIT), low16)
    active_l, grad_lifted_l, back = call(
        local_feed_kernel,
        [tiled_rows, tiled_rows, wide_rows],
        (second_l, top_l) + feed_l,
        [VM] * 2 + [ANY] * FEED_REFS,
        feed_scratch,
        us=7.9,
    )
    other_back = swap(back, "section", 1)
    second_same = order.after(second_same)
    second_cross = swap(second_same, "section", 1)
    far_active, far_lifted, far_second, far_top, same, cross = call(
        far_feed_kernel,
        [tiled_rows, tiled_rows, wide_rows, wide_rows, half_rows, half_rows],
        (second_same, second_cross, top_same, top_cross) + feed_l,
        [VM] * 4 + [ANY] * FEED_REFS,
        feed_scratch,
        us=8.2,
    )

    def from_neighbour(same, cross):
        total = call(
            pair_kernel, [half_rows], (same, cross), [VM] * 2
        )[0]
        return swap(total, "tensor", 1)

    far_same = from_neighbour(same, swap(cross, "section", 1))
    turned_l = pltpu.VMEM((width, rows_l), low16)
    local_feed = Sum(
        order,
        2,
        *call(
            local_feed_grad_kernel,
            [shape((2, 4, UNIT, UNIT), low16)] * 4,
            (
                second_l, far_second, grad_lifted_l, far_lifted, active_l, far_active, top_l,
                far_top,
            ),
            [VM] * 8,
            [pltpu.VMEM((width, 2 * rows_l), low16), pltpu.VMEM((2 * rows_l, width), low16)],
            us=7.6,
        ),
    )
    own_branch, branch_same, branch_cross = call(
        local_drop_kernel,
        [wide_rows, half_rows, half_rows],
        (active_l, far_active) + feed_l,
        [VM] * 2 + [ANY] * FEED_REFS,
        [
            pltpu.VMEM((tiles, UNIT, width), low16),
            pltpu.VMEM((2 * rows_l, width), f32),
            sem(QUARTERS * tiles),
        ],
        us=6.1,
    )
    branch_cross = swap(branch_cross, "section", 1)
    other_branch = swap(own_branch, "section", 1)
    far_same = order.after(far_same)
    far_back = (far_same, swap(far_same, "section", 1))
    far_branch = from_neighbour(branch_same, branch_cross)
    far_first, far_mixed, far_second_g, far_active_g = (
        swap(order.after(value), "section", 1)
        for value in (first_g, mixed_given, second_g, active_given)
    )
    grad_hidden_l, mid_l, grad_query_keys, grad_values, back, gain2_l = call(
        local_attention_back_kernel,
        [
            shape((rows_l, width), f32),
            shape((rows_l, width), low16),
            shape((4, rows_l, 2 * half), low16),
            shape((4, rows_l, half), low16),
            shape((rows_l, width), low16),
            shape((1, width), f32),
        ],
        (info, hidden_l, back, other_back)
        + far_back
        + (top_l, gain_l, query_keys, values_l, probs_l)
        + mix_w,
        [SM] + [VM] * 10 + [ANY] * MIX_REFS,
        [
            pltpu.VMEM((4, 2, width, UNIT), low16),
            pltpu.VMEM((4 * half, width), low16),
            pltpu.VMEM((rows_l, width), f32),
            sem(32),
        ],
        us=11.4,
    )
    other_back = swap(back, "section", 1)
    order.until(far_branch)
    local_mix = Sum(
        order,
        4,
        *call(
            local_mix_kernel,
            [shape((2, 4, UNIT, UNIT), low16)] * 4,
            (first_l, grad_query_keys, grad_values, mixed_l, mid_l),
            [VM] * 5,
            [turned_l],
            us=6,
        ),
    )
    returned, code_part, gain1_l = call(
        local_end_kernel,
        [
            shape((frames, width), low16),
            shape((utts, code_count, frames, width // 2), f32),
            shape((1, width), f32),
        ],
        (info, back, other_back, start_l, grad_hidden_l, gain_l),
        [SM] + [VM] * 5,
        [pltpu.VMEM((rows_l, width), f32)],
        us=4.4,
    )

    top_blocks = gather(returned)
    local_feed.second()
    order.until(*local_mix.once, far_first, far_mixed, far_second_g, far_active_g)
    top_g, grad_lifted_g, lifted_given, partial = call(
        global_feed_back_kernel,
        [
            shape((rows_g, width), low16),
            shape((rows_g, wide), low16),
            shape((rows_g, wide // 2), low16),
            shape((4, frames, width), low16),
        ],
        (info, top_blocks, lifted_g) + feed_w,
        [SM] + [VM] * 2 + [ANY] * 4,
        [
            pltpu.VMEM((width, wide), low16),
            pltpu.VMEM((wide, width), low16),
            pltpu.VMEM((rows_g, width), f32),
            sem(8),
        ],
        us=6.3,
        limit=28,
    )
    arrived = scatter(partial)
    far_top_g, far_lifted_g = swap(top_g, "section", 1), swap(lifted_given, "section", 1)
    local_feed.third()
    local_mix.second()
    far_branch = order.after(far_branch)
    far_branch = (far_branch, swap(far_branch, "section", 1))
    global_feed = Sum(
        order,
        1,
        *call(
            global_feed_grad_kernel,
            [shape((2, 2, UNIT, UNIT), low16)] * 4,
            (
                info, second_g, far_second_g, grad_lifted_g, far_lifted_g, active_g, far_active_g,
                top_g, far_top_g,
            ),
            [SM] + [VM] * 8,
            [pltpu.VMEM((width, 2 * rows_g), low16), pltpu.VMEM((2 * rows_g, width), low16)],
            us=3.5,
        ),
    )
    grad_hidden_g, mid_rows, gain2_g = call(
        middle_back_kernel,
        [shape((frames, width), f32), shape((frames, width), low16), shape((1, width), f32)],
        (arrived, hidden_g, gain_g, returned),
        [VM] * 4,
        us=2.1,
    )
    mid_blocks = gather(mid_rows)
    order.until(*local_mix.twice)
    mid_g, grads_g, grads_given, partial = call(
        global_attention_back_kernel,
        [
            shape((rows_g, width), low16),
            shape((3, rows_g, heads_width), low16),
            shape((3, rows_g, half), low16),
            shape((4, frames, width), low16),
        ],
        (info, mid_blocks, packed_g, probs_g) + attention_w,
        [SM] + [VM] * 3 + [ANY] * 4,
        [
            pltpu.VMEM((3, width, heads_width), low16),
            pltpu.VMEM((heads_width, width), low16),
            sem(8),
        ],
        us=6.8,
        limit=60,
    )
    arrived = scatter(partial)
    far_mid_g, far_grads_g = swap(mid_g, "section", 1), swap(grads_given, "section", 1)
    global_feed.second()
    local_mix.third()
    global_mix = Sum(
        order,
        1,
        *call(
            global_mix_grad_kernel,
            [shape((2, 1, UNIT, UNIT), low16)] * 4,
            (
                info, first_g, far_first, grads_g, far_grads_g, mixed_g, far_mixed, mid_g,
                far_mid_g,
            ),
            [SM] + [VM] * 8,
            [pltpu.VMEM((width, 2 * rows_g), low16), pltpu.VMEM((2 * rows_g, width), low16)],
            us=3,
        ),
    )
    kept_start, given_start, gain1_g = call(
        start_back_kernel,
        [
            shape((frames, width // 2), f32),
            shape((frames, width // 2), f32),
            shape((1, width), f32),
        ],
        (info, arrived, start_g, gain_g, grad_hidden_g),
        [SM] + [VM] * 4,
        [pltpu.VMEM((frames, width), f32)],
        us=2.1,
    )
    world_feed = global_feed.third()
    global_mix.second()
    local_mix.fourth()
    world_mix = global_mix.third()
    feed_sum = local_feed.gathered(info, world_feed)
    arrived_start = swap(given_start, "section", 1)
    both_start = jnp.stack(
        [
            jnp.where(first_core, kept_start, arrived_start),
            jnp.where(first_core, arrived_start, kept_start),
        ]
    )
    code_grad = jnp.transpose(code_part + both_start[:, None], (0, 2, 1, 3))

    own_gain = jnp.concatenate([gain1_g, gain2_g], axis=0)
    total_gain = own_gain + swap(own_gain, "section", 1)
    local_gain = jnp.concatenate([gain1_l, gain2_l], axis=0)
    gain_total = jnp.where(first_core, total_gain, local_gain)
    gain_total = jnp.concatenate(
        [
            lax.dynamic_slice_in_dim(gain_total, (low ^ m) * UNIT, UNIT, 1)
            for m in range(QUARTERS)
        ],
        axis=1,
    )
    def over(value, axis):
        copies = jnp.broadcast_to(value, (lax.axis_size(axis),) + value.shape)
        return jnp.sum(lax.all_to_all(order.after(copies), axis, 0, 0), axis=0)

    gain_total = over(gain_total, "tensor")
    order.until(gain_total)
    packed_gain = call(
        gain_pack_kernel, [shape((GAIN_ROWS, UNIT), low16)], (gain_total,), [VM], us=0.7
    )[0]
    mix_sum = local_mix.gathered(info, world_mix, packed_gain)
    output = call(
        output_kernel,
        [shape((utts, code_count, frames, width // 2), low16)],
        (info, hidden_l, own_branch, other_branch) + far_branch,
        [SM] + [VM] * 5,
        us=3.1,
    )[0]
    order.until(*feed_sum.near)
    feed_parts = feed_sum.far()
    def finals(count, rows, columns):
        return [
            pltpu.VMEM((count,) + rows, f32), pltpu.VMEM((count,) + columns, f32), sem(2 * count)
        ]

    feed_shapes = [shape((width, wide), f32), shape((wide, width), f32)]
    mix_shapes = [shape((3, width, heads_width), f32), shape((heads_width, width), f32)]
    feed_part = ((UNIT, wide), (wide, UNIT))
    mix_part = ((3, UNIT, heads_width), (heads_width, UNIT))
    feed_grads = call(
        feed_near_kernel,
        feed_shapes,
        (info,) + feed_parts[:3],
        [SM] + [VM] * 3,
        finals(3, *feed_part),
        us=5,
        place=ANY,
    )
    mix_sum.near = order.after(mix_sum.near)
    mix_parts = mix_sum.far()
    mix_grads = call(
        mix_near_kernel,
        mix_shapes,
        (info,) + mix_parts[:3],
        [SM] + [VM] * 3,
        finals(3, *mix_part),
        us=3,
        place=ANY,
    )
    up_grad, down_grad = call(
        feed_far_kernel,
        feed_shapes,
        (info,) + feed_parts[3:] + tuple(feed_grads),
        [SM] + [VM] * 2 + [ANY] * 2,
        finals(1, *feed_part),
        us=2,
        place=ANY,
        aliases=((3, 0), (4, 1)),
    )
    qkv_grad, out_grad, gain_total = call(
        mix_far_kernel,
        mix_shapes + [shape((2, width), f32)],
        (info,) + mix_parts + tuple(mix_grads),
        [SM] + [VM] * 5 + [ANY] * 2,
        finals(1, *mix_part),
        us=1.5,
        place=(ANY, ANY, VM),
        aliases=((6, 0), (7, 1)),
    )
    step = QUARTERS
    while step < lax.axis_size("dp"):
        gain_total = gain_total + swap(gain_total, "dp", step)
        step *= 2
    return (
        jnp.transpose(output, (0, 2, 1, 3)),
        code_grad,
        gain_total[None],
        jnp.transpose(qkv_grad, (1, 0, 2))[None],
        out_grad[None],
        up_grad[None],
        down_grad[None],
    )


def solution(mesh):
    in_specs = (
        P("dp", "tensor", None, None),
        P("dp"),
        P("section", None, None),
        P("section", None, None, "tensor"),
        P("section", "tensor", None),
        P("section", None, "tensor"),
        P("section", "tensor", None),
        P("dp", "tensor", None, None),
    )
    out_specs = (
        P("dp", "tensor", None, "section"),
        P("dp", "tensor", None, "section"),
        P("section", None, None),
        P("section", None, None, "tensor"),
        P("section", "tensor", None),
        P("section", None, "tensor"),
        P("section", "tensor", None),
    )
    return jax.shard_map(
        on_device, mesh=mesh, in_specs=in_specs, out_specs=out_specs, check_vma=False
    )
```

```python
import functools

import jax
import jax.numpy as jnp
from jax import lax
from jax.experimental import pallas as pl
from jax.experimental.pallas import tpu as pltpu
from jax.sharding import PartitionSpec as P

HEAD_DIM = 64
SCALE = HEAD_DIM ** (-0.5)
QUARTERS = 4
UNIT = 256
epsilon = 1e-06
negative = -1e30
f32 = jnp.float32
low16 = jnp.bfloat16

VM = pl.BlockSpec(memory_space=pltpu.VMEM)
SM = pl.BlockSpec(memory_space=pltpu.SMEM)
ANY = pl.BlockSpec(memory_space=pltpu.HBM)
MIB = 1 << 20
PACE = 0

LOW, SEC, SHARD, LENGTHS = 0, 1, 2, 3


def shape(dims, dtype):
    return jax.ShapeDtypeStruct(tuple(dims), dtype)


class Order:
    def __init__(self):
        self.tokens = ()

    def after(self, value):
        if not self.tokens:
            return value
        return lax.optimization_barrier((value,) + self.tokens)[0]

    def until(self, *values):
        self.tokens += values

    def call(self, body, outs, args, specs, scratch=(), limit=36, us=2.0, grid=(), place=VM, aliases=()):
        args = (self.after(args[0]),) + tuple(args[1:])
        results = pl.pallas_call(
            body,
            out_shape=tuple(outs),
            grid=grid,
            in_specs=list(specs),
            out_specs=place if isinstance(place, tuple) else (place,) * len(outs),
            input_output_aliases=dict(aliases),
            scratch_shapes=list(scratch),
            compiler_params=pltpu.CompilerParams(vmem_limit_bytes=limit * MIB),
            cost_estimate=pl.CostEstimate(
                flops=int(us * PACE), bytes_accessed=0, transcendentals=0
            ),
        )(*args)
        self.tokens = (results[-1],)
        return results


def swap(value, axis, flip):
    count = lax.axis_size(axis)
    return lax.ppermute(value, axis, [(i, i ^ flip) for i in range(count)])


def dot(a, b):
    return jnp.dot(a, b, preferred_element_type=f32)


def dot_tn(a, b):
    return lax.dot_general(a, b, (((0,), (0,)), ((), ())), preferred_element_type=f32)


def dot_nt(a, b):
    return lax.dot_general(a, b, (((1,), (1,)), ((), ())), preferred_element_type=f32)


def factor_of(values):
    return lax.rsqrt(jnp.mean(values * values, axis=-1, keepdims=True) + epsilon)


def norm_back(values, gain, upstream):
    factor = factor_of(values)
    weighted = upstream * gain
    inner = jnp.mean(weighted * values, axis=-1, keepdims=True)
    through = factor * weighted - values * (factor * factor * factor) * inner
    return through, jnp.sum(upstream * values * factor, axis=0, keepdims=True)


def normal_cdf(values):
    return 0.5 * (1.0 + lax.erf(values * (0.5**0.5)))


def gelu_slope(values, cdf):
    return cdf + values * (jnp.exp(-0.5 * values * values) * 0.3989422804014327)


def block_at(low, m):
    return pl.multiple_of((low ^ m) * UNIT, UNIT)


def span(m):
    return slice(m * UNIT, (m + 1) * UNIT)


class Copies:
    def __init__(self, sems):
        self.sems = sems
        self.made = []

    def start(self, src, dst):
        copy = pltpu.make_async_copy(src, dst, self.sems.at[len(self.made)])
        copy.start()
        self.made.append(copy)
        return copy

    def pick(self, own_first, sec, own, other, dst):
        sem = self.sems.at[len(self.made)]

        @pl.when((sec == 0) == own_first)
        def _():
            pltpu.make_async_copy(own, dst, sem).start()

        @pl.when((sec == 0) != own_first)
        def _():
            pltpu.make_async_copy(other, dst, sem).start()

        copy = pltpu.make_async_copy(own, dst, sem)
        self.made.append(copy)
        return copy

    def wait(self, begin=0, end=None):
        for copy in self.made[begin:end]:
            copy.wait()


def start_kernel(info, codes, own_gain, other_gain, first, start, gain_g, gain_l):
    low, sec = info[LOW], info[SEC]
    for m in range(QUARTERS):
        at = pl.ds(block_at(low, m), UNIT)
        own, other = own_gain[:, at], other_gain[:, at]
        gain_g[:, span(m)] = jnp.where(sec == 0, own, other)
        gain_l[:, span(m)] = jnp.where(sec == 0, other, own)
        total = codes[sec, 0, :, at].astype(f32)
        for c in range(1, codes.shape[1]):
            total = total + codes[sec, c, :, at].astype(f32)
        start[:, span(m)] = total
    values = start[...]
    first[...] = (values * factor_of(values) * gain_g[0:1, :]).astype(low16)


def from_local(sec, own, other, branch):
    @pl.when(sec == 0)
    def _():
        branch(0, *other)

    @pl.when(sec != 0)
    def _():
        branch(1, *own)


def mix_piece_kernel(info, own_qkv, other_qkv, own_out, other_out, piece, whole, sems):
    low, sec = info[LOW], info[SEC]
    half = own_qkv.shape[2] // 2

    def branch(half_index, qkv, out):
        made = Copies(sems)
        for m in range(QUARTERS):
            at = pl.ds(block_at(low, m), UNIT)
            at_right = pl.ds(pl.multiple_of(block_at(low, m) + half, half), half)
            at_left = pl.ds(block_at(low, m), half)
            lanes = slice(half_index * half, (half_index + 1) * half)
            target = whole.at[m]
            made.start(qkv.at[0, at, lanes], target.at[0, :, 0:half])
            made.start(qkv.at[1, at, lanes], target.at[0, :, half : 2 * half])
            made.start(qkv.at[2, at, lanes], target.at[1, :, 0:half])
            made.start(out.at[lanes, at_left], target.at[1, 0:half, half : 2 * half])
            made.start(out.at[lanes, at_right], target.at[1, half : 2 * half, half : 2 * half])
        made.wait()

    from_local(sec, (own_qkv, own_out), (other_qkv, other_out), branch)
    piece[...] = whole[0]


def feed_piece_kernel(info, own_up, other_up, own_down, other_down, piece, whole, sems):
    low, sec = info[LOW], info[SEC]
    wide = own_up.shape[1] // 2

    def branch(half_index, up, down):
        made = Copies(sems)
        for m in range(QUARTERS):
            at = pl.ds(block_at(low, m), UNIT)
            for part in range(2):
                begin = half_index * wide + part * UNIT
                hidden = slice(begin, begin + UNIT)
                made.start(up.at[at, hidden], whole.at[m, part])
                made.start(down.at[hidden, at], whole.at[m, 2 + part])
        made.wait()

    from_local(sec, (own_up, own_down), (other_up, other_down), branch)
    piece[...] = whole[0]


def fetch_attention(made, low, sec, own_qkv, other_qkv, own_out, other_out, qkv, out):
    for m in range(QUARTERS):
        at = pl.ds(block_at(low, m), UNIT)
        made.pick(True, sec, own_qkv.at[:, at, :], other_qkv.at[:, at, :], qkv.at[:, span(m), :])
    for m in range(QUARTERS):
        at = pl.ds(block_at(low, m), UNIT)
        made.pick(True, sec, own_out.at[:, at], other_out.at[:, at], out.at[:, span(m)])


def by_shard(info, blocks):
    count = blocks.shape[0]
    return jnp.concatenate([blocks[info[SHARD] ^ k] for k in range(count)], axis=0)


def other_half(info, width):
    half = width // 2
    return pl.ds(pl.multiple_of((1 - info[SEC]) * half, half), half)


def spread_blocks(info, target, values):
    frames = target.shape[1]
    for k in range(target.shape[0]):
        target[info[SHARD] ^ k] = values[k * frames : (k + 1) * frames].astype(low16)


def row_places(info, count, frames, dimension):
    at = lax.broadcasted_iota(jnp.int32, (count, count), dimension)
    return (lax.div(at, frames) ^ info[SHARD]) * frames + lax.rem(at, frames)


def global_attention_kernel(info, *rest):
    (blocks, own_qkv, other_qkv, own_out, other_out,
     rows, packed, probs, mixed, given, partial, qkv, out, sems) = rest
    low, sec = info[LOW], info[SEC]
    made = Copies(sems)
    fetch_attention(made, low, sec, own_qkv, other_qkv, own_out, other_out, qkv, out)
    count, frames = rows.shape[0], blocks.shape[1]
    length = info[LENGTHS + sec]
    query_at = row_places(info, count, frames, 0)
    key_at = row_places(info, count, frames, 1)
    allowed = (key_at <= query_at) & (key_at < length)
    values = by_shard(info, blocks)
    rows[...] = values
    made.wait(0, QUARTERS)
    for c in range(3):
        packed[c] = dot(values, qkv[c]).astype(low16)
    heads = []
    for h in range(packed.shape[2] // HEAD_DIM):
        lanes = slice(h * HEAD_DIM, (h + 1) * HEAD_DIM)
        scores = dot_nt(packed[0, :, lanes], packed[1, :, lanes]) * SCALE
        scores = jnp.where(allowed, scores, negative)
        raised = jnp.exp(scores - jnp.max(scores, axis=-1, keepdims=True))
        exact = raised / jnp.sum(raised, axis=-1, keepdims=True)
        probs[h] = exact.astype(low16)
        heads.append(dot(exact.astype(low16), packed[2, :, lanes]).astype(low16))
    mixed[...] = jnp.concatenate(heads, axis=1)
    given[...] = mixed[:, other_half(info, mixed.shape[1])]
    made.wait(QUARTERS)
    spread_blocks(info, partial, dot(mixed[...], out[...]))


def total_of(arrived):
    total = arrived[0].astype(f32)
    for k in range(1, arrived.shape[0]):
        total = total + arrived[k].astype(f32)
    return total


def middle_kernel(start, arrived, gain, hidden, second):
    values = start[...] + total_of(arrived)
    hidden[...] = values
    second[...] = (values * factor_of(values) * gain[1:2, :]).astype(low16)


def fetch_feed(made, low, sec, own_up, other_up, own_down, other_down, up, down):
    for m in range(QUARTERS):
        at = pl.ds(block_at(low, m), UNIT)
        made.pick(True, sec, own_up.at[at, :], other_up.at[at, :], up.at[span(m), :])
    for m in range(QUARTERS):
        at = pl.ds(block_at(low, m), UNIT)
        made.pick(True, sec, own_down.at[:, at], other_down.at[:, at], down.at[:, span(m)])


def global_feed_kernel(info, *rest):
    (blocks, own_up, other_up, own_down, other_down,
     rows, lifted, active, given, partial, up, down, total, sems) = rest
    made = Copies(sems)
    fetch_feed(made, info[LOW], info[SEC], own_up, other_up, own_down, other_down, up, down)
    values = by_shard(info, blocks)
    rows[...] = values
    made.wait(0, QUARTERS)
    for t in range(up.shape[1] // UNIT):
        tile = dot(values, up[:, span(t)])
        lifted[:, span(t)] = tile
        low_tile = (tile * normal_cdf(tile)).astype(low16)
        active[:, span(t)] = low_tile
        if t == 0:
            made.wait(QUARTERS)
        branch = dot(low_tile, down[span(t), :])
        total[...] = branch if t == 0 else total[...] + branch
    spread_blocks(info, partial, total[...])
    given[...] = active[:, other_half(info, active.shape[1])]


def sent_kernel(hidden, arrived, sent):
    sent[...] = (hidden[...] + total_of(arrived)).astype(low16)


def global_feed_back_kernel(info, *rest):
    (blocks, lifted, own_up, other_up, own_down, other_down,
     rows, grad_lifted, given, partial, up, down, total, sems) = rest
    made = Copies(sems)
    fetch_feed(made, info[LOW], info[SEC], own_up, other_up, own_down, other_down, up, down)
    values = by_shard(info, blocks)
    rows[...] = values
    made.wait(QUARTERS)
    for t in range(up.shape[1] // UNIT):
        tile = lifted[:, span(t)]
        grad = dot_nt(values, down[span(t), :]) * gelu_slope(tile, normal_cdf(tile))
        grad = grad.astype(low16)
        grad_lifted[:, span(t)] = grad
        if t == 0:
            made.wait(0, QUARTERS)
        back = dot_nt(grad, up[:, span(t)])
        total[...] = back if t == 0 else total[...] + back
    spread_blocks(info, partial, total[...])
    given[...] = grad_lifted[:, other_half(info, grad_lifted.shape[1])]


def middle_back_kernel(arrived, hidden, gain, returned, grad_hidden, mid, gain_grad):
    through, gain_grad[...] = norm_back(hidden[...], gain[1:2, :], total_of(arrived))
    values = returned[...].astype(f32) + through
    grad_hidden[...] = values
    mid[...] = values.astype(low16)


def global_attention_back_kernel(info, *rest):
    (blocks, packed, probs, own_qkv, other_qkv, own_out, other_out,
     rows, grads, given, partial, qkv, out, sems) = rest
    low, sec = info[LOW], info[SEC]
    made = Copies(sems)
    fetch_attention(made, low, sec, own_qkv, other_qkv, own_out, other_out, qkv, out)
    values = by_shard(info, blocks)
    rows[...] = values
    made.wait(QUARTERS)
    grad_mixed = dot_nt(values, out[...]).astype(low16)
    columns = [[], [], []]
    for h in range(packed.shape[2] // HEAD_DIM):
        lanes = slice(h * HEAD_DIM, (h + 1) * HEAD_DIM)
        exact = probs[h].astype(f32)
        grad = grad_mixed[:, lanes]
        columns[2].append(dot_tn(exact.astype(low16), grad).astype(low16))
        grad_probs = dot_nt(grad, packed[2, :, lanes])
        center = jnp.sum(grad_probs * exact, axis=-1, keepdims=True)
        grad_scores = (exact * (grad_probs - center)).astype(low16)
        columns[0].append((dot(grad_scores, packed[1, :, lanes]) * SCALE).astype(low16))
        columns[1].append((dot_tn(grad_scores, packed[0, :, lanes]) * SCALE).astype(low16))
    total = None
    made.wait(0, QUARTERS)
    for c in range(3):
        grads[c] = jnp.concatenate(columns[c], axis=1)
        back = dot_nt(grads[c], qkv[c])
        total = back if c == 0 else total + back
    spread_blocks(info, partial, total)
    given[...] = grads[:, :, other_half(info, grads.shape[2])]


def start_back_kernel(info, arrived, start, gain, grad_hidden, kept, given, gain_grad, values):
    low, sec = info[LOW], info[SEC]
    through, gain_grad[...] = norm_back(start[...], gain[0:1, :], total_of(arrived))
    values[...] = grad_hidden[...] + through
    for j in range(2):
        kept[:, span(j)] = values[:, pl.ds(block_at(low, 2 * sec + j), UNIT)]
        given[:, span(j)] = values[:, pl.ds(block_at(low, 2 * (1 - sec) + j), UNIT)]


def mix_unit(refs, k, m, u):
    whole, near, x_part, y_part, far = refs[0], refs[1:4], refs[4], refs[5], refs[6:8]
    if k == 0:
        return whole.at[m, u]
    if m == 0:
        return near[k - 1].at[u]
    if m == 3:
        return far[u].at[k - 1]
    return (x_part if m == 1 else y_part).at[u, k - 1]


def feed_unit(refs, k, m, u):
    if k == 0:
        return refs[0].at[m, u]
    if m < 3:
        return refs[1 + m].at[u]
    return refs[4].at[u] if u < 2 else refs[5].at[u - 2]


MIX_REFS, FEED_REFS = 8, 6


def pair_rows(a, b, size):
    return jnp.concatenate([a * b, a[size:] * b[: 2 * size], a[2 * size :] * b[:size]], axis=0)


def by_pair(stacked, size):
    names = [(0, 0), (1, 1), (2, 2), (1, 0), (2, 1), (2, 0)]
    return {name: stacked[n * size : (n + 1) * size] for n, name in enumerate(names)}


def from_pairs(pairs):
    names = [(0, 0), (1, 1), (2, 2), (1, 0), (2, 1), (2, 0)]
    return jnp.concatenate([pairs[name] for name in names], axis=0)


def head_sums(products, table):
    upper = products.astype(low16)
    lower = (products - upper.astype(f32)).astype(low16)
    return dot(upper, table) + dot(lower, table)


def head_table(width):
    row = lax.broadcasted_iota(jnp.int32, (width, width), 0) // HEAD_DIM
    column = lax.broadcasted_iota(jnp.int32, (width, width), 1) // HEAD_DIM
    return (row == column).astype(f32).astype(low16)


def gather_mix(weights, mix, k, half):
    for m in range(QUARTERS):
        begin = m * UNIT
        mix[k * half : (k + 1) * half, begin : begin + half] = weights[
            k, 1, begin : begin + half, half:
        ]
        mix[k * half : (k + 1) * half, begin + half : begin + UNIT] = weights[
            k, 1, begin + half : begin + UNIT, half:
        ]


def local_attention_kernel(info, codes, sent_own, sent_other, gain, *rest):
    refs, (start, first, query_keys, values_out, probs, mixed, partial, weights, mix, sems) = (
        rest[:MIX_REFS], rest[MIX_REFS:]
    )
    low, sec = info[LOW], info[SEC]
    made = Copies(sems)
    groups = []
    for k in range(4):
        groups.append(
            [
                made.start(mix_unit(refs, k, m, u), weights.at[k, u, span(m), :])
                for u in range(2)
                for m in range(QUARTERS)
            ]
        )
    utts, code_count, frames, _ = codes.shape
    for u in range(utts):
        sent = jnp.where(sec == u, sent_own[...], sent_other[...]).astype(f32)
        for c in range(code_count):
            row = (u * code_count + c) * frames
            for m in range(QUARTERS):
                code = codes[u, c, :, pl.ds(block_at(low, m), UNIT)].astype(f32)
                start[row : row + frames, span(m)] = sent[:, span(m)] + code
    values = start[...]
    first[...] = (values * factor_of(values) * gain[0:1, :]).astype(low16)
    half = values_out.shape[2]
    table = head_table(half)
    rows = first[...]
    size = frames
    group = code_count * frames
    for k in range(4):
        for copy in groups[k]:
            copy.wait()
        query_keys[k] = dot(rows, weights[k, 0]).astype(low16)
        values_out[k] = dot(rows, weights[k, 1, :, :half]).astype(low16)
        gather_mix(weights, mix, k, half)
        for u in range(utts):
            at = slice(u * group, (u + 1) * group)
            q = query_keys[k, at, :half].astype(f32)
            key = query_keys[k, at, half:].astype(f32)
            val = values_out[k, at, :].astype(f32)
            scores = by_pair(head_sums(pair_rows(q, key, size), table) * SCALE, size)
            exact = {}
            for i in range(3):
                peak = scores[(i, 0)]
                for j in range(1, i + 1):
                    peak = jnp.maximum(peak, scores[(i, j)])
                raised = [jnp.exp(scores[(i, j)] - peak) for j in range(i + 1)]
                whole = raised[0]
                for j in range(1, i + 1):
                    whole = whole + raised[j]
                for j in range(i + 1):
                    exact[(i, j)] = raised[j] / whole
            probs[k, u] = from_pairs(exact).astype(low16)
            for i in range(3):
                total = None
                for j in range(i + 1):
                    weight = exact[(i, j)].astype(low16).astype(f32)
                    term = weight * val[j * size : (j + 1) * size]
                    total = term if total is None else total + term
                begin = u * group + i * size
                mixed[begin : begin + size, k * half : (k + 1) * half] = total.astype(low16)
    partial[...] = dot(mixed[...], mix[...]).astype(low16)


def local_top_kernel(info, cotangent, top, given):
    low, sec = info[LOW], info[SEC]
    utts, code_count, frames, _ = cotangent.shape
    group = code_count * frames
    frame_at = lax.broadcasted_iota(jnp.int32, (frames, 1), 0) + info[SHARD] * frames
    for u in range(utts):
        valid = frame_at < info[LENGTHS + u]
        for c in range(code_count):
            row = u * group + c * frames
            for m in range(QUARTERS):
                part = cotangent[u, c, :, pl.ds(block_at(low, m), UNIT)].astype(f32)
                top[row : row + frames, span(m)] = jnp.where(valid, part, 0.0).astype(low16)
    given[...] = top[pl.ds(pl.multiple_of(sec * group, group), group), :]


def local_norm_kernel(info, start, own_part, other_part, gain, hidden, second, given):
    values = start[...] + (own_part[...].astype(f32) + other_part[...].astype(f32))
    hidden[...] = values
    second[...] = (values * factor_of(values) * gain[1:2, :]).astype(low16)
    group = given.shape[0]
    given[...] = second[pl.ds(pl.multiple_of(info[SEC] * group, group), group), :]


def feed_tiles(refs, second, top, active, grad_lifted, up, down, back, sems):
    tiles = active.shape[0]
    made = Copies(sems)
    for t in range(tiles):
        for m in range(QUARTERS):
            made.start(feed_unit(refs, t // 2, m, t % 2), up.at[t, span(m), :])
        for m in range(QUARTERS):
            made.start(feed_unit(refs, t // 2, m, 2 + t % 2), down.at[t, :, span(m)])
    back[...] = jnp.zeros_like(back)

    @pl.loop(0, tiles)
    def _(t):
        for m in range(QUARTERS):
            pltpu.make_async_copy(
                refs[0].at[0, 0], up.at[t, span(m), :], sems.at[8 * t + m]
            ).wait()
        for m in range(QUARTERS):
            pltpu.make_async_copy(
                refs[0].at[0, 0], down.at[t, :, span(m)], sems.at[8 * t + 4 + m]
            ).wait()
        tile = dot(second[...], up[t])
        cdf = normal_cdf(tile)
        active[t] = (tile * cdf).astype(low16)
        grad = (dot_nt(top[...], down[t]) * gelu_slope(tile, cdf)).astype(low16)
        grad_lifted[t] = grad
        back[...] += dot_nt(grad, up[t])


def local_feed_kernel(second, top, *rest):
    refs, (active, grad_lifted, grad_second, up, down, back, sems) = (
        rest[:FEED_REFS], rest[FEED_REFS:]
    )
    feed_tiles(refs, second, top, active, grad_lifted, up, down, back, sems)
    grad_second[...] = back[...].astype(low16)


def far_feed_kernel(second_same, second_cross, top_same, top_cross, *rest):
    refs = rest[:FEED_REFS]
    (active, grad_lifted, second, top, same, cross, up, down, back, sems) = rest[FEED_REFS:]
    group = same.shape[0]
    second[:group] = second_same[...]
    second[group:] = second_cross[...]
    top[:group] = top_same[...]
    top[group:] = top_cross[...]
    feed_tiles(refs, second, top, active, grad_lifted, up, down, back, sems)
    same[...] = back[:group].astype(low16)
    cross[...] = back[group:].astype(low16)


def pair_kernel(a, b, total):
    total[...] = add16(a[...], b[...])


def with_far(sec, rows, own, other, far_same, far_cross):
    group = far_same.shape[0]
    parts = []
    for u in range(rows // group):
        at = slice(u * group, (u + 1) * group)
        far = jnp.where(sec == u, far_same[...], far_cross[...]).astype(f32)
        parts.append(own[at, :].astype(f32) + other[at, :].astype(f32) + far)
    return jnp.concatenate(parts, axis=0)


def local_attention_back_kernel(info, hidden, own_back, other_back, far_same, far_cross, top, gain,
                                query_keys, values_in, probs, *rest):
    refs = rest[:MIX_REFS]
    (grad_hidden, mid, grad_query_keys, grad_values, grad_first, gain_grad,
     weights, mix, total, sems) = rest[MIX_REFS:]
    made = Copies(sems)
    groups = []
    for k in range(4):
        groups.append(
            [
                made.start(mix_unit(refs, k, m, u), weights.at[k, u, span(m), :])
                for u in range(2)
                for m in range(QUARTERS)
            ]
        )
    upstream = with_far(info[SEC], hidden.shape[0], own_back, other_back, far_same, far_cross)
    through, gain_grad[...] = norm_back(hidden[...], gain[1:2, :], upstream)
    grads = top[...].astype(f32) + through
    grad_hidden[...] = grads
    mid[...] = grads.astype(low16)
    utts = probs.shape[1]
    half = values_in.shape[2]
    group = query_keys.shape[1] // utts
    size = group // 3
    table = head_table(half)
    for k in range(4):
        for copy in groups[k]:
            copy.wait()
        gather_mix(weights, mix, k, half)
        grad_mixed = dot_nt(mid[...], mix[k * half : (k + 1) * half, :]).astype(low16)
        grad_mixed = grad_mixed.astype(f32)
        for u in range(utts):
            at = slice(u * group, (u + 1) * group)
            q = query_keys[k, at, :half].astype(f32)
            key = query_keys[k, at, half:].astype(f32)
            val = values_in[k, at, :].astype(f32)
            grad = grad_mixed[at]
            exact = by_pair(probs[k, u].astype(f32), size)
            grad_probs = by_pair(head_sums(pair_rows(grad, val, size), table), size)
            scored = {}
            for i in range(3):
                center = grad_probs[(i, 0)] * exact[(i, 0)]
                for j in range(1, i + 1):
                    center = center + grad_probs[(i, j)] * exact[(i, j)]
                for j in range(i + 1):
                    score = exact[(i, j)] * (grad_probs[(i, j)] - center)
                    scored[(i, j)] = score.astype(low16).astype(f32)

            def rows_of(array, n):
                return array[n * size : (n + 1) * size]

            for i in range(3):
                begin = u * group + i * size
                to_query = sum(scored[(i, j)] * rows_of(key, j) for j in range(i + 1))
                to_key = sum(scored[(n, i)] * rows_of(q, n) for n in range(i, 3))
                to_value = sum(
                    exact[(n, i)].astype(low16).astype(f32) * rows_of(grad, n)
                    for n in range(i, 3)
                )
                grad_query_keys[k, begin : begin + size, :half] = (to_query * SCALE).astype(low16)
                grad_query_keys[k, begin : begin + size, half:] = (to_key * SCALE).astype(low16)
                grad_values[k, begin : begin + size, :] = to_value.astype(low16)
        back = dot_nt(grad_query_keys[k], weights[k, 0])
        back = back + dot_nt(grad_values[k], weights[k, 1, :, :half])
        total[...] = back if k == 0 else total[...] + back
    grad_first[...] = total[...].astype(low16)


def local_end_kernel(info, own_back, other_back, start, grad_hidden, gain,
                     returned, code_part, gain_grad, values):
    low, sec = info[LOW], info[SEC]
    upstream = own_back[...].astype(f32) + other_back[...].astype(f32)
    through, gain_grad[...] = norm_back(start[...], gain[0:1, :], upstream)
    values[...] = grad_hidden[...] + through
    utts, code_count, frames, _ = code_part.shape
    total = None
    for c in range(code_count):
        begin = pl.multiple_of((sec * code_count + c) * frames, frames)
        part = values[pl.ds(begin, frames), :]
        total = part if total is None else total + part
    returned[...] = total.astype(low16)
    for u in range(utts):
        for c in range(code_count):
            row = (u * code_count + c) * frames
            for j in range(2):
                at = pl.ds(block_at(low, 2 * sec + j), UNIT)
                code_part[u, c, :, span(j)] = values[row : row + frames, at]


def output_kernel(info, hidden, own_part, other_part, far_same, far_cross, output):
    low, sec = info[LOW], info[SEC]
    utts, code_count, frames, _ = output.shape
    group = code_count * frames
    frame_at = lax.broadcasted_iota(jnp.int32, (frames, 1), 0) + info[SHARD] * frames
    for u in range(utts):
        valid = frame_at < info[LENGTHS + u]
        for c in range(code_count):
            rows = slice(u * group + c * frames, u * group + (c + 1) * frames)
            inner = slice(c * frames, (c + 1) * frames)
            for j in range(2):
                at = pl.ds(block_at(low, 2 * sec + j), UNIT)
                far = jnp.where(sec == u, far_same[inner, at], far_cross[inner, at])
                value = hidden[rows, at] + (
                    own_part[rows, at].astype(f32)
                    + other_part[rows, at].astype(f32)
                    + far.astype(f32)
                )
                output[u, c, :, span(j)] = jnp.where(valid, value, 0.0).astype(low16)


SEND_A, KEEP_A, SEND_B, KEEP_B = (1, 3), (0, 2), (2, 3), (0, 1)


def local_drop_kernel(own_active, far_active, *rest):
    refs, (own_branch, same, cross, down, branch, sems) = rest[:FEED_REFS], rest[FEED_REFS:]
    tiles, count, _ = own_active.shape
    made = Copies(sems)
    for t in range(tiles):
        for m in range(QUARTERS):
            made.start(feed_unit(refs, t // 2, m, 2 + t % 2), down.at[t, :, span(m)])
    branch[...] = jnp.zeros_like(branch)

    @pl.loop(0, tiles)
    def _(t):
        for m in range(QUARTERS):
            pltpu.make_async_copy(
                refs[0].at[0, 0], down.at[t, :, span(m)], sems.at[QUARTERS * t + m]
            ).wait()
        branch[:count] += dot(own_active[t], down[t])
        branch[count:] += dot(far_active[t], down[t])

    own_branch[...] = branch[:count].astype(low16)
    group = same.shape[0]
    same[...] = branch[count : count + group].astype(low16)
    cross[...] = branch[count + group :].astype(low16)


def local_feed_grad_kernel(second, far_second, own_lifted, far_lifted, own_active, far_active,
                           top, far_top, send_a, send_b, keep_a, keep_b, turned, tops):
    count = second.shape[0]
    turned[:, :count] = jnp.transpose(second[...])
    turned[:, count:] = jnp.transpose(far_second[...])
    tops[:count] = top[...]
    tops[count:] = far_top[...]
    for k in range(2):
        for part, pairs in enumerate(
            (((send_a, SEND_A), (keep_a, KEEP_A)), ((send_b, SEND_B), (keep_b, KEEP_B)))
        ):
            t = 2 * k + part
            right = jnp.concatenate([own_lifted[t], far_lifted[t]], axis=0)
            left = jnp.concatenate(
                [jnp.transpose(own_active[t]), jnp.transpose(far_active[t])], axis=1
            )
            for target, order in pairs:
                for place, m in enumerate(order):
                    target[place, 2 * k] = dot(turned[span(m), :], right).astype(low16)
                    target[place, 2 * k + 1] = dot(left, tops[:, span(m)]).astype(low16)


def local_mix_kernel(first, grad_query_keys, grad_values, mixed, mid,
                     send_a, send_b, keep_a, keep_b, turned):
    turned[...] = jnp.transpose(first[...])
    half = grad_values.shape[2]
    for k in range(4):
        left = jnp.transpose(mixed[:, k * half : (k + 1) * half])
        for target, order in ((send_a, SEND_A), (keep_a, KEEP_A)):
            for place, m in enumerate(order):
                target[place, k] = dot(turned[span(m), :], grad_query_keys[k]).astype(low16)
        for target, order in ((send_b, SEND_B), (keep_b, KEEP_B)):
            for place, m in enumerate(order):
                value = dot(turned[span(m), :], grad_values[k]).astype(low16)
                out = dot(left, mid[:, span(m)]).astype(low16)
                target[place, k, :, :half] = value
                target[place, k, :half, half:] = out[:, :half]
                target[place, k, half:, half:] = out[:, half:]


def by_order(send_a, send_b, keep_a, keep_b):
    return (
        (0, ((send_a, SEND_A), (keep_a, KEEP_A))),
        (1, ((send_b, SEND_B), (keep_b, KEEP_B))),
    )


def global_feed_grad_kernel(info, second, far_second, grad_lifted, far_lifted, active, far_active,
                            top, far_top, send_a, send_b, keep_a, keep_b, turned, tops):
    sec, count = info[SEC], second.shape[0]
    turned[:, :count] = jnp.transpose(second[...])
    turned[:, count:] = jnp.transpose(far_second[...])
    tops[:count] = top[...]
    tops[count:] = far_top[...]
    wide = active.shape[1] // 2
    for part, pairs in by_order(send_a, send_b, keep_a, keep_b):
        at = pl.ds(pl.multiple_of(sec * wide + part * UNIT, UNIT), UNIT)
        right = jnp.concatenate([grad_lifted[:, at], far_lifted[:, span(part)]], axis=0)
        left = jnp.concatenate(
            [jnp.transpose(active[:, at]), jnp.transpose(far_active[:, span(part)])], axis=1
        )
        for target, order in pairs:
            for place, m in enumerate(order):
                target[place, 0] = dot(turned[span(m), :], right).astype(low16)
                target[place, 1] = dot(left, tops[:, span(m)]).astype(low16)


def global_mix_grad_kernel(info, first, far_first, grads, far_grads, mixed, far_mixed, mid,
                           far_mid, send_a, send_b, keep_a, keep_b, turned, mids):
    sec, count = info[SEC], first.shape[0]
    turned[:, :count] = jnp.transpose(first[...])
    turned[:, count:] = jnp.transpose(far_first[...])
    mids[:count] = mid[...]
    mids[count:] = far_mid[...]
    width = mixed.shape[1] // 2
    at = pl.ds(pl.multiple_of(sec * width, width), width)
    right = [jnp.concatenate([grads[c, :, at], far_grads[c]], axis=0) for c in range(3)]
    left = jnp.concatenate([jnp.transpose(mixed[:, at]), jnp.transpose(far_mixed[...])], axis=1)
    for part, pairs in by_order(send_a, send_b, keep_a, keep_b):
        for target, order in pairs:
            for place, m in enumerate(order):
                rows = turned[span(m), :]
                if part == 0:
                    for c in range(2):
                        target[place, 0, :, c * width : (c + 1) * width] = dot(
                            rows, right[c]
                        ).astype(low16)
                else:
                    target[place, 0, :, :width] = dot(rows, right[2]).astype(low16)
                    out = dot(left, mids[:, span(m)]).astype(low16)
                    target[place, 0, :width, width:] = out[:, :width]
                    target[place, 0, width:, width:] = out[:, width:]


def add16(a, b):
    return (a.astype(f32) + b.astype(f32)).astype(low16)


def far_kernel(keep_a, from_x, keep_b, from_y, far_a, far_b):
    far_a[...] = add16(keep_a[0], from_x[0])
    far_b[...] = add16(keep_b[0], from_y[0])


def sum_kernel(shards, *refs):
    parts, outs = (refs[:3], refs[3:6]), refs[6:]
    for part, (keep, once, twice) in enumerate(parts):
        total = keep[0].astype(f32) + once[0].astype(f32) + twice[...].astype(f32)
        total = total.astype(low16)
        count = total.shape[0] // shards
        at = slice(part * count, (part + 1) * count)
        if shards == 1:
            outs[0][at] = total
        elif shards == 2:
            outs[1][0, at] = total[:count]
            outs[0][0, at] = total[count:]
        else:
            for k in range(4):
                outs[(k + 1) % 2][k // 2, at] = total[k * count : (k + 1) * count]


def far_tensor_kernel(keep, arrived, far):
    far[...] = add16(keep[0], arrived[0])


def pick_kernel(info, *refs):
    *terms, world, given, kept = refs
    sec = info[SEC]
    local = terms[0][0].astype(f32)
    for term in terms[1:]:
        local = local + (term[0] if len(term.shape) == 4 else term[...]).astype(f32)
    local = local.astype(low16)
    other = world[...]
    given[...] = jnp.where(sec == 0, local, other)
    kept[...] = jnp.where(sec == 0, other, local)


def half_at(index, count):
    return pl.BlockSpec(
        (1, count, UNIT, UNIT), lambda i: (index, 0, 0, 0), memory_space=pltpu.VMEM
    )


def quarter_unit(refs, m, index):
    own, x_part, y_part, far_kept, far_arrived = refs
    count = own.shape[0] // 2
    if m < 3:
        return (own, x_part, y_part)[m][index].astype(f32)
    return (far_kept[index] if index < count else far_arrived[index - count]).astype(f32)


def write_feed(info, quarters, unit, count, up, down, rows, columns, sems):
    low, sec = info[LOW], info[SEC]
    wide = up.shape[1] // 2
    made = Copies(sems)
    for place, m in enumerate(quarters):
        at = pl.ds(block_at(low, m), UNIT)
        for source, half in ((0, sec), (count, 1 - sec)):
            for part in range(2):
                hidden = pl.ds(pl.multiple_of(half * wide + part * UNIT, UNIT), UNIT)
                rows[place, :, hidden] = unit(m, source + 2 * part)
                columns[place, hidden, :] = unit(m, source + 2 * part + 1)
        made.start(rows.at[place], up.at[at, :])
        made.start(columns.at[place], down.at[:, at])
    made.wait()


def feed_near_kernel(info, own, x_part, y_part, up, down, rows, columns, sems):
    parts = (own, x_part, y_part)
    write_feed(
        info, (0, 1, 2), lambda m, n: parts[m][n].astype(f32), own.shape[0] // 2,
        up, down, rows, columns, sems,
    )


def feed_far_kernel(info, far_kept, far_arrived, up_before, down_before,
                    up, down, rows, columns, sems):
    count = far_kept.shape[0]

    def unit(m, n):
        return (far_kept[n] if n < count else far_arrived[n - count]).astype(f32)

    write_feed(info, (3,), unit, count, up, down, rows, columns, sems)


def write_mix(info, quarters, unit, count, qkv, out, rows, columns, sems):
    low, sec = info[LOW], info[SEC]
    width = out.shape[0] // 2
    made = Copies(sems)
    for place, m in enumerate(quarters):
        at = pl.ds(block_at(low, m), UNIT)
        for source, half in ((0, sec), (count, 1 - sec)):
            lanes = pl.ds(pl.multiple_of(half * width, width), width)
            query_keys = unit(m, source)
            rows[place, 0, :, lanes] = query_keys[:, :width]
            rows[place, 1, :, lanes] = query_keys[:, width:]
            rest_unit = unit(m, source + 1)
            rows[place, 2, :, lanes] = rest_unit[:, :width]
            columns[place, lanes, :width] = rest_unit[:width, width:]
            columns[place, lanes, width:] = rest_unit[width:, width:]
        made.start(rows.at[place], qkv.at[:, at, :])
        made.start(columns.at[place], out.at[:, at])
    made.wait()


GAIN_ROWS = 32


def gain_pack_kernel(gain, packed):
    rows = []
    for g in range(gain.shape[0]):
        rest = gain[g : g + 1, :]
        for _ in range(3):
            part = rest.astype(low16).astype(f32)
            rest = rest - part
            rows += [part[:, span(m)] for m in range(QUARTERS)]
    rows.append(jnp.zeros((GAIN_ROWS - len(rows), UNIT), f32))
    packed[...] = jnp.concatenate(rows, axis=0).astype(low16)


def unit_rows(ref, n):
    return ref[n * UNIT : (n + 1) * UNIT, :].astype(f32)


def mix_near_kernel(info, own, x_part, y_part, qkv, out, rows, columns, sems):
    parts = (own, x_part, y_part)
    count = (own.shape[0] - GAIN_ROWS) // (2 * UNIT)
    write_mix(
        info, (0, 1, 2), lambda m, n: unit_rows(parts[m], n), count, qkv, out, rows, columns, sems
    )


def mix_far_kernel(info, own, x_part, y_part, far_kept, far_arrived, qkv_before, out_before,
                   qkv, out, gain, rows, columns, sems):
    count = far_kept.shape[0] // UNIT

    def unit(m, n):
        return unit_rows(far_kept, n) if n < count else unit_rows(far_arrived, n - count)

    total = None
    for ref in (own, x_part, y_part, far_arrived):
        part = ref[ref.shape[0] - GAIN_ROWS :, :].astype(f32)
        total = part if total is None else total + part
    for g in range(gain.shape[0]):
        for m in range(QUARTERS):
            at = [3 * QUARTERS * g + QUARTERS * t + m for t in range(3)]
            gain[g : g + 1, span(m)] = (
                total[at[0] : at[0] + 1] + total[at[1] : at[1] + 1] + total[at[2] : at[2] + 1]
            )
    write_mix(info, (3,), unit, count, qkv, out, rows, columns, sems)


def sum_rest(value):
    step = QUARTERS
    while step < lax.axis_size("dp"):
        value = add16(value, swap(value, "dp", step))
        step *= 2
    return value


class Sum:
    def __init__(self, order, shards, send_a, send_b, keep_a, keep_b):
        self.order, self.shards = order, shards
        self.keep = (keep_a, keep_b)
        self.count = keep_a.shape[1]
        self.once = (swap(send_a, "dp", 1), swap(send_b, "dp", 2))

    def second(self):
        far = half_at(1, self.count)
        far_a, far_b = self.order.call(
            far_kernel,
            [shape((self.count, UNIT, UNIT), low16)] * 2,
            (self.keep[0], self.once[0], self.keep[1], self.once[1]),
            [far] * 4,
            grid=(1,),
        )
        self.twice = (swap(far_a, "dp", 2), swap(far_b, "dp", 1))

    def third(self):
        count = 2 * self.count // self.shards
        if self.shards == 1:
            outs = [shape((count, UNIT, UNIT), low16)]
        else:
            outs = [shape((self.shards // 2, count, UNIT, UNIT), low16)] * 2
        near = half_at(0, self.count)
        totals = self.order.call(
            functools.partial(sum_kernel, self.shards),
            outs,
            (self.keep[0], self.once[0], self.twice[0], self.keep[1], self.once[1], self.twice[1]),
            [near, near, VM] * 2,
            grid=(1,),
        )
        totals = [sum_rest(total) for total in totals]
        self.count = count
        if self.shards == 1:
            return totals[0]
        self.keep = totals[1]
        if self.shards == 2:
            self.terms = (self.keep, swap(totals[0], "tensor", 2))
        else:
            self.once = swap(totals[0], "tensor", 1)

    def fourth(self):
        far = self.order.call(
            far_tensor_kernel,
            [shape((self.count, UNIT, UNIT), low16)],
            (self.keep, self.once),
            [half_at(1, self.count)] * 2,
            grid=(1,),
        )[0]
        self.terms = (self.keep, self.once, swap(far, "tensor", 2))

    def gathered(self, info, world, extra=None):
        near = half_at(0, self.count)
        given, kept = self.order.call(
            pick_kernel,
            [shape((self.count, UNIT, UNIT), low16)] * 2,
            (info,) + self.terms + (world,),
            [SM] + [near if term.ndim == 4 else VM for term in self.terms] + [VM],
            grid=(1,),
        )
        arrived = swap(given, "section", 1)
        if extra is None:
            return Gather(jnp.concatenate([kept, arrived]), self.count)
        rows = [kept.reshape(-1, UNIT), arrived.reshape(-1, UNIT), extra]
        return Gather(jnp.concatenate(rows), self.count * UNIT)


class Gather:
    def __init__(self, units, count):
        self.units, self.count = units, count
        self.near = (swap(units, "dp", 1), swap(units, "dp", 2))

    def far(self):
        x_part, y_part = self.near
        rest = (swap(x_part[: self.count], "dp", 2), swap(y_part[self.count :], "dp", 1))
        return (self.units,) + self.near + rest


def on_device(codes, lengths, gains, w_qkv, w_out, w_up, w_down, cotangent):
    sec = lax.axis_index("section")
    low = lax.axis_index("dp") % QUARTERS
    z = lax.axis_index("tensor")
    first_core = sec == 0
    utts, frames, code_count, width = codes.shape
    heads_width = w_out.shape[1]
    half = heads_width // 2
    wide = w_up.shape[2]
    rows_g = 4 * frames
    rows_l = utts * code_count * frames
    tiles = wide // UNIT
    info = jnp.concatenate([jnp.stack([low, sec, z]).astype(jnp.int32), lengths])
    order = Order()
    call = order.call

    code_rows = jnp.transpose(codes, (0, 2, 1, 3))
    cot_rows = jnp.transpose(cotangent, (0, 2, 1, 3))
    own_w = (jnp.transpose(w_qkv[0], (1, 0, 2)), w_out[0], w_up[0], w_down[0])

    def sem(count):
        return pltpu.SemaphoreType.DMA((count,))

    def gather(rows):
        gathered = lax.all_gather(rows, "tensor")
        order.tokens = (gathered,)
        return gathered

    def scatter(partial):
        return lax.all_to_all(partial, "tensor", 0, 0)

    other_gain = swap(gains[0], "section", 1)
    own_w, other_gain = lax.optimization_barrier((own_w, other_gain))

    def with_other(weights):
        return tuple(w for own in weights for w in (own, swap(own, "section", 1)))

    attention_w = with_other(own_w[:2])

    first_rows, start_g, gain_g, gain_l = call(
        start_kernel,
        [
            shape((frames, width), low16),
            shape((frames, width), f32),
            shape((2, width), f32),
            shape((2, width), f32),
        ],
        (info, code_rows, gains[0], other_gain),
        [SM, VM, VM, VM],
        us=2,
    )
    first_rows, *attention_w = lax.optimization_barrier((first_rows,) + attention_w)
    attention_w = tuple(attention_w)
    first_blocks = gather(first_rows)
    feed_w = with_other(order.after(own_w[2:]))

    first_g, packed_g, probs_g, mixed_g, mixed_given, partial = call(
        global_attention_kernel,
        [
            shape((rows_g, width), low16),
            shape((3, rows_g, heads_width), low16),
            shape((heads_width // HEAD_DIM, rows_g, rows_g), low16),
            shape((rows_g, heads_width), low16),
            shape((rows_g, half), low16),
            shape((4, frames, width), low16),
        ],
        (info, first_blocks) + attention_w,
        [SM, VM] + [ANY] * 4,
        [
            pltpu.VMEM((3, width, heads_width), low16),
            pltpu.VMEM((heads_width, width), low16),
            sem(8),
        ],
        us=5.7,
        limit=60,
    )
    arrived = scatter(partial)
    mix_piece, mix_whole = call(
        mix_piece_kernel,
        [shape((2, UNIT, UNIT), low16), shape((QUARTERS, 2, UNIT, UNIT), low16)],
        (info,) + attention_w,
        [SM] + [ANY] * 4,
        [sem(5 * QUARTERS)],
        us=3.2,
    )
    mix_z1 = swap(mix_piece, "tensor", 1)
    mix_z2 = swap(mix_piece, "tensor", 2)
    feed_piece, feed_whole = call(
        feed_piece_kernel,
        [shape((4, UNIT, UNIT), low16), shape((QUARTERS, 4, UNIT, UNIT), low16)],
        (info,) + feed_w,
        [SM] + [ANY] * 4,
        [sem(4 * QUARTERS)],
        us=4,
    )
    top_l, top_given = call(
        local_top_kernel,
        [shape((rows_l, width), low16), shape((rows_l // utts, width), low16)],
        (info, cot_rows),
        [SM, VM],
        us=2.3,
    )
    hidden_g, second_rows = call(
        middle_kernel,
        [shape((frames, width), f32), shape((frames, width), low16)],
        (start_g, arrived, gain_g),
        [VM] * 3,
        us=2,
    )
    second_rows, mix_z1, mix_z2, feed_piece = lax.optimization_barrier(
        (second_rows, mix_z1, mix_z2, feed_piece)
    )
    mix_z3 = swap(mix_z2, "tensor", 1)
    second_blocks = gather(second_rows)
    feed_z2 = swap(order.after(feed_piece), "tensor", 2)
    order.until(mix_z3)
    second_g, lifted_g, active_g, active_given, partial = call(
        global_feed_kernel,
        [
            shape((rows_g, width), low16),
            shape((rows_g, wide), f32),
            shape((rows_g, wide), low16),
            shape((rows_g, wide // 2), low16),
            shape((4, frames, width), low16),
        ],
        (info, second_blocks) + feed_w,
        [SM, VM] + [ANY] * 4,
        [
            pltpu.VMEM((width, wide), low16),
            pltpu.VMEM((wide, width), low16),
            pltpu.VMEM((rows_g, width), f32),
            sem(8),
        ],
        us=5.6,
        limit=60,
    )
    arrived = scatter(partial)
    mix_near = jnp.stack(order.after([mix_z1, mix_z2, mix_z3]), axis=1)
    mix_x = swap(mix_near, "dp", 1)
    mix_y = swap(mix_near, "dp", 2)
    mix_far = (swap(mix_x[0], "dp", 2), swap(mix_y[1], "dp", 1))
    order.until(*mix_far, feed_z2)
    sent = call(
        sent_kernel,
        [shape((frames, width), low16)],
        (hidden_g, arrived),
        [VM] * 2,
        us=1.9,
    )[0]
    other_sent = swap(sent, "section", 1)
    mix_w = (mix_whole, mix_z1, mix_z2, mix_z3, mix_x, mix_y) + mix_far
    feed_z2 = order.after(feed_z2)
    feed_x = swap(feed_z2, "dp", 1)
    feed_y = swap(feed_z2, "dp", 2)
    top_same = swap(order.after(top_given), "tensor", 1)

    start_l, first_l, query_keys, values_l, probs_l, mixed_l, partial = call(
        local_attention_kernel,
        [
            shape((rows_l, width), f32),
            shape((rows_l, width), low16),
            shape((4, rows_l, 2 * half), low16),
            shape((4, rows_l, half), low16),
            shape((4, utts, 2 * rows_l // utts, half), low16),
            shape((rows_l, 4 * half), low16),
            shape((rows_l, width), low16),
        ],
        (info, code_rows, sent, other_sent, gain_l) + mix_w,
        [SM] + [VM] * 4 + [ANY] * MIX_REFS,
        [
            pltpu.VMEM((4, 2, width, UNIT), low16),
            pltpu.VMEM((4 * half, width), low16),
            sem(32),
        ],
        us=9,
        limit=60,
    )
    partial, feed_x, feed_y, top_same = lax.optimization_barrier(
        (partial, feed_x, feed_y, top_same)
    )
    feed_l = (
        feed_whole,
        feed_z2,
        feed_x,
        feed_y,
        swap(feed_x[:2], "dp", 2),
        swap(feed_y[2:], "dp", 1),
    )
    hidden_l, second_l, second_given = call(
        local_norm_kernel,
        [
            shape((rows_l, width), f32),
            shape((rows_l, width), low16),
            shape((rows_l // utts, width), low16),
        ],
        (info, start_l, partial, swap(partial, "section", 1), gain_l),
        [SM] + [VM] * 4,
        us=3.7,
    )
    second_same = swap(second_given, "tensor", 1)
    top_cross = swap(top_same, "section", 1)
    feed_scratch = [
        pltpu.VMEM((tiles, width, UNIT), low16),
        pltpu.VMEM((tiles, UNIT, width), low16),
        pltpu.VMEM((rows_l, width), f32),
        sem(8 * tiles),
    ]
    wide_rows = shape((rows_l, width), low16)
    half_rows = shape((rows_l // utts, width), low16)
    tiled_rows = shape((tiles, rows_l, UNIT), low16)
    active_l, grad_lifted_l, back = call(
        local_feed_kernel,
        [tiled_rows, tiled_rows, wide_rows],
        (second_l, top_l) + feed_l,
        [VM] * 2 + [ANY] * FEED_REFS,
        feed_scratch,
        us=7.9,
    )
    other_back = swap(back, "section", 1)
    second_same = order.after(second_same)
    second_cross = swap(second_same, "section", 1)
    far_active, far_lifted, far_second, far_top, same, cross = call(
        far_feed_kernel,
        [tiled_rows, tiled_rows, wide_rows, wide_rows, half_rows, half_rows],
        (second_same, second_cross, top_same, top_cross) + feed_l,
        [VM] * 4 + [ANY] * FEED_REFS,
        feed_scratch,
        us=8.2,
    )

    def from_neighbour(same, cross):
        total = call(
            pair_kernel, [half_rows], (same, cross), [VM] * 2
        )[0]
        return swap(total, "tensor", 1)

    far_same = from_neighbour(same, swap(cross, "section", 1))
    turned_l = pltpu.VMEM((width, rows_l), low16)
    local_feed = Sum(
        order,
        2,
        *call(
            local_feed_grad_kernel,
            [shape((2, 4, UNIT, UNIT), low16)] * 4,
            (
                second_l, far_second, grad_lifted_l, far_lifted, active_l, far_active, top_l,
                far_top,
            ),
            [VM] * 8,
            [pltpu.VMEM((width, 2 * rows_l), low16), pltpu.VMEM((2 * rows_l, width), low16)],
            us=7.6,
        ),
    )
    own_branch, branch_same, branch_cross = call(
        local_drop_kernel,
        [wide_rows, half_rows, half_rows],
        (active_l, far_active) + feed_l,
        [VM] * 2 + [ANY] * FEED_REFS,
        [
            pltpu.VMEM((tiles, UNIT, width), low16),
            pltpu.VMEM((2 * rows_l, width), f32),
            sem(QUARTERS * tiles),
        ],
        us=6.1,
    )
    branch_cross = swap(branch_cross, "section", 1)
    other_branch = swap(own_branch, "section", 1)
    far_same = order.after(far_same)
    far_back = (far_same, swap(far_same, "section", 1))
    far_branch = from_neighbour(branch_same, branch_cross)
    far_first, far_mixed, far_second_g, far_active_g = (
        swap(order.after(value), "section", 1)
        for value in (first_g, mixed_given, second_g, active_given)
    )
    grad_hidden_l, mid_l, grad_query_keys, grad_values, back, gain2_l = call(
        local_attention_back_kernel,
        [
            shape((rows_l, width), f32),
            shape((rows_l, width), low16),
            shape((4, rows_l, 2 * half), low16),
            shape((4, rows_l, half), low16),
            shape((rows_l, width), low16),
            shape((1, width), f32),
        ],
        (info, hidden_l, back, other_back)
        + far_back
        + (top_l, gain_l, query_keys, values_l, probs_l)
        + mix_w,
        [SM] + [VM] * 10 + [ANY] * MIX_REFS,
        [
            pltpu.VMEM((4, 2, width, UNIT), low16),
            pltpu.VMEM((4 * half, width), low16),
            pltpu.VMEM((rows_l, width), f32),
            sem(32),
        ],
        us=11.4,
        limit=60,
    )
    other_back = swap(back, "section", 1)
    order.until(far_branch)
    local_mix = Sum(
        order,
        4,
        *call(
            local_mix_kernel,
            [shape((2, 4, UNIT, UNIT), low16)] * 4,
            (first_l, grad_query_keys, grad_values, mixed_l, mid_l),
            [VM] * 5,
            [turned_l],
            us=6,
        ),
    )
    returned, code_part, gain1_l = call(
        local_end_kernel,
        [
            shape((frames, width), low16),
            shape((utts, code_count, frames, width // 2), f32),
            shape((1, width), f32),
        ],
        (info, back, other_back, start_l, grad_hidden_l, gain_l),
        [SM] + [VM] * 5,
        [pltpu.VMEM((rows_l, width), f32)],
        us=4.4,
    )

    top_blocks = gather(returned)
    local_feed.second()
    order.until(*local_mix.once, far_first, far_mixed, far_second_g, far_active_g)
    top_g, grad_lifted_g, lifted_given, partial = call(
        global_feed_back_kernel,
        [
            shape((rows_g, width), low16),
            shape((rows_g, wide), low16),
            shape((rows_g, wide // 2), low16),
            shape((4, frames, width), low16),
        ],
        (info, top_blocks, lifted_g) + feed_w,
        [SM] + [VM] * 2 + [ANY] * 4,
        [
            pltpu.VMEM((width, wide), low16),
            pltpu.VMEM((wide, width), low16),
            pltpu.VMEM((rows_g, width), f32),
            sem(8),
        ],
        us=6.3,
        limit=28,
    )
    arrived = scatter(partial)
    far_top_g, far_lifted_g = swap(top_g, "section", 1), swap(lifted_given, "section", 1)
    local_feed.third()
    local_mix.second()
    far_branch = order.after(far_branch)
    far_branch = (far_branch, swap(far_branch, "section", 1))
    global_feed = Sum(
        order,
        1,
        *call(
            global_feed_grad_kernel,
            [shape((2, 2, UNIT, UNIT), low16)] * 4,
            (
                info, second_g, far_second_g, grad_lifted_g, far_lifted_g, active_g, far_active_g,
                top_g, far_top_g,
            ),
            [SM] + [VM] * 8,
            [pltpu.VMEM((width, 2 * rows_g), low16), pltpu.VMEM((2 * rows_g, width), low16)],
            us=3.5,
        ),
    )
    grad_hidden_g, mid_rows, gain2_g = call(
        middle_back_kernel,
        [shape((frames, width), f32), shape((frames, width), low16), shape((1, width), f32)],
        (arrived, hidden_g, gain_g, returned),
        [VM] * 4,
        us=2.1,
    )
    mid_blocks = gather(mid_rows)
    order.until(*local_mix.twice)
    mid_g, grads_g, grads_given, partial = call(
        global_attention_back_kernel,
        [
            shape((rows_g, width), low16),
            shape((3, rows_g, heads_width), low16),
            shape((3, rows_g, half), low16),
            shape((4, frames, width), low16),
        ],
        (info, mid_blocks, packed_g, probs_g) + attention_w,
        [SM] + [VM] * 3 + [ANY] * 4,
        [
            pltpu.VMEM((3, width, heads_width), low16),
            pltpu.VMEM((heads_width, width), low16),
            sem(8),
        ],
        us=6.8,
        limit=60,
    )
    arrived = scatter(partial)
    far_mid_g, far_grads_g = swap(mid_g, "section", 1), swap(grads_given, "section", 1)
    global_feed.second()
    local_mix.third()
    global_mix = Sum(
        order,
        1,
        *call(
            global_mix_grad_kernel,
            [shape((2, 1, UNIT, UNIT), low16)] * 4,
            (
                info, first_g, far_first, grads_g, far_grads_g, mixed_g, far_mixed, mid_g,
                far_mid_g,
            ),
            [SM] + [VM] * 8,
            [pltpu.VMEM((width, 2 * rows_g), low16), pltpu.VMEM((2 * rows_g, width), low16)],
            us=3,
        ),
    )
    kept_start, given_start, gain1_g = call(
        start_back_kernel,
        [
            shape((frames, width // 2), f32),
            shape((frames, width // 2), f32),
            shape((1, width), f32),
        ],
        (info, arrived, start_g, gain_g, grad_hidden_g),
        [SM] + [VM] * 4,
        [pltpu.VMEM((frames, width), f32)],
        us=2.1,
    )
    world_feed = global_feed.third()
    global_mix.second()
    local_mix.fourth()
    world_mix = global_mix.third()
    feed_sum = local_feed.gathered(info, world_feed)
    arrived_start = swap(given_start, "section", 1)
    both_start = jnp.stack(
        [
            jnp.where(first_core, kept_start, arrived_start),
            jnp.where(first_core, arrived_start, kept_start),
        ]
    )
    code_grad = jnp.transpose(code_part + both_start[:, None], (0, 2, 1, 3))

    own_gain = jnp.concatenate([gain1_g, gain2_g], axis=0)
    total_gain = own_gain + swap(own_gain, "section", 1)
    local_gain = jnp.concatenate([gain1_l, gain2_l], axis=0)
    gain_total = jnp.where(first_core, total_gain, local_gain)
    gain_total = jnp.concatenate(
        [
            lax.dynamic_slice_in_dim(gain_total, (low ^ m) * UNIT, UNIT, 1)
            for m in range(QUARTERS)
        ],
        axis=1,
    )
    def over(value, axis):
        copies = jnp.broadcast_to(value, (lax.axis_size(axis),) + value.shape)
        return jnp.sum(lax.all_to_all(order.after(copies), axis, 0, 0), axis=0)

    gain_total = over(gain_total, "tensor")
    order.until(gain_total)
    packed_gain = call(
        gain_pack_kernel, [shape((GAIN_ROWS, UNIT), low16)], (gain_total,), [VM], us=0.7
    )[0]
    mix_sum = local_mix.gathered(info, world_mix, packed_gain)
    output = call(
        output_kernel,
        [shape((utts, code_count, frames, width // 2), low16)],
        (info, hidden_l, own_branch, other_branch) + far_branch,
        [SM] + [VM] * 5,
        us=3.1,
    )[0]
    order.until(*feed_sum.near)
    feed_parts = feed_sum.far()
    def finals(count, rows, columns):
        return [
            pltpu.VMEM((count,) + rows, f32), pltpu.VMEM((count,) + columns, f32), sem(2 * count)
        ]

    feed_shapes = [shape((width, wide), f32), shape((wide, width), f32)]
    mix_shapes = [shape((3, width, heads_width), f32), shape((heads_width, width), f32)]
    feed_part = ((UNIT, wide), (wide, UNIT))
    mix_part = ((3, UNIT, heads_width), (heads_width, UNIT))
    feed_grads = call(
        feed_near_kernel,
        feed_shapes,
        (info,) + feed_parts[:3],
        [SM] + [VM] * 3,
        finals(3, *feed_part),
        us=5,
        place=ANY,
    )
    mix_sum.near = order.after(mix_sum.near)
    mix_parts = mix_sum.far()
    mix_grads = call(
        mix_near_kernel,
        mix_shapes,
        (info,) + mix_parts[:3],
        [SM] + [VM] * 3,
        finals(3, *mix_part),
        us=3,
        place=ANY,
    )
    up_grad, down_grad = call(
        feed_far_kernel,
        feed_shapes,
        (info,) + feed_parts[3:] + tuple(feed_grads),
        [SM] + [VM] * 2 + [ANY] * 2,
        finals(1, *feed_part),
        us=2,
        place=ANY,
        aliases=((3, 0), (4, 1)),
    )
    qkv_grad, out_grad, gain_total = call(
        mix_far_kernel,
        mix_shapes + [shape((2, width), f32)],
        (info,) + mix_parts + tuple(mix_grads),
        [SM] + [VM] * 5 + [ANY] * 2,
        finals(1, *mix_part),
        us=1.5,
        place=(ANY, ANY, VM),
        aliases=((6, 0), (7, 1)),
    )
    step = QUARTERS
    while step < lax.axis_size("dp"):
        gain_total = gain_total + swap(gain_total, "dp", step)
        step *= 2
    return (
        jnp.transpose(output, (0, 2, 1, 3)),
        code_grad,
        gain_total[None],
        jnp.transpose(qkv_grad, (1, 0, 2))[None],
        out_grad[None],
        up_grad[None],
        down_grad[None],
    )


def solution(mesh):
    in_specs = (
        P("dp", "tensor", None, None),
        P("dp"),
        P("section", None, None),
        P("section", None, None, "tensor"),
        P("section", "tensor", None),
        P("section", None, "tensor"),
        P("section", "tensor", None),
        P("dp", "tensor", None, None),
    )
    out_specs = (
        P("dp", "tensor", None, "section"),
        P("dp", "tensor", None, "section"),
        P("section", None, None),
        P("section", None, None, "tensor"),
        P("section", "tensor", None),
        P("section", None, "tensor"),
        P("section", "tensor", None),
    )
    return jax.shard_map(
        on_device, mesh=mesh, in_specs=in_specs, out_specs=out_specs, check_vma=False
    )
```

```python
import functools

import jax
import jax.numpy as jnp
from jax import lax
from jax.experimental import pallas as pl
from jax.experimental.pallas import tpu as pltpu
from jax.sharding import PartitionSpec as P

HEAD_DIM = 64
SCALE = HEAD_DIM ** (-0.5)
QUARTERS = 4
UNIT = 256
epsilon = 1e-06
negative = -1e30
f32 = jnp.float32
low16 = jnp.bfloat16

VM = pl.BlockSpec(memory_space=pltpu.VMEM)
SM = pl.BlockSpec(memory_space=pltpu.SMEM)
ANY = pl.BlockSpec(memory_space=pltpu.HBM)
MIB = 1 << 20
PACE = 0

LOW, SEC, SHARD, LENGTHS = 0, 1, 2, 3


def shape(dims, dtype):
    return jax.ShapeDtypeStruct(tuple(dims), dtype)


class Order:
    def __init__(self):
        self.tokens = ()

    def after(self, value):
        if not self.tokens:
            return value
        return lax.optimization_barrier((value,) + self.tokens)[0]

    def until(self, *values):
        self.tokens += values

    def call(self, body, outs, args, specs, scratch=(), limit=40, us=2.0, grid=(), place=VM, aliases=()):
        args = (self.after(args[0]),) + tuple(args[1:])
        results = pl.pallas_call(
            body,
            out_shape=tuple(outs),
            grid=grid,
            in_specs=list(specs),
            out_specs=place if isinstance(place, tuple) else (place,) * len(outs),
            input_output_aliases=dict(aliases),
            scratch_shapes=list(scratch),
            compiler_params=pltpu.CompilerParams(vmem_limit_bytes=limit * MIB),
            cost_estimate=pl.CostEstimate(
                flops=int(us * PACE), bytes_accessed=0, transcendentals=0
            ),
        )(*args)
        self.tokens = (results[-1],)
        return results


def swap(value, axis, flip):
    count = lax.axis_size(axis)
    return lax.ppermute(value, axis, [(i, i ^ flip) for i in range(count)])


def dot(a, b):
    return jnp.dot(a, b, preferred_element_type=f32)


def dot_tn(a, b):
    return lax.dot_general(a, b, (((0,), (0,)), ((), ())), preferred_element_type=f32)


def dot_nt(a, b):
    return lax.dot_general(a, b, (((1,), (1,)), ((), ())), preferred_element_type=f32)


def factor_of(values):
    return lax.rsqrt(jnp.mean(values * values, axis=-1, keepdims=True) + epsilon)


def norm_back(values, gain, upstream):
    factor = factor_of(values)
    weighted = upstream * gain
    inner = jnp.mean(weighted * values, axis=-1, keepdims=True)
    through = factor * weighted - values * (factor * factor * factor) * inner
    return through, jnp.sum(upstream * values * factor, axis=0, keepdims=True)


def normal_cdf(values):
    return 0.5 * (1.0 + lax.erf(values * (0.5**0.5)))


def gelu_slope(values, cdf):
    return cdf + values * (jnp.exp(-0.5 * values * values) * 0.3989422804014327)


def block_at(low, m):
    return pl.multiple_of((low ^ m) * UNIT, UNIT)


def span(m):
    return slice(m * UNIT, (m + 1) * UNIT)


class Copies:
    def __init__(self, sems):
        self.sems = sems
        self.made = []

    def start(self, src, dst):
        copy = pltpu.make_async_copy(src, dst, self.sems.at[len(self.made)])
        copy.start()
        self.made.append(copy)
        return copy

    def pick(self, own_first, sec, own, other, dst):
        sem = self.sems.at[len(self.made)]

        @pl.when((sec == 0) == own_first)
        def _():
            pltpu.make_async_copy(own, dst, sem).start()

        @pl.when((sec == 0) != own_first)
        def _():
            pltpu.make_async_copy(other, dst, sem).start()

        copy = pltpu.make_async_copy(own, dst, sem)
        self.made.append(copy)
        return copy

    def wait(self, begin=0, end=None):
        for copy in self.made[begin:end]:
            copy.wait()


def start_kernel(info, codes, own_gain, other_gain, first, start, gain_g, gain_l):
    low, sec = info[LOW], info[SEC]
    for m in range(QUARTERS):
        at = pl.ds(block_at(low, m), UNIT)
        own, other = own_gain[:, at], other_gain[:, at]
        gain_g[:, span(m)] = jnp.where(sec == 0, own, other)
        gain_l[:, span(m)] = jnp.where(sec == 0, other, own)
        total = codes[sec, 0, :, at].astype(f32)
        for c in range(1, codes.shape[1]):
            total = total + codes[sec, c, :, at].astype(f32)
        start[:, span(m)] = total
    values = start[...]
    first[...] = (values * factor_of(values) * gain_g[0:1, :]).astype(low16)


def from_local(sec, own, other, branch):
    @pl.when(sec == 0)
    def _():
        branch(0, *other)

    @pl.when(sec != 0)
    def _():
        branch(1, *own)


def mix_piece_kernel(info, own_qkv, other_qkv, own_out, other_out, piece, whole, sems):
    low, sec = info[LOW], info[SEC]
    half = own_qkv.shape[2] // 2

    def branch(half_index, qkv, out):
        made = Copies(sems)
        for m in range(QUARTERS):
            at = pl.ds(block_at(low, m), UNIT)
            at_right = pl.ds(pl.multiple_of(block_at(low, m) + half, half), half)
            at_left = pl.ds(block_at(low, m), half)
            lanes = slice(half_index * half, (half_index + 1) * half)
            target = whole.at[m]
            made.start(qkv.at[0, at, lanes], target.at[0, :, 0:half])
            made.start(qkv.at[1, at, lanes], target.at[0, :, half : 2 * half])
            made.start(qkv.at[2, at, lanes], target.at[1, :, 0:half])
            made.start(out.at[lanes, at_left], target.at[1, 0:half, half : 2 * half])
            made.start(out.at[lanes, at_right], target.at[1, half : 2 * half, half : 2 * half])
        made.wait()

    from_local(sec, (own_qkv, own_out), (other_qkv, other_out), branch)
    piece[...] = whole[0]


def feed_piece_kernel(info, own_up, other_up, own_down, other_down, piece, whole, sems):
    low, sec = info[LOW], info[SEC]
    wide = own_up.shape[1] // 2

    def branch(half_index, up, down):
        made = Copies(sems)
        for m in range(QUARTERS):
            at = pl.ds(block_at(low, m), UNIT)
            for part in range(2):
                begin = half_index * wide + part * UNIT
                hidden = slice(begin, begin + UNIT)
                made.start(up.at[at, hidden], whole.at[m, part])
                made.start(down.at[hidden, at], whole.at[m, 2 + part])
        made.wait()

    from_local(sec, (own_up, own_down), (other_up, other_down), branch)
    piece[...] = whole[0]


def fetch_attention(made, low, sec, own_qkv, other_qkv, own_out, other_out, qkv, out):
    for m in range(QUARTERS):
        at = pl.ds(block_at(low, m), UNIT)
        made.pick(True, sec, own_qkv.at[:, at, :], other_qkv.at[:, at, :], qkv.at[:, span(m), :])
    for m in range(QUARTERS):
        at = pl.ds(block_at(low, m), UNIT)
        made.pick(True, sec, own_out.at[:, at], other_out.at[:, at], out.at[:, span(m)])


def by_shard(info, blocks):
    count = blocks.shape[0]
    return jnp.concatenate([blocks[info[SHARD] ^ k] for k in range(count)], axis=0)


def other_half(info, width):
    half = width // 2
    return pl.ds(pl.multiple_of((1 - info[SEC]) * half, half), half)


def spread_blocks(info, target, values):
    frames = target.shape[1]
    for k in range(target.shape[0]):
        target[info[SHARD] ^ k] = values[k * frames : (k + 1) * frames].astype(low16)


def row_places(info, count, frames, dimension):
    at = lax.broadcasted_iota(jnp.int32, (count, count), dimension)
    return (lax.div(at, frames) ^ info[SHARD]) * frames + lax.rem(at, frames)


def global_attention_kernel(info, *rest):
    (blocks, own_qkv, other_qkv, own_out, other_out,
     rows, packed, probs, mixed, given, partial, qkv, out, sems) = rest
    low, sec = info[LOW], info[SEC]
    made = Copies(sems)
    fetch_attention(made, low, sec, own_qkv, other_qkv, own_out, other_out, qkv, out)
    count, frames = rows.shape[0], blocks.shape[1]
    length = info[LENGTHS + sec]
    query_at = row_places(info, count, frames, 0)
    key_at = row_places(info, count, frames, 1)
    allowed = (key_at <= query_at) & (key_at < length)
    values = by_shard(info, blocks)
    rows[...] = values
    made.wait(0, QUARTERS)
    for c in range(3):
        packed[c] = dot(values, qkv[c]).astype(low16)
    heads = []
    for h in range(packed.shape[2] // HEAD_DIM):
        lanes = slice(h * HEAD_DIM, (h + 1) * HEAD_DIM)
        scores = dot_nt(packed[0, :, lanes], packed[1, :, lanes]) * SCALE
        scores = jnp.where(allowed, scores, negative)
        raised = jnp.exp(scores - jnp.max(scores, axis=-1, keepdims=True))
        exact = raised / jnp.sum(raised, axis=-1, keepdims=True)
        probs[h] = exact.astype(low16)
        heads.append(dot(exact.astype(low16), packed[2, :, lanes]).astype(low16))
    mixed[...] = jnp.concatenate(heads, axis=1)
    given[...] = mixed[:, other_half(info, mixed.shape[1])]
    made.wait(QUARTERS)
    spread_blocks(info, partial, dot(mixed[...], out[...]))


def total_of(arrived):
    total = arrived[0].astype(f32)
    for k in range(1, arrived.shape[0]):
        total = total + arrived[k].astype(f32)
    return total


def middle_kernel(start, arrived, gain, hidden, second):
    values = start[...] + total_of(arrived)
    hidden[...] = values
    second[...] = (values * factor_of(values) * gain[1:2, :]).astype(low16)


def fetch_feed(made, low, sec, own_up, other_up, own_down, other_down, up, down):
    for m in range(QUARTERS):
        at = pl.ds(block_at(low, m), UNIT)
        made.pick(True, sec, own_up.at[at, :], other_up.at[at, :], up.at[span(m), :])
    for m in range(QUARTERS):
        at = pl.ds(block_at(low, m), UNIT)
        made.pick(True, sec, own_down.at[:, at], other_down.at[:, at], down.at[:, span(m)])


def global_feed_kernel(info, *rest):
    (blocks, own_up, other_up, own_down, other_down,
     rows, lifted, active, given, partial, up, down, total, sems) = rest
    made = Copies(sems)
    fetch_feed(made, info[LOW], info[SEC], own_up, other_up, own_down, other_down, up, down)
    values = by_shard(info, blocks)
    rows[...] = values
    made.wait(0, QUARTERS)
    for t in range(up.shape[1] // UNIT):
        tile = dot(values, up[:, span(t)])
        lifted[:, span(t)] = tile
        low_tile = (tile * normal_cdf(tile)).astype(low16)
        active[:, span(t)] = low_tile
        if t == 0:
            made.wait(QUARTERS)
        branch = dot(low_tile, down[span(t), :])
        total[...] = branch if t == 0 else total[...] + branch
    spread_blocks(info, partial, total[...])
    given[...] = active[:, other_half(info, active.shape[1])]


def sent_kernel(hidden, arrived, sent):
    sent[...] = (hidden[...] + total_of(arrived)).astype(low16)


def global_feed_back_kernel(info, *rest):
    (blocks, lifted, own_up, other_up, own_down, other_down,
     rows, grad_lifted, given, partial, up, down, total, sems) = rest
    made = Copies(sems)
    fetch_feed(made, info[LOW], info[SEC], own_up, other_up, own_down, other_down, up, down)
    values = by_shard(info, blocks)
    rows[...] = values
    made.wait(QUARTERS)
    for t in range(up.shape[1] // UNIT):
        tile = lifted[:, span(t)]
        grad = dot_nt(values, down[span(t), :]) * gelu_slope(tile, normal_cdf(tile))
        grad = grad.astype(low16)
        grad_lifted[:, span(t)] = grad
        if t == 0:
            made.wait(0, QUARTERS)
        back = dot_nt(grad, up[:, span(t)])
        total[...] = back if t == 0 else total[...] + back
    spread_blocks(info, partial, total[...])
    given[...] = grad_lifted[:, other_half(info, grad_lifted.shape[1])]


def middle_back_kernel(arrived, hidden, gain, returned, grad_hidden, mid, gain_grad):
    through, gain_grad[...] = norm_back(hidden[...], gain[1:2, :], total_of(arrived))
    values = returned[...].astype(f32) + through
    grad_hidden[...] = values
    mid[...] = values.astype(low16)


def global_attention_back_kernel(info, *rest):
    (blocks, packed, probs, own_qkv, other_qkv, own_out, other_out,
     rows, grads, given, partial, qkv, out, sems) = rest
    low, sec = info[LOW], info[SEC]
    made = Copies(sems)
    fetch_attention(made, low, sec, own_qkv, other_qkv, own_out, other_out, qkv, out)
    values = by_shard(info, blocks)
    rows[...] = values
    made.wait(QUARTERS)
    grad_mixed = dot_nt(values, out[...]).astype(low16)
    columns = [[], [], []]
    for h in range(packed.shape[2] // HEAD_DIM):
        lanes = slice(h * HEAD_DIM, (h + 1) * HEAD_DIM)
        exact = probs[h].astype(f32)
        grad = grad_mixed[:, lanes]
        columns[2].append(dot_tn(exact.astype(low16), grad).astype(low16))
        grad_probs = dot_nt(grad, packed[2, :, lanes])
        center = jnp.sum(grad_probs * exact, axis=-1, keepdims=True)
        grad_scores = (exact * (grad_probs - center)).astype(low16)
        columns[0].append((dot(grad_scores, packed[1, :, lanes]) * SCALE).astype(low16))
        columns[1].append((dot_tn(grad_scores, packed[0, :, lanes]) * SCALE).astype(low16))
    total = None
    made.wait(0, QUARTERS)
    for c in range(3):
        grads[c] = jnp.concatenate(columns[c], axis=1)
        back = dot_nt(grads[c], qkv[c])
        total = back if c == 0 else total + back
    spread_blocks(info, partial, total)
    given[...] = grads[:, :, other_half(info, grads.shape[2])]


def start_back_kernel(info, arrived, start, gain, grad_hidden, kept, given, gain_grad, values):
    low, sec = info[LOW], info[SEC]
    through, gain_grad[...] = norm_back(start[...], gain[0:1, :], total_of(arrived))
    values[...] = grad_hidden[...] + through
    for j in range(2):
        kept[:, span(j)] = values[:, pl.ds(block_at(low, 2 * sec + j), UNIT)]
        given[:, span(j)] = values[:, pl.ds(block_at(low, 2 * (1 - sec) + j), UNIT)]


def mix_unit(refs, k, m, u):
    whole, near, x_part, y_part, far = refs[0], refs[1:4], refs[4], refs[5], refs[6:8]
    if k == 0:
        return whole.at[m, u]
    if m == 0:
        return near[k - 1].at[u]
    if m == 3:
        return far[u].at[k - 1]
    return (x_part if m == 1 else y_part).at[u, k - 1]


def feed_unit(refs, k, m, u):
    if k == 0:
        return refs[0].at[m, u]
    if m < 3:
        return refs[1 + m].at[u]
    return refs[4].at[u] if u < 2 else refs[5].at[u - 2]


MIX_REFS, FEED_REFS = 8, 6


def pair_rows(a, b, size):
    return jnp.concatenate([a * b, a[size:] * b[: 2 * size], a[2 * size :] * b[:size]], axis=0)


def by_pair(stacked, size):
    names = [(0, 0), (1, 1), (2, 2), (1, 0), (2, 1), (2, 0)]
    return {name: stacked[n * size : (n + 1) * size] for n, name in enumerate(names)}


def from_pairs(pairs):
    names = [(0, 0), (1, 1), (2, 2), (1, 0), (2, 1), (2, 0)]
    return jnp.concatenate([pairs[name] for name in names], axis=0)


def head_sums(products, table):
    upper = products.astype(low16)
    lower = (products - upper.astype(f32)).astype(low16)
    return dot(upper, table) + dot(lower, table)


def head_table(width):
    row = lax.broadcasted_iota(jnp.int32, (width, width), 0) // HEAD_DIM
    column = lax.broadcasted_iota(jnp.int32, (width, width), 1) // HEAD_DIM
    return (row == column).astype(f32).astype(low16)


def gather_mix(weights, mix, k, half):
    for m in range(QUARTERS):
        begin = m * UNIT
        mix[k * half : (k + 1) * half, begin : begin + half] = weights[
            k, 1, begin : begin + half, half:
        ]
        mix[k * half : (k + 1) * half, begin + half : begin + UNIT] = weights[
            k, 1, begin + half : begin + UNIT, half:
        ]


def local_attention_kernel(info, codes, sent_own, sent_other, gain, *rest):
    refs, (start, first, query_keys, values_out, probs, mixed, partial, weights, mix, sems) = (
        rest[:MIX_REFS], rest[MIX_REFS:]
    )
    low, sec = info[LOW], info[SEC]
    made = Copies(sems)
    groups = []
    for k in range(4):
        groups.append(
            [
                made.start(mix_unit(refs, k, m, u), weights.at[k, u, span(m), :])
                for u in range(2)
                for m in range(QUARTERS)
            ]
        )
    utts, code_count, frames, _ = codes.shape
    for u in range(utts):
        sent = jnp.where(sec == u, sent_own[...], sent_other[...]).astype(f32)
        for c in range(code_count):
            row = (u * code_count + c) * frames
            for m in range(QUARTERS):
                code = codes[u, c, :, pl.ds(block_at(low, m), UNIT)].astype(f32)
                start[row : row + frames, span(m)] = sent[:, span(m)] + code
    values = start[...]
    first[...] = (values * factor_of(values) * gain[0:1, :]).astype(low16)
    half = values_out.shape[2]
    table = head_table(half)
    rows = first[...]
    size = frames
    group = code_count * frames
    for k in range(4):
        for copy in groups[k]:
            copy.wait()
        query_keys[k] = dot(rows, weights[k, 0]).astype(low16)
        values_out[k] = dot(rows, weights[k, 1, :, :half]).astype(low16)
        gather_mix(weights, mix, k, half)
        for u in range(utts):
            at = slice(u * group, (u + 1) * group)
            q = query_keys[k, at, :half].astype(f32)
            key = query_keys[k, at, half:].astype(f32)
            val = values_out[k, at, :].astype(f32)
            scores = by_pair(head_sums(pair_rows(q, key, size), table) * SCALE, size)
            exact = {}
            for i in range(3):
                peak = scores[(i, 0)]
                for j in range(1, i + 1):
                    peak = jnp.maximum(peak, scores[(i, j)])
                raised = [jnp.exp(scores[(i, j)] - peak) for j in range(i + 1)]
                whole = raised[0]
                for j in range(1, i + 1):
                    whole = whole + raised[j]
                for j in range(i + 1):
                    exact[(i, j)] = raised[j] / whole
            probs[k, u] = from_pairs(exact).astype(low16)
            for i in range(3):
                total = None
                for j in range(i + 1):
                    weight = exact[(i, j)].astype(low16).astype(f32)
                    term = weight * val[j * size : (j + 1) * size]
                    total = term if total is None else total + term
                begin = u * group + i * size
                mixed[begin : begin + size, k * half : (k + 1) * half] = total.astype(low16)
    partial[...] = dot(mixed[...], mix[...]).astype(low16)


def local_top_kernel(info, cotangent, top, given):
    low, sec = info[LOW], info[SEC]
    utts, code_count, frames, _ = cotangent.shape
    group = code_count * frames
    frame_at = lax.broadcasted_iota(jnp.int32, (frames, 1), 0) + info[SHARD] * frames
    for u in range(utts):
        valid = frame_at < info[LENGTHS + u]
        for c in range(code_count):
            row = u * group + c * frames
            for m in range(QUARTERS):
                part = cotangent[u, c, :, pl.ds(block_at(low, m), UNIT)].astype(f32)
                top[row : row + frames, span(m)] = jnp.where(valid, part, 0.0).astype(low16)
    given[...] = top[pl.ds(pl.multiple_of(sec * group, group), group), :]


def local_norm_kernel(info, start, own_part, other_part, gain, hidden, second, given):
    values = start[...] + (own_part[...].astype(f32) + other_part[...].astype(f32))
    hidden[...] = values
    second[...] = (values * factor_of(values) * gain[1:2, :]).astype(low16)
    group = given.shape[0]
    given[...] = second[pl.ds(pl.multiple_of(info[SEC] * group, group), group), :]


def feed_tiles(refs, second, top, active, grad_lifted, up, down, back, sems):
    tiles = active.shape[0]
    made = Copies(sems)
    for t in range(tiles):
        for m in range(QUARTERS):
            made.start(feed_unit(refs, t // 2, m, t % 2), up.at[t, span(m), :])
        for m in range(QUARTERS):
            made.start(feed_unit(refs, t // 2, m, 2 + t % 2), down.at[t, :, span(m)])
    back[...] = jnp.zeros_like(back)

    @pl.loop(0, tiles)
    def _(t):
        for m in range(QUARTERS):
            pltpu.make_async_copy(
                refs[0].at[0, 0], up.at[t, span(m), :], sems.at[8 * t + m]
            ).wait()
        for m in range(QUARTERS):
            pltpu.make_async_copy(
                refs[0].at[0, 0], down.at[t, :, span(m)], sems.at[8 * t + 4 + m]
            ).wait()
        tile = dot(second[...], up[t])
        cdf = normal_cdf(tile)
        active[t] = (tile * cdf).astype(low16)
        grad = (dot_nt(top[...], down[t]) * gelu_slope(tile, cdf)).astype(low16)
        grad_lifted[t] = grad
        back[...] += dot_nt(grad, up[t])


def local_feed_kernel(second, top, *rest):
    refs, (active, grad_lifted, grad_second, up, down, back, sems) = (
        rest[:FEED_REFS], rest[FEED_REFS:]
    )
    feed_tiles(refs, second, top, active, grad_lifted, up, down, back, sems)
    grad_second[...] = back[...].astype(low16)


def far_feed_kernel(second_same, second_cross, top_same, top_cross, *rest):
    refs = rest[:FEED_REFS]
    (active, grad_lifted, second, top, same, cross, up, down, back, sems) = rest[FEED_REFS:]
    group = same.shape[0]
    second[:group] = second_same[...]
    second[group:] = second_cross[...]
    top[:group] = top_same[...]
    top[group:] = top_cross[...]
    feed_tiles(refs, second, top, active, grad_lifted, up, down, back, sems)
    same[...] = back[:group].astype(low16)
    cross[...] = back[group:].astype(low16)


def pair_kernel(a, b, total):
    total[...] = add16(a[...], b[...])


def with_far(sec, rows, own, other, far_same, far_cross):
    group = far_same.shape[0]
    parts = []
    for u in range(rows // group):
        at = slice(u * group, (u + 1) * group)
        far = jnp.where(sec == u, far_same[...], far_cross[...]).astype(f32)
        parts.append(own[at, :].astype(f32) + other[at, :].astype(f32) + far)
    return jnp.concatenate(parts, axis=0)


def local_attention_back_kernel(info, hidden, own_back, other_back, far_same, far_cross, top, gain,
                                query_keys, values_in, probs, *rest):
    refs = rest[:MIX_REFS]
    (grad_hidden, mid, grad_query_keys, grad_values, grad_first, gain_grad,
     weights, mix, total, sems) = rest[MIX_REFS:]
    made = Copies(sems)
    groups = []
    for k in range(4):
        groups.append(
            [
                made.start(mix_unit(refs, k, m, u), weights.at[k, u, span(m), :])
                for u in range(2)
                for m in range(QUARTERS)
            ]
        )
    upstream = with_far(info[SEC], hidden.shape[0], own_back, other_back, far_same, far_cross)
    through, gain_grad[...] = norm_back(hidden[...], gain[1:2, :], upstream)
    grads = top[...].astype(f32) + through
    grad_hidden[...] = grads
    mid[...] = grads.astype(low16)
    utts = probs.shape[1]
    half = values_in.shape[2]
    group = query_keys.shape[1] // utts
    size = group // 3
    table = head_table(half)
    for k in range(4):
        for copy in groups[k]:
            copy.wait()
        gather_mix(weights, mix, k, half)
        grad_mixed = dot_nt(mid[...], mix[k * half : (k + 1) * half, :]).astype(low16)
        grad_mixed = grad_mixed.astype(f32)
        for u in range(utts):
            at = slice(u * group, (u + 1) * group)
            q = query_keys[k, at, :half].astype(f32)
            key = query_keys[k, at, half:].astype(f32)
            val = values_in[k, at, :].astype(f32)
            grad = grad_mixed[at]
            exact = by_pair(probs[k, u].astype(f32), size)
            grad_probs = by_pair(head_sums(pair_rows(grad, val, size), table), size)
            scored = {}
            for i in range(3):
                center = grad_probs[(i, 0)] * exact[(i, 0)]
                for j in range(1, i + 1):
                    center = center + grad_probs[(i, j)] * exact[(i, j)]
                for j in range(i + 1):
                    score = exact[(i, j)] * (grad_probs[(i, j)] - center)
                    scored[(i, j)] = score.astype(low16).astype(f32)

            def rows_of(array, n):
                return array[n * size : (n + 1) * size]

            for i in range(3):
                begin = u * group + i * size
                to_query = sum(scored[(i, j)] * rows_of(key, j) for j in range(i + 1))
                to_key = sum(scored[(n, i)] * rows_of(q, n) for n in range(i, 3))
                to_value = sum(
                    exact[(n, i)].astype(low16).astype(f32) * rows_of(grad, n)
                    for n in range(i, 3)
                )
                grad_query_keys[k, begin : begin + size, :half] = (to_query * SCALE).astype(low16)
                grad_query_keys[k, begin : begin + size, half:] = (to_key * SCALE).astype(low16)
                grad_values[k, begin : begin + size, :] = to_value.astype(low16)
        back = dot_nt(grad_query_keys[k], weights[k, 0])
        back = back + dot_nt(grad_values[k], weights[k, 1, :, :half])
        total[...] = back if k == 0 else total[...] + back
    grad_first[...] = total[...].astype(low16)


def local_end_kernel(info, own_back, other_back, start, grad_hidden, gain,
                     returned, code_part, gain_grad, values):
    low, sec = info[LOW], info[SEC]
    upstream = own_back[...].astype(f32) + other_back[...].astype(f32)
    through, gain_grad[...] = norm_back(start[...], gain[0:1, :], upstream)
    values[...] = grad_hidden[...] + through
    utts, code_count, frames, _ = code_part.shape
    total = None
    for c in range(code_count):
        begin = pl.multiple_of((sec * code_count + c) * frames, frames)
        part = values[pl.ds(begin, frames), :]
        total = part if total is None else total + part
    returned[...] = total.astype(low16)
    for u in range(utts):
        for c in range(code_count):
            row = (u * code_count + c) * frames
            for j in range(2):
                at = pl.ds(block_at(low, 2 * sec + j), UNIT)
                code_part[u, c, :, span(j)] = values[row : row + frames, at]


def output_kernel(info, hidden, own_part, other_part, far_same, far_cross, output):
    low, sec = info[LOW], info[SEC]
    utts, code_count, frames, _ = output.shape
    group = code_count * frames
    frame_at = lax.broadcasted_iota(jnp.int32, (frames, 1), 0) + info[SHARD] * frames
    for u in range(utts):
        valid = frame_at < info[LENGTHS + u]
        for c in range(code_count):
            rows = slice(u * group + c * frames, u * group + (c + 1) * frames)
            inner = slice(c * frames, (c + 1) * frames)
            for j in range(2):
                at = pl.ds(block_at(low, 2 * sec + j), UNIT)
                far = jnp.where(sec == u, far_same[inner, at], far_cross[inner, at])
                value = hidden[rows, at] + (
                    own_part[rows, at].astype(f32)
                    + other_part[rows, at].astype(f32)
                    + far.astype(f32)
                )
                output[u, c, :, span(j)] = jnp.where(valid, value, 0.0).astype(low16)


SEND_A, KEEP_A, SEND_B, KEEP_B = (1, 3), (0, 2), (2, 3), (0, 1)


def local_drop_kernel(own_active, far_active, *rest):
    refs, (own_branch, same, cross, down, branch, sems) = rest[:FEED_REFS], rest[FEED_REFS:]
    tiles, count, _ = own_active.shape
    made = Copies(sems)
    for t in range(tiles):
        for m in range(QUARTERS):
            made.start(feed_unit(refs, t // 2, m, 2 + t % 2), down.at[t, :, span(m)])
    branch[...] = jnp.zeros_like(branch)

    @pl.loop(0, tiles)
    def _(t):
        for m in range(QUARTERS):
            pltpu.make_async_copy(
                refs[0].at[0, 0], down.at[t, :, span(m)], sems.at[QUARTERS * t + m]
            ).wait()
        branch[:count] += dot(own_active[t], down[t])
        branch[count:] += dot(far_active[t], down[t])

    own_branch[...] = branch[:count].astype(low16)
    group = same.shape[0]
    same[...] = branch[count : count + group].astype(low16)
    cross[...] = branch[count + group :].astype(low16)


def local_feed_grad_kernel(second, far_second, own_lifted, far_lifted, own_active, far_active,
                           top, far_top, send_a, send_b, keep_a, keep_b, turned, tops):
    count = second.shape[0]
    turned[:, :count] = jnp.transpose(second[...])
    turned[:, count:] = jnp.transpose(far_second[...])
    tops[:count] = top[...]
    tops[count:] = far_top[...]
    for k in range(2):
        for part, pairs in enumerate(
            (((send_a, SEND_A), (keep_a, KEEP_A)), ((send_b, SEND_B), (keep_b, KEEP_B)))
        ):
            t = 2 * k + part
            right = jnp.concatenate([own_lifted[t], far_lifted[t]], axis=0)
            left = jnp.concatenate(
                [jnp.transpose(own_active[t]), jnp.transpose(far_active[t])], axis=1
            )
            for target, order in pairs:
                for place, m in enumerate(order):
                    target[place, 2 * k] = dot(turned[span(m), :], right).astype(low16)
                    target[place, 2 * k + 1] = dot(left, tops[:, span(m)]).astype(low16)


def local_mix_kernel(first, grad_query_keys, grad_values, mixed, mid,
                     send_a, send_b, keep_a, keep_b, turned):
    turned[...] = jnp.transpose(first[...])
    half = grad_values.shape[2]
    for k in range(4):
        left = jnp.transpose(mixed[:, k * half : (k + 1) * half])
        for target, order in ((send_a, SEND_A), (keep_a, KEEP_A)):
            for place, m in enumerate(order):
                target[place, k] = dot(turned[span(m), :], grad_query_keys[k]).astype(low16)
        for target, order in ((send_b, SEND_B), (keep_b, KEEP_B)):
            for place, m in enumerate(order):
                value = dot(turned[span(m), :], grad_values[k]).astype(low16)
                out = dot(left, mid[:, span(m)]).astype(low16)
                target[place, k, :, :half] = value
                target[place, k, :half, half:] = out[:, :half]
                target[place, k, half:, half:] = out[:, half:]


def by_order(send_a, send_b, keep_a, keep_b):
    return (
        (0, ((send_a, SEND_A), (keep_a, KEEP_A))),
        (1, ((send_b, SEND_B), (keep_b, KEEP_B))),
    )


def global_feed_grad_kernel(info, second, far_second, grad_lifted, far_lifted, active, far_active,
                            top, far_top, send_a, send_b, keep_a, keep_b, turned, tops):
    sec, count = info[SEC], second.shape[0]
    turned[:, :count] = jnp.transpose(second[...])
    turned[:, count:] = jnp.transpose(far_second[...])
    tops[:count] = top[...]
    tops[count:] = far_top[...]
    wide = active.shape[1] // 2
    for part, pairs in by_order(send_a, send_b, keep_a, keep_b):
        at = pl.ds(pl.multiple_of(sec * wide + part * UNIT, UNIT), UNIT)
        right = jnp.concatenate([grad_lifted[:, at], far_lifted[:, span(part)]], axis=0)
        left = jnp.concatenate(
            [jnp.transpose(active[:, at]), jnp.transpose(far_active[:, span(part)])], axis=1
        )
        for target, order in pairs:
            for place, m in enumerate(order):
                target[place, 0] = dot(turned[span(m), :], right).astype(low16)
                target[place, 1] = dot(left, tops[:, span(m)]).astype(low16)


def global_mix_grad_kernel(info, first, far_first, grads, far_grads, mixed, far_mixed, mid,
                           far_mid, send_a, send_b, keep_a, keep_b, turned, mids):
    sec, count = info[SEC], first.shape[0]
    turned[:, :count] = jnp.transpose(first[...])
    turned[:, count:] = jnp.transpose(far_first[...])
    mids[:count] = mid[...]
    mids[count:] = far_mid[...]
    width = mixed.shape[1] // 2
    at = pl.ds(pl.multiple_of(sec * width, width), width)
    right = [jnp.concatenate([grads[c, :, at], far_grads[c]], axis=0) for c in range(3)]
    left = jnp.concatenate([jnp.transpose(mixed[:, at]), jnp.transpose(far_mixed[...])], axis=1)
    for part, pairs in by_order(send_a, send_b, keep_a, keep_b):
        for target, order in pairs:
            for place, m in enumerate(order):
                rows = turned[span(m), :]
                if part == 0:
                    for c in range(2):
                        target[place, 0, :, c * width : (c + 1) * width] = dot(
                            rows, right[c]
                        ).astype(low16)
                else:
                    target[place, 0, :, :width] = dot(rows, right[2]).astype(low16)
                    out = dot(left, mids[:, span(m)]).astype(low16)
                    target[place, 0, :width, width:] = out[:, :width]
                    target[place, 0, width:, width:] = out[:, width:]


def add16(a, b):
    return (a.astype(f32) + b.astype(f32)).astype(low16)


def far_kernel(keep_a, from_x, keep_b, from_y, far_a, far_b):
    far_a[...] = add16(keep_a[0], from_x[0])
    far_b[...] = add16(keep_b[0], from_y[0])


def sum_kernel(shards, *refs):
    parts, outs = (refs[:3], refs[3:6]), refs[6:]
    for part, (keep, once, twice) in enumerate(parts):
        total = keep[0].astype(f32) + once[0].astype(f32) + twice[...].astype(f32)
        total = total.astype(low16)
        count = total.shape[0] // shards
        at = slice(part * count, (part + 1) * count)
        if shards == 1:
            outs[0][at] = total
        elif shards == 2:
            outs[1][0, at] = total[:count]
            outs[0][0, at] = total[count:]
        else:
            for k in range(4):
                outs[(k + 1) % 2][k // 2, at] = total[k * count : (k + 1) * count]


def far_tensor_kernel(keep, arrived, far):
    far[...] = add16(keep[0], arrived[0])


def pick_kernel(info, *refs):
    *terms, world, given, kept = refs
    sec = info[SEC]
    local = terms[0][0].astype(f32)
    for term in terms[1:]:
        local = local + (term[0] if len(term.shape) == 4 else term[...]).astype(f32)
    local = local.astype(low16)
    other = world[...]
    given[...] = jnp.where(sec == 0, local, other)
    kept[...] = jnp.where(sec == 0, other, local)


def half_at(index, count):
    return pl.BlockSpec(
        (1, count, UNIT, UNIT), lambda i: (index, 0, 0, 0), memory_space=pltpu.VMEM
    )


def quarter_unit(refs, m, index):
    own, x_part, y_part, far_kept, far_arrived = refs
    count = own.shape[0] // 2
    if m < 3:
        return (own, x_part, y_part)[m][index].astype(f32)
    return (far_kept[index] if index < count else far_arrived[index - count]).astype(f32)


def write_feed(info, quarters, unit, count, up, down, rows, columns, sems):
    low, sec = info[LOW], info[SEC]
    wide = up.shape[1] // 2
    made = Copies(sems)
    for place, m in enumerate(quarters):
        at = pl.ds(block_at(low, m), UNIT)
        for source, half in ((0, sec), (count, 1 - sec)):
            for part in range(2):
                hidden = pl.ds(pl.multiple_of(half * wide + part * UNIT, UNIT), UNIT)
                rows[place, :, hidden] = unit(m, source + 2 * part)
                columns[place, hidden, :] = unit(m, source + 2 * part + 1)
        made.start(rows.at[place], up.at[at, :])
        made.start(columns.at[place], down.at[:, at])
    made.wait()


def feed_near_kernel(info, own, x_part, y_part, up, down, rows, columns, sems):
    parts = (own, x_part, y_part)
    write_feed(
        info, (0, 1, 2), lambda m, n: parts[m][n].astype(f32), own.shape[0] // 2,
        up, down, rows, columns, sems,
    )


def feed_far_kernel(info, far_kept, far_arrived, up_before, down_before,
                    up, down, rows, columns, sems):
    count = far_kept.shape[0]

    def unit(m, n):
        return (far_kept[n] if n < count else far_arrived[n - count]).astype(f32)

    write_feed(info, (3,), unit, count, up, down, rows, columns, sems)


def write_mix(info, quarters, unit, count, qkv, out, rows, columns, sems):
    low, sec = info[LOW], info[SEC]
    width = out.shape[0] // 2
    made = Copies(sems)
    for place, m in enumerate(quarters):
        at = pl.ds(block_at(low, m), UNIT)
        for source, half in ((0, sec), (count, 1 - sec)):
            lanes = pl.ds(pl.multiple_of(half * width, width), width)
            query_keys = unit(m, source)
            rows[place, 0, :, lanes] = query_keys[:, :width]
            rows[place, 1, :, lanes] = query_keys[:, width:]
            rest_unit = unit(m, source + 1)
            rows[place, 2, :, lanes] = rest_unit[:, :width]
            columns[place, lanes, :width] = rest_unit[:width, width:]
            columns[place, lanes, width:] = rest_unit[width:, width:]
        made.start(rows.at[place], qkv.at[:, at, :])
        made.start(columns.at[place], out.at[:, at])
    made.wait()


GAIN_ROWS = 32


def gain_pack_kernel(gain, packed):
    rows = []
    for g in range(gain.shape[0]):
        rest = gain[g : g + 1, :]
        for _ in range(3):
            part = rest.astype(low16).astype(f32)
            rest = rest - part
            rows += [part[:, span(m)] for m in range(QUARTERS)]
    rows.append(jnp.zeros((GAIN_ROWS - len(rows), UNIT), f32))
    packed[...] = jnp.concatenate(rows, axis=0).astype(low16)


def unit_rows(ref, n):
    return ref[n * UNIT : (n + 1) * UNIT, :].astype(f32)


def mix_near_kernel(info, own, x_part, y_part, qkv, out, rows, columns, sems):
    parts = (own, x_part, y_part)
    count = (own.shape[0] - GAIN_ROWS) // (2 * UNIT)
    write_mix(
        info, (0, 1, 2), lambda m, n: unit_rows(parts[m], n), count, qkv, out, rows, columns, sems
    )


def mix_far_kernel(info, own, x_part, y_part, far_kept, far_arrived, qkv_before, out_before,
                   qkv, out, gain, rows, columns, sems):
    count = far_kept.shape[0] // UNIT

    def unit(m, n):
        return unit_rows(far_kept, n) if n < count else unit_rows(far_arrived, n - count)

    total = None
    for ref in (own, x_part, y_part, far_arrived):
        part = ref[ref.shape[0] - GAIN_ROWS :, :].astype(f32)
        total = part if total is None else total + part
    for g in range(gain.shape[0]):
        for m in range(QUARTERS):
            at = [3 * QUARTERS * g + QUARTERS * t + m for t in range(3)]
            gain[g : g + 1, span(m)] = (
                total[at[0] : at[0] + 1] + total[at[1] : at[1] + 1] + total[at[2] : at[2] + 1]
            )
    write_mix(info, (3,), unit, count, qkv, out, rows, columns, sems)


def sum_rest(value):
    step = QUARTERS
    while step < lax.axis_size("dp"):
        value = add16(value, swap(value, "dp", step))
        step *= 2
    return value


class Sum:
    def __init__(self, order, shards, send_a, send_b, keep_a, keep_b):
        self.order, self.shards = order, shards
        self.keep = (keep_a, keep_b)
        self.count = keep_a.shape[1]
        self.once = (swap(send_a, "dp", 1), swap(send_b, "dp", 2))

    def second(self):
        far = half_at(1, self.count)
        far_a, far_b = self.order.call(
            far_kernel,
            [shape((self.count, UNIT, UNIT), low16)] * 2,
            (self.keep[0], self.once[0], self.keep[1], self.once[1]),
            [far] * 4,
            grid=(1,),
        )
        self.twice = (swap(far_a, "dp", 2), swap(far_b, "dp", 1))

    def third(self):
        count = 2 * self.count // self.shards
        if self.shards == 1:
            outs = [shape((count, UNIT, UNIT), low16)]
        else:
            outs = [shape((self.shards // 2, count, UNIT, UNIT), low16)] * 2
        near = half_at(0, self.count)
        totals = self.order.call(
            functools.partial(sum_kernel, self.shards),
            outs,
            (self.keep[0], self.once[0], self.twice[0], self.keep[1], self.once[1], self.twice[1]),
            [near, near, VM] * 2,
            grid=(1,),
        )
        totals = [sum_rest(total) for total in totals]
        self.count = count
        if self.shards == 1:
            return totals[0]
        self.keep = totals[1]
        if self.shards == 2:
            self.terms = (self.keep, swap(totals[0], "tensor", 2))
        else:
            self.once = swap(totals[0], "tensor", 1)

    def fourth(self):
        far = self.order.call(
            far_tensor_kernel,
            [shape((self.count, UNIT, UNIT), low16)],
            (self.keep, self.once),
            [half_at(1, self.count)] * 2,
            grid=(1,),
        )[0]
        self.terms = (self.keep, self.once, swap(far, "tensor", 2))

    def gathered(self, info, world, extra=None):
        near = half_at(0, self.count)
        given, kept = self.order.call(
            pick_kernel,
            [shape((self.count, UNIT, UNIT), low16)] * 2,
            (info,) + self.terms + (world,),
            [SM] + [near if term.ndim == 4 else VM for term in self.terms] + [VM],
            grid=(1,),
        )
        arrived = swap(given, "section", 1)
        if extra is None:
            return Gather(jnp.concatenate([kept, arrived]), self.count)
        rows = [kept.reshape(-1, UNIT), arrived.reshape(-1, UNIT), extra]
        return Gather(jnp.concatenate(rows), self.count * UNIT)


class Gather:
    def __init__(self, units, count):
        self.units, self.count = units, count
        self.near = (swap(units, "dp", 1), swap(units, "dp", 2))

    def far(self):
        x_part, y_part = self.near
        rest = (swap(x_part[: self.count], "dp", 2), swap(y_part[self.count :], "dp", 1))
        return (self.units,) + self.near + rest


def on_device(codes, lengths, gains, w_qkv, w_out, w_up, w_down, cotangent):
    sec = lax.axis_index("section")
    low = lax.axis_index("dp") % QUARTERS
    z = lax.axis_index("tensor")
    first_core = sec == 0
    utts, frames, code_count, width = codes.shape
    heads_width = w_out.shape[1]
    half = heads_width // 2
    wide = w_up.shape[2]
    rows_g = 4 * frames
    rows_l = utts * code_count * frames
    tiles = wide // UNIT
    info = jnp.concatenate([jnp.stack([low, sec, z]).astype(jnp.int32), lengths])
    order = Order()
    call = order.call

    code_rows = jnp.transpose(codes, (0, 2, 1, 3))
    cot_rows = jnp.transpose(cotangent, (0, 2, 1, 3))
    own_w = (jnp.transpose(w_qkv[0], (1, 0, 2)), w_out[0], w_up[0], w_down[0])

    def sem(count):
        return pltpu.SemaphoreType.DMA((count,))

    def gather(rows):
        gathered = lax.all_gather(rows, "tensor")
        order.tokens = (gathered,)
        return gathered

    def scatter(partial):
        return lax.all_to_all(partial, "tensor", 0, 0)

    other_gain = swap(gains[0], "section", 1)
    own_w, other_gain = lax.optimization_barrier((own_w, other_gain))

    def with_other(weights):
        return tuple(w for own in weights for w in (own, swap(own, "section", 1)))

    attention_w = with_other(own_w[:2])

    first_rows, start_g, gain_g, gain_l = call(
        start_kernel,
        [
            shape((frames, width), low16),
            shape((frames, width), f32),
            shape((2, width), f32),
            shape((2, width), f32),
        ],
        (info, code_rows, gains[0], other_gain),
        [SM, VM, VM, VM],
        us=2,
    )
    first_rows, *attention_w = lax.optimization_barrier((first_rows,) + attention_w)
    attention_w = tuple(attention_w)
    first_blocks = gather(first_rows)
    feed_w = with_other(order.after(own_w[2:]))

    first_g, packed_g, probs_g, mixed_g, mixed_given, partial = call(
        global_attention_kernel,
        [
            shape((rows_g, width), low16),
            shape((3, rows_g, heads_width), low16),
            shape((heads_width // HEAD_DIM, rows_g, rows_g), low16),
            shape((rows_g, heads_width), low16),
            shape((rows_g, half), low16),
            shape((4, frames, width), low16),
        ],
        (info, first_blocks) + attention_w,
        [SM, VM] + [ANY] * 4,
        [
            pltpu.VMEM((3, width, heads_width), low16),
            pltpu.VMEM((heads_width, width), low16),
            sem(8),
        ],
        us=5.7,
        limit=60,
    )
    arrived = scatter(partial)
    mix_piece, mix_whole = call(
        mix_piece_kernel,
        [shape((2, UNIT, UNIT), low16), shape((QUARTERS, 2, UNIT, UNIT), low16)],
        (info,) + attention_w,
        [SM] + [ANY] * 4,
        [sem(5 * QUARTERS)],
        us=3.2,
    )
    mix_z1 = swap(mix_piece, "tensor", 1)
    mix_z2 = swap(mix_piece, "tensor", 2)
    feed_piece, feed_whole = call(
        feed_piece_kernel,
        [shape((4, UNIT, UNIT), low16), shape((QUARTERS, 4, UNIT, UNIT), low16)],
        (info,) + feed_w,
        [SM] + [ANY] * 4,
        [sem(4 * QUARTERS)],
        us=4,
    )
    top_l, top_given = call(
        local_top_kernel,
        [shape((rows_l, width), low16), shape((rows_l // utts, width), low16)],
        (info, cot_rows),
        [SM, VM],
        us=2.3,
    )
    hidden_g, second_rows = call(
        middle_kernel,
        [shape((frames, width), f32), shape((frames, width), low16)],
        (start_g, arrived, gain_g),
        [VM] * 3,
        us=2,
    )
    second_rows, mix_z1, mix_z2, feed_piece = lax.optimization_barrier(
        (second_rows, mix_z1, mix_z2, feed_piece)
    )
    mix_z3 = swap(mix_z2, "tensor", 1)
    second_blocks = gather(second_rows)
    feed_z2 = swap(order.after(feed_piece), "tensor", 2)
    order.until(mix_z3)
    second_g, lifted_g, active_g, active_given, partial = call(
        global_feed_kernel,
        [
            shape((rows_g, width), low16),
            shape((rows_g, wide), f32),
            shape((rows_g, wide), low16),
            shape((rows_g, wide // 2), low16),
            shape((4, frames, width), low16),
        ],
        (info, second_blocks) + feed_w,
        [SM, VM] + [ANY] * 4,
        [
            pltpu.VMEM((width, wide), low16),
            pltpu.VMEM((wide, width), low16),
            pltpu.VMEM((rows_g, width), f32),
            sem(8),
        ],
        us=5.6,
        limit=60,
    )
    arrived = scatter(partial)
    mix_near = jnp.stack(order.after([mix_z1, mix_z2, mix_z3]), axis=1)
    mix_x = swap(mix_near, "dp", 1)
    mix_y = swap(mix_near, "dp", 2)
    mix_far = (swap(mix_x[0], "dp", 2), swap(mix_y[1], "dp", 1))
    order.until(*mix_far, feed_z2)
    sent = call(
        sent_kernel,
        [shape((frames, width), low16)],
        (hidden_g, arrived),
        [VM] * 2,
        us=1.9,
    )[0]
    other_sent = swap(sent, "section", 1)
    mix_w = (mix_whole, mix_z1, mix_z2, mix_z3, mix_x, mix_y) + mix_far
    feed_z2 = order.after(feed_z2)
    feed_x = swap(feed_z2, "dp", 1)
    feed_y = swap(feed_z2, "dp", 2)
    top_same = swap(order.after(top_given), "tensor", 1)

    start_l, first_l, query_keys, values_l, probs_l, mixed_l, partial = call(
        local_attention_kernel,
        [
            shape((rows_l, width), f32),
            shape((rows_l, width), low16),
            shape((4, rows_l, 2 * half), low16),
            shape((4, rows_l, half), low16),
            shape((4, utts, 2 * rows_l // utts, half), low16),
            shape((rows_l, 4 * half), low16),
            shape((rows_l, width), low16),
        ],
        (info, code_rows, sent, other_sent, gain_l) + mix_w,
        [SM] + [VM] * 4 + [ANY] * MIX_REFS,
        [
            pltpu.VMEM((4, 2, width, UNIT), low16),
            pltpu.VMEM((4 * half, width), low16),
            sem(32),
        ],
        us=9,
        limit=60,
    )
    partial, feed_x, feed_y, top_same = lax.optimization_barrier(
        (partial, feed_x, feed_y, top_same)
    )
    feed_l = (
        feed_whole,
        feed_z2,
        feed_x,
        feed_y,
        swap(feed_x[:2], "dp", 2),
        swap(feed_y[2:], "dp", 1),
    )
    hidden_l, second_l, second_given = call(
        local_norm_kernel,
        [
            shape((rows_l, width), f32),
            shape((rows_l, width), low16),
            shape((rows_l // utts, width), low16),
        ],
        (info, start_l, partial, swap(partial, "section", 1), gain_l),
        [SM] + [VM] * 4,
        us=3.7,
    )
    second_same = swap(second_given, "tensor", 1)
    top_cross = swap(top_same, "section", 1)
    feed_scratch = [
        pltpu.VMEM((tiles, width, UNIT), low16),
        pltpu.VMEM((tiles, UNIT, width), low16),
        pltpu.VMEM((rows_l, width), f32),
        sem(8 * tiles),
    ]
    wide_rows = shape((rows_l, width), low16)
    half_rows = shape((rows_l // utts, width), low16)
    tiled_rows = shape((tiles, rows_l, UNIT), low16)
    active_l, grad_lifted_l, back = call(
        local_feed_kernel,
        [tiled_rows, tiled_rows, wide_rows],
        (second_l, top_l) + feed_l,
        [VM] * 2 + [ANY] * FEED_REFS,
        feed_scratch,
        us=7.9,
    )
    other_back = swap(back, "section", 1)
    second_same = order.after(second_same)
    second_cross = swap(second_same, "section", 1)
    far_active, far_lifted, far_second, far_top, same, cross = call(
        far_feed_kernel,
        [tiled_rows, tiled_rows, wide_rows, wide_rows, half_rows, half_rows],
        (second_same, second_cross, top_same, top_cross) + feed_l,
        [VM] * 4 + [ANY] * FEED_REFS,
        feed_scratch,
        us=8.2,
    )

    def from_neighbour(same, cross):
        total = call(
            pair_kernel, [half_rows], (same, cross), [VM] * 2
        )[0]
        return swap(total, "tensor", 1)

    far_same = from_neighbour(same, swap(cross, "section", 1))
    turned_l = pltpu.VMEM((width, rows_l), low16)
    local_feed = Sum(
        order,
        2,
        *call(
            local_feed_grad_kernel,
            [shape((2, 4, UNIT, UNIT), low16)] * 4,
            (
                second_l, far_second, grad_lifted_l, far_lifted, active_l, far_active, top_l,
                far_top,
            ),
            [VM] * 8,
            [pltpu.VMEM((width, 2 * rows_l), low16), pltpu.VMEM((2 * rows_l, width), low16)],
            us=7.6,
        ),
    )
    own_branch, branch_same, branch_cross = call(
        local_drop_kernel,
        [wide_rows, half_rows, half_rows],
        (active_l, far_active) + feed_l,
        [VM] * 2 + [ANY] * FEED_REFS,
        [
            pltpu.VMEM((tiles, UNIT, width), low16),
            pltpu.VMEM((2 * rows_l, width), f32),
            sem(QUARTERS * tiles),
        ],
        us=6.1,
    )
    branch_cross = swap(branch_cross, "section", 1)
    other_branch = swap(own_branch, "section", 1)
    far_same = order.after(far_same)
    far_back = (far_same, swap(far_same, "section", 1))
    far_branch = from_neighbour(branch_same, branch_cross)
    far_first, far_mixed, far_second_g, far_active_g = (
        swap(order.after(value), "section", 1)
        for value in (first_g, mixed_given, second_g, active_given)
    )
    grad_hidden_l, mid_l, grad_query_keys, grad_values, back, gain2_l = call(
        local_attention_back_kernel,
        [
            shape((rows_l, width), f32),
            shape((rows_l, width), low16),
            shape((4, rows_l, 2 * half), low16),
            shape((4, rows_l, half), low16),
            shape((rows_l, width), low16),
            shape((1, width), f32),
        ],
        (info, hidden_l, back, other_back)
        + far_back
        + (top_l, gain_l, query_keys, values_l, probs_l)
        + mix_w,
        [SM] + [VM] * 10 + [ANY] * MIX_REFS,
        [
            pltpu.VMEM((4, 2, width, UNIT), low16),
            pltpu.VMEM((4 * half, width), low16),
            pltpu.VMEM((rows_l, width), f32),
            sem(32),
        ],
        us=11.4,
        limit=60,
    )
    other_back = swap(back, "section", 1)
    order.until(far_branch)
    local_mix = Sum(
        order,
        4,
        *call(
            local_mix_kernel,
            [shape((2, 4, UNIT, UNIT), low16)] * 4,
            (first_l, grad_query_keys, grad_values, mixed_l, mid_l),
            [VM] * 5,
            [turned_l],
            us=6,
        ),
    )
    returned, code_part, gain1_l = call(
        local_end_kernel,
        [
            shape((frames, width), low16),
            shape((utts, code_count, frames, width // 2), f32),
            shape((1, width), f32),
        ],
        (info, back, other_back, start_l, grad_hidden_l, gain_l),
        [SM] + [VM] * 5,
        [pltpu.VMEM((rows_l, width), f32)],
        us=4.4,
    )

    top_blocks = gather(returned)
    local_feed.second()
    order.until(*local_mix.once, far_first, far_mixed, far_second_g, far_active_g)
    top_g, grad_lifted_g, lifted_given, partial = call(
        global_feed_back_kernel,
        [
            shape((rows_g, width), low16),
            shape((rows_g, wide), low16),
            shape((rows_g, wide // 2), low16),
            shape((4, frames, width), low16),
        ],
        (info, top_blocks, lifted_g) + feed_w,
        [SM] + [VM] * 2 + [ANY] * 4,
        [
            pltpu.VMEM((width, wide), low16),
            pltpu.VMEM((wide, width), low16),
            pltpu.VMEM((rows_g, width), f32),
            sem(8),
        ],
        us=6.3,
        limit=28,
    )
    arrived = scatter(partial)
    far_top_g, far_lifted_g = swap(top_g, "section", 1), swap(lifted_given, "section", 1)
    local_feed.third()
    local_mix.second()
    far_branch = order.after(far_branch)
    far_branch = (far_branch, swap(far_branch, "section", 1))
    global_feed = Sum(
        order,
        1,
        *call(
            global_feed_grad_kernel,
            [shape((2, 2, UNIT, UNIT), low16)] * 4,
            (
                info, second_g, far_second_g, grad_lifted_g, far_lifted_g, active_g, far_active_g,
                top_g, far_top_g,
            ),
            [SM] + [VM] * 8,
            [pltpu.VMEM((width, 2 * rows_g), low16), pltpu.VMEM((2 * rows_g, width), low16)],
            us=3.5,
        ),
    )
    grad_hidden_g, mid_rows, gain2_g = call(
        middle_back_kernel,
        [shape((frames, width), f32), shape((frames, width), low16), shape((1, width), f32)],
        (arrived, hidden_g, gain_g, returned),
        [VM] * 4,
        us=2.1,
    )
    mid_blocks = gather(mid_rows)
    order.until(*local_mix.twice)
    mid_g, grads_g, grads_given, partial = call(
        global_attention_back_kernel,
        [
            shape((rows_g, width), low16),
            shape((3, rows_g, heads_width), low16),
            shape((3, rows_g, half), low16),
            shape((4, frames, width), low16),
        ],
        (info, mid_blocks, packed_g, probs_g) + attention_w,
        [SM] + [VM] * 3 + [ANY] * 4,
        [
            pltpu.VMEM((3, width, heads_width), low16),
            pltpu.VMEM((heads_width, width), low16),
            sem(8),
        ],
        us=6.8,
        limit=60,
    )
    arrived = scatter(partial)
    far_mid_g, far_grads_g = swap(mid_g, "section", 1), swap(grads_given, "section", 1)
    global_feed.second()
    local_mix.third()
    global_mix = Sum(
        order,
        1,
        *call(
            global_mix_grad_kernel,
            [shape((2, 1, UNIT, UNIT), low16)] * 4,
            (
                info, first_g, far_first, grads_g, far_grads_g, mixed_g, far_mixed, mid_g,
                far_mid_g,
            ),
            [SM] + [VM] * 8,
            [pltpu.VMEM((width, 2 * rows_g), low16), pltpu.VMEM((2 * rows_g, width), low16)],
            us=3,
        ),
    )
    kept_start, given_start, gain1_g = call(
        start_back_kernel,
        [
            shape((frames, width // 2), f32),
            shape((frames, width // 2), f32),
            shape((1, width), f32),
        ],
        (info, arrived, start_g, gain_g, grad_hidden_g),
        [SM] + [VM] * 4,
        [pltpu.VMEM((frames, width), f32)],
        us=2.1,
    )
    world_feed = global_feed.third()
    global_mix.second()
    local_mix.fourth()
    world_mix = global_mix.third()
    feed_sum = local_feed.gathered(info, world_feed)
    arrived_start = swap(given_start, "section", 1)
    both_start = jnp.stack(
        [
            jnp.where(first_core, kept_start, arrived_start),
            jnp.where(first_core, arrived_start, kept_start),
        ]
    )
    code_grad = jnp.transpose(code_part + both_start[:, None], (0, 2, 1, 3))

    own_gain = jnp.concatenate([gain1_g, gain2_g], axis=0)
    total_gain = own_gain + swap(own_gain, "section", 1)
    local_gain = jnp.concatenate([gain1_l, gain2_l], axis=0)
    gain_total = jnp.where(first_core, total_gain, local_gain)
    gain_total = jnp.concatenate(
        [
            lax.dynamic_slice_in_dim(gain_total, (low ^ m) * UNIT, UNIT, 1)
            for m in range(QUARTERS)
        ],
        axis=1,
    )
    def over(value, axis):
        copies = jnp.broadcast_to(value, (lax.axis_size(axis),) + value.shape)
        return jnp.sum(lax.all_to_all(order.after(copies), axis, 0, 0), axis=0)

    gain_total = over(gain_total, "tensor")
    order.until(gain_total)
    packed_gain = call(
        gain_pack_kernel, [shape((GAIN_ROWS, UNIT), low16)], (gain_total,), [VM], us=0.7
    )[0]
    mix_sum = local_mix.gathered(info, world_mix, packed_gain)
    output = call(
        output_kernel,
        [shape((utts, code_count, frames, width // 2), low16)],
        (info, hidden_l, own_branch, other_branch) + far_branch,
        [SM] + [VM] * 5,
        us=3.1,
    )[0]
    order.until(*feed_sum.near)
    feed_parts = feed_sum.far()
    def finals(count, rows, columns):
        return [
            pltpu.VMEM((count,) + rows, f32), pltpu.VMEM((count,) + columns, f32), sem(2 * count)
        ]

    feed_shapes = [shape((width, wide), f32), shape((wide, width), f32)]
    mix_shapes = [shape((3, width, heads_width), f32), shape((heads_width, width), f32)]
    feed_part = ((UNIT, wide), (wide, UNIT))
    mix_part = ((3, UNIT, heads_width), (heads_width, UNIT))
    feed_grads = call(
        feed_near_kernel,
        feed_shapes,
        (info,) + feed_parts[:3],
        [SM] + [VM] * 3,
        finals(3, *feed_part),
        us=5,
        place=ANY,
    )
    mix_sum.near = order.after(mix_sum.near)
    mix_parts = mix_sum.far()
    mix_grads = call(
        mix_near_kernel,
        mix_shapes,
        (info,) + mix_parts[:3],
        [SM] + [VM] * 3,
        finals(3, *mix_part),
        us=3,
        place=ANY,
    )
    up_grad, down_grad = call(
        feed_far_kernel,
        feed_shapes,
        (info,) + feed_parts[3:] + tuple(feed_grads),
        [SM] + [VM] * 2 + [ANY] * 2,
        finals(1, *feed_part),
        us=2,
        place=ANY,
        aliases=((3, 0), (4, 1)),
    )
    qkv_grad, out_grad, gain_total = call(
        mix_far_kernel,
        mix_shapes + [shape((2, width), f32)],
        (info,) + mix_parts + tuple(mix_grads),
        [SM] + [VM] * 5 + [ANY] * 2,
        finals(1, *mix_part),
        us=1.5,
        place=(ANY, ANY, VM),
        aliases=((6, 0), (7, 1)),
    )
    step = QUARTERS
    while step < lax.axis_size("dp"):
        gain_total = gain_total + swap(gain_total, "dp", step)
        step *= 2
    return (
        jnp.transpose(output, (0, 2, 1, 3)),
        code_grad,
        gain_total[None],
        jnp.transpose(qkv_grad, (1, 0, 2))[None],
        out_grad[None],
        up_grad[None],
        down_grad[None],
    )


def solution(mesh):
    in_specs = (
        P("dp", "tensor", None, None),
        P("dp"),
        P("section", None, None),
        P("section", None, None, "tensor"),
        P("section", "tensor", None),
        P("section", None, "tensor"),
        P("section", "tensor", None),
        P("dp", "tensor", None, None),
    )
    out_specs = (
        P("dp", "tensor", None, "section"),
        P("dp", "tensor", None, "section"),
        P("section", None, None),
        P("section", None, None, "tensor"),
        P("section", "tensor", None),
        P("section", None, "tensor"),
        P("section", "tensor", None),
    )
    return jax.shard_map(
        on_device, mesh=mesh, in_specs=in_specs, out_specs=out_specs, check_vma=False
    )
```
